32 devices in a mesh: rep: 4 (over y, x), seq: 4 (over z), grp: 2 (over core).
Axes of the slice: x: 2, y: 2, z: 4, core: 2. Of those that a mesh axis runs over, the one named last changes fastest.
Arguments:
- tokens: bfloat16 [8192, 768], P(('rep', 'seq', 'grp')), may hold values from -24 to 24
- cotangent: bfloat16 [8192, 768], P(('rep', 'seq', 'grp')), may hold values from -6 to 6
- item_lengths: int32 [4, 4], P('rep'), may hold values from 64 to 1792, as said below
- qkv_weight: float32 [768, 2304], P(('seq', 'grp')), may hold values from -0.3125 to 0.3125
- qkv_first: float32 [768, 2304], P(('seq', 'grp')), may hold values from -0.00061035156 to 0.00061035156
- qkv_second: float32 [768, 2304], P(('seq', 'grp')), may hold values from 7.064254e-11 to 1.1302806e-09
- out_weight: float32 [768, 768], P(('seq', 'grp')), may hold values from -0.21875 to 0.21875
- out_first: float32 [768, 768], P(('seq', 'grp')), may hold values from -0.00061035156 to 0.00061035156
- out_second: float32 [768, 768], P(('seq', 'grp')), may hold values from 7.064254e-11 to 1.1302806e-09
- up_weight: float32 [768, 3072], P(('seq', 'grp')), may hold values from -0.21875 to 0.21875
- up_first: float32 [768, 3072], P(('seq', 'grp')), may hold values from -0.00061035156 to 0.00061035156
- up_second: float32 [768, 3072], P(('seq', 'grp')), may hold values from 7.064254e-11 to 1.1302806e-09
- down_weight: float32 [3072, 768], P(('seq', 'grp')), may hold values from -0.109375 to 0.109375
- down_first: float32 [3072, 768], P(('seq', 'grp')), may hold values from -0.00061035156 to 0.00061035156
- down_second: float32 [3072, 768], P(('seq', 'grp')), may hold values from 7.064254e-11 to 1.1302806e-09
- norm_params: float32 [4, 768], P(None, ('seq', 'grp')), may hold values from -1.2 to 2.4, as said below
- norm_first: float32 [4, 768], P(None, ('seq', 'grp')), may hold values from -0.001953125 to 0.001953125
- norm_second: float32 [4, 768], P(None, ('seq', 'grp')), may hold values from 6.3578287e-10 to 1.0172526e-08
- conv_kernel: float32 [12, 33], replicated, may hold values from -1 to 1
- conv_first: float32 [12, 33], replicated, may hold values from -0.005859375 to 0.005859375
- conv_second: float32 [12, 33], replicated, may hold values from 7.064254e-09 to 1.13028065e-07
Outputs:
- output: bfloat16 [8192, 768], P(('rep', 'seq', 'grp'))
- input_grad: bfloat16 [8192, 768], P(('rep', 'seq', 'grp'))
- grad_norm: float32 [], replicated
- qkv_new: float32 [768, 2304], P(('seq', 'grp'))
- qkv_first_new: float32 [768, 2304], P(('seq', 'grp'))
- qkv_second_new: float32 [768, 2304], P(('seq', 'grp'))
- out_new: float32 [768, 768], P(('seq', 'grp'))
- out_first_new: float32 [768, 768], P(('seq', 'grp'))
- out_second_new: float32 [768, 768], P(('seq', 'grp'))
- up_new: float32 [768, 3072], P(('seq', 'grp'))
- up_first_new: float32 [768, 3072], P(('seq', 'grp'))
- up_second_new: float32 [768, 3072], P(('seq', 'grp'))
- down_new: float32 [3072, 768], P(('seq', 'grp'))
- down_first_new: float32 [3072, 768], P(('seq', 'grp'))
- down_second_new: float32 [3072, 768], P(('seq', 'grp'))
- norm_new: float32 [4, 768], P(None, ('seq', 'grp'))
- norm_first_new: float32 [4, 768], P(None, ('seq', 'grp'))
- norm_second_new: float32 [4, 768], P(None, ('seq', 'grp'))
- conv_new: float32 [12, 33], replicated
- conv_first_new: float32 [12, 33], replicated
- conv_second_new: float32 [12, 33], replicated
The draws below stay inside these ranges and needn't reach their ends.
Inputs may be any that keep to these rules, and one draw needn't show every extreme that they name: `item_lengths`: items 0, 2 and 3 have 64 to 96 tokens: one of them exactly 96, the other two together 64 + 96; item 1 takes the rest of the group's 2048 tokens, 1792. `norm_params`: rows 0 and 2 are positive gains.
All inputs are finite; a program needn't handle non-finite values.
Results may differ from the reference program's by a relative error of at most 0.018.
Values may be sent and summed in bfloat16 or wider, within the bound.
A program may use at most 256 MiB of HBM per device.

```python
import math
import jax
import jax.numpy as jnp
from jax import lax

D = 768
HEADS = 12
HEAD = 64
FF = 3072
LAND = 64
KERNEL = 33
HALO = 16
NS_STEPS = 6
ITEMS = 4
STEP = 10
GROUP = 2048
TOKENS = 8192
SHORT_MAX = 96
N_REP = 4


def draw_tokens(key, part):
    key = jax.random.fold_in(key, 11)
    key_period, key_phase, key_vector, key_rough = jax.random.split(key, 4)
    positions = jnp.arange(TOKENS, dtype=jnp.int32)
    group_ids = positions // GROUP
    local_pos = (positions % GROUP).astype(jnp.float32)
    periods = GROUP * jnp.exp(jax.random.uniform(key_period, (8,), minval=math.log(min(8.0 / LAND, 0.5)), maxval=0.0))
    phases = jax.random.uniform(key_phase, (N_REP, 8), minval=0.0, maxval=2.0 * math.pi)
    vectors = jnp.clip(jax.random.normal(key_vector, (8, D)), -3.0, 3.0)
    smooth = jnp.zeros((TOKENS, D), jnp.float32)
    for wave_idx in range(8):
        phase_now = local_pos * (2.0 * math.pi / periods[wave_idx]) + phases[group_ids, wave_idx]
        smooth = smooth + jnp.cos(phase_now)[:, None] * vectors[wave_idx][None, :]
    smooth = smooth * 0.5
    ramp_line = jnp.arange(D, dtype=jnp.float32) / D
    rough_part = jnp.clip(jax.random.normal(key_rough, (TOKENS, D)), -4.0, 4.0)
    column_scale = 0.5 + ramp_line
    return ((0.6 * rough_part + 0.8 * smooth) * column_scale[None, :]).astype(jnp.bfloat16)


def draw_item_lengths(key, part):
    key = jax.random.fold_in(key, 5)
    key_short, key_slot = jax.random.split(key, 2)
    split_len = jax.random.randint(key_short, (N_REP,), LAND, SHORT_MAX + 1).astype(jnp.int32)
    other_len = (LAND + SHORT_MAX - split_len).astype(jnp.int32)
    forced_slot = jax.random.randint(key_slot, (N_REP,), 0, 3).astype(jnp.int32)
    triple = jnp.stack([jnp.full((N_REP,), SHORT_MAX, jnp.int32), split_len, other_len], axis=1)
    order = (jnp.arange(3, dtype=jnp.int32)[None, :] - forced_slot[:, None]) % 3
    shorts = jnp.take_along_axis(triple, order, axis=1).astype(jnp.int32)
    longest = (GROUP - 2 * SHORT_MAX - LAND) * jnp.ones((N_REP, 1), jnp.int32)
    return jnp.concatenate([shorts[:, :1], longest, shorts[:, 1:]], axis=1).astype(jnp.int32)


def draw_norm_params(key, part):
    key = jax.random.fold_in(key, 7)
    key_gain, key_shift = jax.random.split(key, 2)
    ramp_line = jnp.arange(D, dtype=jnp.float32) / D
    rising = 0.5 + ramp_line
    jitter = jax.random.uniform(key_gain, (2, D), minval=0.8, maxval=1.2)
    gains = rising[None, :] * jitter
    shifts = jnp.clip(0.3 * jax.random.normal(key_shift, (2, D)), -1.2, 1.2)
    return jnp.stack([gains[0], shifts[0], gains[1], shifts[1]]).astype(jnp.float32)


def block_scale(rng, dims, cuts, least, high):
    level = 1.0
    for position, shards_of in cuts:
        steps = jax.random.uniform(jax.random.fold_in(jax.random.fold_in(rng, 6), position), (shards_of,), jnp.float32, least / len(cuts), high / len(cuts))
        level = level * jnp.repeat(jnp.exp(steps), dims[position] // shards_of).reshape((-1,) + (1,) * (len(dims) - 1 - position))
    return level


def noise(stream_key, shape, width, most, shards=(), kind=jnp.bfloat16):
    values = width * jax.random.normal(stream_key, shape, jnp.float32)
    if shards:
        values = values * block_scale(stream_key, shape, shards, -0.22, 0.18)
    return jnp.clip(values, -most, most).astype(kind)


def setup_inputs(seed: int = 0) -> dict:
    arg_keys = jax.random.split(jax.random.key(seed), 22)
    tokens = draw_tokens(jax.random.fold_in(arg_keys[21], 71), 0)
    cotangent = noise(arg_keys[1], (TOKENS, D), 1.0, 6.0, ((0, 32),))
    item_lengths = draw_item_lengths(jax.random.fold_in(arg_keys[21], 71), 0)
    qkv_weight = noise(arg_keys[3], (D, 3 * D), (D // 2) ** -0.5, 0.3125, ((0, 8),), jnp.float32)
    qkv_first = noise(arg_keys[4], (D, 3 * D), (0.11 / (4 * D * D + 2 * D * FF) ** 0.5), 0.00061035156, ((0, 8),), jnp.float32)
    qkv_second = jnp.clip(jnp.exp(math.log(1.130280646854942e-09) - 2.7725887 * jax.random.uniform(arg_keys[5], (D, 3 * D), jnp.float32) ** block_scale(arg_keys[5], (D, 3 * D), ((0, 8),), -0.2, 0.2)), 7.064254042843388e-11, 1.130280646854942e-09)
    out_weight = noise(arg_keys[6], (D, D), D ** -0.5, 0.21875, ((0, 8),), jnp.float32)
    out_first = noise(arg_keys[7], (D, D), (0.11 / (4 * D * D + 2 * D * FF) ** 0.5), 0.00061035156, ((0, 8),), jnp.float32)
    out_second = jnp.clip(jnp.exp(math.log(1.130280646854942e-09) - 2.7725887 * jax.random.uniform(arg_keys[8], (D, D), jnp.float32) ** block_scale(arg_keys[8], (D, D), ((0, 8),), -0.2, 0.2)), 7.064254042843388e-11, 1.130280646854942e-09)
    up_weight = noise(arg_keys[9], (D, FF), D ** -0.5, 0.21875, ((0, 8),), jnp.float32)
    up_first = noise(arg_keys[10], (D, FF), (0.11 / (4 * D * D + 2 * D * FF) ** 0.5), 0.00061035156, ((0, 8),), jnp.float32)
    up_second = jnp.clip(jnp.exp(math.log(1.130280646854942e-09) - 2.7725887 * jax.random.uniform(arg_keys[11], (D, FF), jnp.float32) ** block_scale(arg_keys[11], (D, FF), ((0, 8),), -0.2, 0.2)), 7.064254042843388e-11, 1.130280646854942e-09)
    down_weight = noise(arg_keys[12], (FF, D), FF ** -0.5, 0.109375, ((0, 8),), jnp.float32)
    down_first = noise(arg_keys[13], (FF, D), (0.11 / (4 * D * D + 2 * D * FF) ** 0.5), 0.00061035156, ((0, 8),), jnp.float32)
    down_second = jnp.clip(jnp.exp(math.log(1.130280646854942e-09) - 2.7725887 * jax.random.uniform(arg_keys[14], (FF, D), jnp.float32) ** block_scale(arg_keys[14], (FF, D), ((0, 8),), -0.2, 0.2)), 7.064254042843388e-11, 1.130280646854942e-09)
    norm_params = draw_norm_params(jax.random.fold_in(arg_keys[21], 71), 0)
    norm_first = noise(arg_keys[16], (4, D), (0.33 / (4 * D * D + 2 * D * FF) ** 0.5), 0.001953125, ((1, 8),), jnp.float32)
    norm_second = jnp.clip(jnp.exp(math.log(1.017252593271678e-08) - 2.7725887 * jax.random.uniform(arg_keys[17], (4, D), jnp.float32) ** block_scale(arg_keys[17], (4, D), ((1, 8),), -0.2, 0.2)), 6.357828707947988e-10, 1.017252593271678e-08)
    conv_kernel = noise(arg_keys[18], (HEADS, KERNEL), KERNEL ** -0.5, 1.0, (), jnp.float32)
    conv_first = noise(arg_keys[19], (HEADS, KERNEL), (1.1 / (4 * D * D + 2 * D * FF) ** 0.5), 0.005859375, (), jnp.float32)
    conv_second = jnp.clip(jnp.exp(jax.random.uniform(arg_keys[20], (HEADS, KERNEL), jnp.float32, math.log(7.064254070598963e-09), math.log(1.1302806512958341e-07))), 7.064254070598963e-09, 1.1302806512958341e-07)
    return {"tokens": tokens, "cotangent": cotangent, "item_lengths": item_lengths, "qkv_weight": qkv_weight, "qkv_first": qkv_first, "qkv_second": qkv_second, "out_weight": out_weight, "out_first": out_first, "out_second": out_second, "up_weight": up_weight, "up_first": up_first, "up_second": up_second, "down_weight": down_weight, "down_first": down_first, "down_second": down_second, "norm_params": norm_params, "norm_first": norm_first, "norm_second": norm_second, "conv_kernel": conv_kernel, "conv_first": conv_first, "conv_second": conv_second}


HIGHEST_PREC = lax.Precision.HIGHEST
EPS_NORM = 1e-05
BETA_ONE = 0.9
BETA_TWO = 0.999
ADAM_EPS = 1e-08
RATE_MATRIX = 0.02
RATE_NORM = 0.3
RATE_CONV = 0.1
DECAY_RATE = 0.01
MAX_NORM = 1.0

@jax.custom_vjp
def low(v):
    return lax.optimization_barrier(v.astype(jnp.bfloat16)).astype(jnp.float32)

@jax.custom_vjp
def low_back(v):
    return v

def low_keep(v):
    return (low(v), None)

def low_pass(kept, grad):
    return (grad,)

def back_keep(v):
    return (v, None)

def back_low(kept, grad):
    return (low(grad),)
low.defvjp(low_keep, low_pass)
low_back.defvjp(back_keep, back_low)

def locate(positions, lengths):
    ends = jnp.cumsum(lengths).astype(jnp.int32)
    starts = (ends - lengths).astype(jnp.int32)
    inside = (positions[:, None] >= starts[None, :]) & (positions[:, None] < ends[None, :])
    item_ids = lax.optimization_barrier(jnp.sum((positions[:, None] >= ends[None, :]).astype(jnp.int32), axis=1)).astype(jnp.int32)
    valid = (positions >= 0) & (positions < ends[-1])
    item_ids = jnp.where(valid, item_ids, -1).astype(jnp.int32)
    own_len = lax.optimization_barrier(jnp.sum(jnp.where(inside, lengths[None, :], 0), axis=1)).astype(jnp.int32)
    own_start = lax.optimization_barrier(jnp.sum(jnp.where(inside, starts[None, :], 0), axis=1)).astype(jnp.int32)
    segment = (positions - own_start) * LAND // jnp.maximum(own_len, 1)
    columns = jnp.where(valid, item_ids * LAND + segment, -1).astype(jnp.int32)
    return (item_ids, columns)

def landmark_counts(lengths):
    marks = jnp.arange(LAND + 1, dtype=jnp.int32)
    edges = (marks[None, :] * lengths[:, None] + LAND - 1) // LAND
    return (edges[:, 1:] - edges[:, :-1]).reshape(-1).astype(jnp.int32)

def layer_norm(hidden, gain_row, shift_row):
    row_mean = lax.optimization_barrier(jnp.mean(hidden, axis=-1, keepdims=True))
    centred = hidden - row_mean
    variance = lax.optimization_barrier(jnp.mean(centred * centred, axis=-1, keepdims=True))
    return centred * lax.rsqrt(variance + EPS_NORM) * gain_row + shift_row

def mixing(mean_q, mean_k, num_all, den_all):
    temper = HEAD ** (-0.5)
    key_values = num_all.reshape(ITEMS, LAND, HEADS, HEAD) / den_all.reshape(ITEMS, LAND, HEADS)[..., None]
    query_marks = mean_q.reshape(ITEMS, LAND, HEADS, HEAD)
    key_marks = mean_k.reshape(ITEMS, LAND, HEADS, HEAD)
    kernel_two = jax.nn.softmax(jnp.einsum('ajhd,akhd->ahjk', query_marks, key_marks, precision=HIGHEST_PREC) * temper, axis=-1)
    frobenius = lax.optimization_barrier(jnp.sum(kernel_two * kernel_two, axis=(2, 3), keepdims=True))
    inverse = jnp.swapaxes(kernel_two, 2, 3) / frobenius
    identity = jnp.eye(LAND, dtype=kernel_two.dtype)
    for iteration in range(NS_STEPS):
        product = jnp.einsum('ahjk,ahkl->ahjl', kernel_two, inverse, precision=HIGHEST_PREC)
        inner = 7.0 * identity - product
        inner = 15.0 * identity - jnp.einsum('ahjk,ahkl->ahjl', product, inner, precision=HIGHEST_PREC)
        inner = 13.0 * identity - jnp.einsum('ahjk,ahkl->ahjl', product, inner, precision=HIGHEST_PREC)
        inverse = 0.25 * jnp.einsum('ahjk,ahkl->ahjl', inverse, inner, precision=HIGHEST_PREC)
    mixed_rows = jnp.einsum('ahjk,akhd->ajhd', inverse, key_values, precision=HIGHEST_PREC)
    return mixed_rows.reshape(ITEMS * LAND, HEADS * HEAD)

def key_block(mean_q, key_blk, value_blk, member_blk):
    temper = HEAD ** (-0.5)
    col_total = ITEMS * LAND
    query_marks = mean_q.reshape(col_total, HEADS, HEAD)
    scores = low_back(jnp.einsum('chd,phd->chp', query_marks, key_blk, precision=HIGHEST_PREC) * temper)
    weights_exp = jnp.exp(scores) * jnp.transpose(member_blk)[:, None, :]
    num_blk = jnp.einsum('chp,phd->chd', low(weights_exp), value_blk, precision=HIGHEST_PREC).reshape(col_total, HEADS * HEAD)
    return (num_blk, lax.optimization_barrier(jnp.sum(weights_exp, axis=2)))

def token_block(mean_k, mixed_rows, conv_vals, query_blk, value_ext, item_ext, member_blk):
    temper = HEAD ** (-0.5)
    col_total = ITEMS * LAND
    block = query_blk.shape[0]
    key_marks = mean_k.reshape(col_total, HEADS, HEAD)
    scores = low_back(jnp.einsum('phd,chd->phc', query_blk, key_marks, precision=HIGHEST_PREC) * temper)
    weights_exp = jnp.exp(scores) * member_blk[:, None, :]
    attn_probs = low(weights_exp / lax.optimization_barrier(jnp.sum(weights_exp, axis=2, keepdims=True)))
    attended = jnp.einsum('phc,chd->phd', attn_probs, mixed_rows.reshape(col_total, HEADS, HEAD), precision=HIGHEST_PREC).reshape(block, HEADS * HEAD)
    channel_taps = jnp.repeat(conv_vals, HEAD, axis=0)
    item_mid = item_ext[HALO:HALO + block]
    conv_out = jnp.zeros((block, HEADS * HEAD), attended.dtype)
    for offset in range(KERNEL):
        same_item = (item_ext[offset:offset + block] == item_mid).astype(attended.dtype)
        conv_out = conv_out + value_ext[offset:offset + block] * (channel_taps[:, offset][None, :] * same_item[:, None])
    return attended + conv_out

def group_layer(rows_in, lengths, weights):
    col_total = ITEMS * LAND
    block = min(4096, GROUP)
    block_count = GROUP // block
    positions = jnp.arange(GROUP, dtype=jnp.int32)
    item_ids, columns = locate(positions, lengths)
    col_ids = jnp.arange(col_total, dtype=jnp.int32)
    col_hot = (columns[:, None] == col_ids[None, :]).astype(rows_in.dtype)
    member = (item_ids[:, None] == (col_ids // LAND)[None, :]).astype(rows_in.dtype)
    counts_f = landmark_counts(lengths).astype(rows_in.dtype)
    item_pad = jnp.pad(item_ids, (HALO, HALO), constant_values=-1)
    item_blocks = jnp.stack([item_pad[block_idx * block:block_idx * block + block + 2 * HALO] for block_idx in range(block_count)])
    member_blocks = member.reshape(block_count, block, col_total)

    def forward(x_rows, w_qkv, w_out, w_up, w_down, norm_vals, conv_vals):
        projected = low_back(jnp.dot(x_rows, w_qkv, precision=HIGHEST_PREC))
        queries = low(projected[:, :D])
        key_rows = low(projected[:, D:2 * D])
        value_rows = low(projected[:, 2 * D:])
        land_sums = jnp.dot(jnp.transpose(col_hot), jnp.concatenate([queries, key_rows], axis=1), precision=HIGHEST_PREC)
        mean_q = low(land_sums[:, :D] / counts_f[:, None])
        mean_k = low(land_sums[:, D:] / counts_f[:, None])
        key_blocks = key_rows.reshape(block_count, block, HEADS, HEAD)
        value_blocks = value_rows.reshape(block_count, block, HEADS, HEAD)
        num_parts, den_parts = lax.map(lambda block_parts: jax.checkpoint(key_block)(mean_q, block_parts[0], block_parts[1], block_parts[2]), (key_blocks, value_blocks, member_blocks))
        mixed_rows = low(mixing(mean_q, mean_k, lax.optimization_barrier(jnp.sum(num_parts, axis=0)), lax.optimization_barrier(jnp.sum(den_parts, axis=0))))
        query_blocks = queries.reshape(block_count, block, HEADS, HEAD)
        value_pad = jnp.pad(value_rows, ((HALO, HALO), (0, 0)))
        value_blocks_ext = jnp.stack([value_pad[block_idx * block:block_idx * block + block + 2 * HALO] for block_idx in range(block_count)])
        attended = lax.map(lambda block_parts: jax.checkpoint(token_block)(mean_k, mixed_rows, conv_vals, block_parts[0], block_parts[1], block_parts[2], block_parts[3]), (query_blocks, value_blocks_ext, item_blocks, member_blocks))
        branch = low(low_back(attended.reshape(GROUP, D)))
        attn_out = low_back(jnp.dot(branch, w_out, precision=HIGHEST_PREC))
        normed_one = layer_norm(x_rows + attn_out, norm_vals[0], norm_vals[1])
        up_out = low_back(jnp.dot(low(normed_one), w_up, precision=HIGHEST_PREC))
        down_out = low_back(jnp.dot(low(jax.nn.gelu(up_out, approximate=False)), w_down, precision=HIGHEST_PREC))
        return layer_norm(normed_one + down_out, norm_vals[2], norm_vals[3])
    return jax.vjp(forward, rows_in, *weights)

def adamw(weight, moment_one, moment_two, gradient, clip_factor, rate_value, decay_value):
    clipped = gradient * clip_factor
    moment_one = BETA_ONE * moment_one + (1.0 - BETA_ONE) * clipped
    moment_two = BETA_TWO * moment_two + (1.0 - BETA_TWO) * clipped * clipped
    first_hat = moment_one / (1.0 - BETA_ONE ** STEP)
    second_hat = moment_two / (1.0 - BETA_TWO ** STEP)
    weight = weight - rate_value * (first_hat / (jnp.sqrt(second_hat) + ADAM_EPS) + decay_value * weight)
    return (weight, moment_one, moment_two)

def reference(tokens, cotangent, item_lengths, qkv_weight, qkv_first, qkv_second, out_weight, out_first, out_second, up_weight, up_first, up_second, down_weight, down_first, down_second, norm_params, norm_first, norm_second, conv_kernel, conv_first, conv_second):
    masters = (qkv_weight, out_weight, up_weight, down_weight, norm_params)
    rounded = tuple((master.astype(jnp.bfloat16).astype(jnp.float32) for master in masters)) + (conv_kernel,)
    outputs = []
    input_grads = []
    totals = None
    for group_idx in range(N_REP):
        rows_in = tokens[group_idx * GROUP:(group_idx + 1) * GROUP].astype(jnp.float32)
        result, pullback = group_layer(rows_in, item_lengths[group_idx].astype(jnp.int32), rounded)
        grads = pullback(cotangent[group_idx * GROUP:(group_idx + 1) * GROUP].astype(jnp.float32))
        outputs.append(result.astype(jnp.bfloat16))
        input_grads.append(grads[0].astype(jnp.bfloat16))
        totals = grads[1:] if totals is None else tuple((left + right for left, right in zip(totals, grads[1:])))
    squares = sum((jnp.sum(gradient * gradient) for gradient in totals))
    grad_norm = jnp.sqrt(squares)
    clip_factor = MAX_NORM / jnp.maximum(grad_norm, MAX_NORM)
    qkv_new = adamw(qkv_weight, qkv_first, qkv_second, totals[0], clip_factor, RATE_MATRIX, DECAY_RATE)
    out_new = adamw(out_weight, out_first, out_second, totals[1], clip_factor, RATE_MATRIX, DECAY_RATE)
    up_new = adamw(up_weight, up_first, up_second, totals[2], clip_factor, RATE_MATRIX, DECAY_RATE)
    down_new = adamw(down_weight, down_first, down_second, totals[3], clip_factor, RATE_MATRIX, DECAY_RATE)
    norm_new = adamw(norm_params, norm_first, norm_second, totals[4], clip_factor, RATE_NORM, 0.0)
    conv_new = adamw(conv_kernel, conv_first, conv_second, totals[5], clip_factor, RATE_CONV, 0.0)
    return (jnp.concatenate(outputs, axis=0), jnp.concatenate(input_grads, axis=0), grad_norm, qkv_new[0], qkv_new[1], qkv_new[2], out_new[0], out_new[1], out_new[2], up_new[0], up_new[1], up_new[2], down_new[0], down_new[1], down_new[2], norm_new[0], norm_new[1], norm_new[2], conv_new[0], conv_new[1], conv_new[2])
```

```python
import jax
import jax.numpy as jnp
from jax import lax
from jax.experimental import pallas as pl
from jax.experimental.pallas import tpu as pltpu
from jax.sharding import PartitionSpec as P

D = 768
FF = 3072
HEADS = 12
HEAD = 64
LAND = 64
KERNEL = 33
HALO = 16
NS_STEPS = 6
ITEMS = 4
STEP = 10
TOK_DEV = 256
HIGHEST_PREC = lax.Precision.HIGHEST
EPS_NORM = 1e-05
BETA_ONE = 0.9
BETA_TWO = 0.999
ADAM_EPS = 1e-08
RATE_MATRIX = 0.02
RATE_NORM = 0.3
RATE_CONV = 0.1
DECAY_RATE = 0.01
MAX_NORM = 1.0


def extended(cells, sides, width):
    for axis, dim in sides:
        count = lax.axis_size(axis)
        ends = count - 1
        head = lax.slice_in_dim(cells, 0, width, axis=dim)
        tail = lax.slice_in_dim(cells, cells.shape[dim] - width, cells.shape[dim], axis=dim)
        cells = jnp.concatenate(
            [
                lax.ppermute(tail, axis, [(i, (i + 1) % count) for i in range(ends)]),
                cells,
                lax.ppermute(head, axis, [((i + 1) % count, i) for i in range(ends)]),
            ],
            axis=dim,
        )
    return cells


def locate(positions, lengths):
    ends = jnp.cumsum(lengths)
    starts = ends - lengths
    inside = (positions[:, None] >= starts[None, :]) & (positions[:, None] < ends[None, :])
    item_ids = jnp.sum((positions[:, None] >= ends[None, :]).astype(jnp.int32), axis=1)
    valid = (positions >= 0) & (positions < ends[-1])
    item_ids = jnp.where(valid, item_ids, -1)
    own_len = jnp.sum(jnp.where(inside, lengths[None, :], 0), axis=1)
    own_start = jnp.sum(jnp.where(inside, starts[None, :], 0), axis=1)
    segment = (positions - own_start) * LAND // jnp.maximum(own_len, 1)
    columns = jnp.where(valid, item_ids * LAND + segment, -1)
    return (item_ids, columns)


def landmark_counts(lengths):
    marks = jnp.arange(LAND + 1, dtype=jnp.int32)
    edges = (marks[None, :] * lengths[:, None] + LAND - 1) // LAND
    return (edges[:, 1:] - edges[:, :-1]).reshape(-1)


def layer_norm(hidden, gain_row, shift_row):
    row_mean = jnp.mean(hidden, axis=-1, keepdims=True)
    centred = hidden - row_mean
    variance = jnp.mean(centred * centred, axis=-1, keepdims=True)
    return centred * lax.rsqrt(variance + EPS_NORM) * gain_row + shift_row


def gelu_exact(values):
    return jax.nn.gelu(values, approximate=False)


def mixing_rest(mark_scores, num_all, den_all):
    key_values = (
        num_all.reshape(ITEMS, LAND, HEADS, HEAD) / den_all.reshape(ITEMS, LAND, HEADS)[..., None]
    )
    kernel_two = jax.nn.softmax(mark_scores, axis=-1)
    frobenius = jnp.sum(kernel_two * kernel_two, axis=(2, 3), keepdims=True)
    inverse = jnp.swapaxes(kernel_two, 2, 3) / frobenius
    identity = jnp.eye(LAND, dtype=kernel_two.dtype)
    for iteration in range(NS_STEPS):
        product = jnp.einsum("ahjk,ahkl->ahjl", kernel_two, inverse, precision=HIGHEST_PREC)
        inner = 7.0 * identity - product
        inner = 15.0 * identity - jnp.einsum(
            "ahjk,ahkl->ahjl", product, inner, precision=HIGHEST_PREC
        )
        inner = 13.0 * identity - jnp.einsum(
            "ahjk,ahkl->ahjl", product, inner, precision=HIGHEST_PREC
        )
        inverse = 0.25 * jnp.einsum("ahjk,ahkl->ahjl", inverse, inner, precision=HIGHEST_PREC)
    mixed_rows = jnp.einsum("ahjk,akhd->ajhd", inverse, key_values, precision=HIGHEST_PREC)
    return mixed_rows.reshape(ITEMS * LAND, HEADS * HEAD)


def adamw(weight, moment_one, moment_two, gradient, clip_factor, rate_value, decay_value):
    clipped = gradient * clip_factor
    moment_one = BETA_ONE * moment_one + (1.0 - BETA_ONE) * clipped
    moment_two = BETA_TWO * moment_two + (1.0 - BETA_TWO) * clipped * clipped
    first_hat = moment_one / (1.0 - BETA_ONE**STEP)
    second_hat = moment_two / (1.0 - BETA_TWO**STEP)
    weight = weight - rate_value * (
        first_hat / (jnp.sqrt(second_hat) + ADAM_EPS) + decay_value * weight
    )
    return (weight, moment_one, moment_two)


def contract_rows(left, right):
    return lax.dot_general(
        left, right, (((0,), (0,)), ((), ())), preferred_element_type=jnp.float32
    )


def contract_cols(left, right):
    return lax.dot_general(
        left, right, (((1,), (1,)), ((), ())), preferred_element_type=jnp.float32
    )


def on_device(
    tokens,
    cotangent,
    item_lengths,
    qkv_weight,
    qkv_first,
    qkv_second,
    out_weight,
    out_first,
    out_second,
    up_weight,
    up_first,
    up_second,
    down_weight,
    down_first,
    down_second,
    norm_params,
    norm_first,
    norm_second,
    conv_kernel,
    conv_first,
    conv_second,
):
    temper = HEAD ** (-0.5)
    col_total = ITEMS * LAND
    w_qkv, w_out, w_up, w_down, gains_low = (
        lax.all_gather(qkv_weight.astype(jnp.bfloat16), ("seq", "grp"), axis=0, tiled=True),
        lax.all_gather(out_weight.astype(jnp.bfloat16), ("seq", "grp"), axis=0, tiled=True),
        lax.all_gather(up_weight.astype(jnp.bfloat16), ("seq", "grp"), axis=0, tiled=True),
        lax.all_gather(down_weight.astype(jnp.bfloat16), ("seq", "grp"), axis=0, tiled=True),
        lax.all_gather(norm_params.astype(jnp.bfloat16), ("seq", "grp"), axis=1, tiled=True),
    )
    gains_all = gains_low.astype(jnp.float32)
    lengths = item_lengths[0]
    first_row = lax.axis_index(("seq", "grp")) * TOK_DEV
    positions = first_row - HALO + jnp.arange(TOK_DEV + 2 * HALO, dtype=jnp.int32)
    item_ext, column_ext = locate(positions, lengths)
    item_mid = item_ext[HALO : HALO + TOK_DEV]
    column_mid = column_ext[HALO : HALO + TOK_DEV]
    col_ids = jnp.arange(col_total, dtype=jnp.int32)
    col_hot = (column_mid[:, None] == col_ids[None, :]).astype(jnp.bfloat16)
    member = (item_mid[:, None] == (col_ids // LAND)[None, :]).astype(jnp.float32)
    counts_f = landmark_counts(lengths).astype(jnp.float32)
    projected = jnp.dot(tokens, w_qkv, preferred_element_type=jnp.float32)
    proj_low = projected.astype(jnp.bfloat16)
    queries = proj_low[:, :D]
    key_rows = proj_low[:, D : 2 * D]
    value_rows = proj_low[:, 2 * D :]
    land_sums = lax.psum(contract_rows(col_hot, proj_low[:, : 2 * D]), ("seq", "grp"))
    mean_q = (land_sums[:, :D] / counts_f[:, None]).astype(jnp.bfloat16)
    mean_k = (land_sums[:, D:] / counts_f[:, None]).astype(jnp.bfloat16)
    query_heads = queries.reshape(TOK_DEV, HEADS, HEAD)
    key_heads = key_rows.reshape(TOK_DEV, HEADS, HEAD)
    value_heads = value_rows.reshape(TOK_DEV, HEADS, HEAD)
    mean_q3 = mean_q.reshape(col_total, HEADS, HEAD)
    mean_k3 = mean_k.reshape(col_total, HEADS, HEAD)
    scores_key = (
        jnp.einsum("chd,phd->chp", mean_q3, key_heads, preferred_element_type=jnp.float32) * temper
    )
    expo_key = jnp.exp(scores_key) * jnp.transpose(member)[:, None, :]
    expo_low = expo_key.astype(jnp.bfloat16)
    num_part = jnp.einsum(
        "chp,phd->chd", expo_low, value_heads, preferred_element_type=jnp.float32
    ).reshape(col_total, D)
    num_all, den_all = lax.psum((num_part, jnp.sum(expo_key, axis=2)), ("seq", "grp"))
    query_marks4 = mean_q.reshape(ITEMS, LAND, HEADS, HEAD)
    key_marks4 = mean_k.reshape(ITEMS, LAND, HEADS, HEAD)
    mark_scores = (
        jnp.einsum("ajhd,akhd->ahjk", query_marks4, key_marks4, preferred_element_type=jnp.float32)
        * temper
    )
    mixed_rows, mix_pull = jax.vjp(mixing_rest, mark_scores, num_all, den_all)
    mixed3 = mixed_rows.astype(jnp.bfloat16).reshape(col_total, HEADS, HEAD)
    scores_tok = (
        jnp.einsum("phd,chd->phc", query_heads, mean_k3, preferred_element_type=jnp.float32)
        * temper
    )
    expo_tok = jnp.exp(scores_tok) * member[:, None, :]
    attn_probs = expo_tok / jnp.sum(expo_tok, axis=2, keepdims=True)
    probs_low = attn_probs.astype(jnp.bfloat16)
    attended = jnp.einsum(
        "phc,chd->phd", probs_low, mixed3, preferred_element_type=jnp.float32
    ).reshape(TOK_DEV, D)
    value_ext = extended(value_rows, ((("seq", "grp"), 0),), HALO)
    channel_taps = jnp.repeat(conv_kernel, HEAD, axis=0)
    same_masks = [
        (item_ext[offset : offset + TOK_DEV] == item_mid).astype(jnp.float32)
        for offset in range(KERNEL)
    ]
    conv_out = jnp.zeros((TOK_DEV, D), jnp.float32)
    for offset in range(KERNEL):
        conv_out = conv_out + value_ext[offset : offset + TOK_DEV] * (
            channel_taps[:, offset][None, :] * same_masks[offset][:, None]
        )
    branch = (attended + conv_out).astype(jnp.bfloat16)
    attn_out = jnp.dot(branch, w_out, preferred_element_type=jnp.float32)
    normed_one, norm_one_pull = jax.vjp(
        layer_norm, tokens.astype(jnp.float32) + attn_out, gains_all[0], gains_all[1]
    )
    normed_low = normed_one.astype(jnp.bfloat16)
    up_out = jnp.dot(normed_low, w_up, preferred_element_type=jnp.float32)
    activated, gelu_pull = jax.vjp(gelu_exact, up_out)
    act_low = activated.astype(jnp.bfloat16)
    down_out = jnp.dot(act_low, w_down, preferred_element_type=jnp.float32)
    result, norm_two_pull = jax.vjp(layer_norm, normed_one + down_out, gains_all[2], gains_all[3])
    d_hidden_two, d_gain_two, d_shift_two = norm_two_pull(cotangent.astype(jnp.float32))
    d_down_low = d_hidden_two.astype(jnp.bfloat16)
    grad_down = contract_rows(act_low, d_down_low)
    (d_up,) = gelu_pull(contract_cols(d_down_low, w_down))
    d_up_low = d_up.astype(jnp.bfloat16)
    grad_up = contract_rows(normed_low, d_up_low)
    d_normed = d_hidden_two + contract_cols(d_up_low, w_up)
    d_hidden_one, d_gain_one, d_shift_one = norm_one_pull(d_normed)
    d_attn_low = d_hidden_one.astype(jnp.bfloat16)
    grad_out = contract_rows(branch, d_attn_low)
    d_branch_low = contract_cols(d_attn_low, w_out).astype(jnp.bfloat16)
    d_branch_f = d_branch_low.astype(jnp.float32)
    d_branch_ext = extended(d_branch_low, ((("seq", "grp"), 0),), HALO)
    d_values_conv = jnp.zeros((TOK_DEV, D), jnp.float32)
    tap_grads = []
    for offset in range(KERNEL):
        d_values_conv = d_values_conv + d_branch_ext[offset : offset + TOK_DEV] * (
            channel_taps[:, KERNEL - 1 - offset][None, :] * same_masks[offset][:, None]
        )
        tap_grads.append(
            jnp.sum(
                d_branch_f * value_ext[offset : offset + TOK_DEV] * same_masks[offset][:, None],
                axis=0,
            )
        )
    grad_conv = jnp.sum(jnp.stack(tap_grads, axis=1).reshape(HEADS, HEAD, KERNEL), axis=1)
    d_attended = d_branch_low.reshape(TOK_DEV, HEADS, HEAD)
    d_mixed_part = jnp.einsum(
        "phc,phd->chd", probs_low, d_attended, preferred_element_type=jnp.float32
    ).reshape(col_total, D)
    d_probs = jnp.einsum("phd,chd->phc", d_attended, mixed3, preferred_element_type=jnp.float32)
    d_scores_tok = (
        attn_probs * (d_probs - jnp.sum(attn_probs * d_probs, axis=2, keepdims=True))
    ).astype(jnp.bfloat16)
    d_query_tok = (
        jnp.einsum("phc,chd->phd", d_scores_tok, mean_k3, preferred_element_type=jnp.float32)
        * temper
    )
    d_meank_part = (
        jnp.einsum(
            "phc,phd->chd", d_scores_tok, query_heads, preferred_element_type=jnp.float32
        ).reshape(col_total, D)
        * temper
    )
    d_mixed, d_meank_tok = lax.psum((d_mixed_part, d_meank_part), ("seq", "grp"))
    d_mark_scores, d_num, d_den = mix_pull(d_mixed)
    d_mark_scaled = d_mark_scores * temper
    d_mean_q_mix = jnp.einsum(
        "ahjk,akhd->ajhd", d_mark_scaled, key_marks4.astype(jnp.float32), precision=HIGHEST_PREC
    ).reshape(col_total, D)
    d_mean_k_mix = jnp.einsum(
        "ahjk,ajhd->akhd", d_mark_scaled, query_marks4.astype(jnp.float32), precision=HIGHEST_PREC
    ).reshape(col_total, D)
    d_num3 = d_num.reshape(col_total, HEADS, HEAD)
    d_expo = d_den[:, :, None] + jnp.einsum(
        "chd,phd->chp", d_num3, value_heads.astype(jnp.float32), precision=HIGHEST_PREC
    )
    d_scores_key = (expo_key * d_expo).astype(jnp.bfloat16)
    d_key_mix = (
        jnp.einsum("chp,chd->phd", d_scores_key, mean_q3, preferred_element_type=jnp.float32)
        * temper
    )
    d_meanq_part = (
        jnp.einsum(
            "chp,phd->chd", d_scores_key, key_heads, preferred_element_type=jnp.float32
        ).reshape(col_total, D)
        * temper
    )
    d_value_mix = jnp.einsum(
        "chp,chd->phd", expo_low.astype(jnp.float32), d_num3, precision=HIGHEST_PREC
    )
    d_meanq_tok = lax.psum(d_meanq_part, ("seq", "grp"))
    d_sums = (
        jnp.concatenate([d_mean_q_mix + d_meanq_tok, d_mean_k_mix + d_meank_tok], axis=1)
        / counts_f[:, None]
    )
    d_land_rows = jnp.dot(col_hot.astype(jnp.float32), d_sums, precision=HIGHEST_PREC)
    d_queries = d_query_tok.reshape(TOK_DEV, D) + d_land_rows[:, :D]
    d_keys = d_key_mix.reshape(TOK_DEV, D) + d_land_rows[:, D:]
    d_values = d_value_mix.reshape(TOK_DEV, D) + d_values_conv
    d_proj_low = jnp.concatenate([d_queries, d_keys, d_values], axis=1).astype(jnp.bfloat16)
    grad_qkv = contract_rows(tokens, d_proj_low)
    input_grad = (d_hidden_one + contract_cols(d_proj_low, w_qkv)).astype(jnp.bfloat16)
    grad_norms = jnp.stack([d_gain_one, d_shift_one, d_gain_two, d_shift_two])
    group_qkv, group_out, group_up, group_down, group_norm = (
        lax.psum_scatter(grad_qkv, ("seq", "grp"), scatter_dimension=0, tiled=True),
        lax.psum_scatter(grad_out, ("seq", "grp"), scatter_dimension=0, tiled=True),
        lax.psum_scatter(grad_up, ("seq", "grp"), scatter_dimension=0, tiled=True),
        lax.psum_scatter(grad_down, ("seq", "grp"), scatter_dimension=0, tiled=True),
        lax.psum_scatter(grad_norms, ("seq", "grp"), scatter_dimension=1, tiled=True),
    )
    shard_qkv, shard_out, shard_up, shard_down, shard_norm, conv_rep = (
        lax.psum(group_qkv.astype(jnp.bfloat16), "rep").astype(jnp.float32),
        lax.psum(group_out.astype(jnp.bfloat16), "rep").astype(jnp.float32),
        lax.psum(group_up.astype(jnp.bfloat16), "rep").astype(jnp.float32),
        lax.psum(group_down.astype(jnp.bfloat16), "rep").astype(jnp.float32),
        lax.psum(group_norm.astype(jnp.bfloat16), "rep").astype(jnp.float32),
        lax.psum(grad_conv.astype(jnp.bfloat16), "rep").astype(jnp.float32),
    )
    local_sq = (
        jnp.sum(shard_qkv * shard_qkv)
        + jnp.sum(shard_out * shard_out)
        + jnp.sum(shard_up * shard_up)
        + jnp.sum(shard_down * shard_down)
        + jnp.sum(shard_norm * shard_norm)
    )
    total_sq, conv_total = lax.psum((local_sq, conv_rep), ("seq", "grp"))
    grad_total = jnp.sqrt(total_sq + jnp.sum(conv_total * conv_total))
    clip_factor = MAX_NORM / jnp.maximum(grad_total, MAX_NORM)
    qkv_new = adamw(
        qkv_weight, qkv_first, qkv_second, shard_qkv, clip_factor, RATE_MATRIX, DECAY_RATE
    )
    out_new = adamw(
        out_weight, out_first, out_second, shard_out, clip_factor, RATE_MATRIX, DECAY_RATE
    )
    up_new = adamw(up_weight, up_first, up_second, shard_up, clip_factor, RATE_MATRIX, DECAY_RATE)
    down_new = adamw(
        down_weight, down_first, down_second, shard_down, clip_factor, RATE_MATRIX, DECAY_RATE
    )
    norm_new = adamw(norm_params, norm_first, norm_second, shard_norm, clip_factor, RATE_NORM, 0.0)
    conv_new = adamw(conv_kernel, conv_first, conv_second, conv_total, clip_factor, RATE_CONV, 0.0)
    return (
        result.astype(jnp.bfloat16),
        input_grad,
        grad_total,
        qkv_new[0],
        qkv_new[1],
        qkv_new[2],
        out_new[0],
        out_new[1],
        out_new[2],
        up_new[0],
        up_new[1],
        up_new[2],
        down_new[0],
        down_new[1],
        down_new[2],
        norm_new[0],
        norm_new[1],
        norm_new[2],
        conv_new[0],
        conv_new[1],
        conv_new[2],
    )


TOK = 256
GRP_DEV = 8
TEMPER = HEAD ** (-0.5)
MESH_ID = pl.DeviceIdType.MESH
BF = jnp.bfloat16
F32 = jnp.float32
EXT = 384


def nn(left, right):
    return jnp.dot(left, right, preferred_element_type=F32)


def nt(left, right):
    return lax.dot_general(left, right, (((1,), (1,)), ((), ())), preferred_element_type=F32)


def tn(left, right):
    return lax.dot_general(left, right, (((0,), (0,)), ((), ())), preferred_element_type=F32)


def iota(shape, dim):
    return lax.broadcasted_iota(jnp.int32, shape, dim)


def split(value):
    high = value.astype(BF)
    return high, (value - high.astype(F32)).astype(BF)


def lane_head(shape):
    return iota(shape, len(shape) - 1) // HEAD


def block_diag(value):
    width = value.shape[1]
    heads = width // HEAD
    tiled = jnp.concatenate([value] * heads, axis=0)
    keep = (iota((width, width), 0) // HEAD) == (iota((width, width), 1) // HEAD)
    return jnp.where(keep, tiled, jnp.zeros_like(tiled))


def left_of(value):
    high, low = split(value)
    return jnp.concatenate([high, low], axis=0)


def right_of(value):
    high, low = split(value)
    return block_diag(high), block_diag(low)


def mm_parts(left, right):
    rows = left.shape[0] // 2
    both = nn(left, right[0])
    return both[:rows] + both[rows:] + nn(left[:rows], right[1])


def mm(left, right):
    return mm_parts(left_of(left), right_of(right))


def packed_eye(width):
    return (iota((LAND, width), 0) == iota((LAND, width), 1) % HEAD).astype(F32)


def head_total(row):
    heads = lane_head(row.shape)
    out = jnp.zeros_like(row)
    for head in range(row.shape[1] // HEAD):
        mine = heads == head
        out = jnp.where(mine, jnp.sum(jnp.where(mine, row, 0.0), axis=1, keepdims=True), out)
    return out


def head_rows(value, reduce_fn, neutral):
    heads = lane_head(value.shape)
    out = jnp.zeros_like(value)
    for head in range(value.shape[1] // HEAD):
        mine = heads == head
        out = jnp.where(mine, reduce_fn(jnp.where(mine, value, neutral), axis=1, keepdims=True), out)
    return out


def kernel_two(query_marks, key_marks):
    scores = nt(query_marks, block_diag(key_marks)) * TEMPER
    scores_t = nt(key_marks, block_diag(query_marks)) * TEMPER
    expo = jnp.exp(scores - head_rows(scores, jnp.max, -jnp.inf))
    plain = expo / head_rows(expo, jnp.sum, 0.0)
    expo_t = jnp.exp(scores_t - jnp.max(scores_t, axis=0, keepdims=True))
    flipped = expo_t / jnp.sum(expo_t, axis=0, keepdims=True)
    return plain, flipped


def newton(plains, flippeds, save):
    eye = packed_eye(plains[0].shape[1])
    lefts = [left_of(p) for p in plains]
    invs = [
        f / head_total(jnp.sum(f * f, axis=0, keepdims=True)) for f in flippeds
    ]
    for it in range(NS_STEPS):
        prods = [mm_parts(a, right_of(z)) for a, z in zip(lefts, invs)]
        plefts = [left_of(p) for p in prods]
        twos = [15.0 * eye - mm_parts(a, right_of(7.0 * eye - p)) for a, p in zip(plefts, prods)]
        threes = [13.0 * eye - mm_parts(a, right_of(t)) for a, t in zip(plefts, twos)]
        for index in range(len(invs)):
            save(it, index, invs[index], prods[index], twos[index], threes[index])
        invs = [0.25 * mm(z, t) for z, t in zip(invs, threes)]
    return invs


def lens_of(len_ref):
    l0, l1, l2, l3 = len_ref[0, 0], len_ref[0, 1], len_ref[0, 2], len_ref[0, 3]
    return (l0, l1, l2, l3), (0, l0, l0 + l1, l0 + l1 + l2)


def choose(item, values):
    out = jnp.where(item == 0, values[0], values[1])
    out = jnp.where(item == 2, values[2], out)
    return jnp.where(item == 3, values[3], out)


def column_edges(col, lens, starts):
    item = col // LAND
    seg = col % LAND
    length = choose(item, lens)
    start = choose(item, starts)
    low_edge = start + ((seg * length + LAND - 1) >> 6)
    high_edge = start + (((seg + 1) * length + LAND - 1) >> 6)
    return low_edge, high_edge, start, start + length


def item_of(pos, starts):
    return (
        (pos >= starts[1]).astype(jnp.int32)
        + (pos >= starts[2]).astype(jnp.int32)
        + (pos >= starts[3]).astype(jnp.int32)
    )


def pair_lanes(hp):
    return slice(128 * hp, 128 * hp + 128)


def both_heads(value):
    first = iota(value.shape, 1) < HEAD
    zero = jnp.zeros_like(value)
    return jnp.concatenate([jnp.where(first, value, zero), jnp.where(first, zero, value)], axis=0)


def pick_heads(value):
    rows = value.shape[0] // 2
    first = iota((rows, 128), 1) < HEAD
    return jnp.where(first, value[:rows], value[rows:])


def toeplitz(tap_row, same):
    wide = jnp.broadcast_to(tap_row, (TOK, EXT))
    return split(pltpu.roll(wide, 0, 1, stride=1, stride_axis=0) * same)


def conv_pair(taps_ref, hp, same, ext_pair):
    outs = []
    for head in (2 * hp, 2 * hp + 1):
        high, low = toeplitz(taps_ref[head : head + 1, :], same)
        outs.append(nn(high, ext_pair) + nn(low, ext_pair))
    first = iota((TOK, 128), 1) < HEAD
    return jnp.where(first, outs[0], outs[1])


def same_item(first_row, lens, starts, reverse=False):
    shape = (TOK, EXT)
    row = iota(shape, 0)
    if reverse:
        row = TOK - 1 - row
    pos = first_row + row
    other = first_row + iota(shape, 1) - HALO
    total = starts[3] + lens[3]
    inside = (other >= 0) & (other < total) & (item_of(pos, starts) == item_of(other, starts))
    return inside.astype(F32)


def group_peers(me):
    for step in range(1, GRP_DEV):
        yield step, lax.rem(me + step, GRP_DEV)


def place(rep, index):
    return (rep, index // 2, lax.rem(index, 2))


def greet(rep, me):
    barrier = pltpu.get_barrier_semaphore()
    for _, other in group_peers(me):
        pl.semaphore_signal(barrier, inc=1, device_id=place(rep, other), device_id_type=MESH_ID)
    pl.semaphore_wait(barrier, GRP_DEV - 1)


def push(src, dst, send_sem, recv_sem, device):
    copy = pltpu.make_async_remote_copy(
        src_ref=src, dst_ref=dst, send_sem=send_sem, recv_sem=recv_sem,
        device_id=device, device_id_type=MESH_ID,
    )
    copy.start()
    return copy


def attend_kernel(
    len_ref, x_ref, w_ref, taps_ref,
    q_ref, k_ref, v_ref, qm_ref, km_ref, wm_ref, a_ref, ext_ref,
    res_ref, vloc_ref, dloc_ref, resl_ref, vl_ref, dl_ref,
    win, halo, nd_src, nd_buf, wml, bias_cp, bias_pc, num_s, den_s, probs,
    win_s, win_r, halo_s, halo_r, nd_s, nd_r, wml_s, wml_r,
):
    rep, seq, grp = lax.axis_index("rep"), lax.axis_index("seq"), lax.axis_index("grp")
    me = seq * 2 + grp
    first_row = me * TOK
    is_owner = (me >= 1) & (me <= 6)
    lens, starts = lens_of(len_ref)
    greet(rep, me)

    for part, ref in enumerate((q_ref, k_ref, v_ref)):
        ref[...] = nn(x_ref[...], w_ref[:, D * part : D * part + D]).astype(BF)

    @pl.when(me < GRP_DEV - 1)
    def _():
        push(v_ref.at[pl.ds(TOK - HALO, HALO)], halo.at[0], halo_s.at[0], halo_r.at[0], place(rep, me + 1))

    @pl.when(me > 0)
    def _():
        push(v_ref.at[pl.ds(0, HALO)], halo.at[1], halo_s.at[1], halo_r.at[1], place(rep, me - 1))

    qk = jnp.concatenate([q_ref[...], k_ref[...]], axis=1)
    shape = (COLS, TOK)
    pos = first_row + iota(shape, 1)
    lo, hi, begin, end = column_edges(iota(shape, 0), lens, starts)
    hot = ((pos >= lo) & (pos < hi)).astype(BF)
    bias_cp[...] = jnp.where((pos >= begin) & (pos < end), 0.0, -1e30)
    wshape = (16, TOK)
    seg_hi = lens_edge(iota((LAND, TOK), 0) + 1, lens[1], starts[1])
    base = jnp.sum((seg_hi <= first_row).astype(jnp.int32).astype(F32), axis=0, keepdims=True).astype(jnp.int32)
    seg_w = base + iota(wshape, 0)
    wpos = first_row + iota(wshape, 1)
    whot = (
        (wpos >= lens_edge(seg_w, lens[1], starts[1]))
        & (wpos < lens_edge(seg_w + 1, lens[1], starts[1]))
        & (seg_w < LAND)
    ).astype(BF)
    wsum = nn(whot, qk)
    seg_c = base[:, :128] + iota((16, 128), 0)
    wcount = (lens_edge(seg_c + 1, lens[1], starts[1]) - lens_edge(seg_c, lens[1], starts[1])).astype(F32)
    wcount = jnp.concatenate([wcount] * 12, axis=1)
    win[me] = (wsum / wcount).astype(BF)
    for step, other in group_peers(me):
        push(win.at[me], win.at[me], win_s.at[step - 1], win_r.at[me], place(rep, other))

    sums = nn(hot, qk)
    clo, chi, _, _ = column_edges(iota((COLS, 128), 0), lens, starts)
    counts = (chi - clo).astype(F32)
    counts6 = jnp.concatenate([counts] * 6, axis=1)
    qm_ref[...] = (sums[:, :D] / counts6).astype(BF)
    km_ref[...] = (sums[:, D:] / counts6).astype(BF)

    pshape = (TOK, COLS)
    ppos = first_row + iota(pshape, 0)
    _, _, pbegin, pend = column_edges(iota(pshape, 1), lens, starts)
    bias_pc[...] = jnp.where((ppos >= pbegin) & (ppos < pend), 0.0, -1e30)

    for step, other in group_peers(me):
        pltpu.make_async_copy(win.at[other], win.at[other], win_r.at[other]).wait()
    sshape = (LAND, 128)
    lane_dev = iota((LAND, 128), 1) // 16
    lane_w = iota((LAND, 128), 1) % 16
    seg_end = lens_edge(iota((LAND, 128), 0) + 1, lens[1], starts[1])
    bases = jnp.sum((seg_end <= lane_dev * TOK).astype(jnp.int32).astype(F32), axis=0, keepdims=True).astype(jnp.int32)
    scatter = (iota(sshape, 0) == bases + lane_w).astype(BF)
    long_rows = nn(scatter, win[...].reshape(128, 2 * D))
    qm_ref[LAND : 2 * LAND, :] = long_rows[:, :D].astype(BF)
    km_ref[LAND : 2 * LAND, :] = long_rows[:, D:].astype(BF)

    ones_wide = jnp.ones((TOK, 128), BF)
    ones_row = jnp.ones((8, TOK), BF)
    for hp in range(6):
        lanes = pair_lanes(hp)
        marks = both_heads(qm_ref[:, lanes])
        scores = nt(marks, k_ref[:, lanes]) * TEMPER
        expo = jnp.exp(scores + jnp.concatenate([bias_cp[...]] * 2, axis=0)).astype(BF)
        nd = nn(expo, jnp.concatenate([v_ref[:, lanes], ones_wide], axis=1))
        num = pick_heads(nd[:, :128])
        nd_src[hp, 0:LAND, :] = num[LAND : 2 * LAND]
        nd_src[hp, LAND : LAND + 8, :] = nt(
            ones_row, jnp.concatenate([expo[LAND : 2 * LAND], expo[COLS + LAND : COLS + 2 * LAND]], axis=0)
        )
        num_s[:, lanes] = num
        den_s[:, lanes] = pick_heads(nd[:, 128:])
    for owner in range(1, 7):
        @pl.when(me == owner)
        def _():
            nd_buf[owner] = nd_src[owner - 1]

        @pl.when(me != owner)
        def _():
            push(nd_src.at[owner - 1], nd_buf.at[me], nd_s.at[owner - 1], nd_r.at[me], place(rep, owner))

    wm_ref[...] = jnp.zeros_like(wm_ref)
    n_local = jnp.where(me == 0, 1, jnp.where(me == GRP_DEV - 1, 2, 0))

    def local_item(slot, carry):
        row = jnp.where(me == 0, 0, 2 * LAND + slot * LAND)
        rows = pl.ds(pl.multiple_of(row, LAND), LAND)
        plains, flippeds = [], []
        for part in range(3):
            lanes = slice(256 * part, 256 * part + 256)
            plain, flipped = kernel_two(qm_ref[rows, lanes], km_ref[rows, lanes])
            plains.append(plain)
            flippeds.append(flipped)

        def save(it, index, *mats):
            for m, mat in enumerate(mats):
                res_ref[slot, index, it, m] = mat

        invs = newton(plains, flippeds, save)
        for part in range(3):
            lanes = slice(256 * part, 256 * part + 256)
            den = den_s[rows, lanes]
            val = num_s[rows, lanes] / den
            vloc_ref[slot, :, lanes] = val
            dloc_ref[slot, :, lanes] = den
            wm_ref[rows, lanes] = mm(invs[part], val).astype(BF)
        return carry

    lax.fori_loop(0, n_local, local_item, 0)

    @pl.when(is_owner)
    def _():
        lanes = pl.ds(pl.multiple_of((me - 1) * 128, 128), 128)
        plain, flipped = kernel_two(qm_ref[LAND : 2 * LAND, lanes], km_ref[LAND : 2 * LAND, lanes])

        def save(it, index, *mats):
            for m, mat in enumerate(mats):
                resl_ref[it, m] = mat

        (inv,) = newton([plain], [flipped], save)
        for step, other in group_peers(me):
            pltpu.make_async_copy(nd_buf.at[other], nd_buf.at[other], nd_r.at[other]).wait()
        total = nd_buf[0]
        for j in range(1, GRP_DEV):
            total = total + nd_buf[j]
        row = total[LAND : LAND + 1, :]
        other_row = pltpu.roll(row, HEAD, 1)
        spread = jnp.where(iota((128, 128), 0) < HEAD, row, other_row)
        den = jnp.transpose(spread)[:LAND]
        val = total[:LAND] / den
        vl_ref[...] = val
        dl_ref[...] = den
        wml[me - 1] = mm(inv, val).astype(BF)
        for step, other in group_peers(me):
            push(wml.at[me - 1], wml.at[me - 1], wml_s.at[step - 1], wml_r.at[me - 1], place(rep, other))

    for hp in range(6):
        lanes = pair_lanes(hp)
        scores = nt(q_ref[:, lanes], both_heads(km_ref[:, lanes])) * TEMPER
        for half in range(2):
            expo = jnp.exp(scores[:, COLS * half : COLS * half + COLS] + bias_pc[...])
            probs[hp, :, COLS * half : COLS * half + COLS] = (
                expo / jnp.sum(expo, axis=1, keepdims=True)
            ).astype(BF)

    @pl.when(me > 0)
    def _():
        pltpu.make_async_copy(halo.at[0], halo.at[0], halo_r.at[0]).wait()
        ext_ref[0:HALO] = halo[0]

    @pl.when(me == 0)
    def _():
        ext_ref[0:HALO] = jnp.zeros((HALO, D), BF)

    @pl.when(me < GRP_DEV - 1)
    def _():
        pltpu.make_async_copy(halo.at[1], halo.at[1], halo_r.at[1]).wait()
        ext_ref[HALO + TOK : 2 * HALO + TOK] = halo[1]

    @pl.when(me == GRP_DEV - 1)
    def _():
        ext_ref[HALO + TOK : 2 * HALO + TOK] = jnp.zeros((HALO, D), BF)

    ext_ref[HALO : HALO + TOK] = v_ref[...]
    ext_ref[2 * HALO + TOK :] = jnp.zeros((EXT - TOK - 2 * HALO, D), BF)
    same = same_item(first_row, lens, starts)

    for owner in range(1, 7):
        @pl.when(me != owner)
        def _():
            pltpu.make_async_copy(wml.at[owner - 1], wml.at[owner - 1], wml_r.at[owner - 1]).wait()

        wm_ref[LAND : 2 * LAND, pair_lanes(owner - 1)] = wml[owner - 1]
    for hp in range(6):
        lanes = pair_lanes(hp)
        att = nn(probs[hp], both_heads(wm_ref[:, lanes]))
        a_ref[:, lanes] = (att + conv_pair(taps_ref, hp, same, ext_ref[:, lanes])).astype(BF)

    for step, other in group_peers(me):
        pltpu.make_async_copy(win.at[me], win.at[me], win_s.at[step - 1]).wait()
    for owner in range(1, 7):
        @pl.when(me != owner)
        def _():
            pltpu.make_async_copy(nd_src.at[owner - 1], nd_src.at[owner - 1], nd_s.at[owner - 1]).wait()

    @pl.when(is_owner)
    def _():
        for step, other in group_peers(me):
            pltpu.make_async_copy(wml.at[0], wml.at[0], wml_s.at[step - 1]).wait()

    @pl.when(me < GRP_DEV - 1)
    def _():
        pltpu.make_async_copy(halo.at[0], halo.at[0], halo_s.at[0]).wait()

    @pl.when(me > 0)
    def _():
        pltpu.make_async_copy(halo.at[1], halo.at[1], halo_s.at[1]).wait()


def lens_edge(seg, length, start):
    return start + ((seg * length + LAND - 1) >> 6)


COLS = ITEMS * LAND
VM = pl.BlockSpec(memory_space=pltpu.VMEM)
SM = pl.BlockSpec(memory_space=pltpu.SMEM)


def attend(item_lengths, tokens, w_all, taps):
    sds = jax.ShapeDtypeStruct
    row = sds((TOK, D), BF)
    outs = [row, row, row, row, row, row, row, sds((EXT, D), BF),
            sds((2, 3, NS_STEPS, 4, LAND, 256), F32), sds((2, LAND, D), F32), sds((2, LAND, D), F32),
            sds((NS_STEPS, 4, LAND, 128), F32), sds((LAND, 128), F32), sds((LAND, 128), F32)]
    dma = pltpu.SemaphoreType.DMA
    scratch = [
        pltpu.VMEM((8, 16, 2 * D), BF), pltpu.VMEM((2, HALO, D), BF), pltpu.VMEM((6, LAND + 8, 128), F32),
        pltpu.VMEM((8, LAND + 8, 128), F32), pltpu.VMEM((6, LAND, 128), BF),
        pltpu.VMEM((COLS, TOK), F32), pltpu.VMEM((TOK, COLS), F32), pltpu.VMEM((COLS, D), F32),
        pltpu.VMEM((COLS, D), F32), pltpu.VMEM((6, TOK, 2 * COLS), BF),
        dma((7,)), dma((8,)), dma((2,)), dma((2,)), dma((6,)), dma((8,)), dma((7,)), dma((6,)),
    ]
    return pl.pallas_call(
        attend_kernel, out_shape=outs, in_specs=[SM, VM, VM, VM], out_specs=[VM] * len(outs),
        scratch_shapes=scratch, name="attend",
        compiler_params=pltpu.CompilerParams(collective_id=1, has_side_effects=True, vmem_limit_bytes=56 * 2**20),
    )(item_lengths, tokens, w_all, taps)


def full_marks(marks):
    index = lax.axis_index(("seq", "grp"))
    rows = jnp.arange(ITEMS * LAND)[:, None]
    keep = ((rows // LAND != 1) | (index == 0)).astype(jnp.bfloat16)
    return lax.psum(marks * keep, ("seq", "grp"))


def on_device_fast(
    tokens,
    cotangent,
    item_lengths,
    qkv_weight,
    qkv_first,
    qkv_second,
    out_weight,
    out_first,
    out_second,
    up_weight,
    up_first,
    up_second,
    down_weight,
    down_first,
    down_second,
    norm_params,
    norm_first,
    norm_second,
    conv_kernel,
    conv_first,
    conv_second,
):
    temper = HEAD ** (-0.5)
    col_total = ITEMS * LAND
    w_qkv, w_out, w_up, w_down, gains_low = (
        lax.all_gather(qkv_weight.astype(jnp.bfloat16), ("seq", "grp"), axis=0, tiled=True),
        lax.all_gather(out_weight.astype(jnp.bfloat16), ("seq", "grp"), axis=0, tiled=True),
        lax.all_gather(up_weight.astype(jnp.bfloat16), ("seq", "grp"), axis=0, tiled=True),
        lax.all_gather(down_weight.astype(jnp.bfloat16), ("seq", "grp"), axis=0, tiled=True),
        lax.all_gather(norm_params.astype(jnp.bfloat16), ("seq", "grp"), axis=1, tiled=True),
    )
    gains_all = gains_low.astype(jnp.float32)
    lengths = item_lengths[0]
    taps = jnp.pad(conv_kernel, ((0, 4), (0, EXT - KERNEL)))
    queries, key_rows, value_rows, mean_q, mean_k, mixed_low, branch, value_pad = attend(
        item_lengths, tokens, w_qkv, taps
    )[:8]
    value_ext = value_pad[: TOK_DEV + 2 * HALO]
    first_row = lax.axis_index(("seq", "grp")) * TOK_DEV
    positions = first_row - HALO + jnp.arange(TOK_DEV + 2 * HALO, dtype=jnp.int32)
    item_ext, column_ext = locate(positions, lengths)
    item_mid = item_ext[HALO : HALO + TOK_DEV]
    column_mid = column_ext[HALO : HALO + TOK_DEV]
    col_ids = jnp.arange(col_total, dtype=jnp.int32)
    col_hot = (column_mid[:, None] == col_ids[None, :]).astype(jnp.bfloat16)
    member = (item_mid[:, None] == (col_ids // LAND)[None, :]).astype(jnp.float32)
    counts_f = landmark_counts(lengths).astype(jnp.float32)
    mean_q, mean_k = full_marks(mean_q), full_marks(mean_k)
    query_heads = queries.reshape(TOK_DEV, HEADS, HEAD)
    key_heads = key_rows.reshape(TOK_DEV, HEADS, HEAD)
    value_heads = value_rows.reshape(TOK_DEV, HEADS, HEAD)
    mean_q3 = mean_q.reshape(col_total, HEADS, HEAD)
    mean_k3 = mean_k.reshape(col_total, HEADS, HEAD)
    scores_key = (
        jnp.einsum("chd,phd->chp", mean_q3, key_heads, preferred_element_type=jnp.float32) * temper
    )
    expo_key = jnp.exp(scores_key) * jnp.transpose(member)[:, None, :]
    expo_low = expo_key.astype(jnp.bfloat16)
    num_part = jnp.einsum(
        "chp,phd->chd", expo_low, value_heads, preferred_element_type=jnp.float32
    ).reshape(col_total, D)
    num_all, den_all = lax.psum((num_part, jnp.sum(expo_key, axis=2)), ("seq", "grp"))
    query_marks4 = mean_q.reshape(ITEMS, LAND, HEADS, HEAD)
    key_marks4 = mean_k.reshape(ITEMS, LAND, HEADS, HEAD)
    mark_scores = (
        jnp.einsum("ajhd,akhd->ahjk", query_marks4, key_marks4, preferred_element_type=jnp.float32)
        * temper
    )
    mixed_rows, mix_pull = jax.vjp(mixing_rest, mark_scores, num_all, den_all)
    mixed3 = mixed_rows.astype(jnp.bfloat16).reshape(col_total, HEADS, HEAD)
    scores_tok = (
        jnp.einsum("phd,chd->phc", query_heads, mean_k3, preferred_element_type=jnp.float32)
        * temper
    )
    expo_tok = jnp.exp(scores_tok) * member[:, None, :]
    attn_probs = expo_tok / jnp.sum(expo_tok, axis=2, keepdims=True)
    probs_low = attn_probs.astype(jnp.bfloat16)
    channel_taps = jnp.repeat(conv_kernel, HEAD, axis=0)
    same_masks = [
        (item_ext[offset : offset + TOK_DEV] == item_mid).astype(jnp.float32)
        for offset in range(KERNEL)
    ]
    attn_out = jnp.dot(branch, w_out, preferred_element_type=jnp.float32)
    normed_one, norm_one_pull = jax.vjp(
        layer_norm, tokens.astype(jnp.float32) + attn_out, gains_all[0], gains_all[1]
    )
    normed_low = normed_one.astype(jnp.bfloat16)
    up_out = jnp.dot(normed_low, w_up, preferred_element_type=jnp.float32)
    activated, gelu_pull = jax.vjp(gelu_exact, up_out)
    act_low = activated.astype(jnp.bfloat16)
    down_out = jnp.dot(act_low, w_down, preferred_element_type=jnp.float32)
    result, norm_two_pull = jax.vjp(layer_norm, normed_one + down_out, gains_all[2], gains_all[3])
    d_hidden_two, d_gain_two, d_shift_two = norm_two_pull(cotangent.astype(jnp.float32))
    d_down_low = d_hidden_two.astype(jnp.bfloat16)
    grad_down = contract_rows(act_low, d_down_low)
    (d_up,) = gelu_pull(contract_cols(d_down_low, w_down))
    d_up_low = d_up.astype(jnp.bfloat16)
    grad_up = contract_rows(normed_low, d_up_low)
    d_normed = d_hidden_two + contract_cols(d_up_low, w_up)
    d_hidden_one, d_gain_one, d_shift_one = norm_one_pull(d_normed)
    d_attn_low = d_hidden_one.astype(jnp.bfloat16)
    grad_out = contract_rows(branch, d_attn_low)
    d_branch_low = contract_cols(d_attn_low, w_out).astype(jnp.bfloat16)
    d_branch_f = d_branch_low.astype(jnp.float32)
    d_branch_ext = extended(d_branch_low, ((("seq", "grp"), 0),), HALO)
    d_values_conv = jnp.zeros((TOK_DEV, D), jnp.float32)
    tap_grads = []
    for offset in range(KERNEL):
        d_values_conv = d_values_conv + d_branch_ext[offset : offset + TOK_DEV] * (
            channel_taps[:, KERNEL - 1 - offset][None, :] * same_masks[offset][:, None]
        )
        tap_grads.append(
            jnp.sum(
                d_branch_f * value_ext[offset : offset + TOK_DEV] * same_masks[offset][:, None],
                axis=0,
            )
        )
    grad_conv = jnp.sum(jnp.stack(tap_grads, axis=1).reshape(HEADS, HEAD, KERNEL), axis=1)
    d_attended = d_branch_low.reshape(TOK_DEV, HEADS, HEAD)
    d_mixed_part = jnp.einsum(
        "phc,phd->chd", probs_low, d_attended, preferred_element_type=jnp.float32
    ).reshape(col_total, D)
    d_probs = jnp.einsum("phd,chd->phc", d_attended, mixed3, preferred_element_type=jnp.float32)
    d_scores_tok = (
        attn_probs * (d_probs - jnp.sum(attn_probs * d_probs, axis=2, keepdims=True))
    ).astype(jnp.bfloat16)
    d_query_tok = (
        jnp.einsum("phc,chd->phd", d_scores_tok, mean_k3, preferred_element_type=jnp.float32)
        * temper
    )
    d_meank_part = (
        jnp.einsum(
            "phc,phd->chd", d_scores_tok, query_heads, preferred_element_type=jnp.float32
        ).reshape(col_total, D)
        * temper
    )
    d_mixed, d_meank_tok = lax.psum((d_mixed_part, d_meank_part), ("seq", "grp"))
    d_mark_scores, d_num, d_den = mix_pull(d_mixed)
    d_mark_scaled = d_mark_scores * temper
    d_mean_q_mix = jnp.einsum(
        "ahjk,akhd->ajhd", d_mark_scaled, key_marks4.astype(jnp.float32), precision=HIGHEST_PREC
    ).reshape(col_total, D)
    d_mean_k_mix = jnp.einsum(
        "ahjk,ajhd->akhd", d_mark_scaled, query_marks4.astype(jnp.float32), precision=HIGHEST_PREC
    ).reshape(col_total, D)
    d_num3 = d_num.reshape(col_total, HEADS, HEAD)
    d_expo = d_den[:, :, None] + jnp.einsum(
        "chd,phd->chp", d_num3, value_heads.astype(jnp.float32), precision=HIGHEST_PREC
    )
    d_scores_key = (expo_key * d_expo).astype(jnp.bfloat16)
    d_key_mix = (
        jnp.einsum("chp,chd->phd", d_scores_key, mean_q3, preferred_element_type=jnp.float32)
        * temper
    )
    d_meanq_part = (
        jnp.einsum(
            "chp,phd->chd", d_scores_key, key_heads, preferred_element_type=jnp.float32
        ).reshape(col_total, D)
        * temper
    )
    d_value_mix = jnp.einsum(
        "chp,chd->phd", expo_low.astype(jnp.float32), d_num3, precision=HIGHEST_PREC
    )
    d_meanq_tok = lax.psum(d_meanq_part, ("seq", "grp"))
    d_sums = (
        jnp.concatenate([d_mean_q_mix + d_meanq_tok, d_mean_k_mix + d_meank_tok], axis=1)
        / counts_f[:, None]
    )
    d_land_rows = jnp.dot(col_hot.astype(jnp.float32), d_sums, precision=HIGHEST_PREC)
    d_queries = d_query_tok.reshape(TOK_DEV, D) + d_land_rows[:, :D]
    d_keys = d_key_mix.reshape(TOK_DEV, D) + d_land_rows[:, D:]
    d_values = d_value_mix.reshape(TOK_DEV, D) + d_values_conv
    d_proj_low = jnp.concatenate([d_queries, d_keys, d_values], axis=1).astype(jnp.bfloat16)
    grad_qkv = contract_rows(tokens, d_proj_low)
    input_grad = (d_hidden_one + contract_cols(d_proj_low, w_qkv)).astype(jnp.bfloat16)
    grad_norms = jnp.stack([d_gain_one, d_shift_one, d_gain_two, d_shift_two])
    group_qkv, group_out, group_up, group_down, group_norm = (
        lax.psum_scatter(grad_qkv, ("seq", "grp"), scatter_dimension=0, tiled=True),
        lax.psum_scatter(grad_out, ("seq", "grp"), scatter_dimension=0, tiled=True),
        lax.psum_scatter(grad_up, ("seq", "grp"), scatter_dimension=0, tiled=True),
        lax.psum_scatter(grad_down, ("seq", "grp"), scatter_dimension=0, tiled=True),
        lax.psum_scatter(grad_norms, ("seq", "grp"), scatter_dimension=1, tiled=True),
    )
    shard_qkv, shard_out, shard_up, shard_down, shard_norm, conv_rep = (
        lax.psum(group_qkv.astype(jnp.bfloat16), "rep").astype(jnp.float32),
        lax.psum(group_out.astype(jnp.bfloat16), "rep").astype(jnp.float32),
        lax.psum(group_up.astype(jnp.bfloat16), "rep").astype(jnp.float32),
        lax.psum(group_down.astype(jnp.bfloat16), "rep").astype(jnp.float32),
        lax.psum(group_norm.astype(jnp.bfloat16), "rep").astype(jnp.float32),
        lax.psum(grad_conv.astype(jnp.bfloat16), "rep").astype(jnp.float32),
    )
    local_sq = (
        jnp.sum(shard_qkv * shard_qkv)
        + jnp.sum(shard_out * shard_out)
        + jnp.sum(shard_up * shard_up)
        + jnp.sum(shard_down * shard_down)
        + jnp.sum(shard_norm * shard_norm)
    )
    total_sq, conv_total = lax.psum((local_sq, conv_rep), ("seq", "grp"))
    grad_total = jnp.sqrt(total_sq + jnp.sum(conv_total * conv_total))
    clip_factor = MAX_NORM / jnp.maximum(grad_total, MAX_NORM)
    qkv_new = adamw(
        qkv_weight, qkv_first, qkv_second, shard_qkv, clip_factor, RATE_MATRIX, DECAY_RATE
    )
    out_new = adamw(
        out_weight, out_first, out_second, shard_out, clip_factor, RATE_MATRIX, DECAY_RATE
    )
    up_new = adamw(up_weight, up_first, up_second, shard_up, clip_factor, RATE_MATRIX, DECAY_RATE)
    down_new = adamw(
        down_weight, down_first, down_second, shard_down, clip_factor, RATE_MATRIX, DECAY_RATE
    )
    norm_new = adamw(norm_params, norm_first, norm_second, shard_norm, clip_factor, RATE_NORM, 0.0)
    conv_new = adamw(conv_kernel, conv_first, conv_second, conv_total, clip_factor, RATE_CONV, 0.0)
    return (
        result.astype(jnp.bfloat16),
        input_grad,
        grad_total,
        qkv_new[0],
        qkv_new[1],
        qkv_new[2],
        out_new[0],
        out_new[1],
        out_new[2],
        up_new[0],
        up_new[1],
        up_new[2],
        down_new[0],
        down_new[1],
        down_new[2],
        norm_new[0],
        norm_new[1],
        norm_new[2],
        conv_new[0],
        conv_new[1],
        conv_new[2],
    )


def solution(mesh):
    in_specs = (
        P(("rep", "seq", "grp"), None),
        P(("rep", "seq", "grp"), None),
        P("rep", None),
        P(("seq", "grp"), None),
        P(("seq", "grp"), None),
        P(("seq", "grp"), None),
        P(("seq", "grp"), None),
        P(("seq", "grp"), None),
        P(("seq", "grp"), None),
        P(("seq", "grp"), None),
        P(("seq", "grp"), None),
        P(("seq", "grp"), None),
        P(("seq", "grp"), None),
        P(("seq", "grp"), None),
        P(("seq", "grp"), None),
        P(None, ("seq", "grp")),
        P(None, ("seq", "grp")),
        P(None, ("seq", "grp")),
        P(),
        P(),
        P(),
    )
    out_specs = (
        P(("rep", "seq", "grp"), None),
        P(("rep", "seq", "grp"), None),
        P(),
        P(("seq", "grp"), None),
        P(("seq", "grp"), None),
        P(("seq", "grp"), None),
        P(("seq", "grp"), None),
        P(("seq", "grp"), None),
        P(("seq", "grp"), None),
        P(("seq", "grp"), None),
        P(("seq", "grp"), None),
        P(("seq", "grp"), None),
        P(("seq", "grp"), None),
        P(("seq", "grp"), None),
        P(("seq", "grp"), None),
        P(None, ("seq", "grp")),
        P(None, ("seq", "grp")),
        P(None, ("seq", "grp")),
        P(),
        P(),
        P(),
    )
    fast = dict(mesh.shape) == {"rep": 4, "seq": 4, "grp": 2}
    body = on_device_fast if fast else on_device
    return jax.shard_map(
        body, mesh=mesh, in_specs=in_specs, out_specs=out_specs, check_vma=False
    )
```

```python
import jax
import jax.numpy as jnp
from jax import lax
from jax.experimental import pallas as pl
from jax.experimental.pallas import tpu as pltpu
from jax.sharding import PartitionSpec as P

D = 768
FF = 3072
HEADS = 12
HEAD = 64
LAND = 64
KERNEL = 33
HALO = 16
NS_STEPS = 6
ITEMS = 4
STEP = 10
TOK_DEV = 256
GRP_DEV = 8
HIGHEST_PREC = lax.Precision.HIGHEST
EPS_NORM = 1e-05
BETA_ONE = 0.9
BETA_TWO = 0.999
ADAM_EPS = 1e-08
RATE_MATRIX = 0.02
RATE_NORM = 0.3
RATE_CONV = 0.1
DECAY_RATE = 0.01
MAX_NORM = 1.0


def extended(cells, sides, width):
    for axis, dim in sides:
        count = lax.axis_size(axis)
        ends = count - 1
        head = lax.slice_in_dim(cells, 0, width, axis=dim)
        tail = lax.slice_in_dim(cells, cells.shape[dim] - width, cells.shape[dim], axis=dim)
        cells = jnp.concatenate(
            [
                lax.ppermute(tail, axis, [(i, (i + 1) % count) for i in range(ends)]),
                cells,
                lax.ppermute(head, axis, [((i + 1) % count, i) for i in range(ends)]),
            ],
            axis=dim,
        )
    return cells


def locate(positions, lengths):
    ends = jnp.cumsum(lengths)
    starts = ends - lengths
    inside = (positions[:, None] >= starts[None, :]) & (positions[:, None] < ends[None, :])
    item_ids = jnp.sum((positions[:, None] >= ends[None, :]).astype(jnp.int32), axis=1)
    valid = (positions >= 0) & (positions < ends[-1])
    item_ids = jnp.where(valid, item_ids, -1)
    own_len = jnp.sum(jnp.where(inside, lengths[None, :], 0), axis=1)
    own_start = jnp.sum(jnp.where(inside, starts[None, :], 0), axis=1)
    segment = (positions - own_start) * LAND // jnp.maximum(own_len, 1)
    columns = jnp.where(valid, item_ids * LAND + segment, -1)
    return (item_ids, columns)


def landmark_counts(lengths):
    marks = jnp.arange(LAND + 1, dtype=jnp.int32)
    edges = (marks[None, :] * lengths[:, None] + LAND - 1) // LAND
    return (edges[:, 1:] - edges[:, :-1]).reshape(-1)


def layer_norm(hidden, gain_row, shift_row):
    row_mean = jnp.mean(hidden, axis=-1, keepdims=True)
    centred = hidden - row_mean
    variance = jnp.mean(centred * centred, axis=-1, keepdims=True)
    return centred * lax.rsqrt(variance + EPS_NORM) * gain_row + shift_row


def gelu_exact(values):
    return jax.nn.gelu(values, approximate=False)


def mixing_rest(mark_scores, num_all, den_all):
    key_values = (
        num_all.reshape(ITEMS, LAND, HEADS, HEAD) / den_all.reshape(ITEMS, LAND, HEADS)[..., None]
    )
    kernel_two = jax.nn.softmax(mark_scores, axis=-1)
    frobenius = jnp.sum(kernel_two * kernel_two, axis=(2, 3), keepdims=True)
    inverse = jnp.swapaxes(kernel_two, 2, 3) / frobenius
    identity = jnp.eye(LAND, dtype=kernel_two.dtype)
    for iteration in range(NS_STEPS):
        product = jnp.einsum("ahjk,ahkl->ahjl", kernel_two, inverse, precision=HIGHEST_PREC)
        inner = 7.0 * identity - product
        inner = 15.0 * identity - jnp.einsum(
            "ahjk,ahkl->ahjl", product, inner, precision=HIGHEST_PREC
        )
        inner = 13.0 * identity - jnp.einsum(
            "ahjk,ahkl->ahjl", product, inner, precision=HIGHEST_PREC
        )
        inverse = 0.25 * jnp.einsum("ahjk,ahkl->ahjl", inverse, inner, precision=HIGHEST_PREC)
    mixed_rows = jnp.einsum("ahjk,akhd->ajhd", inverse, key_values, precision=HIGHEST_PREC)
    return mixed_rows.reshape(ITEMS * LAND, HEADS * HEAD)


def adamw(weight, moment_one, moment_two, gradient, clip_factor, rate_value, decay_value):
    clipped = gradient * clip_factor
    moment_one = BETA_ONE * moment_one + (1.0 - BETA_ONE) * clipped
    moment_two = BETA_TWO * moment_two + (1.0 - BETA_TWO) * clipped * clipped
    first_hat = moment_one / (1.0 - BETA_ONE**STEP)
    second_hat = moment_two / (1.0 - BETA_TWO**STEP)
    weight = weight - rate_value * (
        first_hat / (jnp.sqrt(second_hat) + ADAM_EPS) + decay_value * weight
    )
    return (weight, moment_one, moment_two)


def contract_rows(left, right):
    return lax.dot_general(
        left, right, (((0,), (0,)), ((), ())), preferred_element_type=jnp.float32
    )


def contract_cols(left, right):
    return lax.dot_general(
        left, right, (((1,), (1,)), ((), ())), preferred_element_type=jnp.float32
    )


def on_device(
    tokens,
    cotangent,
    item_lengths,
    qkv_weight,
    qkv_first,
    qkv_second,
    out_weight,
    out_first,
    out_second,
    up_weight,
    up_first,
    up_second,
    down_weight,
    down_first,
    down_second,
    norm_params,
    norm_first,
    norm_second,
    conv_kernel,
    conv_first,
    conv_second,
):
    temper = HEAD ** (-0.5)
    col_total = ITEMS * LAND
    w_qkv, w_out, w_up, w_down, gains_low = (
        lax.all_gather(qkv_weight.astype(jnp.bfloat16), ("seq", "grp"), axis=0, tiled=True),
        lax.all_gather(out_weight.astype(jnp.bfloat16), ("seq", "grp"), axis=0, tiled=True),
        lax.all_gather(up_weight.astype(jnp.bfloat16), ("seq", "grp"), axis=0, tiled=True),
        lax.all_gather(down_weight.astype(jnp.bfloat16), ("seq", "grp"), axis=0, tiled=True),
        lax.all_gather(norm_params.astype(jnp.bfloat16), ("seq", "grp"), axis=1, tiled=True),
    )
    gains_all = gains_low.astype(jnp.float32)
    lengths = item_lengths[0]
    first_row = lax.axis_index(("seq", "grp")) * TOK_DEV
    positions = first_row - HALO + jnp.arange(TOK_DEV + 2 * HALO, dtype=jnp.int32)
    item_ext, column_ext = locate(positions, lengths)
    item_mid = item_ext[HALO : HALO + TOK_DEV]
    column_mid = column_ext[HALO : HALO + TOK_DEV]
    col_ids = jnp.arange(col_total, dtype=jnp.int32)
    col_hot = (column_mid[:, None] == col_ids[None, :]).astype(jnp.bfloat16)
    member = (item_mid[:, None] == (col_ids // LAND)[None, :]).astype(jnp.float32)
    counts_f = landmark_counts(lengths).astype(jnp.float32)
    projected = jnp.dot(tokens, w_qkv, preferred_element_type=jnp.float32)
    proj_low = projected.astype(jnp.bfloat16)
    queries = proj_low[:, :D]
    key_rows = proj_low[:, D : 2 * D]
    value_rows = proj_low[:, 2 * D :]
    land_sums = lax.psum(contract_rows(col_hot, proj_low[:, : 2 * D]), ("seq", "grp"))
    mean_q = (land_sums[:, :D] / counts_f[:, None]).astype(jnp.bfloat16)
    mean_k = (land_sums[:, D:] / counts_f[:, None]).astype(jnp.bfloat16)
    query_heads = queries.reshape(TOK_DEV, HEADS, HEAD)
    key_heads = key_rows.reshape(TOK_DEV, HEADS, HEAD)
    value_heads = value_rows.reshape(TOK_DEV, HEADS, HEAD)
    mean_q3 = mean_q.reshape(col_total, HEADS, HEAD)
    mean_k3 = mean_k.reshape(col_total, HEADS, HEAD)
    scores_key = (
        jnp.einsum("chd,phd->chp", mean_q3, key_heads, preferred_element_type=jnp.float32) * temper
    )
    expo_key = jnp.exp(scores_key) * jnp.transpose(member)[:, None, :]
    expo_low = expo_key.astype(jnp.bfloat16)
    num_part = jnp.einsum(
        "chp,phd->chd", expo_low, value_heads, preferred_element_type=jnp.float32
    ).reshape(col_total, D)
    num_all, den_all = lax.psum((num_part, jnp.sum(expo_key, axis=2)), ("seq", "grp"))
    query_marks4 = mean_q.reshape(ITEMS, LAND, HEADS, HEAD)
    key_marks4 = mean_k.reshape(ITEMS, LAND, HEADS, HEAD)
    mark_scores = (
        jnp.einsum("ajhd,akhd->ahjk", query_marks4, key_marks4, preferred_element_type=jnp.float32)
        * temper
    )
    mixed_rows, mix_pull = jax.vjp(mixing_rest, mark_scores, num_all, den_all)
    mixed3 = mixed_rows.astype(jnp.bfloat16).reshape(col_total, HEADS, HEAD)
    scores_tok = (
        jnp.einsum("phd,chd->phc", query_heads, mean_k3, preferred_element_type=jnp.float32)
        * temper
    )
    expo_tok = jnp.exp(scores_tok) * member[:, None, :]
    attn_probs = expo_tok / jnp.sum(expo_tok, axis=2, keepdims=True)
    probs_low = attn_probs.astype(jnp.bfloat16)
    attended = jnp.einsum(
        "phc,chd->phd", probs_low, mixed3, preferred_element_type=jnp.float32
    ).reshape(TOK_DEV, D)
    value_ext = extended(value_rows, ((("seq", "grp"), 0),), HALO)
    channel_taps = jnp.repeat(conv_kernel, HEAD, axis=0)
    same_masks = [
        (item_ext[offset : offset + TOK_DEV] == item_mid).astype(jnp.float32)
        for offset in range(KERNEL)
    ]
    conv_out = jnp.zeros((TOK_DEV, D), jnp.float32)
    for offset in range(KERNEL):
        conv_out = conv_out + value_ext[offset : offset + TOK_DEV] * (
            channel_taps[:, offset][None, :] * same_masks[offset][:, None]
        )
    branch = (attended + conv_out).astype(jnp.bfloat16)
    attn_out = jnp.dot(branch, w_out, preferred_element_type=jnp.float32)
    normed_one, norm_one_pull = jax.vjp(
        layer_norm, tokens.astype(jnp.float32) + attn_out, gains_all[0], gains_all[1]
    )
    normed_low = normed_one.astype(jnp.bfloat16)
    up_out = jnp.dot(normed_low, w_up, preferred_element_type=jnp.float32)
    activated, gelu_pull = jax.vjp(gelu_exact, up_out)
    act_low = activated.astype(jnp.bfloat16)
    down_out = jnp.dot(act_low, w_down, preferred_element_type=jnp.float32)
    result, norm_two_pull = jax.vjp(layer_norm, normed_one + down_out, gains_all[2], gains_all[3])
    d_hidden_two, d_gain_two, d_shift_two = norm_two_pull(cotangent.astype(jnp.float32))
    d_down_low = d_hidden_two.astype(jnp.bfloat16)
    grad_down = contract_rows(act_low, d_down_low)
    (d_up,) = gelu_pull(contract_cols(d_down_low, w_down))
    d_up_low = d_up.astype(jnp.bfloat16)
    grad_up = contract_rows(normed_low, d_up_low)
    d_normed = d_hidden_two + contract_cols(d_up_low, w_up)
    d_hidden_one, d_gain_one, d_shift_one = norm_one_pull(d_normed)
    d_attn_low = d_hidden_one.astype(jnp.bfloat16)
    grad_out = contract_rows(branch, d_attn_low)
    d_branch_low = contract_cols(d_attn_low, w_out).astype(jnp.bfloat16)
    d_branch_f = d_branch_low.astype(jnp.float32)
    d_branch_ext = extended(d_branch_low, ((("seq", "grp"), 0),), HALO)
    d_values_conv = jnp.zeros((TOK_DEV, D), jnp.float32)
    tap_grads = []
    for offset in range(KERNEL):
        d_values_conv = d_values_conv + d_branch_ext[offset : offset + TOK_DEV] * (
            channel_taps[:, KERNEL - 1 - offset][None, :] * same_masks[offset][:, None]
        )
        tap_grads.append(
            jnp.sum(
                d_branch_f * value_ext[offset : offset + TOK_DEV] * same_masks[offset][:, None],
                axis=0,
            )
        )
    grad_conv = jnp.sum(jnp.stack(tap_grads, axis=1).reshape(HEADS, HEAD, KERNEL), axis=1)
    d_attended = d_branch_low.reshape(TOK_DEV, HEADS, HEAD)
    d_mixed_part = jnp.einsum(
        "phc,phd->chd", probs_low, d_attended, preferred_element_type=jnp.float32
    ).reshape(col_total, D)
    d_probs = jnp.einsum("phd,chd->phc", d_attended, mixed3, preferred_element_type=jnp.float32)
    d_scores_tok = (
        attn_probs * (d_probs - jnp.sum(attn_probs * d_probs, axis=2, keepdims=True))
    ).astype(jnp.bfloat16)
    d_query_tok = (
        jnp.einsum("phc,chd->phd", d_scores_tok, mean_k3, preferred_element_type=jnp.float32)
        * temper
    )
    d_meank_part = (
        jnp.einsum(
            "phc,phd->chd", d_scores_tok, query_heads, preferred_element_type=jnp.float32
        ).reshape(col_total, D)
        * temper
    )
    d_mixed, d_meank_tok = lax.psum((d_mixed_part, d_meank_part), ("seq", "grp"))
    d_mark_scores, d_num, d_den = mix_pull(d_mixed)
    d_mark_scaled = d_mark_scores * temper
    d_mean_q_mix = jnp.einsum(
        "ahjk,akhd->ajhd", d_mark_scaled, key_marks4.astype(jnp.float32), precision=HIGHEST_PREC
    ).reshape(col_total, D)
    d_mean_k_mix = jnp.einsum(
        "ahjk,ajhd->akhd", d_mark_scaled, query_marks4.astype(jnp.float32), precision=HIGHEST_PREC
    ).reshape(col_total, D)
    d_num3 = d_num.reshape(col_total, HEADS, HEAD)
    d_expo = d_den[:, :, None] + jnp.einsum(
        "chd,phd->chp", d_num3, value_heads.astype(jnp.float32), precision=HIGHEST_PREC
    )
    d_scores_key = (expo_key * d_expo).astype(jnp.bfloat16)
    d_key_mix = (
        jnp.einsum("chp,chd->phd", d_scores_key, mean_q3, preferred_element_type=jnp.float32)
        * temper
    )
    d_meanq_part = (
        jnp.einsum(
            "chp,phd->chd", d_scores_key, key_heads, preferred_element_type=jnp.float32
        ).reshape(col_total, D)
        * temper
    )
    d_value_mix = jnp.einsum(
        "chp,chd->phd", expo_low.astype(jnp.float32), d_num3, precision=HIGHEST_PREC
    )
    d_meanq_tok = lax.psum(d_meanq_part, ("seq", "grp"))
    d_sums = (
        jnp.concatenate([d_mean_q_mix + d_meanq_tok, d_mean_k_mix + d_meank_tok], axis=1)
        / counts_f[:, None]
    )
    d_land_rows = jnp.dot(col_hot.astype(jnp.float32), d_sums, precision=HIGHEST_PREC)
    d_queries = d_query_tok.reshape(TOK_DEV, D) + d_land_rows[:, :D]
    d_keys = d_key_mix.reshape(TOK_DEV, D) + d_land_rows[:, D:]
    d_values = d_value_mix.reshape(TOK_DEV, D) + d_values_conv
    d_proj_low = jnp.concatenate([d_queries, d_keys, d_values], axis=1).astype(jnp.bfloat16)
    grad_qkv = contract_rows(tokens, d_proj_low)
    input_grad = (d_hidden_one + contract_cols(d_proj_low, w_qkv)).astype(jnp.bfloat16)
    grad_norms = jnp.stack([d_gain_one, d_shift_one, d_gain_two, d_shift_two])
    group_qkv, group_out, group_up, group_down, group_norm = (
        lax.psum_scatter(grad_qkv, ("seq", "grp"), scatter_dimension=0, tiled=True),
        lax.psum_scatter(grad_out, ("seq", "grp"), scatter_dimension=0, tiled=True),
        lax.psum_scatter(grad_up, ("seq", "grp"), scatter_dimension=0, tiled=True),
        lax.psum_scatter(grad_down, ("seq", "grp"), scatter_dimension=0, tiled=True),
        lax.psum_scatter(grad_norms, ("seq", "grp"), scatter_dimension=1, tiled=True),
    )
    shard_qkv, shard_out, shard_up, shard_down, shard_norm, conv_rep = (
        lax.psum(group_qkv.astype(jnp.bfloat16), "rep").astype(jnp.float32),
        lax.psum(group_out.astype(jnp.bfloat16), "rep").astype(jnp.float32),
        lax.psum(group_up.astype(jnp.bfloat16), "rep").astype(jnp.float32),
        lax.psum(group_down.astype(jnp.bfloat16), "rep").astype(jnp.float32),
        lax.psum(group_norm.astype(jnp.bfloat16), "rep").astype(jnp.float32),
        lax.psum(grad_conv.astype(jnp.bfloat16), "rep").astype(jnp.float32),
    )
    local_sq = (
        jnp.sum(shard_qkv * shard_qkv)
        + jnp.sum(shard_out * shard_out)
        + jnp.sum(shard_up * shard_up)
        + jnp.sum(shard_down * shard_down)
        + jnp.sum(shard_norm * shard_norm)
    )
    total_sq, conv_total = lax.psum((local_sq, conv_rep), ("seq", "grp"))
    grad_total = jnp.sqrt(total_sq + jnp.sum(conv_total * conv_total))
    clip_factor = MAX_NORM / jnp.maximum(grad_total, MAX_NORM)
    qkv_new = adamw(
        qkv_weight, qkv_first, qkv_second, shard_qkv, clip_factor, RATE_MATRIX, DECAY_RATE
    )
    out_new = adamw(
        out_weight, out_first, out_second, shard_out, clip_factor, RATE_MATRIX, DECAY_RATE
    )
    up_new = adamw(up_weight, up_first, up_second, shard_up, clip_factor, RATE_MATRIX, DECAY_RATE)
    down_new = adamw(
        down_weight, down_first, down_second, shard_down, clip_factor, RATE_MATRIX, DECAY_RATE
    )
    norm_new = adamw(norm_params, norm_first, norm_second, shard_norm, clip_factor, RATE_NORM, 0.0)
    conv_new = adamw(conv_kernel, conv_first, conv_second, conv_total, clip_factor, RATE_CONV, 0.0)
    return (
        result.astype(jnp.bfloat16),
        input_grad,
        grad_total,
        qkv_new[0],
        qkv_new[1],
        qkv_new[2],
        out_new[0],
        out_new[1],
        out_new[2],
        up_new[0],
        up_new[1],
        up_new[2],
        down_new[0],
        down_new[1],
        down_new[2],
        norm_new[0],
        norm_new[1],
        norm_new[2],
        conv_new[0],
        conv_new[1],
        conv_new[2],
    )


SHARD = D // GRP_DEV
BLK = (SHARD, D)


class Spot:
    def __init__(self):
        self.rep, self.seq, self.grp = lax.axis_index("rep"), lax.axis_index("seq"), lax.axis_index("grp")
        self.me = self.seq * 2 + self.grp
        self.xn = self.rep + 1 - 2 * lax.rem(self.rep, 2)
        self.yn = lax.rem(self.rep + 2, 4)
        self.dn = 3 - self.rep
        self.to_x = (self.xn, self.seq, self.grp)
        self.to_y = (self.yn, self.seq, self.grp)
        self.to_d = (self.dn, self.seq, self.grp)
        self.to_core = (self.rep, self.seq, 1 - self.grp)

    def z(self, step):
        return lax.rem(self.seq + step, 4)

    def to_z(self, step):
        return (self.rep, self.z(step), self.grp)

    def greet_all(self):
        self.signal_all()
        self.wait_all()

    def wait_all(self):
        pl.semaphore_wait(pltpu.get_barrier_semaphore(), GRP_DEV + 2)

    def signal_all(self):
        barrier = pltpu.get_barrier_semaphore()
        for device in (self.to_x, self.to_y, self.to_d):
            pl.semaphore_signal(barrier, inc=1, device_id=device, device_id_type=MESH_ID)
        for _, other in group_peers(self.me):
            pl.semaphore_signal(barrier, inc=1, device_id=place(self.rep, other), device_id_type=MESH_ID)


CHUNKS = 3
CHUNK = SHARD // CHUNKS
EARLY = tuple(range(CHUNKS))
UP, DOWN = CHUNKS, CHUNKS + 1


def unit_of(refs, part, shard, quarter):
    if part < UP:
        row = pl.multiple_of(shard * SHARD + part * CHUNK, CHUNK)
        return refs[0].at[pl.ds(row, CHUNK), pl.ds(pl.multiple_of(quarter * D, D), D)]
    if part == UP:
        row = pl.multiple_of(shard * SHARD, SHARD)
        return refs[1].at[pl.ds(row, SHARD), pl.ds(pl.multiple_of(quarter * D, D), D)]
    row = pl.multiple_of(shard * 4 * SHARD + quarter * SHARD, SHARD)
    return refs[2].at[pl.ds(row, SHARD), :]


def shard_of(refs, part, shard):
    if part < UP:
        row = pl.multiple_of(shard * SHARD + part * CHUNK, CHUNK)
        return refs[0].at[pl.ds(row, CHUNK), :]
    rows = SHARD if part == UP else 4 * SHARD
    return refs[part - UP + 1].at[pl.ds(pl.multiple_of(shard * rows, SHARD), rows), :]


class Gather:
    def __init__(self, spot, refs, sems):
        self.spot, self.refs = spot, refs
        (self.zs, self.zr, self.xs, self.xr, self.ys, self.yr, self.fs, self.fr, self.cs, self.cr) = sems

    def unit(self, part, seq, quarter):
        return unit_of(self.refs, part, seq * 2 + self.spot.grp, quarter)

    def when(self, part, quarter, late):
        if part >= UP:
            return lambda step: step()
        return pl.when((quarter == 3) if late else (quarter != 3))

    def sources(self):
        return [(step, self.spot.z(4 - step)) for step in range(1, 4)]

    def start(self, part):
        spot = self.spot
        mine = self.unit(part, spot.seq, spot.rep)
        for step in range(1, 4):
            push(mine, mine, self.zs.at[part, step - 1], self.zr.at[part, spot.seq], spot.to_z(step))
        own = shard_of(self.refs, part, spot.me)
        push(own, own, self.cs.at[part, 12], self.cr.at[part, 12], spot.to_core)

    def spread(self, part, late=False):
        spot = self.spot
        for step, src in self.sources():
            @self.when(part, spot.rep, late)
            def _():
                unit = self.unit(part, src, spot.rep)
                arrive(unit, self.zr.at[part, src])
                push(unit, unit, self.xs.at[part, step - 1], self.xr.at[part, src], spot.to_x)
                push(unit, unit, self.ys.at[part, step - 1], self.yr.at[part, src], spot.to_y)
                push(unit, unit, self.cs.at[part, step - 1], self.cr.at[part, src], spot.to_core)

    def relay(self, part, late=False):
        spot = self.spot
        for step, src in self.sources():
            @self.when(part, spot.xn, late)
            def _():
                unit = self.unit(part, src, spot.xn)
                arrive(unit, self.xr.at[part, src])

                @pl.when(lax.rem(src + part, 2) == 0)
                def _():
                    push(unit, unit, self.fs.at[part, step - 1], self.fr.at[part, src], spot.to_y)

                push(unit, unit, self.cs.at[part, 2 + step], self.cr.at[part, 4 + src], spot.to_core)

            @self.when(part, spot.yn, late)
            def _():
                unit = self.unit(part, src, spot.yn)
                arrive(unit, self.yr.at[part, src])

                @pl.when(lax.rem(src + part, 2) == 1)
                def _():
                    push(unit, unit, self.fs.at[part, step - 1], self.fr.at[part, src], spot.to_x)

                push(unit, unit, self.cs.at[part, 5 + step], self.cr.at[part, 8 + src], spot.to_core)

    def last(self, part, late=False):
        spot = self.spot
        for step, src in self.sources():
            @self.when(part, spot.dn, late)
            def _():
                unit = self.unit(part, src, spot.dn)
                arrive(unit, self.fr.at[part, src])
                push(unit, unit, self.cs.at[part, 8 + step], self.cr.at[part, 13 + src], spot.to_core)

    def finish(self, part, late=False):
        spot = self.spot
        other = 1 - spot.grp
        if not late:
            arrive(shard_of(self.refs, part, spot.seq * 2 + other), self.cr.at[part, 12])
        for base, quarter in ((0, spot.rep), (4, spot.xn), (8, spot.yn), (13, spot.dn)):
            @self.when(part, quarter, late)
            def _():
                for step, src in self.sources():
                    arrive(unit_of(self.refs, part, src * 2 + other, quarter), self.cr.at[part, base + src])

    def sent(self, part):
        spot = self.spot
        unit = self.unit(part, spot.seq, spot.rep)
        for step in range(3):
            for sem in (self.zs, self.xs, self.ys, self.fs):
                arrive(unit, sem.at[part, step])
        for index in range(12):
            arrive(unit, self.cs.at[part, index])
        arrive(shard_of(self.refs, part, spot.me), self.cs.at[part, 12])


def gather_sems():
    dma = pltpu.SemaphoreType.DMA
    return [dma((CHUNKS + 2, n)) for n in (3, 4, 3, 4, 3, 4, 3, 4, 13, 17)]


class Reduce:
    def __init__(self, spot, own, kept, bufs, sems):
        self.spot, self.own, self.kept = spot, own, kept
        self.rc, self.rx, self.ry, self.r2x, self.r2y, self.rz, self.fin = bufs
        (self.cs, self.cr, self.xs, self.xr, self.ys, self.yr, self.x2s, self.x2r, self.y2s, self.y2r,
         self.zs, self.zr, self.fs, self.fr) = sems

    def chip(self, m):
        spot = self.spot
        for seq in range(4):
            for quarter in range(4):
                push(self.own(m, seq * 2 + 1 - spot.grp, quarter), self.rc.at[m, seq, quarter],
                     self.cs.at[m], self.cr.at[m], spot.to_core)

    def add(self, left, right):
        return (left.astype(F32) + right.astype(F32)).astype(BF)

    def plane(self, m):
        spot = self.spot
        rc = self.rc
        arrive(rc.at[m], self.cr.at[m])
        for quarter in range(4):
            @pl.loop(0, 4)
            def _(seq):
                rc[m, seq, quarter] = self.add(rc[m, seq, quarter], self.kept(m, seq, quarter)[...])

        for j in range(2):
            for slot, quarter in enumerate((spot.xn, spot.dn)):
                push(rc.at[m, j, quarter], self.rx.at[m, j, slot], self.xs.at[m], self.xr.at[m], spot.to_x)
            for slot, quarter in enumerate((spot.yn, spot.dn)):
                push(rc.at[m, 2 + j, quarter], self.ry.at[m, j, slot], self.ys.at[m], self.yr.at[m], spot.to_y)

    def plane_two(self, m):
        spot = self.spot
        rc = self.rc
        arrive(self.rx.at[m], self.xr.at[m])

        @pl.loop(0, 2)
        def _(j):
            rc[m, j, spot.yn] = self.add(rc[m, j, spot.yn], self.rx[m, j, 1])

        for j in range(2):
            push(rc.at[m, j, spot.yn], self.r2y.at[m, j], self.y2s.at[m], self.y2r.at[m], spot.to_y)
        arrive(self.ry.at[m], self.yr.at[m])

        @pl.loop(0, 2)
        def _(j):
            rc[m, 2 + j, spot.xn] = self.add(rc[m, 2 + j, spot.xn], self.ry[m, j, 1])

        for j in range(2):
            push(rc.at[m, 2 + j, spot.xn], self.r2x.at[m, j], self.x2s.at[m], self.x2r.at[m], spot.to_x)

    def line(self, m):
        spot = self.spot
        rc = self.rc
        arrive(self.r2y.at[m], self.y2r.at[m])
        arrive(self.r2x.at[m], self.x2r.at[m])

        @pl.loop(0, 2)
        def _(j):
            rc[m, j, spot.rep] = (
                rc[m, j, spot.rep].astype(F32) + self.rx[m, j, 0].astype(F32) + self.r2y[m, j].astype(F32)
            ).astype(BF)
            rc[m, 2 + j, spot.rep] = (
                rc[m, 2 + j, spot.rep].astype(F32) + self.ry[m, j, 0].astype(F32) + self.r2x[m, j].astype(F32)
            ).astype(BF)

        for step in range(1, 4):
            push(rc.at[m, spot.z(step), spot.rep], self.rz.at[m, spot.seq],
                 self.zs.at[m, step - 1], self.zr.at[m, spot.seq], spot.to_z(step))

    def share(self, m):
        spot = self.spot
        total = self.rc[m, spot.seq, spot.rep].astype(F32)
        for step in range(1, 4):
            arrive(self.rz.at[m, spot.z(step)], self.zr.at[m, spot.z(step)])
            total = total + self.rz[m, spot.z(step)].astype(F32)
        self.fin[m, spot.rep] = total.astype(BF)
        mine = self.fin.at[m, spot.rep]
        for step, device in enumerate((spot.to_x, spot.to_y, spot.to_d)):
            push(mine, mine, self.fs.at[m, step], self.fr.at[m, spot.rep], device)

    def done(self, m):
        spot = self.spot
        for other in (spot.xn, spot.yn, spot.dn):
            arrive(self.fin.at[m, other], self.fr.at[m, other])

    def sent(self, m):
        arrive(self.rc.at[m], self.cs.at[m])
        arrive(self.rx.at[m], self.xs.at[m])
        arrive(self.ry.at[m], self.ys.at[m])
        arrive(self.r2x.at[m], self.x2s.at[m])
        arrive(self.r2y.at[m], self.y2s.at[m])
        for step in range(3):
            arrive(self.fin.at[m, 0], self.zs.at[m, step])
            arrive(self.fin.at[m, 0], self.fs.at[m, step])


def reduce_bufs():
    vm = pltpu.VMEM
    return [vm((3, 4, 4, *BLK), BF), vm((3, 2, 2, *BLK), BF), vm((3, 2, 2, *BLK), BF),
            vm((3, 2, *BLK), BF), vm((3, 2, *BLK), BF), vm((3, 4, *BLK), BF)]


def reduce_sems():
    dma = pltpu.SemaphoreType.DMA
    return [dma((3,)) for _ in range(10)] + [dma((3, 3)), dma((3, 4)), dma((3, 3)), dma((3, 4))]


class Small:
    def __init__(self, spot, src, one, two, pair, sems):
        self.spot, self.src, self.one, self.two, self.pair = spot, src, one, two, pair
        self.s1, self.r1, self.sp, self.rp, self.s2, self.r2 = sems

    def start(self):
        spot = self.spot
        for step, device in enumerate((spot.to_x, spot.to_y, spot.to_d)):
            push(self.src, self.one.at[spot.rep], self.s1.at[step], self.r1.at[spot.rep], device)

    def middle(self):
        spot = self.spot
        total = self.src[...]
        for other in (spot.xn, spot.yn, spot.dn):
            arrive(self.one.at[other], self.r1.at[other])
            total = total + self.one[other]
        self.pair[0] = total
        push(self.pair.at[0], self.pair.at[1], self.sp.at[0], self.rp.at[0], spot.to_core)

    def across(self):
        spot = self.spot
        arrive(self.pair.at[1], self.rp.at[0])
        self.two[spot.seq] = self.pair[0] + self.pair[1]
        mine = self.two.at[spot.seq]
        for step in range(1, 4):
            push(mine, mine, self.s2.at[step - 1], self.r2.at[spot.seq], spot.to_z(step))

    def end(self):
        spot = self.spot
        for step in range(1, 4):
            arrive(self.two.at[spot.z(step)], self.r2.at[spot.z(step)])
        total = self.two[0] + self.two[1] + self.two[2] + self.two[3]
        arrive(self.pair.at[0], self.sp.at[0])
        for step in range(3):
            arrive(self.one.at[0], self.s1.at[step])
            arrive(self.two.at[0], self.s2.at[step])
        return total


def square_sum(spot, fin, sq, ss, sr, extra):
    total = jnp.zeros((8, 128), F32)
    for m in range(3):
        for quarter in range(4):
            value = fin[m, quarter].astype(F32)
            value = value * value
            rows = value[0:8]
            for k in range(1, SHARD // 8):
                rows = rows + value[8 * k : 8 * k + 8]
            for k in range(D // 128):
                total = total + rows[:, 128 * k : 128 * k + 128]
    sq[spot.me] = total
    for step, other in group_peers(spot.me):
        push(sq.at[spot.me], sq.at[spot.me], ss.at[step - 1], sr.at[spot.me], place(spot.rep, other))
    for step, other in group_peers(spot.me):
        arrive(sq.at[other], sr.at[other])
    total = sq[0]
    for j in range(1, GRP_DEV):
        total = total + sq[j]
    for step in range(GRP_DEV - 1):
        arrive(sq.at[0], ss.at[step])
    return jnp.sum(total, keepdims=True) + extra


TOK = 256

TEMPER = HEAD ** (-0.5)
MESH_ID = pl.DeviceIdType.MESH
BF = jnp.bfloat16
F32 = jnp.float32
EXT = 384


def nn(left, right):
    return jnp.dot(left, right, preferred_element_type=F32)


def nt(left, right):
    return lax.dot_general(left, right, (((1,), (1,)), ((), ())), preferred_element_type=F32)


def tn(left, right):
    return lax.dot_general(left, right, (((0,), (0,)), ((), ())), preferred_element_type=F32)


def iota(shape, dim):
    return lax.broadcasted_iota(jnp.int32, shape, dim)


def split(value):
    high = value.astype(BF)
    return high, (value - high.astype(F32)).astype(BF)


def lane_head(shape):
    return iota(shape, len(shape) - 1) // HEAD


def block_diag(value):
    width = value.shape[1]
    heads = width // HEAD
    tiled = jnp.concatenate([value] * heads, axis=0)
    keep = (iota((width, width), 0) // HEAD) == (iota((width, width), 1) // HEAD)
    return jnp.where(keep, tiled, jnp.zeros_like(tiled))


def left_of(value):
    high, low = split(value)
    return jnp.concatenate([high, low], axis=0)


def right_of(value):
    high, low = split(value)
    return block_diag(high), block_diag(low)


def mm_parts(left, right):
    rows = left.shape[0] // 2
    both = nn(left, right[0])
    return both[:rows] + both[rows:] + nn(left[:rows], right[1])


def mm(left, right):
    return mm_parts(left_of(left), right_of(right))


def packed_eye(width):
    return (iota((LAND, width), 0) == iota((LAND, width), 1) % HEAD).astype(F32)


def head_total(row):
    heads = lane_head(row.shape)
    out = jnp.zeros_like(row)
    for head in range(row.shape[1] // HEAD):
        mine = heads == head
        out = jnp.where(mine, jnp.sum(jnp.where(mine, row, 0.0), axis=1, keepdims=True), out)
    return out


def head_rows(value, reduce_fn, neutral):
    heads = lane_head(value.shape)
    out = jnp.zeros_like(value)
    for head in range(value.shape[1] // HEAD):
        mine = heads == head
        out = jnp.where(mine, reduce_fn(jnp.where(mine, value, neutral), axis=1, keepdims=True), out)
    return out


def kernel_two(query_marks, key_marks):
    scores = nt(query_marks, block_diag(key_marks)) * TEMPER
    scores_t = nt(key_marks, block_diag(query_marks)) * TEMPER
    expo = jnp.exp(scores - head_rows(scores, jnp.max, -jnp.inf))
    plain = expo / head_rows(expo, jnp.sum, 0.0)
    expo_t = jnp.exp(scores_t - jnp.max(scores_t, axis=0, keepdims=True))
    flipped = expo_t / jnp.sum(expo_t, axis=0, keepdims=True)
    return plain, flipped


def newton(plains, flippeds, save):
    lefts = [left_of(p) for p in plains]
    invs = [
        f / head_total(jnp.sum(f * f, axis=0, keepdims=True)) for f in flippeds
    ]
    for it in range(NS_STEPS):
        prods = [mm_parts(a, right_of(z)) for a, z in zip(lefts, invs)]
        prights = [right_of(p) for p in prods]
        squares = [mm_parts(left_of(p), r) for p, r in zip(prods, prights)]
        steps = [mm_parts(left_of(z), r) for z, r in zip(invs, prights)]
        for index in range(len(invs)):
            save(it, index, invs[index], prods[index], squares[index], steps[index])
        invs = [
            0.25 * (13.0 * z - 15.0 * s + mm(7.0 * z - s, q)) for z, s, q in zip(invs, steps, squares)
        ]
    return invs


def lens_of(len_ref):
    l0, l1, l2, l3 = len_ref[0, 0], len_ref[0, 1], len_ref[0, 2], len_ref[0, 3]
    return (l0, l1, l2, l3), (0, l0, l0 + l1, l0 + l1 + l2)


def choose(item, values):
    out = jnp.where(item == 0, values[0], values[1])
    out = jnp.where(item == 2, values[2], out)
    return jnp.where(item == 3, values[3], out)


def column_edges(col, lens, starts):
    item = col // LAND
    seg = col % LAND
    length = choose(item, lens)
    start = choose(item, starts)
    low_edge = start + ((seg * length + LAND - 1) >> 6)
    high_edge = start + (((seg + 1) * length + LAND - 1) >> 6)
    return low_edge, high_edge, start, start + length


def item_of(pos, starts):
    return (
        (pos >= starts[1]).astype(jnp.int32)
        + (pos >= starts[2]).astype(jnp.int32)
        + (pos >= starts[3]).astype(jnp.int32)
    )


def pair_lanes(hp):
    return slice(128 * hp, 128 * hp + 128)


def both_heads(value):
    first = iota(value.shape, 1) < HEAD
    zero = jnp.zeros_like(value)
    return jnp.concatenate([jnp.where(first, value, zero), jnp.where(first, zero, value)], axis=0)


def pick_heads(value):
    rows = value.shape[0] // 2
    first = iota((rows, 128), 1) < HEAD
    return jnp.where(first, value[:rows], value[rows:])


def toeplitz(tap_row, same):
    wide = jnp.broadcast_to(tap_row, (TOK, EXT))
    return split(pltpu.roll(wide, 0, 1, stride=1, stride_axis=0) * same)


def conv_pair(taps_ref, hp, same, ext_pair):
    outs = []
    for head in (2 * hp, 2 * hp + 1):
        high, low = toeplitz(taps_ref[head : head + 1, :], same)
        outs.append(nn(high, ext_pair) + nn(low, ext_pair))
    first = iota((TOK, 128), 1) < HEAD
    return jnp.where(first, outs[0], outs[1])


def same_item(first_row, lens, starts, reverse=False):
    shape = (TOK, EXT)
    row = iota(shape, 0)
    if reverse:
        row = TOK - 1 - row
    pos = first_row + row
    other = first_row + iota(shape, 1) - HALO
    total = starts[3] + lens[3]
    inside = (other >= 0) & (other < total) & (item_of(pos, starts) == item_of(other, starts))
    return inside.astype(F32)


def group_peers(me):
    for step in range(1, GRP_DEV):
        yield step, lax.rem(me + step, GRP_DEV)


def place(rep, index):
    return (rep, index // 2, lax.rem(index, 2))


def greet(rep, me):
    barrier = pltpu.get_barrier_semaphore()
    for _, other in group_peers(me):
        pl.semaphore_signal(barrier, inc=1, device_id=place(rep, other), device_id_type=MESH_ID)
    pl.semaphore_wait(barrier, GRP_DEV - 1)


def push(src, dst, send_sem, recv_sem, device):
    copy = pltpu.make_async_remote_copy(
        src_ref=src, dst_ref=dst, send_sem=send_sem, recv_sem=recv_sem,
        device_id=device, device_id_type=MESH_ID,
    )
    copy.start()
    return copy


def attend_kernel(
    len_ref, x_ref, qkv_hbm, out_hbm, up_hbm, down_hbm, norm_ref, taps_ref,
    w_ref, wu_ref, wd_ref, wn_ref, q_ref, k_ref, v_ref, qm_ref, km_ref, wm_ref, a_ref, ext_ref,
    res_ref, vloc_ref, dloc_ref, resl_ref, vl_ref, dl_ref,
    win, halo, nd_src, nd_buf, wml, bias_cp, bias_pc, num_s, den_s, probs,
    qkv_st, out_st, up_st, down_st, hot_s, same_s, cv_s, res_s, wu_st, wd_st,
    win_s, win_r, halo_s, halo_r, nd_s, nd_r, wml_s, wml_r, load_s, norm_s, norm_r, *gather_sem,
):
    loads = [
        pltpu.make_async_copy(src, dst, load_s.at[i])
        for i, (src, dst) in enumerate(
            ((qkv_hbm, qkv_st), (out_hbm, out_st), (up_hbm, up_st), (down_hbm, down_st))
        )
    ]
    for load in loads:
        load.start()
    spot = Spot()
    rep, me = spot.rep, spot.me
    first_row = me * TOK
    is_owner = (me >= 1) & (me <= 6)
    lens, starts = lens_of(len_ref)
    def masks_for_columns():
        shape = (COLS, TOK)
        pos = first_row + iota(shape, 1)
        lo, hi, begin, end = column_edges(iota(shape, 0), lens, starts)
        hot_s[...] = ((pos >= lo) & (pos < hi)).astype(BF)
        bias_cp[...] = jnp.where((pos >= begin) & (pos < end), 0.0, -1e30)
        pshape = (TOK, COLS)
        ppos = first_row + iota(pshape, 0)
        _, _, pbegin, pend = column_edges(iota(pshape, 1), lens, starts)
        bias_pc[...] = jnp.where((ppos >= pbegin) & (ppos < pend), 0.0, -1e30)
        same_s[...] = same_item(first_row, lens, starts)

    gather = Gather(spot, (w_ref, wu_ref, wd_ref), gather_sem)
    row = pl.multiple_of(me * SHARD, SHARD)
    spot.signal_all()
    masks_for_columns()
    loads[0].wait()
    loads[1].wait()
    w_ref[pl.ds(row, SHARD), : 3 * D] = qkv_st[...].astype(BF)
    w_ref[pl.ds(row, SHARD), 3 * D :] = out_st[...].astype(BF)
    spot.wait_all()
    for part in EARLY:
        gather.start(part)
    loads[2].wait()
    loads[3].wait()
    wu_st[...] = up_st[...].astype(BF)
    wd_st[...] = down_st[...].astype(BF)
    own_up = pltpu.make_async_copy(wu_st, shard_of(gather.refs, UP, me), load_s.at[5])
    own_down = pltpu.make_async_copy(wd_st, shard_of(gather.refs, DOWN, me), load_s.at[6])
    own_up.start()
    own_down.start()
    wn_ref[me] = norm_ref[...].astype(BF)
    for step, other in group_peers(me):
        push(wn_ref.at[me], wn_ref.at[me], norm_s.at[step - 1], norm_r.at[me], place(rep, other))
    own_up.wait()
    own_down.wait()
    for index, part in enumerate(EARLY):
        gather.spread(part)
        if index > 0:
            gather.relay(EARLY[index - 1])
        if index > 1:
            gather.last(EARLY[index - 2])
    gather.start(UP)
    gather.relay(EARLY[-1])
    gather.last(EARLY[-2])
    gather.last(EARLY[-1])
    for part in EARLY:
        gather.finish(part)

    for part, ref in enumerate((q_ref, k_ref, v_ref)):
        ref[...] = nn(x_ref[...], w_ref[:, D * part : D * part + D]).astype(BF)

    @pl.when(me < GRP_DEV - 1)
    def _():
        push(v_ref.at[pl.ds(TOK - HALO, HALO)], halo.at[0], halo_s.at[0], halo_r.at[0], place(rep, me + 1))

    @pl.when(me > 0)
    def _():
        push(v_ref.at[pl.ds(0, HALO)], halo.at[1], halo_s.at[1], halo_r.at[1], place(rep, me - 1))

    qk = jnp.concatenate([q_ref[...], k_ref[...]], axis=1)
    hot = hot_s[...]
    wshape = (16, TOK)
    seg_hi = lens_edge(iota((LAND, TOK), 0) + 1, lens[1], starts[1])
    base = jnp.sum((seg_hi <= first_row).astype(jnp.int32).astype(F32), axis=0, keepdims=True).astype(jnp.int32)
    seg_w = base + iota(wshape, 0)
    wpos = first_row + iota(wshape, 1)
    whot = (
        (wpos >= lens_edge(seg_w, lens[1], starts[1]))
        & (wpos < lens_edge(seg_w + 1, lens[1], starts[1]))
        & (seg_w < LAND)
    ).astype(BF)
    wsum = nn(whot, qk)
    seg_c = base[:, :128] + iota((16, 128), 0)
    wcount = (lens_edge(seg_c + 1, lens[1], starts[1]) - lens_edge(seg_c, lens[1], starts[1])).astype(F32)
    wcount = jnp.concatenate([wcount] * 12, axis=1)
    win[me] = (wsum / wcount).astype(BF)
    for step, other in group_peers(me):
        push(win.at[me], win.at[me], win_s.at[step - 1], win_r.at[me], place(rep, other))

    sums = nn(hot, qk)
    clo, chi, _, _ = column_edges(iota((COLS, 128), 0), lens, starts)
    counts = (chi - clo).astype(F32)
    counts6 = jnp.concatenate([counts] * 6, axis=1)
    qm_ref[...] = (sums[:, :D] / counts6).astype(BF)
    km_ref[...] = (sums[:, D:] / counts6).astype(BF)

    gather.spread(UP)
    gather.start(DOWN)
    for part in EARLY:
        gather.spread(part, True)
    @pl.when(me > 0)
    def _():
        pltpu.make_async_copy(halo.at[0], halo.at[0], halo_r.at[0]).wait()
        ext_ref[0:HALO] = halo[0]

    @pl.when(me == 0)
    def _():
        ext_ref[0:HALO] = jnp.zeros((HALO, D), BF)

    @pl.when(me < GRP_DEV - 1)
    def _():
        pltpu.make_async_copy(halo.at[1], halo.at[1], halo_r.at[1]).wait()
        ext_ref[HALO + TOK : 2 * HALO + TOK] = halo[1]

    @pl.when(me == GRP_DEV - 1)
    def _():
        ext_ref[HALO + TOK : 2 * HALO + TOK] = jnp.zeros((HALO, D), BF)

    ext_ref[HALO : HALO + TOK] = v_ref[...]
    ext_ref[2 * HALO + TOK :] = jnp.zeros((EXT - TOK - 2 * HALO, D), BF)
    for hp in range(6):
        lanes = pair_lanes(hp)
        cv_s[:, lanes] = conv_pair(taps_ref, hp, same_s[...], ext_ref[:, lanes])
    gather.relay(UP)
    for step, other in group_peers(me):
        pltpu.make_async_copy(win.at[other], win.at[other], win_r.at[other]).wait()
    sshape = (LAND, 128)
    lane_dev = iota((LAND, 128), 1) // 16
    lane_w = iota((LAND, 128), 1) % 16
    seg_end = lens_edge(iota((LAND, 128), 0) + 1, lens[1], starts[1])
    bases = jnp.sum((seg_end <= lane_dev * TOK).astype(jnp.int32).astype(F32), axis=0, keepdims=True).astype(jnp.int32)
    scatter = (iota(sshape, 0) == bases + lane_w).astype(BF)
    long_rows = nn(scatter, win[...].reshape(128, 2 * D))
    qm_ref[LAND : 2 * LAND, :] = long_rows[:, :D].astype(BF)
    km_ref[LAND : 2 * LAND, :] = long_rows[:, D:].astype(BF)

    ones_wide = jnp.ones((TOK, 128), BF)
    ones_row = jnp.ones((8, TOK), BF)
    for hp in range(6):
        lanes = pair_lanes(hp)
        marks = both_heads(qm_ref[:, lanes])
        scores = nt(marks, k_ref[:, lanes]) * TEMPER
        expo = jnp.exp(scores + jnp.concatenate([bias_cp[...]] * 2, axis=0)).astype(BF)
        nd = nn(expo, jnp.concatenate([v_ref[:, lanes], ones_wide], axis=1))
        num = pick_heads(nd[:, :128])
        nd_src[hp, 0:LAND, :] = num[LAND : 2 * LAND]
        nd_src[hp, LAND : LAND + 8, :] = nt(
            ones_row, jnp.concatenate([expo[LAND : 2 * LAND], expo[COLS + LAND : COLS + 2 * LAND]], axis=0)
        )
        num_s[:, lanes] = num
        den_s[:, lanes] = pick_heads(nd[:, 128:])
    for owner in range(1, 7):
        @pl.when(me == owner)
        def _():
            nd_buf[owner] = nd_src[owner - 1]

        @pl.when(me != owner)
        def _():
            push(nd_src.at[owner - 1], nd_buf.at[me], nd_s.at[owner - 1], nd_r.at[me], place(rep, owner))

    wm_ref[...] = jnp.zeros_like(wm_ref)
    has_local = (me == 0) | (me == GRP_DEV - 1)
    slot_rows = (pl.multiple_of(jnp.where(me == 0, 0, 2 * LAND), LAND), 3 * LAND)
    cuts = [(slot, slice(256 * part, 256 * part + 256)) for slot in range(2) for part in range(3)]

    @pl.when(has_local)
    def _():
        def at(ref, slot, lanes):
            return ref[pl.ds(slot_rows[slot], LAND), lanes]

        plains, flippeds = zip(*[kernel_two(at(qm_ref, *c), at(km_ref, *c)) for c in cuts])

        def save(it, index, *mats):
            for m, mat in enumerate(mats):
                res_s[index, it, m] = mat

        invs = newton(plains, flippeds, save)
        keep = pltpu.make_async_copy(res_s, res_ref, load_s.at[4])
        keep.start()
        for (slot, lanes), inv in zip(cuts, invs):
            den = at(den_s, slot, lanes)
            den = jnp.where(den == 0.0, 1.0, den)
            val = at(num_s, slot, lanes) / den
            vloc_ref[slot, :, lanes] = val
            dloc_ref[slot, :, lanes] = den
            wm_ref[pl.ds(slot_rows[slot], LAND), lanes] = mm(inv, val).astype(BF)

    @pl.when(is_owner)
    def _():
        lanes = pl.ds(pl.multiple_of((me - 1) * 128, 128), 128)
        plain, flipped = kernel_two(qm_ref[LAND : 2 * LAND, lanes], km_ref[LAND : 2 * LAND, lanes])

        def save(it, index, *mats):
            for m, mat in enumerate(mats):
                resl_ref[it, m] = mat

        (inv,) = newton([plain], [flipped], save)
        for step, other in group_peers(me):
            pltpu.make_async_copy(nd_buf.at[other], nd_buf.at[other], nd_r.at[other]).wait()
        total = nd_buf[0]
        for j in range(1, GRP_DEV):
            total = total + nd_buf[j]
        row = total[LAND : LAND + 1, :]
        other_row = pltpu.roll(row, HEAD, 1)
        spread = jnp.where(iota((128, 128), 0) < HEAD, row, other_row)
        den = jnp.transpose(spread)[:LAND]
        val = total[:LAND] / den
        vl_ref[...] = val
        dl_ref[...] = den
        wml[me - 1] = mm(inv, val).astype(BF)
        for step, other in group_peers(me):
            push(wml.at[me - 1], wml.at[me - 1], wml_s.at[step - 1], wml_r.at[me - 1], place(rep, other))

    gather.spread(DOWN)
    for part in EARLY:
        gather.relay(part, True)
    for hp in range(6):
        lanes = pair_lanes(hp)
        scores = nt(q_ref[:, lanes], both_heads(km_ref[:, lanes])) * TEMPER
        for half in range(2):
            expo = jnp.exp(scores[:, COLS * half : COLS * half + COLS] + bias_pc[...])
            probs[hp, :, COLS * half : COLS * half + COLS] = (
                expo / jnp.sum(expo, axis=1, keepdims=True)
            ).astype(BF)

    gather.last(UP)
    gather.relay(DOWN)
    for owner in range(1, 7):
        @pl.when(me != owner)
        def _():
            pltpu.make_async_copy(wml.at[owner - 1], wml.at[owner - 1], wml_r.at[owner - 1]).wait()

        wm_ref[LAND : 2 * LAND, pair_lanes(owner - 1)] = wml[owner - 1]
    for hp in range(6):
        lanes = pair_lanes(hp)
        att = nn(probs[hp], both_heads(wm_ref[:, lanes]))
        a_ref[:, lanes] = (att + cv_s[:, lanes]).astype(BF)

    for part in EARLY:
        gather.last(part, True)
    gather.last(DOWN)
    for step, other in group_peers(me):
        arrive(wn_ref.at[other], norm_r.at[other])
        arrive(wn_ref.at[other], norm_s.at[step - 1])
    for part in EARLY:
        gather.finish(part, True)
    for part in (UP, DOWN):
        gather.finish(part)
    for part in (*EARLY, UP, DOWN):
        gather.sent(part)
    @pl.when(has_local)
    def _():
        pltpu.make_async_copy(res_s, res_ref, load_s.at[4]).wait()

    for step, other in group_peers(me):
        pltpu.make_async_copy(win.at[me], win.at[me], win_s.at[step - 1]).wait()
    for owner in range(1, 7):
        @pl.when(me != owner)
        def _():
            pltpu.make_async_copy(nd_src.at[owner - 1], nd_src.at[owner - 1], nd_s.at[owner - 1]).wait()

    @pl.when(is_owner)
    def _():
        for step, other in group_peers(me):
            pltpu.make_async_copy(wml.at[0], wml.at[0], wml_s.at[step - 1]).wait()

    @pl.when(me < GRP_DEV - 1)
    def _():
        pltpu.make_async_copy(halo.at[0], halo.at[0], halo_s.at[0]).wait()

    @pl.when(me > 0)
    def _():
        pltpu.make_async_copy(halo.at[1], halo.at[1], halo_s.at[1]).wait()


def arrive(ref, sem):
    pltpu.make_async_copy(ref, ref, sem).wait()


def lens_edge(seg, length, start):
    return start + ((seg * length + LAND - 1) >> 6)


COLS = ITEMS * LAND
VM = pl.BlockSpec(memory_space=pltpu.VMEM)
SM = pl.BlockSpec(memory_space=pltpu.SMEM)


def attend(item_lengths, tokens, qkv_weight, out_weight, up_weight, down_weight, norm_params, taps):
    sds = jax.ShapeDtypeStruct
    row = sds((TOK, D), BF)
    norm_pad = jnp.pad(norm_params, ((0, 12), (0, 128 - SHARD)))
    outs = [sds((D, 4 * D), BF), sds((D, FF), BF), sds((FF, D), BF), sds((8, 16, 128), BF),
            row, row, row, row, row, row, row, sds((EXT, D), BF),
            sds((6, NS_STEPS, 4, LAND, 256), F32), sds((2, LAND, D), F32), sds((2, LAND, D), F32),
            sds((NS_STEPS, 4, LAND, 128), F32), sds((LAND, 128), F32), sds((LAND, 128), F32)]
    dma = pltpu.SemaphoreType.DMA
    vm = pltpu.VMEM
    scratch = [
        vm((8, 16, 2 * D), BF), vm((2, HALO, D), BF), vm((6, LAND + 8, 128), F32),
        vm((8, LAND + 8, 128), F32), vm((6, LAND, 128), BF),
        vm((COLS, TOK), F32), vm((TOK, COLS), F32), vm((COLS, D), F32),
        vm((COLS, D), F32), vm((6, TOK, 2 * COLS), BF),
        vm((SHARD, 3 * D), F32), vm((SHARD, D), F32), vm((SHARD, FF), F32), vm((4 * SHARD, D), F32),
        vm((COLS, TOK), BF), vm((TOK, EXT), F32), vm((TOK, D), F32),
        vm((6, NS_STEPS, 4, LAND, 256), F32), vm((SHARD, FF), BF), vm((4 * SHARD, D), BF),
        dma((7,)), dma((8,)), dma((2,)), dma((2,)), dma((6,)), dma((8,)), dma((7,)), dma((6,)),
        dma((7,)), dma((7,)), dma((8,)), *gather_sems(),
    ]
    anyspace = pl.BlockSpec(memory_space=pl.ANY)
    w_all, w_up, w_down, norms, *rest = pl.pallas_call(
        attend_kernel, out_shape=outs, in_specs=[SM, VM, anyspace, anyspace, anyspace, anyspace, VM, VM],
        out_specs=[VM, anyspace, anyspace] + [VM] * 9 + [anyspace] + [VM] * 5, scratch_shapes=scratch, name="attend",
        compiler_params=pltpu.CompilerParams(collective_id=1, has_side_effects=True, vmem_limit_bytes=60 * 2**20),
    )(item_lengths, tokens, qkv_weight, out_weight, up_weight, down_weight, norm_pad, taps)
    gains = jnp.transpose(norms[:, :4, :SHARD], (1, 0, 2)).reshape(4, D)
    return w_all, w_up, w_down, gains, rest


def nt_parts(left, right):
    rows = left.shape[0] // 2
    both = nt(left, right[0])
    return both[:rows] + both[rows:] + nt(left[:rows], right[1])


def flip(value):
    high, low = split(value)
    eye = packed_eye(value.shape[1]).astype(BF)
    return nt(eye, block_diag(high)) + nt(eye, block_diag(low))


def half_sum(value):
    rows = value.shape[0] // 2
    return value[:rows] + value[rows:]


def newton_back(qms, kms, vals, dens, dwms, load):
    count = len(qms)
    plains = [kernel_two(q, k)[0] for q, k in zip(qms, kms)]
    krights = [right_of(p) for p in plains]
    ups = [nt_parts(left_of(v), right_of(d)) for v, d in zip(vals, dwms)]
    last = [load(NS_STEPS - 1, i) for i in range(count)]
    finals = [0.25 * (13.0 * m[0] - 15.0 * m[3] + mm(7.0 * m[0] - m[3], m[2])) for m in last]
    dvals = [mm(flip(z), d) for z, d in zip(finals, dwms)]
    dkts = [jnp.zeros_like(p) for p in plains]
    for it in reversed(range(NS_STEPS)):
        mats = [load(it, i) for i in range(count)]
        plefts = [left_of(m[1]) for m in mats]
        dys = [0.25 * mm(m[2], u) for m, u in zip(mats, ups)]
        dqs = [0.25 * mm(u, 7.0 * m[0] - m[3]) for m, u in zip(mats, ups)]
        drs = [-3.75 * u - dy for u, dy in zip(ups, dys)]
        dqrs = [right_of(d) for d in dqs]
        dps = [
            mm(dr, m[0]) + mm_parts(pl_, dqr) + mm(dq, m[1])
            for dr, m, pl_, dqr, dq in zip(drs, mats, plefts, dqrs, dqs)
        ]
        nexts = [
            3.25 * u + 7.0 * dy + mm_parts(pl_, right_of(dr))
            for u, dy, pl_, dr in zip(ups, dys, plefts, drs)
        ]
        dkts = [a + mm(m[0], d) for a, m, d in zip(dkts, mats, dps)]
        ups = [n + mm_parts(left_of(d), kr) for n, d, kr in zip(nexts, dps, krights)]
    outs = []
    for i in range(count):
        plain = plains[i]
        fro = head_total(jnp.sum(plain * plain, axis=0, keepdims=True))
        cross = head_total(jnp.sum(ups[i] * plain, axis=0, keepdims=True))
        dk = flip(dkts[i]) + ups[i] / fro - 2.0 * plain * (cross / (fro * fro))
        dscore = plain * (dk - head_rows(plain * dk, jnp.sum, 0.0)) * TEMPER
        dqm = half_sum(nn(left_of(dscore), block_diag(kms[i])))
        dkm = half_sum(nn(left_of(flip(dscore)), block_diag(qms[i])))
        dnum = (dvals[i] / dens[i]).astype(BF)
        dden = -head_rows(dnum.astype(F32) * vals[i], jnp.sum, 0.0)
        outs.append((dnum, dden, dqm, dkm))
    return outs


def twice(value):
    return jnp.concatenate([value, value], axis=0)


def attend_back_kernel(
    len_ref, x_ref, w_hbm, taps_ref, q_ref, k_ref, v_ref, qm_ref, km_ref, wm_ref, ext_ref,
    res_ref, vloc_ref, dloc_ref, resl_ref, vl_ref, dl_ref, da_ref, dh_ref,
    out_ref, up_hbm, down_hbm, norms_ref,
    gx_ref, fin_ref, total_ref, norm_ref,
    gw_ref, w_ref, stage, small_s, rc, rx, ry, r2x, r2y, rz, one, two, pair, sq,
    halo, dext, dwm_src, dwm_buf, dk1_src, dk1_buf, dn_buf, dq3_src, dq3_buf, ds_buf,
    bias_cp, dwm_s, dkm_s, dqm_s, dnum_s, dden_s, dq_s, dk_s, dv_s, dsum_s, dp_s, res_s, load_s,
    halo_s, halo_r, dwm_ss, dwm_r, dk1_ss, dk1_r, dn_ss, dn_r, dq3_ss, dq3_r, ds_ss, ds_r,
    stage_s, s1, r1, s2, r2, sp, rp, ss, sr, *red_sems,
):
    spot = Spot()
    spot.signal_all()
    rep, me = spot.rep, spot.me
    first_row = me * TOK
    is_owner = (me >= 1) & (me <= 6)
    lens, starts = lens_of(len_ref)
    has_local = (me == 0) | (me == GRP_DEV - 1)

    @pl.when(has_local)
    def _():
        pltpu.make_async_copy(res_ref, res_s, load_s.at[0]).start()

    load_w = pltpu.make_async_copy(w_hbm.at[:, pl.ds(0, 3 * D)], w_ref, load_s.at[1])

    def own(m, shard, quarter):
        row = pl.multiple_of(shard * SHARD, SHARD)
        if m == 0 and quarter == 3:
            return out_ref.at[pl.ds(row, SHARD), :]
        if m == 0:
            return gw_ref.at[pl.ds(row, SHARD), D * quarter : D * quarter + D]
        if m == 1:
            return up_hbm.at[pl.ds(row, SHARD), D * quarter : D * quarter + D]
        return down_hbm.at[pl.ds(pl.multiple_of(4 * row + SHARD * quarter, SHARD), SHARD), :]

    def kept(m, seq, quarter):
        if m == 0:
            return own(m, seq * 2 + spot.grp, quarter)
        return stage.at[m - 1, seq, quarter]

    for m in (2, 1):
        for seq in range(4):
            for quarter in range(4):
                pltpu.make_async_copy(
                    own(m, seq * 2 + spot.grp, quarter), stage.at[m - 1, seq, quarter], stage_s.at[m - 1]
                ).start()
    red = Reduce(spot, own, kept, (rc, rx, ry, r2x, r2y, rz, fin_ref), red_sems)
    small = Small(spot, small_s, one, two, pair, (s1, r1, sp, rp, s2, r2))
    spot.wait_all()

    @pl.when(me < GRP_DEV - 1)
    def _():
        push(da_ref.at[pl.ds(TOK - HALO, HALO)], halo.at[0], halo_s.at[0], halo_r.at[0], place(rep, me + 1))

    @pl.when(me > 0)
    def _():
        push(da_ref.at[pl.ds(0, HALO)], halo.at[1], halo_s.at[1], halo_r.at[1], place(rep, me - 1))

    red.chip(2)
    red.chip(1)
    shape = (COLS, TOK)
    pos = first_row + iota(shape, 1)
    _, _, begin, end = column_edges(iota(shape, 0), lens, starts)
    bias_cp[...] = jnp.where((pos >= begin) & (pos < end), 0.0, -1e30)

    def to_owner(src, buf, send, recv, hp):
        owner = hp + 1

        @pl.when(me == owner)
        def _():
            buf[owner] = src[hp]

        @pl.when(me != owner)
        def _():
            push(src.at[hp], buf.at[me], send.at[hp], recv.at[me], place(rep, owner))

    for hp in range(6):
        lanes = pair_lanes(hp)
        marks = both_heads(km_ref[:, lanes])
        scores = nt(marks, q_ref[:, lanes]) * TEMPER + twice(bias_cp[...])
        expo = jnp.exp(scores)
        dprob = nt(both_heads(wm_ref[:, lanes]), da_ref[:, lanes])
        lows, dss = [], []
        for half in range(2):
            part = slice(COLS * half, COLS * half + COLS)
            prob = expo[part] / jnp.sum(expo[part], axis=0, keepdims=True)
            inner = jnp.sum(prob * dprob[part], axis=0, keepdims=True)
            lows.append(prob.astype(BF))
            dss.append((prob * (dprob[part] - inner)).astype(BF))
        dscore = jnp.concatenate(dss, axis=0)
        dwm = pick_heads(nn(jnp.concatenate(lows, axis=0), da_ref[:, lanes]))
        dkm = pick_heads(nn(dscore, q_ref[:, lanes])) * TEMPER
        dq_s[:, lanes] = tn(dscore, marks) * TEMPER
        dwm_s[:, lanes] = dwm
        dkm_s[:, lanes] = dkm
        dwm_src[hp] = dwm[LAND : 2 * LAND]
        dk1_src[hp] = dkm[LAND : 2 * LAND].astype(BF)
        to_owner(dwm_src, dwm_buf, dwm_ss, dwm_r, hp)
        to_owner(dk1_src, dk1_buf, dk1_ss, dk1_r, hp)

    arrive(stage.at[1], stage_s.at[1])
    red.plane(2)
    dnum_s[...] = jnp.zeros_like(dnum_s)
    dden_s[...] = jnp.zeros_like(dden_s)
    dqm_s[...] = jnp.zeros_like(dqm_s)
    slot_rows = (pl.multiple_of(jnp.where(me == 0, 0, 2 * LAND), LAND), 3 * LAND)
    cuts = [(slot, slice(256 * part, 256 * part + 256)) for slot in range(2) for part in range(3)]

    @pl.when(has_local)
    def _():
        def at(ref, slot, lanes):
            return ref[pl.ds(slot_rows[slot], LAND), lanes]

        pltpu.make_async_copy(res_ref, res_s, load_s.at[0]).wait()
        outs = newton_back(
            [at(qm_ref, *c) for c in cuts], [at(km_ref, *c) for c in cuts],
            [vloc_ref[slot, :, c] for slot, c in cuts], [dloc_ref[slot, :, c] for slot, c in cuts],
            [at(dwm_s, *c) for c in cuts],
            lambda it, i: [res_s[i, it, m] for m in range(4)],
        )
        for (slot, c), (dnum, dden, dqm, dkm) in zip(cuts, outs):
            rows = pl.ds(slot_rows[slot], LAND)
            dnum_s[rows, c] = dnum
            dden_s[rows, c] = dden
            dqm_s[rows, c] = dqm
            dkm_s[rows, c] = dkm_s[rows, c] + dkm

    @pl.when(is_owner)
    def _():
        lanes = pl.ds(pl.multiple_of((me - 1) * 128, 128), 128)
        for step, other in group_peers(me):
            arrive(dwm_buf.at[other], dwm_r.at[other])
        total = dwm_buf[0]
        for j in range(1, GRP_DEV):
            total = total + dwm_buf[j]
        ((dnum, dden, dqm, dkm),) = newton_back(
            [qm_ref[LAND : 2 * LAND, lanes]], [km_ref[LAND : 2 * LAND, lanes]],
            [vl_ref[...]], [dl_ref[...]], [total],
            lambda it, i: [resl_ref[it, m] for m in range(4)],
        )
        high, low = split(dden)
        dn_buf[me - 1, 0:LAND] = dnum
        dn_buf[me - 1, LAND : 2 * LAND] = jnp.where(iota((LAND, 128), 1) % HEAD < 32, high, low)
        for step, other in group_peers(me):
            push(dn_buf.at[me - 1], dn_buf.at[me - 1], dn_ss.at[step - 1], dn_r.at[me - 1], place(rep, other))
        dqm_s[LAND : 2 * LAND, 0:128] = dqm
        dqm_s[LAND : 2 * LAND, 128:256] = dkm

    arrive(stage.at[0], stage_s.at[0])
    red.plane(1)
    @pl.when(me > 0)
    def _():
        arrive(halo.at[0], halo_r.at[0])
        dext[0:HALO] = halo[0]

    @pl.when(me == 0)
    def _():
        dext[0:HALO] = jnp.zeros((HALO, D), BF)

    @pl.when(me < GRP_DEV - 1)
    def _():
        arrive(halo.at[1], halo_r.at[1])
        dext[HALO + TOK : 2 * HALO + TOK] = halo[1]

    @pl.when(me == GRP_DEV - 1)
    def _():
        dext[HALO + TOK : 2 * HALO + TOK] = jnp.zeros((HALO, D), BF)

    dext[HALO : HALO + TOK] = da_ref[...]
    dext[2 * HALO + TOK :] = jnp.zeros((EXT - TOK - 2 * HALO, D), BF)
    same = same_item(first_row, lens, starts)
    for hp in range(6):
        lanes = pair_lanes(hp)
        dv_s[:, lanes] = conv_pair(taps_ref, hp, same, dext[:, lanes])
    same_back = same_item(first_row, lens, starts, reverse=True)
    turn = (iota((TOK, TOK), 0) + iota((TOK, TOK), 1) == TOK - 1).astype(BF)
    turned = nn(turn, da_ref[...]).astype(BF)
    for hp in range(6):
        lanes = pair_lanes(hp)
        pairs = nt(both_heads(turned[:, lanes]), ext_ref[:, lanes])
        for half in range(2):
            band = pltpu.roll(pairs[TOK * half : TOK * half + TOK] * same_back, 0, 1, stride=1, stride_axis=0)
            small_s[4 + 2 * hp + half : 5 + 2 * hp + half, :EXT] = jnp.sum(band, axis=0, keepdims=True)
    small_s[4:, EXT:] = jnp.zeros((HEADS, D - EXT), F32)
    small_s[:4, :] = norms_ref[...]
    small.start()
    red.plane_two(2)
    load_w.start()

    for owner in range(1, 7):
        lanes = pair_lanes(owner - 1)

        @pl.when(me != owner)
        def _():
            arrive(dn_buf.at[owner - 1], dn_r.at[owner - 1])

        dnum_s[LAND : 2 * LAND, lanes] = dn_buf[owner - 1, 0:LAND]
        packed = dn_buf[owner - 1, LAND : 2 * LAND].astype(F32)
        one = packed[:, 0:1] + packed[:, 32:33]
        two = packed[:, 64:65] + packed[:, 96:97]
        dden_s[LAND : 2 * LAND, lanes] = jnp.where(iota((LAND, 128), 1) < HEAD, one, two)
    for hp in range(6):
        lanes = pair_lanes(hp)
        marks = both_heads(qm_ref[:, lanes])
        expo = jnp.exp(nt(marks, k_ref[:, lanes]) * TEMPER + twice(bias_cp[...]))
        dnum = both_heads(dnum_s[:, lanes])
        dden = jnp.concatenate([dden_s[:, 128 * hp : 128 * hp + 1], dden_s[:, 128 * hp + 64 : 128 * hp + 65]], axis=0)
        dscore = (expo * (nt(dnum, v_ref[:, lanes]) + dden)).astype(BF)
        dqm = pick_heads(nn(dscore, k_ref[:, lanes])) * TEMPER
        dk_s[:, lanes] = tn(dscore, marks) * TEMPER
        dv_s[:, lanes] += tn(expo.astype(BF), dnum)
        dq3_src[hp] = dqm[LAND : 2 * LAND].astype(BF)
        to_owner(dq3_src, dq3_buf, dq3_ss, dq3_r, hp)

        @pl.when(jnp.logical_not(is_owner))
        def _():
            dqm_s[:, lanes] += dqm

    red.plane_two(1)
    clo, chi, _, _ = column_edges(iota((COLS, 128), 0), lens, starts)
    counts = (chi - clo).astype(F32)

    @pl.when(is_owner)
    def _():
        lanes = pl.ds(pl.multiple_of((me - 1) * 128, 128), 128)
        for step, other in group_peers(me):
            arrive(dk1_buf.at[other], dk1_r.at[other])
            arrive(dq3_buf.at[other], dq3_r.at[other])
        total_q = dqm_s[LAND : 2 * LAND, 0:128]
        total_k = dqm_s[LAND : 2 * LAND, 128:256]
        for j in range(GRP_DEV):
            total_q = total_q + dq3_buf[j].astype(F32)
            total_k = total_k + dk1_buf[j].astype(F32)
        ds_buf[me - 1, 0] = (total_q / counts[LAND : 2 * LAND]).astype(BF)
        ds_buf[me - 1, 1] = (total_k / counts[LAND : 2 * LAND]).astype(BF)
        for step, other in group_peers(me):
            push(ds_buf.at[me - 1], ds_buf.at[me - 1], ds_ss.at[step - 1], ds_r.at[me - 1], place(rep, other))

    for hp in range(6):
        lanes = pair_lanes(hp)
        dsum_s[:, lanes] = (dqm_s[:, lanes] / counts).astype(BF)
        dsum_s[:, D + 128 * hp : D + 128 * hp + 128] = (dkm_s[:, lanes] / counts).astype(BF)
    for owner in range(1, 7):
        @pl.when(me != owner)
        def _():
            arrive(ds_buf.at[owner - 1], ds_r.at[owner - 1])

        hp = owner - 1
        dsum_s[LAND : 2 * LAND, pair_lanes(hp)] = ds_buf[owner - 1, 0]
        dsum_s[LAND : 2 * LAND, D + 128 * hp : D + 128 * hp + 128] = ds_buf[owner - 1, 1]
    pshape = (TOK, COLS)
    ppos = first_row + iota(pshape, 0)
    plo, phi, _, _ = column_edges(iota(pshape, 1), lens, starts)
    hot = ((ppos >= plo) & (ppos < phi)).astype(BF)
    dp_s[:, :D] = (dq_s[...] + nn(hot, dsum_s[:, :D])).astype(BF)
    dp_s[:, D : 2 * D] = (dk_s[...] + nn(hot, dsum_s[:, D:])).astype(BF)
    dp_s[:, 2 * D :] = dv_s[...].astype(BF)
    for part in range(3):
        cols = slice(D * part, D * part + D)
        gw_ref[:, cols] = tn(x_ref[...], dp_s[:, cols]).astype(BF)
    red.chip(0)
    red.line(2)
    red.plane(0)
    red.line(1)
    load_w.wait()
    gx_ref[...] = (dh_ref[...] + nt(dp_s[...], w_ref[...])).astype(BF)
    small.middle()
    red.plane_two(0)
    red.share(2)
    red.line(0)
    red.share(1)
    small.across()
    red.share(0)
    total = small.end()
    total_ref[...] = total
    lane = iota((16, D), 1)
    real = (iota((16, D), 0) < 4) | ((lane >= TOK - 1) & (lane < TOK - 1 + KERNEL))
    extra = jnp.sum(jnp.where(real, total * total, 0.0), keepdims=True)
    for m in (2, 1, 0):
        red.done(m)
    norm_ref[...] = jnp.broadcast_to(jnp.sqrt(square_sum(spot, fin_ref, sq, ss, sr, extra)), (8, 128))
    for m in range(3):
        red.sent(m)

    for hp in range(6):
        @pl.when(me != hp + 1)
        def _():
            arrive(dwm_src.at[hp], dwm_ss.at[hp])
            arrive(dk1_src.at[hp], dk1_ss.at[hp])
            arrive(dq3_src.at[hp], dq3_ss.at[hp])

    @pl.when(is_owner)
    def _():
        for step, other in group_peers(me):
            arrive(dn_buf.at[0], dn_ss.at[step - 1])
            arrive(ds_buf.at[0], ds_ss.at[step - 1])

    @pl.when(me < GRP_DEV - 1)
    def _():
        arrive(halo.at[0], halo_s.at[0])

    @pl.when(me > 0)
    def _():
        arrive(halo.at[1], halo_s.at[1])


def attend_back(item_lengths, tokens, w_all, taps_back, kept, d_branch, d_hidden, grad_out, grad_up, grad_down, grad_norms):
    sds = jax.ShapeDtypeStruct
    outs = [sds((TOK, D), BF), sds((3, 4, *BLK), BF), sds((16, D), F32), sds((8, 128), F32)]
    dma = pltpu.SemaphoreType.DMA
    vm = pltpu.VMEM
    scratch = [
        vm((D, 3 * D), BF), vm((D, 3 * D), BF), vm((2, 4, 4, *BLK), BF), vm((16, D), F32), *reduce_bufs(),
        vm((4, 16, D), F32), vm((4, 16, D), F32), vm((2, 16, D), F32), vm((8, 8, 128), F32),
        vm((2, HALO, D), BF), vm((EXT, D), BF), vm((6, LAND, 128), F32), vm((8, LAND, 128), F32),
        vm((6, LAND, 128), BF), vm((8, LAND, 128), BF), vm((6, 2 * LAND, 128), BF),
        vm((6, LAND, 128), BF), vm((8, LAND, 128), BF), vm((6, 2, LAND, 128), BF),
        vm((COLS, TOK), F32), vm((COLS, D), F32), vm((COLS, D), F32), vm((COLS, D), F32),
        vm((COLS, D), BF), vm((COLS, D), F32), vm((TOK, D), F32), vm((TOK, D), F32), vm((TOK, D), F32),
        vm((COLS, 2 * D), BF), vm((TOK, 3 * D), BF), vm((6, NS_STEPS, 4, LAND, 256), F32), dma((2,)),
        dma((2,)), dma((2,)), dma((6,)), dma((8,)), dma((6,)), dma((8,)), dma((7,)), dma((6,)),
        dma((6,)), dma((8,)), dma((7,)), dma((6,)),
        dma((2,)), dma((3,)), dma((4,)), dma((3,)), dma((4,)), dma((1,)), dma((1,)), dma((7,)), dma((8,)),
        *reduce_sems(),
    ]
    args = (item_lengths, tokens, w_all, taps_back, *kept, d_branch, d_hidden, grad_out, grad_up, grad_down, grad_norms)
    anyspace = pl.BlockSpec(memory_space=pl.ANY)
    in_specs = [SM] + [VM] * (len(args) - 1)
    for index in (2, 11, 20, 21):
        in_specs[index] = anyspace
    return pl.pallas_call(
        attend_back_kernel, out_shape=outs, in_specs=in_specs,
        out_specs=[VM] * len(outs), scratch_shapes=scratch, name="attend_back",
        compiler_params=pltpu.CompilerParams(collective_id=2, has_side_effects=True, vmem_limit_bytes=62 * 2**20),
    )(*args)


def on_device_fast(
    tokens, cotangent, item_lengths,
    qkv_weight, qkv_first, qkv_second, out_weight, out_first, out_second,
    up_weight, up_first, up_second, down_weight, down_first, down_second,
    norm_params, norm_first, norm_second, conv_kernel, conv_first, conv_second,
):
    taps = jnp.pad(conv_kernel, ((0, 4), (0, EXT - KERNEL)))
    taps_back = jnp.pad(conv_kernel[:, ::-1], ((0, 4), (0, EXT - KERNEL)))
    w_all, w_up, w_down, gains_low, rest = attend(
        item_lengths, tokens, qkv_weight, out_weight, up_weight, down_weight, norm_params, taps
    )
    queries, key_rows, value_rows, mean_q, mean_k, mixed, branch, value_ext, *resid = rest
    w_out = w_all[:, 3 * D :]
    gains_all = gains_low.astype(F32)
    attn_out = jnp.dot(branch, w_out, preferred_element_type=F32)
    normed_one, norm_one_pull = jax.vjp(
        layer_norm, tokens.astype(F32) + attn_out, gains_all[0], gains_all[1]
    )
    normed_low = normed_one.astype(BF)
    up_out = jnp.dot(normed_low, w_up, preferred_element_type=F32)
    activated, gelu_pull = jax.vjp(gelu_exact, up_out)
    act_low = activated.astype(BF)
    down_out = jnp.dot(act_low, w_down, preferred_element_type=F32)
    result, norm_two_pull = jax.vjp(layer_norm, normed_one + down_out, gains_all[2], gains_all[3])
    d_hidden_two, d_gain_two, d_shift_two = norm_two_pull(cotangent.astype(F32))
    d_down_low = d_hidden_two.astype(BF)
    grad_down = contract_rows(act_low, d_down_low).astype(BF)
    (d_up,) = gelu_pull(contract_cols(d_down_low, w_down))
    d_up_low = d_up.astype(BF)
    grad_up = contract_rows(normed_low, d_up_low).astype(BF)
    d_normed = d_hidden_two + contract_cols(d_up_low, w_up)
    d_hidden_one, d_gain_one, d_shift_one = norm_one_pull(d_normed)
    d_attn_low = d_hidden_one.astype(BF)
    grad_out = contract_rows(branch, d_attn_low).astype(BF)
    d_branch_low = contract_cols(d_attn_low, w_out).astype(BF)
    grad_norms = jnp.stack([d_gain_one, d_shift_one, d_gain_two, d_shift_two])
    input_grad, fin, total, norm = attend_back(
        item_lengths, tokens, w_all, taps_back,
        (queries, key_rows, value_rows, mean_q, mean_k, mixed, value_ext, *resid),
        d_branch_low, d_hidden_one, grad_out, grad_up, grad_down, grad_norms,
    )
    wide = lambda part: jnp.transpose(part, (1, 0, 2)).reshape(SHARD, -1)
    column = lax.axis_index(("seq", "grp")) * SHARD
    shard_qkv, shard_out, shard_up = wide(fin[0, :3]), fin[0, 3], wide(fin[1])
    shard_down, shard_norm = fin[2].reshape(4 * SHARD, D), lax.dynamic_slice(total, (0, column), (4, SHARD))
    conv_total, grad_total = total[4:, TOK - 1 : TOK - 1 + KERNEL], norm[0, 0]
    clip_factor = MAX_NORM / jnp.maximum(grad_total, MAX_NORM)
    news = []
    for weight, one, two, grad, rate, decay in (
        (qkv_weight, qkv_first, qkv_second, shard_qkv, RATE_MATRIX, DECAY_RATE),
        (out_weight, out_first, out_second, shard_out, RATE_MATRIX, DECAY_RATE),
        (up_weight, up_first, up_second, shard_up, RATE_MATRIX, DECAY_RATE),
        (down_weight, down_first, down_second, shard_down, RATE_MATRIX, DECAY_RATE),
        (norm_params, norm_first, norm_second, shard_norm, RATE_NORM, 0.0),
        (conv_kernel, conv_first, conv_second, conv_total, RATE_CONV, 0.0),
    ):
        news.extend(adamw(weight, one, two, grad.astype(F32), clip_factor, rate, decay))
    return (result.astype(BF), input_grad, grad_total, *news)


def solution(mesh):
    in_specs = (
        P(("rep", "seq", "grp"), None),
        P(("rep", "seq", "grp"), None),
        P("rep", None),
        P(("seq", "grp"), None),
        P(("seq", "grp"), None),
        P(("seq", "grp"), None),
        P(("seq", "grp"), None),
        P(("seq", "grp"), None),
        P(("seq", "grp"), None),
        P(("seq", "grp"), None),
        P(("seq", "grp"), None),
        P(("seq", "grp"), None),
        P(("seq", "grp"), None),
        P(("seq", "grp"), None),
        P(("seq", "grp"), None),
        P(None, ("seq", "grp")),
        P(None, ("seq", "grp")),
        P(None, ("seq", "grp")),
        P(),
        P(),
        P(),
    )
    out_specs = (
        P(("rep", "seq", "grp"), None),
        P(("rep", "seq", "grp"), None),
        P(),
        P(("seq", "grp"), None),
        P(("seq", "grp"), None),
        P(("seq", "grp"), None),
        P(("seq", "grp"), None),
        P(("seq", "grp"), None),
        P(("seq", "grp"), None),
        P(("seq", "grp"), None),
        P(("seq", "grp"), None),
        P(("seq", "grp"), None),
        P(("seq", "grp"), None),
        P(("seq", "grp"), None),
        P(("seq", "grp"), None),
        P(None, ("seq", "grp")),
        P(None, ("seq", "grp")),
        P(None, ("seq", "grp")),
        P(),
        P(),
        P(),
    )
    fast = dict(mesh.shape) == {"rep": 4, "seq": 4, "grp": 2}
    body = on_device_fast if fast else on_device
    return jax.shard_map(
        body, mesh=mesh, in_specs=in_specs, out_specs=out_specs, check_vma=False
    )
```

```python
import jax
import jax.numpy as jnp
from jax import lax
from jax.experimental import pallas as pl
from jax.experimental.pallas import tpu as pltpu
from jax.sharding import PartitionSpec as P

D = 768
FF = 3072
HEADS = 12
HEAD = 64
LAND = 64
KERNEL = 33
HALO = 16
NS_STEPS = 6
ITEMS = 4
STEP = 10
TOK_DEV = 256
GRP_DEV = 8
HIGHEST_PREC = lax.Precision.HIGHEST
EPS_NORM = 1e-05
BETA_ONE = 0.9
BETA_TWO = 0.999
ADAM_EPS = 1e-08
RATE_MATRIX = 0.02
RATE_NORM = 0.3
RATE_CONV = 0.1
DECAY_RATE = 0.01
MAX_NORM = 1.0


def extended(cells, sides, width):
    for axis, dim in sides:
        count = lax.axis_size(axis)
        ends = count - 1
        head = lax.slice_in_dim(cells, 0, width, axis=dim)
        tail = lax.slice_in_dim(cells, cells.shape[dim] - width, cells.shape[dim], axis=dim)
        cells = jnp.concatenate(
            [
                lax.ppermute(tail, axis, [(i, (i + 1) % count) for i in range(ends)]),
                cells,
                lax.ppermute(head, axis, [((i + 1) % count, i) for i in range(ends)]),
            ],
            axis=dim,
        )
    return cells


def locate(positions, lengths):
    ends = jnp.cumsum(lengths)
    starts = ends - lengths
    inside = (positions[:, None] >= starts[None, :]) & (positions[:, None] < ends[None, :])
    item_ids = jnp.sum((positions[:, None] >= ends[None, :]).astype(jnp.int32), axis=1)
    valid = (positions >= 0) & (positions < ends[-1])
    item_ids = jnp.where(valid, item_ids, -1)
    own_len = jnp.sum(jnp.where(inside, lengths[None, :], 0), axis=1)
    own_start = jnp.sum(jnp.where(inside, starts[None, :], 0), axis=1)
    segment = (positions - own_start) * LAND // jnp.maximum(own_len, 1)
    columns = jnp.where(valid, item_ids * LAND + segment, -1)
    return (item_ids, columns)


def landmark_counts(lengths):
    marks = jnp.arange(LAND + 1, dtype=jnp.int32)
    edges = (marks[None, :] * lengths[:, None] + LAND - 1) // LAND
    return (edges[:, 1:] - edges[:, :-1]).reshape(-1)


def layer_norm(hidden, gain_row, shift_row):
    row_mean = jnp.mean(hidden, axis=-1, keepdims=True)
    centred = hidden - row_mean
    variance = jnp.mean(centred * centred, axis=-1, keepdims=True)
    return centred * lax.rsqrt(variance + EPS_NORM) * gain_row + shift_row


def gelu_exact(values):
    return jax.nn.gelu(values, approximate=False)


def mixing_rest(mark_scores, num_all, den_all):
    key_values = (
        num_all.reshape(ITEMS, LAND, HEADS, HEAD) / den_all.reshape(ITEMS, LAND, HEADS)[..., None]
    )
    kernel_two = jax.nn.softmax(mark_scores, axis=-1)
    frobenius = jnp.sum(kernel_two * kernel_two, axis=(2, 3), keepdims=True)
    inverse = jnp.swapaxes(kernel_two, 2, 3) / frobenius
    identity = jnp.eye(LAND, dtype=kernel_two.dtype)
    for iteration in range(NS_STEPS):
        product = jnp.einsum("ahjk,ahkl->ahjl", kernel_two, inverse, precision=HIGHEST_PREC)
        inner = 7.0 * identity - product
        inner = 15.0 * identity - jnp.einsum(
            "ahjk,ahkl->ahjl", product, inner, precision=HIGHEST_PREC
        )
        inner = 13.0 * identity - jnp.einsum(
            "ahjk,ahkl->ahjl", product, inner, precision=HIGHEST_PREC
        )
        inverse = 0.25 * jnp.einsum("ahjk,ahkl->ahjl", inverse, inner, precision=HIGHEST_PREC)
    mixed_rows = jnp.einsum("ahjk,akhd->ajhd", inverse, key_values, precision=HIGHEST_PREC)
    return mixed_rows.reshape(ITEMS * LAND, HEADS * HEAD)


def adamw(weight, moment_one, moment_two, gradient, clip_factor, rate_value, decay_value):
    clipped = gradient * clip_factor
    moment_one = BETA_ONE * moment_one + (1.0 - BETA_ONE) * clipped
    moment_two = BETA_TWO * moment_two + (1.0 - BETA_TWO) * clipped * clipped
    first_hat = moment_one / (1.0 - BETA_ONE**STEP)
    second_hat = moment_two / (1.0 - BETA_TWO**STEP)
    weight = weight - rate_value * (
        first_hat / (jnp.sqrt(second_hat) + ADAM_EPS) + decay_value * weight
    )
    return (weight, moment_one, moment_two)


def contract_rows(left, right):
    return lax.dot_general(
        left, right, (((0,), (0,)), ((), ())), preferred_element_type=jnp.float32
    )


def contract_cols(left, right):
    return lax.dot_general(
        left, right, (((1,), (1,)), ((), ())), preferred_element_type=jnp.float32
    )


def on_device(
    tokens,
    cotangent,
    item_lengths,
    qkv_weight,
    qkv_first,
    qkv_second,
    out_weight,
    out_first,
    out_second,
    up_weight,
    up_first,
    up_second,
    down_weight,
    down_first,
    down_second,
    norm_params,
    norm_first,
    norm_second,
    conv_kernel,
    conv_first,
    conv_second,
):
    temper = HEAD ** (-0.5)
    col_total = ITEMS * LAND
    w_qkv, w_out, w_up, w_down, gains_low = (
        lax.all_gather(qkv_weight.astype(jnp.bfloat16), ("seq", "grp"), axis=0, tiled=True),
        lax.all_gather(out_weight.astype(jnp.bfloat16), ("seq", "grp"), axis=0, tiled=True),
        lax.all_gather(up_weight.astype(jnp.bfloat16), ("seq", "grp"), axis=0, tiled=True),
        lax.all_gather(down_weight.astype(jnp.bfloat16), ("seq", "grp"), axis=0, tiled=True),
        lax.all_gather(norm_params.astype(jnp.bfloat16), ("seq", "grp"), axis=1, tiled=True),
    )
    gains_all = gains_low.astype(jnp.float32)
    lengths = item_lengths[0]
    first_row = lax.axis_index(("seq", "grp")) * TOK_DEV
    positions = first_row - HALO + jnp.arange(TOK_DEV + 2 * HALO, dtype=jnp.int32)
    item_ext, column_ext = locate(positions, lengths)
    item_mid = item_ext[HALO : HALO + TOK_DEV]
    column_mid = column_ext[HALO : HALO + TOK_DEV]
    col_ids = jnp.arange(col_total, dtype=jnp.int32)
    col_hot = (column_mid[:, None] == col_ids[None, :]).astype(jnp.bfloat16)
    member = (item_mid[:, None] == (col_ids // LAND)[None, :]).astype(jnp.float32)
    counts_f = landmark_counts(lengths).astype(jnp.float32)
    projected = jnp.dot(tokens, w_qkv, preferred_element_type=jnp.float32)
    proj_low = projected.astype(jnp.bfloat16)
    queries = proj_low[:, :D]
    key_rows = proj_low[:, D : 2 * D]
    value_rows = proj_low[:, 2 * D :]
    land_sums = lax.psum(contract_rows(col_hot, proj_low[:, : 2 * D]), ("seq", "grp"))
    mean_q = (land_sums[:, :D] / counts_f[:, None]).astype(jnp.bfloat16)
    mean_k = (land_sums[:, D:] / counts_f[:, None]).astype(jnp.bfloat16)
    query_heads = queries.reshape(TOK_DEV, HEADS, HEAD)
    key_heads = key_rows.reshape(TOK_DEV, HEADS, HEAD)
    value_heads = value_rows.reshape(TOK_DEV, HEADS, HEAD)
    mean_q3 = mean_q.reshape(col_total, HEADS, HEAD)
    mean_k3 = mean_k.reshape(col_total, HEADS, HEAD)
    scores_key = (
        jnp.einsum("chd,phd->chp", mean_q3, key_heads, preferred_element_type=jnp.float32) * temper
    )
    expo_key = jnp.exp(scores_key) * jnp.transpose(member)[:, None, :]
    expo_low = expo_key.astype(jnp.bfloat16)
    num_part = jnp.einsum(
        "chp,phd->chd", expo_low, value_heads, preferred_element_type=jnp.float32
    ).reshape(col_total, D)
    num_all, den_all = lax.psum((num_part, jnp.sum(expo_key, axis=2)), ("seq", "grp"))
    query_marks4 = mean_q.reshape(ITEMS, LAND, HEADS, HEAD)
    key_marks4 = mean_k.reshape(ITEMS, LAND, HEADS, HEAD)
    mark_scores = (
        jnp.einsum("ajhd,akhd->ahjk", query_marks4, key_marks4, preferred_element_type=jnp.float32)
        * temper
    )
    mixed_rows, mix_pull = jax.vjp(mixing_rest, mark_scores, num_all, den_all)
    mixed3 = mixed_rows.astype(jnp.bfloat16).reshape(col_total, HEADS, HEAD)
    scores_tok = (
        jnp.einsum("phd,chd->phc", query_heads, mean_k3, preferred_element_type=jnp.float32)
        * temper
    )
    expo_tok = jnp.exp(scores_tok) * member[:, None, :]
    attn_probs = expo_tok / jnp.sum(expo_tok, axis=2, keepdims=True)
    probs_low = attn_probs.astype(jnp.bfloat16)
    attended = jnp.einsum(
        "phc,chd->phd", probs_low, mixed3, preferred_element_type=jnp.float32
    ).reshape(TOK_DEV, D)
    value_ext = extended(value_rows, ((("seq", "grp"), 0),), HALO)
    channel_taps = jnp.repeat(conv_kernel, HEAD, axis=0)
    same_masks = [
        (item_ext[offset : offset + TOK_DEV] == item_mid).astype(jnp.float32)
        for offset in range(KERNEL)
    ]
    conv_out = jnp.zeros((TOK_DEV, D), jnp.float32)
    for offset in range(KERNEL):
        conv_out = conv_out + value_ext[offset : offset + TOK_DEV] * (
            channel_taps[:, offset][None, :] * same_masks[offset][:, None]
        )
    branch = (attended + conv_out).astype(jnp.bfloat16)
    attn_out = jnp.dot(branch, w_out, preferred_element_type=jnp.float32)
    normed_one, norm_one_pull = jax.vjp(
        layer_norm, tokens.astype(jnp.float32) + attn_out, gains_all[0], gains_all[1]
    )
    normed_low = normed_one.astype(jnp.bfloat16)
    up_out = jnp.dot(normed_low, w_up, preferred_element_type=jnp.float32)
    activated, gelu_pull = jax.vjp(gelu_exact, up_out)
    act_low = activated.astype(jnp.bfloat16)
    down_out = jnp.dot(act_low, w_down, preferred_element_type=jnp.float32)
    result, norm_two_pull = jax.vjp(layer_norm, normed_one + down_out, gains_all[2], gains_all[3])
    d_hidden_two, d_gain_two, d_shift_two = norm_two_pull(cotangent.astype(jnp.float32))
    d_down_low = d_hidden_two.astype(jnp.bfloat16)
    grad_down = contract_rows(act_low, d_down_low)
    (d_up,) = gelu_pull(contract_cols(d_down_low, w_down))
    d_up_low = d_up.astype(jnp.bfloat16)
    grad_up = contract_rows(normed_low, d_up_low)
    d_normed = d_hidden_two + contract_cols(d_up_low, w_up)
    d_hidden_one, d_gain_one, d_shift_one = norm_one_pull(d_normed)
    d_attn_low = d_hidden_one.astype(jnp.bfloat16)
    grad_out = contract_rows(branch, d_attn_low)
    d_branch_low = contract_cols(d_attn_low, w_out).astype(jnp.bfloat16)
    d_branch_f = d_branch_low.astype(jnp.float32)
    d_branch_ext = extended(d_branch_low, ((("seq", "grp"), 0),), HALO)
    d_values_conv = jnp.zeros((TOK_DEV, D), jnp.float32)
    tap_grads = []
    for offset in range(KERNEL):
        d_values_conv = d_values_conv + d_branch_ext[offset : offset + TOK_DEV] * (
            channel_taps[:, KERNEL - 1 - offset][None, :] * same_masks[offset][:, None]
        )
        tap_grads.append(
            jnp.sum(
                d_branch_f * value_ext[offset : offset + TOK_DEV] * same_masks[offset][:, None],
                axis=0,
            )
        )
    grad_conv = jnp.sum(jnp.stack(tap_grads, axis=1).reshape(HEADS, HEAD, KERNEL), axis=1)
    d_attended = d_branch_low.reshape(TOK_DEV, HEADS, HEAD)
    d_mixed_part = jnp.einsum(
        "phc,phd->chd", probs_low, d_attended, preferred_element_type=jnp.float32
    ).reshape(col_total, D)
    d_probs = jnp.einsum("phd,chd->phc", d_attended, mixed3, preferred_element_type=jnp.float32)
    d_scores_tok = (
        attn_probs * (d_probs - jnp.sum(attn_probs * d_probs, axis=2, keepdims=True))
    ).astype(jnp.bfloat16)
    d_query_tok = (
        jnp.einsum("phc,chd->phd", d_scores_tok, mean_k3, preferred_element_type=jnp.float32)
        * temper
    )
    d_meank_part = (
        jnp.einsum(
            "phc,phd->chd", d_scores_tok, query_heads, preferred_element_type=jnp.float32
        ).reshape(col_total, D)
        * temper
    )
    d_mixed, d_meank_tok = lax.psum((d_mixed_part, d_meank_part), ("seq", "grp"))
    d_mark_scores, d_num, d_den = mix_pull(d_mixed)
    d_mark_scaled = d_mark_scores * temper
    d_mean_q_mix = jnp.einsum(
        "ahjk,akhd->ajhd", d_mark_scaled, key_marks4.astype(jnp.float32), precision=HIGHEST_PREC
    ).reshape(col_total, D)
    d_mean_k_mix = jnp.einsum(
        "ahjk,ajhd->akhd", d_mark_scaled, query_marks4.astype(jnp.float32), precision=HIGHEST_PREC
    ).reshape(col_total, D)
    d_num3 = d_num.reshape(col_total, HEADS, HEAD)
    d_expo = d_den[:, :, None] + jnp.einsum(
        "chd,phd->chp", d_num3, value_heads.astype(jnp.float32), precision=HIGHEST_PREC
    )
    d_scores_key = (expo_key * d_expo).astype(jnp.bfloat16)
    d_key_mix = (
        jnp.einsum("chp,chd->phd", d_scores_key, mean_q3, preferred_element_type=jnp.float32)
        * temper
    )
    d_meanq_part = (
        jnp.einsum(
            "chp,phd->chd", d_scores_key, key_heads, preferred_element_type=jnp.float32
        ).reshape(col_total, D)
        * temper
    )
    d_value_mix = jnp.einsum(
        "chp,chd->phd", expo_low.astype(jnp.float32), d_num3, precision=HIGHEST_PREC
    )
    d_meanq_tok = lax.psum(d_meanq_part, ("seq", "grp"))
    d_sums = (
        jnp.concatenate([d_mean_q_mix + d_meanq_tok, d_mean_k_mix + d_meank_tok], axis=1)
        / counts_f[:, None]
    )
    d_land_rows = jnp.dot(col_hot.astype(jnp.float32), d_sums, precision=HIGHEST_PREC)
    d_queries = d_query_tok.reshape(TOK_DEV, D) + d_land_rows[:, :D]
    d_keys = d_key_mix.reshape(TOK_DEV, D) + d_land_rows[:, D:]
    d_values = d_value_mix.reshape(TOK_DEV, D) + d_values_conv
    d_proj_low = jnp.concatenate([d_queries, d_keys, d_values], axis=1).astype(jnp.bfloat16)
    grad_qkv = contract_rows(tokens, d_proj_low)
    input_grad = (d_hidden_one + contract_cols(d_proj_low, w_qkv)).astype(jnp.bfloat16)
    grad_norms = jnp.stack([d_gain_one, d_shift_one, d_gain_two, d_shift_two])
    group_qkv, group_out, group_up, group_down, group_norm = (
        lax.psum_scatter(grad_qkv, ("seq", "grp"), scatter_dimension=0, tiled=True),
        lax.psum_scatter(grad_out, ("seq", "grp"), scatter_dimension=0, tiled=True),
        lax.psum_scatter(grad_up, ("seq", "grp"), scatter_dimension=0, tiled=True),
        lax.psum_scatter(grad_down, ("seq", "grp"), scatter_dimension=0, tiled=True),
        lax.psum_scatter(grad_norms, ("seq", "grp"), scatter_dimension=1, tiled=True),
    )
    shard_qkv, shard_out, shard_up, shard_down, shard_norm, conv_rep = (
        lax.psum(group_qkv.astype(jnp.bfloat16), "rep").astype(jnp.float32),
        lax.psum(group_out.astype(jnp.bfloat16), "rep").astype(jnp.float32),
        lax.psum(group_up.astype(jnp.bfloat16), "rep").astype(jnp.float32),
        lax.psum(group_down.astype(jnp.bfloat16), "rep").astype(jnp.float32),
        lax.psum(group_norm.astype(jnp.bfloat16), "rep").astype(jnp.float32),
        lax.psum(grad_conv.astype(jnp.bfloat16), "rep").astype(jnp.float32),
    )
    local_sq = (
        jnp.sum(shard_qkv * shard_qkv)
        + jnp.sum(shard_out * shard_out)
        + jnp.sum(shard_up * shard_up)
        + jnp.sum(shard_down * shard_down)
        + jnp.sum(shard_norm * shard_norm)
    )
    total_sq, conv_total = lax.psum((local_sq, conv_rep), ("seq", "grp"))
    grad_total = jnp.sqrt(total_sq + jnp.sum(conv_total * conv_total))
    clip_factor = MAX_NORM / jnp.maximum(grad_total, MAX_NORM)
    qkv_new = adamw(
        qkv_weight, qkv_first, qkv_second, shard_qkv, clip_factor, RATE_MATRIX, DECAY_RATE
    )
    out_new = adamw(
        out_weight, out_first, out_second, shard_out, clip_factor, RATE_MATRIX, DECAY_RATE
    )
    up_new = adamw(up_weight, up_first, up_second, shard_up, clip_factor, RATE_MATRIX, DECAY_RATE)
    down_new = adamw(
        down_weight, down_first, down_second, shard_down, clip_factor, RATE_MATRIX, DECAY_RATE
    )
    norm_new = adamw(norm_params, norm_first, norm_second, shard_norm, clip_factor, RATE_NORM, 0.0)
    conv_new = adamw(conv_kernel, conv_first, conv_second, conv_total, clip_factor, RATE_CONV, 0.0)
    return (
        result.astype(jnp.bfloat16),
        input_grad,
        grad_total,
        qkv_new[0],
        qkv_new[1],
        qkv_new[2],
        out_new[0],
        out_new[1],
        out_new[2],
        up_new[0],
        up_new[1],
        up_new[2],
        down_new[0],
        down_new[1],
        down_new[2],
        norm_new[0],
        norm_new[1],
        norm_new[2],
        conv_new[0],
        conv_new[1],
        conv_new[2],
    )


SHARD = D // GRP_DEV
BLK = (SHARD, D)


class Spot:
    def __init__(self):
        self.rep, self.seq, self.grp = lax.axis_index("rep"), lax.axis_index("seq"), lax.axis_index("grp")
        self.me = self.seq * 2 + self.grp
        self.xn = self.rep + 1 - 2 * lax.rem(self.rep, 2)
        self.yn = lax.rem(self.rep + 2, 4)
        self.dn = 3 - self.rep
        self.to_x = (self.xn, self.seq, self.grp)
        self.to_y = (self.yn, self.seq, self.grp)
        self.to_d = (self.dn, self.seq, self.grp)
        self.to_core = (self.rep, self.seq, 1 - self.grp)

    def z(self, step):
        return lax.rem(self.seq + step, 4)

    def to_z(self, step):
        return (self.rep, self.z(step), self.grp)

    def greet_all(self):
        self.signal_all()
        self.wait_all()

    def wait_all(self):
        pl.semaphore_wait(pltpu.get_barrier_semaphore(), GRP_DEV + 2)

    def signal_all(self):
        barrier = pltpu.get_barrier_semaphore()
        for device in (self.to_x, self.to_y, self.to_d):
            pl.semaphore_signal(barrier, inc=1, device_id=device, device_id_type=MESH_ID)
        for _, other in group_peers(self.me):
            pl.semaphore_signal(barrier, inc=1, device_id=place(self.rep, other), device_id_type=MESH_ID)


CHUNKS = 1
CHUNK = SHARD // CHUNKS
EARLY = tuple(range(CHUNKS))
UP, DOWN = CHUNKS, CHUNKS + 1


def unit_of(refs, part, shard, quarter):
    if part < UP:
        row = pl.multiple_of(shard * SHARD + part * CHUNK, CHUNK)
        return refs[0].at[pl.ds(row, CHUNK), pl.ds(pl.multiple_of(quarter * D, D), D)]
    if part == UP:
        row = pl.multiple_of(shard * SHARD, SHARD)
        return refs[1].at[pl.ds(row, SHARD), pl.ds(pl.multiple_of(quarter * D, D), D)]
    row = pl.multiple_of(shard * 4 * SHARD + quarter * SHARD, SHARD)
    return refs[2].at[pl.ds(row, SHARD), :]


def shard_of(refs, part, shard):
    if part < UP:
        row = pl.multiple_of(shard * SHARD + part * CHUNK, CHUNK)
        return refs[0].at[pl.ds(row, CHUNK), :]
    rows = SHARD if part == UP else 4 * SHARD
    return refs[part - UP + 1].at[pl.ds(pl.multiple_of(shard * rows, SHARD), rows), :]


class Gather:
    def __init__(self, spot, refs, sems):
        self.spot, self.refs = spot, refs
        (self.zs, self.zr, self.xs, self.xr, self.ys, self.yr, self.fs, self.fr, self.cs, self.cr) = sems

    def unit(self, part, seq, quarter):
        return unit_of(self.refs, part, seq * 2 + self.spot.grp, quarter)

    def start(self, part):
        spot = self.spot
        mine = self.unit(part, spot.seq, spot.rep)
        for sign in (1, -1):
            @pl.when((spot.seq + sign >= 0) & (spot.seq + sign <= 3))
            def _():
                push(mine, mine, self.zs.at[part, (sign + 1) // 2, spot.seq], self.zr.at[part, spot.seq],
                     (spot.rep, spot.seq + sign, spot.grp))
        own = shard_of(self.refs, part, spot.me)
        push(own, own, self.cs.at[part, 12], self.cr.at[part, 12], spot.to_core)

    def hop(self, part, far, spread=True):
        spot = self.spot
        for sign in (1, -1):
            src = lax.rem(spot.seq - sign * far + 4, 4)

            @pl.when((spot.seq - sign * far >= 0) & (spot.seq - sign * far <= 3))
            def _():
                unit = self.unit(part, src, spot.rep)
                arrive(unit, self.zr.at[part, src])

                @pl.when((spot.seq + sign >= 0) & (spot.seq + sign <= 3))
                def _():
                    push(unit, unit, self.zs.at[part, (sign + 1) // 2, src], self.zr.at[part, src],
                         (spot.rep, spot.seq + sign, spot.grp))

                if spread:
                    self.give(part, src)

    def give(self, part, src):
        spot = self.spot
        unit = self.unit(part, src, spot.rep)

        push(unit, unit, self.xs.at[part, src], self.xr.at[part, src], spot.to_x)
        push(unit, unit, self.ys.at[part, src], self.yr.at[part, src], spot.to_y)
        push(unit, unit, self.cs.at[part, src], self.cr.at[part, src], spot.to_core)

    def spread(self, part):
        for src in self.others():
            self.give(part, src)

    def others(self):
        return [self.spot.z(step) for step in range(1, 4)]

    def relay(self, part):
        spot = self.spot
        for src in self.others():
            unit = self.unit(part, src, spot.xn)
            arrive(unit, self.xr.at[part, src])

            @pl.when(lax.rem(src + part, 2) == 0)
            def _():
                push(unit, unit, self.fs.at[part, src], self.fr.at[part, src], spot.to_y)

            push(unit, unit, self.cs.at[part, 4 + src], self.cr.at[part, 4 + src], spot.to_core)

            unit = self.unit(part, src, spot.yn)
            arrive(unit, self.yr.at[part, src])

            @pl.when(lax.rem(src + part, 2) == 1)
            def _():
                push(unit, unit, self.fs.at[part, src], self.fr.at[part, src], spot.to_x)

            push(unit, unit, self.cs.at[part, 8 + src], self.cr.at[part, 8 + src], spot.to_core)

    def last(self, part):
        spot = self.spot
        for src in self.others():
            unit = self.unit(part, src, spot.dn)
            arrive(unit, self.fr.at[part, src])
            push(unit, unit, self.cs.at[part, 13 + src], self.cr.at[part, 13 + src], spot.to_core)

    def finish(self, part):
        spot = self.spot
        other = 1 - spot.grp
        arrive(shard_of(self.refs, part, spot.seq * 2 + other), self.cr.at[part, 12])
        for base, quarter in ((0, spot.rep), (4, spot.xn), (8, spot.yn), (13, spot.dn)):
            for src in self.others():
                arrive(unit_of(self.refs, part, src * 2 + other, quarter), self.cr.at[part, base + src])

    def sent(self, part):
        spot = self.spot
        unit = self.unit(part, spot.seq, spot.rep)
        for src in self.others():
            for sem in (self.xs, self.ys, self.fs):
                arrive(unit, sem.at[part, src])
            for base in (0, 4, 8, 13):
                arrive(unit, self.cs.at[part, base + src])
        arrive(shard_of(self.refs, part, spot.me), self.cs.at[part, 12])
        for sign in (1, -1):
            @pl.when((spot.seq + sign >= 0) & (spot.seq + sign <= 3))
            def _():
                arrive(unit, self.zs.at[part, (sign + 1) // 2, spot.seq])

                for far in range(1, 4):
                    src = spot.seq - sign * far

                    @pl.when((src >= 0) & (src <= 3))
                    def _():
                        arrive(unit, self.zs.at[part, (sign + 1) // 2, lax.rem(src + 4, 4)])


def gather_sems():
    dma = pltpu.SemaphoreType.DMA
    return [dma((CHUNKS + 2, 2, 4))] + [dma((CHUNKS + 2, n)) for n in (4, 4, 4, 4, 4, 4, 4, 17, 17)]


class Reduce:
    def __init__(self, spot, own, kept, bufs, sems):
        self.spot, self.own, self.kept = spot, own, kept
        self.rc, self.rx, self.ry, self.r2x, self.r2y, self.rz, self.fin = bufs
        (self.cs, self.cr, self.xs, self.xr, self.ys, self.yr, self.x2s, self.x2r, self.y2s, self.y2r,
         self.zs, self.zr, self.fs, self.fr) = sems

    def chip(self, m):
        spot = self.spot
        for seq in range(4):
            for quarter in range(4):
                push(self.own(m, seq * 2 + 1 - spot.grp, quarter), self.rc.at[m, seq, quarter],
                     self.cs.at[m], self.cr.at[m], spot.to_core)

    def add(self, left, right):
        return (left.astype(F32) + right.astype(F32)).astype(BF)

    def plane(self, m):
        spot = self.spot
        rc = self.rc
        arrive(rc.at[m], self.cr.at[m])
        for quarter in range(4):
            @pl.loop(0, 4)
            def _(seq):
                rc[m, seq, quarter] = self.add(rc[m, seq, quarter], self.kept(m, seq, quarter)[...])

        for j in range(2):
            for slot, quarter in enumerate((spot.xn, spot.dn)):
                push(rc.at[m, j, quarter], self.rx.at[m, j, slot], self.xs.at[m], self.xr.at[m], spot.to_x)
            for slot, quarter in enumerate((spot.yn, spot.dn)):
                push(rc.at[m, 2 + j, quarter], self.ry.at[m, j, slot], self.ys.at[m], self.yr.at[m], spot.to_y)

    def plane_two(self, m):
        spot = self.spot
        rc = self.rc
        arrive(self.rx.at[m], self.xr.at[m])

        @pl.loop(0, 2)
        def _(j):
            rc[m, j, spot.yn] = self.add(rc[m, j, spot.yn], self.rx[m, j, 1])

        for j in range(2):
            push(rc.at[m, j, spot.yn], self.r2y.at[m, j], self.y2s.at[m], self.y2r.at[m], spot.to_y)
        arrive(self.ry.at[m], self.yr.at[m])

        @pl.loop(0, 2)
        def _(j):
            rc[m, 2 + j, spot.xn] = self.add(rc[m, 2 + j, spot.xn], self.ry[m, j, 1])

        for j in range(2):
            push(rc.at[m, 2 + j, spot.xn], self.r2x.at[m, j], self.x2s.at[m], self.x2r.at[m], spot.to_x)

    def line(self, m):
        spot = self.spot
        rc = self.rc
        arrive(self.r2y.at[m], self.y2r.at[m])
        arrive(self.r2x.at[m], self.x2r.at[m])

        @pl.loop(0, 2)
        def _(j):
            rc[m, j, spot.rep] = (
                rc[m, j, spot.rep].astype(F32) + self.rx[m, j, 0].astype(F32) + self.r2y[m, j].astype(F32)
            ).astype(BF)
            rc[m, 2 + j, spot.rep] = (
                rc[m, 2 + j, spot.rep].astype(F32) + self.ry[m, j, 0].astype(F32) + self.r2x[m, j].astype(F32)
            ).astype(BF)

        for step in range(1, 4):
            push(rc.at[m, spot.z(step), spot.rep], self.rz.at[m, spot.seq],
                 self.zs.at[m, step - 1], self.zr.at[m, spot.seq], spot.to_z(step))

    def share(self, m):
        spot = self.spot
        total = self.rc[m, spot.seq, spot.rep].astype(F32)
        for step in range(1, 4):
            arrive(self.rz.at[m, spot.z(step)], self.zr.at[m, spot.z(step)])
            total = total + self.rz[m, spot.z(step)].astype(F32)
        self.fin[m, spot.rep] = total.astype(BF)
        mine = self.fin.at[m, spot.rep]
        for step, device in enumerate((spot.to_x, spot.to_y, spot.to_d)):
            push(mine, mine, self.fs.at[m, step], self.fr.at[m, spot.rep], device)

    def done(self, m):
        spot = self.spot
        for other in (spot.xn, spot.yn, spot.dn):
            arrive(self.fin.at[m, other], self.fr.at[m, other])

    def sent(self, m):
        arrive(self.rc.at[m], self.cs.at[m])
        arrive(self.rx.at[m], self.xs.at[m])
        arrive(self.ry.at[m], self.ys.at[m])
        arrive(self.r2x.at[m], self.x2s.at[m])
        arrive(self.r2y.at[m], self.y2s.at[m])
        for step in range(3):
            arrive(self.fin.at[m, 0], self.zs.at[m, step])
            arrive(self.fin.at[m, 0], self.fs.at[m, step])


def reduce_bufs():
    vm = pltpu.VMEM
    return [vm((3, 4, 4, *BLK), BF), vm((3, 2, 2, *BLK), BF), vm((3, 2, 2, *BLK), BF),
            vm((3, 2, *BLK), BF), vm((3, 2, *BLK), BF), vm((3, 4, *BLK), BF)]


def reduce_sems():
    dma = pltpu.SemaphoreType.DMA
    return [dma((3,)) for _ in range(10)] + [dma((3, 3)), dma((3, 4)), dma((3, 3)), dma((3, 4))]


class Small:
    def __init__(self, spot, src, one, two, pair, sems):
        self.spot, self.src, self.one, self.two, self.pair = spot, src, one, two, pair
        self.s1, self.r1, self.sp, self.rp, self.s2, self.r2 = sems

    def start(self):
        spot = self.spot
        for step, device in enumerate((spot.to_x, spot.to_y, spot.to_d)):
            push(self.src, self.one.at[spot.rep], self.s1.at[step], self.r1.at[spot.rep], device)

    def middle(self):
        spot = self.spot
        total = self.src[...]
        for other in (spot.xn, spot.yn, spot.dn):
            arrive(self.one.at[other], self.r1.at[other])
            total = total + self.one[other]
        self.pair[0] = total
        push(self.pair.at[0], self.pair.at[1], self.sp.at[0], self.rp.at[0], spot.to_core)

    def across(self):
        spot = self.spot
        arrive(self.pair.at[1], self.rp.at[0])
        self.two[spot.seq] = self.pair[0] + self.pair[1]
        mine = self.two.at[spot.seq]
        for step in range(1, 4):
            push(mine, mine, self.s2.at[step - 1], self.r2.at[spot.seq], spot.to_z(step))

    def end(self):
        spot = self.spot
        for step in range(1, 4):
            arrive(self.two.at[spot.z(step)], self.r2.at[spot.z(step)])
        total = self.two[0] + self.two[1] + self.two[2] + self.two[3]
        arrive(self.pair.at[0], self.sp.at[0])
        for step in range(3):
            arrive(self.one.at[0], self.s1.at[step])
            arrive(self.two.at[0], self.s2.at[step])
        return total


def square_sum(spot, fin, sq, ss, sr, extra):
    total = jnp.zeros((8, 128), F32)
    for m in range(3):
        for quarter in range(4):
            value = fin[m, quarter].astype(F32)
            value = value * value
            rows = value[0:8]
            for k in range(1, SHARD // 8):
                rows = rows + value[8 * k : 8 * k + 8]
            for k in range(D // 128):
                total = total + rows[:, 128 * k : 128 * k + 128]
    sq[spot.me] = total
    for step, other in group_peers(spot.me):
        push(sq.at[spot.me], sq.at[spot.me], ss.at[step - 1], sr.at[spot.me], place(spot.rep, other))
    for step, other in group_peers(spot.me):
        arrive(sq.at[other], sr.at[other])
    total = sq[0]
    for j in range(1, GRP_DEV):
        total = total + sq[j]
    for step in range(GRP_DEV - 1):
        arrive(sq.at[0], ss.at[step])
    return jnp.sum(total, keepdims=True) + extra


TOK = 256

TEMPER = HEAD ** (-0.5)
MESH_ID = pl.DeviceIdType.MESH
BF = jnp.bfloat16
F32 = jnp.float32
EXT = 384


def nn(left, right):
    return jnp.dot(left, right, preferred_element_type=F32)


def nt(left, right):
    return lax.dot_general(left, right, (((1,), (1,)), ((), ())), preferred_element_type=F32)


def tn(left, right):
    return lax.dot_general(left, right, (((0,), (0,)), ((), ())), preferred_element_type=F32)


def iota(shape, dim):
    return lax.broadcasted_iota(jnp.int32, shape, dim)


def split(value):
    high = value.astype(BF)
    return high, (value - high.astype(F32)).astype(BF)


def lane_head(shape):
    return iota(shape, len(shape) - 1) // HEAD


def block_diag(value):
    width = value.shape[1]
    heads = width // HEAD
    tiled = jnp.concatenate([value] * heads, axis=0)
    keep = (iota((width, width), 0) // HEAD) == (iota((width, width), 1) // HEAD)
    return jnp.where(keep, tiled, jnp.zeros_like(tiled))


def left_of(value):
    high, low = split(value)
    return jnp.concatenate([high, low], axis=0)


def right_of(value):
    high, low = split(value)
    return block_diag(high), block_diag(low)


def mm_parts(left, right):
    rows = left.shape[0] // 2
    both = nn(left, right[0])
    return both[:rows] + both[rows:] + nn(left[:rows], right[1])


def mm(left, right):
    return mm_parts(left_of(left), right_of(right))


def packed_eye(width):
    return (iota((LAND, width), 0) == iota((LAND, width), 1) % HEAD).astype(F32)


def head_total(row):
    heads = lane_head(row.shape)
    out = jnp.zeros_like(row)
    for head in range(row.shape[1] // HEAD):
        mine = heads == head
        out = jnp.where(mine, jnp.sum(jnp.where(mine, row, 0.0), axis=1, keepdims=True), out)
    return out


def head_rows(value, reduce_fn, neutral):
    heads = lane_head(value.shape)
    out = jnp.zeros_like(value)
    for head in range(value.shape[1] // HEAD):
        mine = heads == head
        out = jnp.where(mine, reduce_fn(jnp.where(mine, value, neutral), axis=1, keepdims=True), out)
    return out


def kernel_two(query_marks, key_marks):
    scores = nt(query_marks, block_diag(key_marks)) * TEMPER
    scores_t = nt(key_marks, block_diag(query_marks)) * TEMPER
    expo = jnp.exp(scores - head_rows(scores, jnp.max, -jnp.inf))
    plain = expo / head_rows(expo, jnp.sum, 0.0)
    expo_t = jnp.exp(scores_t - jnp.max(scores_t, axis=0, keepdims=True))
    flipped = expo_t / jnp.sum(expo_t, axis=0, keepdims=True)
    return plain, flipped


def newton(plains, flippeds, save):
    lefts = [left_of(p) for p in plains]
    invs = [
        f / head_total(jnp.sum(f * f, axis=0, keepdims=True)) for f in flippeds
    ]
    for it in range(NS_STEPS):
        prods = [mm_parts(a, right_of(z)) for a, z in zip(lefts, invs)]
        prights = [right_of(p) for p in prods]
        squares = [mm_parts(left_of(p), r) for p, r in zip(prods, prights)]
        steps = [mm_parts(left_of(z), r) for z, r in zip(invs, prights)]
        for index in range(len(invs)):
            save(it, index, invs[index], prods[index], squares[index], steps[index])
        invs = [
            0.25 * (13.0 * z - 15.0 * s + mm(7.0 * z - s, q)) for z, s, q in zip(invs, steps, squares)
        ]
    return invs


def lens_of(len_ref):
    l0, l1, l2, l3 = len_ref[0, 0], len_ref[0, 1], len_ref[0, 2], len_ref[0, 3]
    return (l0, l1, l2, l3), (0, l0, l0 + l1, l0 + l1 + l2)


def choose(item, values):
    out = jnp.where(item == 0, values[0], values[1])
    out = jnp.where(item == 2, values[2], out)
    return jnp.where(item == 3, values[3], out)


def column_edges(col, lens, starts):
    item = col // LAND
    seg = col % LAND
    length = choose(item, lens)
    start = choose(item, starts)
    low_edge = start + ((seg * length + LAND - 1) >> 6)
    high_edge = start + (((seg + 1) * length + LAND - 1) >> 6)
    return low_edge, high_edge, start, start + length


def item_of(pos, starts):
    return (
        (pos >= starts[1]).astype(jnp.int32)
        + (pos >= starts[2]).astype(jnp.int32)
        + (pos >= starts[3]).astype(jnp.int32)
    )


def pair_lanes(hp):
    return slice(128 * hp, 128 * hp + 128)


def both_heads(value):
    first = iota(value.shape, 1) < HEAD
    zero = jnp.zeros_like(value)
    return jnp.concatenate([jnp.where(first, value, zero), jnp.where(first, zero, value)], axis=0)


def pick_heads(value):
    rows = value.shape[0] // 2
    first = iota((rows, 128), 1) < HEAD
    return jnp.where(first, value[:rows], value[rows:])


def toeplitz(tap_row, same):
    wide = jnp.broadcast_to(tap_row, (TOK, EXT))
    return split(pltpu.roll(wide, 0, 1, stride=1, stride_axis=0) * same)


def conv_pair(taps_ref, hp, same, ext_pair):
    outs = []
    for head in (2 * hp, 2 * hp + 1):
        high, low = toeplitz(taps_ref[head : head + 1, :], same)
        outs.append(nn(high, ext_pair) + nn(low, ext_pair))
    first = iota((TOK, 128), 1) < HEAD
    return jnp.where(first, outs[0], outs[1])


def same_item(first_row, lens, starts, reverse=False):
    shape = (TOK, EXT)
    row = iota(shape, 0)
    if reverse:
        row = TOK - 1 - row
    pos = first_row + row
    other = first_row + iota(shape, 1) - HALO
    total = starts[3] + lens[3]
    inside = (other >= 0) & (other < total) & (item_of(pos, starts) == item_of(other, starts))
    return inside.astype(F32)


def group_peers(me):
    for step in range(1, GRP_DEV):
        yield step, lax.rem(me + step, GRP_DEV)


def place(rep, index):
    return (rep, index // 2, lax.rem(index, 2))


def greet(rep, me):
    barrier = pltpu.get_barrier_semaphore()
    for _, other in group_peers(me):
        pl.semaphore_signal(barrier, inc=1, device_id=place(rep, other), device_id_type=MESH_ID)
    pl.semaphore_wait(barrier, GRP_DEV - 1)


def push(src, dst, send_sem, recv_sem, device):
    copy = pltpu.make_async_remote_copy(
        src_ref=src, dst_ref=dst, send_sem=send_sem, recv_sem=recv_sem,
        device_id=device, device_id_type=MESH_ID,
    )
    copy.start()
    return copy


def attend_kernel(
    len_ref, x_ref, qkv_hbm, out_hbm, up_hbm, down_hbm, norm_ref, taps_ref,
    w_ref, wu_ref, wd_ref, wn_ref, q_ref, k_ref, v_ref, qm_ref, km_ref, wm_ref, a_ref, ext_ref,
    res_ref, vloc_ref, dloc_ref, resl_ref, vl_ref, dl_ref,
    win, halo, nd_src, nd_buf, wml, bias_cp, bias_pc, num_s, den_s, probs,
    qkv_st, out_st, up_st, down_st, hot_s, same_s, cv_s, res_s, wu_st, wd_st, norm_st, taps_s,
    win_s, win_r, halo_s, halo_r, nd_s, nd_r, wml_s, wml_r, load_s, norm_s, norm_r, *gather_sem,
):
    loads = [
        pltpu.make_async_copy(src, dst, load_s.at[i])
        for i, (src, dst) in enumerate(
            ((qkv_hbm, qkv_st), (out_hbm, out_st), (up_hbm, up_st), (down_hbm, down_st))
        )
    ]
    for load in loads:
        load.start()
    spot = Spot()
    rep, me = spot.rep, spot.me
    first_row = me * TOK
    is_owner = (me >= 1) & (me <= 6)
    lens, starts = lens_of(len_ref)
    def masks_for_columns():
        shape = (COLS, TOK)
        pos = first_row + iota(shape, 1)
        lo, hi, begin, end = column_edges(iota(shape, 0), lens, starts)
        hot_s[...] = ((pos >= lo) & (pos < hi)).astype(BF)
        bias_cp[...] = jnp.where((pos >= begin) & (pos < end), 0.0, -1e30)
        pshape = (TOK, COLS)
        ppos = first_row + iota(pshape, 0)
        _, _, pbegin, pend = column_edges(iota(pshape, 1), lens, starts)
        bias_pc[...] = jnp.where((ppos >= pbegin) & (ppos < pend), 0.0, -1e30)
        same_s[...] = same_item(first_row, lens, starts)

    gather = Gather(spot, (w_ref, wu_ref, wd_ref), gather_sem)
    row = pl.multiple_of(me * SHARD, SHARD)
    spot.signal_all()
    masks_for_columns()
    loads[0].wait()
    loads[1].wait()
    w_ref[pl.ds(row, SHARD), : 3 * D] = qkv_st[...].astype(BF)
    w_ref[pl.ds(row, SHARD), 3 * D :] = out_st[...].astype(BF)
    spot.wait_all()
    gather.start(0)
    loads[2].wait()
    loads[3].wait()
    wu_st[...] = up_st[...].astype(BF)
    wd_st[...] = down_st[...].astype(BF)
    own_up = pltpu.make_async_copy(wu_st, shard_of(gather.refs, UP, me), load_s.at[5])
    own_down = pltpu.make_async_copy(wd_st, shard_of(gather.refs, DOWN, me), load_s.at[6])
    own_up.start()
    own_down.start()
    norm_st[...] = jnp.zeros_like(norm_st)
    norm_st[0:4, 0:SHARD] = norm_ref[...]
    wn_ref[me] = norm_st[...].astype(BF)
    taps_s[...] = jnp.zeros_like(taps_s)
    taps_s[0:HEADS, 0:KERNEL] = taps_ref[...]
    own_up.wait()
    own_down.wait()
    gather.hop(0, 1)
    gather.hop(0, 2)
    gather.start(UP)
    gather.hop(0, 3)
    gather.hop(UP, 1, False)
    gather.relay(0)
    gather.hop(UP, 2, False)
    gather.start(DOWN)
    gather.last(0)
    gather.hop(UP, 3, False)
    gather.spread(UP)
    gather.finish(0)

    for part, ref in enumerate((q_ref, k_ref, v_ref)):
        ref[...] = nn(x_ref[...], w_ref[:, D * part : D * part + D]).astype(BF)

    @pl.when(me < GRP_DEV - 1)
    def _():
        push(v_ref.at[pl.ds(TOK - HALO, HALO)], halo.at[0], halo_s.at[0], halo_r.at[0], place(rep, me + 1))

    @pl.when(me > 0)
    def _():
        push(v_ref.at[pl.ds(0, HALO)], halo.at[1], halo_s.at[1], halo_r.at[1], place(rep, me - 1))

    qk = jnp.concatenate([q_ref[...], k_ref[...]], axis=1)
    hot = hot_s[...]
    wshape = (16, TOK)
    seg_hi = lens_edge(iota((LAND, TOK), 0) + 1, lens[1], starts[1])
    base = jnp.sum((seg_hi <= first_row).astype(jnp.int32).astype(F32), axis=0, keepdims=True).astype(jnp.int32)
    seg_w = base + iota(wshape, 0)
    wpos = first_row + iota(wshape, 1)
    whot = (
        (wpos >= lens_edge(seg_w, lens[1], starts[1]))
        & (wpos < lens_edge(seg_w + 1, lens[1], starts[1]))
        & (seg_w < LAND)
    ).astype(BF)
    wsum = nn(whot, qk)
    seg_c = base[:, :128] + iota((16, 128), 0)
    wcount = (lens_edge(seg_c + 1, lens[1], starts[1]) - lens_edge(seg_c, lens[1], starts[1])).astype(F32)
    wcount = jnp.concatenate([wcount] * 12, axis=1)
    win[me] = (wsum / wcount).astype(BF)
    gather.hop(DOWN, 1, False)
    push(win.at[me], win.at[me], win_s.at[0], win_r.at[me], spot.to_core)
    for step in range(1, 4):
        push(win.at[me], win.at[me], win_s.at[step], win_r.at[me], spot.to_z(step))
    for step, other in group_peers(me):
        push(wn_ref.at[me], wn_ref.at[me], norm_s.at[step - 1], norm_r.at[me], place(rep, other))

    sums = nn(hot, qk)
    clo, chi, _, _ = column_edges(iota((COLS, 128), 0), lens, starts)
    counts = (chi - clo).astype(F32)
    counts6 = jnp.concatenate([counts] * 6, axis=1)
    qm_ref[...] = (sums[:, :D] / counts6).astype(BF)
    km_ref[...] = (sums[:, D:] / counts6).astype(BF)

    @pl.when(me > 0)
    def _():
        pltpu.make_async_copy(halo.at[0], halo.at[0], halo_r.at[0]).wait()
        ext_ref[0:HALO] = halo[0]

    @pl.when(me == 0)
    def _():
        ext_ref[0:HALO] = jnp.zeros((HALO, D), BF)

    @pl.when(me < GRP_DEV - 1)
    def _():
        pltpu.make_async_copy(halo.at[1], halo.at[1], halo_r.at[1]).wait()
        ext_ref[HALO + TOK : 2 * HALO + TOK] = halo[1]

    @pl.when(me == GRP_DEV - 1)
    def _():
        ext_ref[HALO + TOK : 2 * HALO + TOK] = jnp.zeros((HALO, D), BF)

    ext_ref[HALO : HALO + TOK] = v_ref[...]
    ext_ref[2 * HALO + TOK :] = jnp.zeros((EXT - TOK - 2 * HALO, D), BF)
    for hp in range(6):
        lanes = pair_lanes(hp)
        cv_s[:, lanes] = conv_pair(taps_s, hp, same_s[...], ext_ref[:, lanes])
    gather.hop(DOWN, 2, False)
    for step in range(1, 4):
        slot = spot.z(4 - step) * 2 + spot.grp
        arrive(win.at[slot], win_r.at[slot])
        push(win.at[slot], win.at[slot], win_s.at[3 + step], win_r.at[slot], spot.to_core)
    for step in range(4):
        slot = spot.z(step) * 2 + 1 - spot.grp
        arrive(win.at[slot], win_r.at[slot])
    sshape = (LAND, 128)
    lane_dev = iota((LAND, 128), 1) // 16
    lane_w = iota((LAND, 128), 1) % 16
    seg_end = lens_edge(iota((LAND, 128), 0) + 1, lens[1], starts[1])
    bases = jnp.sum((seg_end <= lane_dev * TOK).astype(jnp.int32).astype(F32), axis=0, keepdims=True).astype(jnp.int32)
    scatter = (iota(sshape, 0) == bases + lane_w).astype(BF)
    long_rows = nn(scatter, win[...].reshape(128, 2 * D))
    qm_ref[LAND : 2 * LAND, :] = long_rows[:, :D].astype(BF)
    km_ref[LAND : 2 * LAND, :] = long_rows[:, D:].astype(BF)

    ones_wide = jnp.ones((TOK, 128), BF)
    ones_row = jnp.ones((8, TOK), BF)
    for hp in range(6):
        lanes = pair_lanes(hp)
        marks = both_heads(qm_ref[:, lanes])
        scores = nt(marks, k_ref[:, lanes]) * TEMPER
        expo = jnp.exp(scores + jnp.concatenate([bias_cp[...]] * 2, axis=0)).astype(BF)
        nd = nn(expo, jnp.concatenate([v_ref[:, lanes], ones_wide], axis=1))
        num = pick_heads(nd[:, :128])
        nd_src[hp, 0:LAND, :] = num[LAND : 2 * LAND]
        nd_src[hp, LAND : LAND + 8, :] = nt(
            ones_row, jnp.concatenate([expo[LAND : 2 * LAND], expo[COLS + LAND : COLS + 2 * LAND]], axis=0)
        )
        num_s[:, lanes] = num
        den_s[:, lanes] = pick_heads(nd[:, 128:])
    for owner in range(1, 7):
        @pl.when(me == owner)
        def _():
            nd_buf[owner] = nd_src[owner - 1]

        @pl.when(me != owner)
        def _():
            push(nd_src.at[owner - 1], nd_buf.at[me], nd_s.at[owner - 1], nd_r.at[me], place(rep, owner))

    gather.hop(DOWN, 3, False)
    gather.relay(UP)
    gather.spread(DOWN)
    wm_ref[...] = jnp.zeros_like(wm_ref)
    has_local = (me == 0) | (me == GRP_DEV - 1)
    slot_rows = (pl.multiple_of(jnp.where(me == 0, 0, 2 * LAND), LAND), 3 * LAND)
    cuts = [(slot, slice(256 * part, 256 * part + 256)) for slot in range(2) for part in range(3)]

    @pl.when(has_local)
    def _():
        def at(ref, slot, lanes):
            return ref[pl.ds(slot_rows[slot], LAND), lanes]

        plains, flippeds = zip(*[kernel_two(at(qm_ref, *c), at(km_ref, *c)) for c in cuts])

        def save(it, index, *mats):
            for m, mat in enumerate(mats):
                res_s[index, it, m] = mat

        invs = newton(plains, flippeds, save)
        keep = pltpu.make_async_copy(res_s, res_ref, load_s.at[4])
        keep.start()
        for (slot, lanes), inv in zip(cuts, invs):
            den = at(den_s, slot, lanes)
            den = jnp.where(den == 0.0, 1.0, den)
            val = at(num_s, slot, lanes) / den
            vloc_ref[slot, :, lanes] = val
            dloc_ref[slot, :, lanes] = den
            wm_ref[pl.ds(slot_rows[slot], LAND), lanes] = mm(inv, val).astype(BF)

    @pl.when(is_owner)
    def _():
        lanes = pl.ds(pl.multiple_of((me - 1) * 128, 128), 128)
        plain, flipped = kernel_two(qm_ref[LAND : 2 * LAND, lanes], km_ref[LAND : 2 * LAND, lanes])

        def save(it, index, *mats):
            for m, mat in enumerate(mats):
                resl_ref[it, m] = mat

        (inv,) = newton([plain], [flipped], save)
        for step, other in group_peers(me):
            pltpu.make_async_copy(nd_buf.at[other], nd_buf.at[other], nd_r.at[other]).wait()
        total = nd_buf[0]
        for j in range(1, GRP_DEV):
            total = total + nd_buf[j]
        row = total[LAND : LAND + 1, :]
        other_row = pltpu.roll(row, HEAD, 1)
        spread = jnp.where(iota((128, 128), 0) < HEAD, row, other_row)
        den = jnp.transpose(spread)[:LAND]
        val = total[:LAND] / den
        vl_ref[...] = val
        dl_ref[...] = den
        wml[me - 1] = mm(inv, val).astype(BF)
        for step, other in group_peers(me):
            push(wml.at[me - 1], wml.at[me - 1], wml_s.at[step - 1], wml_r.at[me - 1], place(rep, other))

    for hp in range(6):
        lanes = pair_lanes(hp)
        scores = nt(q_ref[:, lanes], both_heads(km_ref[:, lanes])) * TEMPER
        for half in range(2):
            expo = jnp.exp(scores[:, COLS * half : COLS * half + COLS] + bias_pc[...])
            probs[hp, :, COLS * half : COLS * half + COLS] = (
                expo / jnp.sum(expo, axis=1, keepdims=True)
            ).astype(BF)

    gather.last(UP)
    gather.relay(DOWN)
    for owner in range(1, 7):
        @pl.when(me != owner)
        def _():
            pltpu.make_async_copy(wml.at[owner - 1], wml.at[owner - 1], wml_r.at[owner - 1]).wait()

        wm_ref[LAND : 2 * LAND, pair_lanes(owner - 1)] = wml[owner - 1]
    for hp in range(6):
        lanes = pair_lanes(hp)
        att = nn(probs[hp], both_heads(wm_ref[:, lanes]))
        a_ref[:, lanes] = (att + cv_s[:, lanes]).astype(BF)

    gather.last(DOWN)
    for step, other in group_peers(me):
        arrive(wn_ref.at[other], norm_r.at[other])
        arrive(wn_ref.at[other], norm_s.at[step - 1])
    for part in (UP, DOWN):
        gather.finish(part)
    for part in (*EARLY, UP, DOWN):
        gather.sent(part)
    @pl.when(has_local)
    def _():
        pltpu.make_async_copy(res_s, res_ref, load_s.at[4]).wait()

    for step, other in group_peers(me):
        pltpu.make_async_copy(win.at[me], win.at[me], win_s.at[step - 1]).wait()
    for owner in range(1, 7):
        @pl.when(me != owner)
        def _():
            pltpu.make_async_copy(nd_src.at[owner - 1], nd_src.at[owner - 1], nd_s.at[owner - 1]).wait()

    @pl.when(is_owner)
    def _():
        for step, other in group_peers(me):
            pltpu.make_async_copy(wml.at[0], wml.at[0], wml_s.at[step - 1]).wait()

    @pl.when(me < GRP_DEV - 1)
    def _():
        pltpu.make_async_copy(halo.at[0], halo.at[0], halo_s.at[0]).wait()

    @pl.when(me > 0)
    def _():
        pltpu.make_async_copy(halo.at[1], halo.at[1], halo_s.at[1]).wait()


def arrive(ref, sem):
    pltpu.make_async_copy(ref, ref, sem).wait()


def lens_edge(seg, length, start):
    return start + ((seg * length + LAND - 1) >> 6)


COLS = ITEMS * LAND
VM = pl.BlockSpec(memory_space=pltpu.VMEM)
SM = pl.BlockSpec(memory_space=pltpu.SMEM)


def attend(item_lengths, tokens, qkv_weight, out_weight, up_weight, down_weight, norm_params, taps):
    sds = jax.ShapeDtypeStruct
    row = sds((TOK, D), BF)
    outs = [sds((D, 4 * D), BF), sds((D, FF), BF), sds((FF, D), BF), sds((8, 16, 128), BF),
            row, row, row, row, row, row, row, sds((EXT, D), BF),
            sds((6, NS_STEPS, 4, LAND, 256), F32), sds((2, LAND, D), F32), sds((2, LAND, D), F32),
            sds((NS_STEPS, 4, LAND, 128), F32), sds((LAND, 128), F32), sds((LAND, 128), F32)]
    dma = pltpu.SemaphoreType.DMA
    vm = pltpu.VMEM
    scratch = [
        vm((8, 16, 2 * D), BF), vm((2, HALO, D), BF), vm((6, LAND + 8, 128), F32),
        vm((8, LAND + 8, 128), F32), vm((6, LAND, 128), BF),
        vm((COLS, TOK), F32), vm((TOK, COLS), F32), vm((COLS, D), F32),
        vm((COLS, D), F32), vm((6, TOK, 2 * COLS), BF),
        vm((SHARD, 3 * D), F32), vm((SHARD, D), F32), vm((SHARD, FF), F32), vm((4 * SHARD, D), F32),
        vm((COLS, TOK), BF), vm((TOK, EXT), F32), vm((TOK, D), F32),
        vm((6, NS_STEPS, 4, LAND, 256), F32), vm((SHARD, FF), BF), vm((4 * SHARD, D), BF),
        vm((16, 128), F32), vm((16, EXT), F32),
        dma((7,)), dma((8,)), dma((2,)), dma((2,)), dma((6,)), dma((8,)), dma((7,)), dma((6,)),
        dma((7,)), dma((7,)), dma((8,)), *gather_sems(),
    ]
    anyspace = pl.BlockSpec(memory_space=pl.ANY)
    w_all, w_up, w_down, norms, *rest = pl.pallas_call(
        attend_kernel, out_shape=outs, in_specs=[SM, VM, anyspace, anyspace, anyspace, anyspace, VM, VM],
        out_specs=[VM, anyspace, anyspace] + [VM] * 9 + [anyspace] + [VM] * 5, scratch_shapes=scratch, name="attend",
        compiler_params=pltpu.CompilerParams(collective_id=1, has_side_effects=True, vmem_limit_bytes=60 * 2**20),
    )(item_lengths, tokens, qkv_weight, out_weight, up_weight, down_weight, norm_params, taps)
    return w_all, w_up, w_down, norms, rest


ERF_NUM = (0.00022905065861350646, 0.0034082910107109506, 0.050955695062380861, 0.18520832239976145, 1.128379143519084)
ERF_DEN = (-1.1791602954361697e-7, 0.000023547966471313185, 0.0010179625278914885, 0.014070470171167667,
           0.11098505178285362, 0.49746925110067538, 1.0)


def horner(value, coefs):
    out = jnp.full_like(value, coefs[0])
    for coef in coefs[1:]:
        out = out * value + coef
    return out


def erf_of(value):
    value = jnp.clip(value, -3.832506856900711, 3.832506856900711)
    square = value * value
    return value * horner(square, ERF_NUM) / horner(square, ERF_DEN)


def norm_stats(hidden):
    centred = hidden - jnp.mean(hidden, axis=-1, keepdims=True)
    scale = lax.rsqrt(jnp.mean(centred * centred, axis=-1, keepdims=True) + EPS_NORM)
    return centred * scale, scale


def norm_back(unit, scale, gain, grad):
    inner = grad * gain
    mean_one = jnp.mean(inner, axis=-1, keepdims=True)
    mean_two = jnp.mean(inner * unit, axis=-1, keepdims=True)
    return scale * (inner - mean_one - unit * mean_two)


FPART = 512


def ffn_kernel(
    x_ref, a_ref, cot_ref, wn_ref, wa_hbm, wu_hbm, wd_hbm,
    y_ref, dh_ref, da_ref, gn_ref, go_ref, gu_hbm, gd_hbm,
    wo, wu, wd, act, slope, du_s, gu, gd, acc, unit_s, h2_s, gains_ref, load_s, keep_s,
):
    parts = FF // FPART
    loads = [pltpu.make_async_copy(wa_hbm.at[:, pl.ds(3 * D, D)], wo, load_s.at[0])]
    for j in range(parts):
        cols = pl.ds(j * FPART, FPART)
        loads.append(pltpu.make_async_copy(wu_hbm.at[:, cols], wu.at[:, cols], load_s.at[1 + j]))
    for j in range(parts):
        cols = pl.ds(j * FPART, FPART)
        loads.append(pltpu.make_async_copy(wd_hbm.at[cols], wd.at[cols], load_s.at[1 + parts + j]))
    for load in loads:
        load.start()
    gains = jnp.zeros((16, D), F32)
    lane = iota((16, D), 1)
    for i in range(GRP_DEV):
        wide = jnp.concatenate([wn_ref[i].astype(F32), jnp.zeros((16, D - 128), F32)], axis=1)
        gains = jnp.where((lane >= SHARD * i) & (lane < SHARD * i + SHARD), pltpu.roll(wide, SHARD * i, 1), gains)
    gains_ref[...] = gains
    loads[0].wait()
    hidden = x_ref[...].astype(F32) + nn(a_ref[...], wo[...])
    unit, scale = norm_stats(hidden)
    unit_s[...] = unit
    gain_one, shift_one = gains_ref[0:1, :], gains_ref[1:2, :]
    normed_low = (unit * gain_one + shift_one).astype(BF)
    acc[...] = jnp.zeros_like(acc)
    for j in range(parts):
        cols = slice(j * FPART, j * FPART + FPART)
        loads[1 + j].wait()
        loads[1 + parts + j].wait()
        up = nn(normed_low, wu[:, cols])
        cdf = 0.5 + 0.5 * erf_of(up * (0.5**0.5))
        low = (up * cdf).astype(BF)
        act[:, cols] = low
        slope[:, cols] = cdf + up * jnp.exp(-0.5 * up * up) * ((2.0 * 3.141592653589793) ** -0.5)
        acc[...] += nn(low, wd[cols, :])
    h2 = unit_s[...] * gain_one + shift_one + acc[...]
    unit_two, scale_two = norm_stats(h2)
    gain_two, shift_two = gains_ref[2:3, :], gains_ref[3:4, :]
    y_ref[...] = (unit_two * gain_two + shift_two).astype(BF)
    cot = cot_ref[...].astype(F32)
    gn_ref[2:3, :] = jnp.sum(cot * unit_two, axis=0, keepdims=True)
    gn_ref[3:4, :] = jnp.sum(cot, axis=0, keepdims=True)
    dh2 = norm_back(unit_two, scale_two, gain_two, cot)
    h2_s[...] = dh2
    down_low = dh2.astype(BF)
    acc[...] = jnp.zeros_like(acc)
    for j in range(parts):
        cols = slice(j * FPART, j * FPART + FPART)
        gd[cols, :] = tn(act[:, cols], down_low).astype(BF)
        pltpu.make_async_copy(gd.at[cols], gd_hbm.at[cols], keep_s.at[j]).start()
        du_s[:, cols] = (slope[:, cols] * nt(down_low, wd[cols, :])).astype(BF)
    for j in range(parts):
        cols = slice(j * FPART, j * FPART + FPART)
        du = du_s[:, cols]
        acc[...] += nt(du, wu[:, cols])
        gu[:, cols] = tn(normed_low, du).astype(BF)
        pltpu.make_async_copy(gu.at[:, cols], gu_hbm.at[:, cols], keep_s.at[parts + j]).start()
    dx = h2_s[...] + acc[...]
    unit = unit_s[...]
    gn_ref[0:1, :] = jnp.sum(dx * unit, axis=0, keepdims=True)
    gn_ref[1:2, :] = jnp.sum(dx, axis=0, keepdims=True)
    dh = norm_back(unit, scale, gain_one, dx)
    dh_ref[...] = dh
    low = dh.astype(BF)
    da_ref[...] = nt(low, wo[...]).astype(BF)
    go_ref[...] = tn(a_ref[...], low).astype(BF)
    for j in range(parts):
        cols = slice(j * FPART, j * FPART + FPART)
        pltpu.make_async_copy(gd.at[cols], gd_hbm.at[cols], keep_s.at[j]).wait()
        pltpu.make_async_copy(gu.at[:, cols], gu_hbm.at[:, cols], keep_s.at[parts + j]).wait()


def feed_forward(tokens, branch, cotangent, gains, w_all, w_up, w_down):
    sds = jax.ShapeDtypeStruct
    vm = pltpu.VMEM
    dma = pltpu.SemaphoreType.DMA
    anyspace = pl.BlockSpec(memory_space=pl.ANY)
    parts = FF // FPART
    return pl.pallas_call(
        ffn_kernel, name="feed_forward",
        out_shape=[sds((TOK, D), BF), sds((TOK, D), F32), sds((TOK, D), BF), sds((4, D), F32), sds((D, D), BF),
                   sds((D, FF), BF), sds((FF, D), BF)],
        in_specs=[VM] * 4 + [anyspace] * 3, out_specs=[VM] * 5 + [anyspace] * 2,
        scratch_shapes=[vm((D, D), BF), vm((D, FF), BF), vm((FF, D), BF), vm((TOK, FF), BF), vm((TOK, FF), F32),
                        vm((TOK, FF), BF), vm((D, FF), BF), vm((FF, D), BF), vm((TOK, D), F32), vm((TOK, D), F32),
                        vm((TOK, D), F32), vm((16, D), F32), dma((1 + 2 * parts,)), dma((2 * parts,))],
        compiler_params=pltpu.CompilerParams(vmem_limit_bytes=56 * 2**20),
        cost_estimate=pl.CostEstimate(flops=8 * 10**9, bytes_accessed=22 * 10**6, transcendentals=10**6),
    )(tokens, branch, cotangent, gains, w_all, w_up, w_down)


ASTEPS = 6
AROWS = SHARD // ASTEPS


def adam_math(weight, one, two, grad, clip, rate, decay):
    grad = grad * clip
    one = BETA_ONE * one + (1.0 - BETA_ONE) * grad
    two = BETA_TWO * two + (1.0 - BETA_TWO) * grad * grad
    first_hat = one * (1.0 / (1.0 - BETA_ONE**STEP))
    second_hat = two * (1.0 / (1.0 - BETA_TWO**STEP))
    return weight - rate * (first_hat / (jnp.sqrt(second_hat) + ADAM_EPS) + decay * weight), one, two


def adam_kernel(norm_ref, total_ref, fin_ref, down_g_ref, *refs):
    ins, outs = refs[:18], refs[18:]
    clip = MAX_NORM / jnp.maximum(norm_ref[0, 0], MAX_NORM)

    def update(group, rows_cols, grad, rate, decay):
        got = [ref[rows_cols] for ref in ins[3 * group : 3 * group + 3]]
        for ref, value in zip(outs[3 * group : 3 * group + 3], adam_math(*got, grad, clip, rate, decay)):
            ref[rows_cols] = value

    for quarter in range(3):
        at = (slice(None), slice(D * quarter, D * quarter + D))
        update(0, at, fin_ref[0, quarter].astype(F32), RATE_MATRIX, DECAY_RATE)
    update(1, (slice(None), slice(None)), fin_ref[0, 3].astype(F32), RATE_MATRIX, DECAY_RATE)
    for quarter in range(4):
        at = (slice(None), slice(D * quarter, D * quarter + D))
        update(2, at, fin_ref[1, quarter].astype(F32), RATE_MATRIX, DECAY_RATE)
    update(3, (slice(None), slice(None)), down_g_ref[...].astype(F32), RATE_MATRIX, DECAY_RATE)
    whole = (slice(None), slice(None))
    update(4, whole, total_ref[0:4, 0:SHARD], RATE_NORM, 0.0)
    update(5, whole, total_ref[4:16, 128 : 128 + KERNEL], RATE_CONV, 0.0)


def adam(norm, total, fin, triples):
    sds = jax.ShapeDtypeStruct
    flat = [a for triple in triples for a in triple]
    row = lambda cols, rows=AROWS: pl.BlockSpec((rows, cols), lambda i: (i, 0))
    keep = lambda shape: pl.BlockSpec(shape, lambda i: (0, 0))
    specs = [row(3 * D)] * 3 + [row(D)] * 3 + [row(FF)] * 3 + [row(D, 4 * AROWS)] * 3
    specs += [keep((4, SHARD))] * 3 + [keep((HEADS, KERNEL))] * 3
    return pl.pallas_call(
        adam_kernel, name="adam", grid=(ASTEPS,),
        out_shape=[sds(a.shape, F32) for a in flat],
        in_specs=[pl.BlockSpec(memory_space=pltpu.SMEM), keep((16, 2 * 128)),
                  pl.BlockSpec((2, 4, AROWS, D), lambda i: (0, 0, i, 0)),
                  pl.BlockSpec((4 * AROWS, D), lambda i: (i + 2 * ASTEPS, 0)), *specs],
        out_specs=specs,
        compiler_params=pltpu.CompilerParams(vmem_limit_bytes=62 * 2**20),
    )(norm, total, fin, fin.reshape(12 * SHARD, D), *flat)


def nt_parts(left, right):
    rows = left.shape[0] // 2
    both = nt(left, right[0])
    return both[:rows] + both[rows:] + nt(left[:rows], right[1])


def flip(value):
    high, low = split(value)
    eye = packed_eye(value.shape[1]).astype(BF)
    return nt(eye, block_diag(high)) + nt(eye, block_diag(low))


def half_sum(value):
    rows = value.shape[0] // 2
    return value[:rows] + value[rows:]


def newton_back(qms, kms, vals, dens, dwms, load):
    count = len(qms)
    plains = [kernel_two(q, k)[0] for q, k in zip(qms, kms)]
    krights = [right_of(p) for p in plains]
    ups = [nt_parts(left_of(v), right_of(d)) for v, d in zip(vals, dwms)]
    last = [load(NS_STEPS - 1, i) for i in range(count)]
    finals = [0.25 * (13.0 * m[0] - 15.0 * m[3] + mm(7.0 * m[0] - m[3], m[2])) for m in last]
    dvals = [mm(flip(z), d) for z, d in zip(finals, dwms)]
    dkts = [jnp.zeros_like(p) for p in plains]
    for it in reversed(range(NS_STEPS)):
        mats = [load(it, i) for i in range(count)]
        plefts = [left_of(m[1]) for m in mats]
        dys = [0.25 * mm(m[2], u) for m, u in zip(mats, ups)]
        dqs = [0.25 * mm(u, 7.0 * m[0] - m[3]) for m, u in zip(mats, ups)]
        drs = [-3.75 * u - dy for u, dy in zip(ups, dys)]
        dqrs = [right_of(d) for d in dqs]
        dps = [
            mm(dr, m[0]) + mm_parts(pl_, dqr) + mm(dq, m[1])
            for dr, m, pl_, dqr, dq in zip(drs, mats, plefts, dqrs, dqs)
        ]
        nexts = [
            3.25 * u + 7.0 * dy + mm_parts(pl_, right_of(dr))
            for u, dy, pl_, dr in zip(ups, dys, plefts, drs)
        ]
        dkts = [a + mm(m[0], d) for a, m, d in zip(dkts, mats, dps)]
        ups = [n + mm_parts(left_of(d), kr) for n, d, kr in zip(nexts, dps, krights)]
    outs = []
    for i in range(count):
        plain = plains[i]
        fro = head_total(jnp.sum(plain * plain, axis=0, keepdims=True))
        cross = head_total(jnp.sum(ups[i] * plain, axis=0, keepdims=True))
        dk = flip(dkts[i]) + ups[i] / fro - 2.0 * plain * (cross / (fro * fro))
        dscore = plain * (dk - head_rows(plain * dk, jnp.sum, 0.0)) * TEMPER
        dqm = half_sum(nn(left_of(dscore), block_diag(kms[i])))
        dkm = half_sum(nn(left_of(flip(dscore)), block_diag(qms[i])))
        dnum = (dvals[i] / dens[i]).astype(BF)
        dden = -head_rows(dnum.astype(F32) * vals[i], jnp.sum, 0.0)
        outs.append((dnum, dden, dqm, dkm))
    return outs


def twice(value):
    return jnp.concatenate([value, value], axis=0)


def attend_back_kernel(
    len_ref, x_ref, w_hbm, taps_ref, q_ref, k_ref, v_ref, qm_ref, km_ref, wm_ref, ext_ref,
    res_ref, vloc_ref, dloc_ref, resl_ref, vl_ref, dl_ref, da_ref, dh_ref,
    out_ref, up_hbm, down_hbm, norms_ref,
    gx_ref, fin_ref, total_ref, norm_ref,
    gw_ref, w_ref, stage, small_s, rc, rx, ry, r2x, r2y, rz, one, two, pair, sq,
    halo, dext, dwm_src, dwm_buf, dk1_src, dk1_buf, dn_buf, dq3_src, dq3_buf, ds_buf,
    bias_cp, dwm_s, dkm_s, dqm_s, dnum_s, dden_s, dq_s, dk_s, dv_s, dsum_s, dp_s, res_s, load_s,
    halo_s, halo_r, dwm_ss, dwm_r, dk1_ss, dk1_r, dn_ss, dn_r, dq3_ss, dq3_r, ds_ss, ds_r,
    stage_s, s1, r1, s2, r2, sp, rp, ss, sr, *red_sems,
):
    spot = Spot()
    spot.signal_all()
    rep, me = spot.rep, spot.me
    first_row = me * TOK
    is_owner = (me >= 1) & (me <= 6)
    lens, starts = lens_of(len_ref)
    has_local = (me == 0) | (me == GRP_DEV - 1)

    @pl.when(has_local)
    def _():
        pltpu.make_async_copy(res_ref, res_s, load_s.at[0]).start()

    load_w = pltpu.make_async_copy(w_hbm.at[:, pl.ds(0, 3 * D)], w_ref, load_s.at[1])

    def own(m, shard, quarter):
        row = pl.multiple_of(shard * SHARD, SHARD)
        if m == 0 and quarter == 3:
            return out_ref.at[pl.ds(row, SHARD), :]
        if m == 0:
            return gw_ref.at[pl.ds(row, SHARD), D * quarter : D * quarter + D]
        if m == 1:
            return up_hbm.at[pl.ds(row, SHARD), D * quarter : D * quarter + D]
        return down_hbm.at[pl.ds(pl.multiple_of(4 * row + SHARD * quarter, SHARD), SHARD), :]

    def kept(m, seq, quarter):
        if m == 0:
            return own(m, seq * 2 + spot.grp, quarter)
        return stage.at[m - 1, seq, quarter]

    for m in (2, 1):
        for seq in range(4):
            for quarter in range(4):
                pltpu.make_async_copy(
                    own(m, seq * 2 + spot.grp, quarter), stage.at[m - 1, seq, quarter], stage_s.at[m - 1]
                ).start()
    red = Reduce(spot, own, kept, (rc, rx, ry, r2x, r2y, rz, fin_ref), red_sems)
    small = Small(spot, small_s, one, two, pair, (s1, r1, sp, rp, s2, r2))
    spot.wait_all()

    @pl.when(me < GRP_DEV - 1)
    def _():
        push(da_ref.at[pl.ds(TOK - HALO, HALO)], halo.at[0], halo_s.at[0], halo_r.at[0], place(rep, me + 1))

    @pl.when(me > 0)
    def _():
        push(da_ref.at[pl.ds(0, HALO)], halo.at[1], halo_s.at[1], halo_r.at[1], place(rep, me - 1))

    red.chip(2)
    red.chip(1)
    shape = (COLS, TOK)
    pos = first_row + iota(shape, 1)
    _, _, begin, end = column_edges(iota(shape, 0), lens, starts)
    bias_cp[...] = jnp.where((pos >= begin) & (pos < end), 0.0, -1e30)

    def to_owner(src, buf, send, recv, hp):
        owner = hp + 1

        @pl.when(me == owner)
        def _():
            buf[owner] = src[hp]

        @pl.when(me != owner)
        def _():
            push(src.at[hp], buf.at[me], send.at[hp], recv.at[me], place(rep, owner))

    for hp in range(6):
        lanes = pair_lanes(hp)
        marks = both_heads(km_ref[:, lanes])
        scores = nt(marks, q_ref[:, lanes]) * TEMPER + twice(bias_cp[...])
        expo = jnp.exp(scores)
        dprob = nt(both_heads(wm_ref[:, lanes]), da_ref[:, lanes])
        lows, dss = [], []
        for half in range(2):
            part = slice(COLS * half, COLS * half + COLS)
            prob = expo[part] / jnp.sum(expo[part], axis=0, keepdims=True)
            inner = jnp.sum(prob * dprob[part], axis=0, keepdims=True)
            lows.append(prob.astype(BF))
            dss.append((prob * (dprob[part] - inner)).astype(BF))
        dscore = jnp.concatenate(dss, axis=0)
        dwm = pick_heads(nn(jnp.concatenate(lows, axis=0), da_ref[:, lanes]))
        dkm = pick_heads(nn(dscore, q_ref[:, lanes])) * TEMPER
        dq_s[:, lanes] = tn(dscore, marks) * TEMPER
        dwm_s[:, lanes] = dwm
        dkm_s[:, lanes] = dkm
        dwm_src[hp] = dwm[LAND : 2 * LAND]
        dk1_src[hp] = dkm[LAND : 2 * LAND].astype(BF)
        to_owner(dwm_src, dwm_buf, dwm_ss, dwm_r, hp)
        to_owner(dk1_src, dk1_buf, dk1_ss, dk1_r, hp)

    arrive(stage.at[1], stage_s.at[1])
    red.plane(2)
    dnum_s[...] = jnp.zeros_like(dnum_s)
    dden_s[...] = jnp.zeros_like(dden_s)
    dqm_s[...] = jnp.zeros_like(dqm_s)
    slot_rows = (pl.multiple_of(jnp.where(me == 0, 0, 2 * LAND), LAND), 3 * LAND)
    cuts = [(slot, slice(256 * part, 256 * part + 256)) for slot in range(2) for part in range(3)]

    @pl.when(has_local)
    def _():
        def at(ref, slot, lanes):
            return ref[pl.ds(slot_rows[slot], LAND), lanes]

        pltpu.make_async_copy(res_ref, res_s, load_s.at[0]).wait()
        outs = newton_back(
            [at(qm_ref, *c) for c in cuts], [at(km_ref, *c) for c in cuts],
            [vloc_ref[slot, :, c] for slot, c in cuts], [dloc_ref[slot, :, c] for slot, c in cuts],
            [at(dwm_s, *c) for c in cuts],
            lambda it, i: [res_s[i, it, m] for m in range(4)],
        )
        for (slot, c), (dnum, dden, dqm, dkm) in zip(cuts, outs):
            rows = pl.ds(slot_rows[slot], LAND)
            dnum_s[rows, c] = dnum
            dden_s[rows, c] = dden
            dqm_s[rows, c] = dqm
            dkm_s[rows, c] = dkm_s[rows, c] + dkm

    @pl.when(is_owner)
    def _():
        lanes = pl.ds(pl.multiple_of((me - 1) * 128, 128), 128)
        for step, other in group_peers(me):
            arrive(dwm_buf.at[other], dwm_r.at[other])
        total = dwm_buf[0]
        for j in range(1, GRP_DEV):
            total = total + dwm_buf[j]
        ((dnum, dden, dqm, dkm),) = newton_back(
            [qm_ref[LAND : 2 * LAND, lanes]], [km_ref[LAND : 2 * LAND, lanes]],
            [vl_ref[...]], [dl_ref[...]], [total],
            lambda it, i: [resl_ref[it, m] for m in range(4)],
        )
        high, low = split(dden)
        dn_buf[me - 1, 0:LAND] = dnum
        dn_buf[me - 1, LAND : 2 * LAND] = jnp.where(iota((LAND, 128), 1) % HEAD < 32, high, low)
        for step, other in group_peers(me):
            push(dn_buf.at[me - 1], dn_buf.at[me - 1], dn_ss.at[step - 1], dn_r.at[me - 1], place(rep, other))
        dqm_s[LAND : 2 * LAND, 0:128] = dqm
        dqm_s[LAND : 2 * LAND, 128:256] = dkm

    arrive(stage.at[0], stage_s.at[0])
    red.plane(1)
    @pl.when(me > 0)
    def _():
        arrive(halo.at[0], halo_r.at[0])
        dext[0:HALO] = halo[0]

    @pl.when(me == 0)
    def _():
        dext[0:HALO] = jnp.zeros((HALO, D), BF)

    @pl.when(me < GRP_DEV - 1)
    def _():
        arrive(halo.at[1], halo_r.at[1])
        dext[HALO + TOK : 2 * HALO + TOK] = halo[1]

    @pl.when(me == GRP_DEV - 1)
    def _():
        dext[HALO + TOK : 2 * HALO + TOK] = jnp.zeros((HALO, D), BF)

    dext[HALO : HALO + TOK] = da_ref[...]
    dext[2 * HALO + TOK :] = jnp.zeros((EXT - TOK - 2 * HALO, D), BF)
    same = same_item(first_row, lens, starts)
    for hp in range(6):
        lanes = pair_lanes(hp)
        dv_s[:, lanes] = conv_pair(taps_ref, hp, same, dext[:, lanes])
    same_back = same_item(first_row, lens, starts, reverse=True)
    turn = (iota((TOK, TOK), 0) + iota((TOK, TOK), 1) == TOK - 1).astype(BF)
    turned = nn(turn, da_ref[...]).astype(BF)
    for hp in range(6):
        lanes = pair_lanes(hp)
        pairs = nt(both_heads(turned[:, lanes]), ext_ref[:, lanes])
        for half in range(2):
            band = pltpu.roll(pairs[TOK * half : TOK * half + TOK] * same_back, 0, 1, stride=1, stride_axis=0)
            small_s[4 + 2 * hp + half : 5 + 2 * hp + half, :EXT] = jnp.sum(band, axis=0, keepdims=True)
    small_s[4:, EXT:] = jnp.zeros((HEADS, D - EXT), F32)
    small_s[:4, :] = norms_ref[...]
    small.start()
    red.plane_two(2)
    load_w.start()

    for owner in range(1, 7):
        lanes = pair_lanes(owner - 1)

        @pl.when(me != owner)
        def _():
            arrive(dn_buf.at[owner - 1], dn_r.at[owner - 1])

        dnum_s[LAND : 2 * LAND, lanes] = dn_buf[owner - 1, 0:LAND]
        packed = dn_buf[owner - 1, LAND : 2 * LAND].astype(F32)
        one = packed[:, 0:1] + packed[:, 32:33]
        two = packed[:, 64:65] + packed[:, 96:97]
        dden_s[LAND : 2 * LAND, lanes] = jnp.where(iota((LAND, 128), 1) < HEAD, one, two)
    for hp in range(6):
        lanes = pair_lanes(hp)
        marks = both_heads(qm_ref[:, lanes])
        expo = jnp.exp(nt(marks, k_ref[:, lanes]) * TEMPER + twice(bias_cp[...]))
        dnum = both_heads(dnum_s[:, lanes])
        dden = jnp.concatenate([dden_s[:, 128 * hp : 128 * hp + 1], dden_s[:, 128 * hp + 64 : 128 * hp + 65]], axis=0)
        dscore = (expo * (nt(dnum, v_ref[:, lanes]) + dden)).astype(BF)
        dqm = pick_heads(nn(dscore, k_ref[:, lanes])) * TEMPER
        dk_s[:, lanes] = tn(dscore, marks) * TEMPER
        dv_s[:, lanes] += tn(expo.astype(BF), dnum)
        dq3_src[hp] = dqm[LAND : 2 * LAND].astype(BF)
        to_owner(dq3_src, dq3_buf, dq3_ss, dq3_r, hp)

        @pl.when(jnp.logical_not(is_owner))
        def _():
            dqm_s[:, lanes] += dqm

    red.plane_two(1)
    clo, chi, _, _ = column_edges(iota((COLS, 128), 0), lens, starts)
    counts = (chi - clo).astype(F32)

    @pl.when(is_owner)
    def _():
        lanes = pl.ds(pl.multiple_of((me - 1) * 128, 128), 128)
        for step, other in group_peers(me):
            arrive(dk1_buf.at[other], dk1_r.at[other])
            arrive(dq3_buf.at[other], dq3_r.at[other])
        total_q = dqm_s[LAND : 2 * LAND, 0:128]
        total_k = dqm_s[LAND : 2 * LAND, 128:256]
        for j in range(GRP_DEV):
            total_q = total_q + dq3_buf[j].astype(F32)
            total_k = total_k + dk1_buf[j].astype(F32)
        ds_buf[me - 1, 0] = (total_q / counts[LAND : 2 * LAND]).astype(BF)
        ds_buf[me - 1, 1] = (total_k / counts[LAND : 2 * LAND]).astype(BF)
        for step, other in group_peers(me):
            push(ds_buf.at[me - 1], ds_buf.at[me - 1], ds_ss.at[step - 1], ds_r.at[me - 1], place(rep, other))

    for hp in range(6):
        lanes = pair_lanes(hp)
        dsum_s[:, lanes] = (dqm_s[:, lanes] / counts).astype(BF)
        dsum_s[:, D + 128 * hp : D + 128 * hp + 128] = (dkm_s[:, lanes] / counts).astype(BF)
    for owner in range(1, 7):
        @pl.when(me != owner)
        def _():
            arrive(ds_buf.at[owner - 1], ds_r.at[owner - 1])

        hp = owner - 1
        dsum_s[LAND : 2 * LAND, pair_lanes(hp)] = ds_buf[owner - 1, 0]
        dsum_s[LAND : 2 * LAND, D + 128 * hp : D + 128 * hp + 128] = ds_buf[owner - 1, 1]
    pshape = (TOK, COLS)
    ppos = first_row + iota(pshape, 0)
    plo, phi, _, _ = column_edges(iota(pshape, 1), lens, starts)
    hot = ((ppos >= plo) & (ppos < phi)).astype(BF)
    dp_s[:, :D] = (dq_s[...] + nn(hot, dsum_s[:, :D])).astype(BF)
    dp_s[:, D : 2 * D] = (dk_s[...] + nn(hot, dsum_s[:, D:])).astype(BF)
    dp_s[:, 2 * D :] = dv_s[...].astype(BF)
    for part in range(3):
        cols = slice(D * part, D * part + D)
        gw_ref[:, cols] = tn(x_ref[...], dp_s[:, cols]).astype(BF)
    red.chip(0)
    red.line(2)
    red.plane(0)
    red.line(1)
    load_w.wait()
    gx_ref[...] = (dh_ref[...] + nt(dp_s[...], w_ref[...])).astype(BF)
    small.middle()
    red.plane_two(0)
    red.share(2)
    red.line(0)
    red.share(1)
    small.across()
    red.share(0)
    total = small.end()
    mine = pltpu.roll(total, lax.rem(D - me * SHARD, D), 1)
    taps_sum = pltpu.roll(total, D - (TOK - 1), 1)
    total_ref[:, :128] = mine[:, :128]
    total_ref[:, 128:] = taps_sum[:, :128]
    lane = iota((16, D), 1)
    real = (iota((16, D), 0) < 4) | ((lane >= TOK - 1) & (lane < TOK - 1 + KERNEL))
    extra = jnp.sum(jnp.where(real, total * total, 0.0), keepdims=True)
    for m in (2, 1, 0):
        red.done(m)
    norm_ref[...] = jnp.broadcast_to(jnp.sqrt(square_sum(spot, fin_ref, sq, ss, sr, extra)), (8, 128))
    for m in range(3):
        red.sent(m)

    for hp in range(6):
        @pl.when(me != hp + 1)
        def _():
            arrive(dwm_src.at[hp], dwm_ss.at[hp])
            arrive(dk1_src.at[hp], dk1_ss.at[hp])
            arrive(dq3_src.at[hp], dq3_ss.at[hp])

    @pl.when(is_owner)
    def _():
        for step, other in group_peers(me):
            arrive(dn_buf.at[0], dn_ss.at[step - 1])
            arrive(ds_buf.at[0], ds_ss.at[step - 1])

    @pl.when(me < GRP_DEV - 1)
    def _():
        arrive(halo.at[0], halo_s.at[0])

    @pl.when(me > 0)
    def _():
        arrive(halo.at[1], halo_s.at[1])


def attend_back(item_lengths, tokens, w_all, taps_back, kept, d_branch, d_hidden, grad_out, grad_up, grad_down, grad_norms):
    sds = jax.ShapeDtypeStruct
    outs = [sds((TOK, D), BF), sds((3, 4, *BLK), BF), sds((16, 256), F32), sds((8, 128), F32)]
    dma = pltpu.SemaphoreType.DMA
    vm = pltpu.VMEM
    scratch = [
        vm((D, 3 * D), BF), vm((D, 3 * D), BF), vm((2, 4, 4, *BLK), BF), vm((16, D), F32), *reduce_bufs(),
        vm((4, 16, D), F32), vm((4, 16, D), F32), vm((2, 16, D), F32), vm((8, 8, 128), F32),
        vm((2, HALO, D), BF), vm((EXT, D), BF), vm((6, LAND, 128), F32), vm((8, LAND, 128), F32),
        vm((6, LAND, 128), BF), vm((8, LAND, 128), BF), vm((6, 2 * LAND, 128), BF),
        vm((6, LAND, 128), BF), vm((8, LAND, 128), BF), vm((6, 2, LAND, 128), BF),
        vm((COLS, TOK), F32), vm((COLS, D), F32), vm((COLS, D), F32), vm((COLS, D), F32),
        vm((COLS, D), BF), vm((COLS, D), F32), vm((TOK, D), F32), vm((TOK, D), F32), vm((TOK, D), F32),
        vm((COLS, 2 * D), BF), vm((TOK, 3 * D), BF), vm((6, NS_STEPS, 4, LAND, 256), F32), dma((2,)),
        dma((2,)), dma((2,)), dma((6,)), dma((8,)), dma((6,)), dma((8,)), dma((7,)), dma((6,)),
        dma((6,)), dma((8,)), dma((7,)), dma((6,)),
        dma((2,)), dma((3,)), dma((4,)), dma((3,)), dma((4,)), dma((1,)), dma((1,)), dma((7,)), dma((8,)),
        *reduce_sems(),
    ]
    args = (item_lengths, tokens, w_all, taps_back, *kept, d_branch, d_hidden, grad_out, grad_up, grad_down, grad_norms)
    anyspace = pl.BlockSpec(memory_space=pl.ANY)
    in_specs = [SM] + [VM] * (len(args) - 1)
    for index in (2, 11, 20, 21):
        in_specs[index] = anyspace
    return pl.pallas_call(
        attend_back_kernel, out_shape=outs, in_specs=in_specs,
        out_specs=[VM] * len(outs), scratch_shapes=scratch, name="attend_back",
        compiler_params=pltpu.CompilerParams(collective_id=2, has_side_effects=True, vmem_limit_bytes=62 * 2**20),
    )(*args)


def on_device_fast(
    tokens, cotangent, item_lengths,
    qkv_weight, qkv_first, qkv_second, out_weight, out_first, out_second,
    up_weight, up_first, up_second, down_weight, down_first, down_second,
    norm_params, norm_first, norm_second, conv_kernel, conv_first, conv_second,
):
    taps_back = jnp.pad(conv_kernel[:, ::-1], ((0, 4), (0, EXT - KERNEL)))
    w_all, w_up, w_down, norms, rest = attend(
        item_lengths, tokens, qkv_weight, out_weight, up_weight, down_weight, norm_params, conv_kernel
    )
    queries, key_rows, value_rows, mean_q, mean_k, mixed, branch, value_ext, *resid = rest
    result, d_hidden_one, d_branch_low, grad_norms, grad_out, grad_up, grad_down = feed_forward(
        tokens, branch, cotangent, norms, w_all, w_up, w_down
    )
    input_grad, fin, total, norm = attend_back(
        item_lengths, tokens, w_all, taps_back,
        (queries, key_rows, value_rows, mean_q, mean_k, mixed, value_ext, *resid),
        d_branch_low, d_hidden_one, grad_out, grad_up, grad_down, grad_norms,
    )
    news = adam(
        norm, total, fin,
        (
            (qkv_weight, qkv_first, qkv_second), (out_weight, out_first, out_second),
            (up_weight, up_first, up_second), (down_weight, down_first, down_second),
            (norm_params, norm_first, norm_second), (conv_kernel, conv_first, conv_second),
        ),
    )
    return (result, input_grad, norm[0, 0], *news)


def solution(mesh):
    in_specs = (
        P(("rep", "seq", "grp"), None),
        P(("rep", "seq", "grp"), None),
        P("rep", None),
        P(("seq", "grp"), None),
        P(("seq", "grp"), None),
        P(("seq", "grp"), None),
        P(("seq", "grp"), None),
        P(("seq", "grp"), None),
        P(("seq", "grp"), None),
        P(("seq", "grp"), None),
        P(("seq", "grp"), None),
        P(("seq", "grp"), None),
        P(("seq", "grp"), None),
        P(("seq", "grp"), None),
        P(("seq", "grp"), None),
        P(None, ("seq", "grp")),
        P(None, ("seq", "grp")),
        P(None, ("seq", "grp")),
        P(),
        P(),
        P(),
    )
    out_specs = (
        P(("rep", "seq", "grp"), None),
        P(("rep", "seq", "grp"), None),
        P(),
        P(("seq", "grp"), None),
        P(("seq", "grp"), None),
        P(("seq", "grp"), None),
        P(("seq", "grp"), None),
        P(("seq", "grp"), None),
        P(("seq", "grp"), None),
        P(("seq", "grp"), None),
        P(("seq", "grp"), None),
        P(("seq", "grp"), None),
        P(("seq", "grp"), None),
        P(("seq", "grp"), None),
        P(("seq", "grp"), None),
        P(None, ("seq", "grp")),
        P(None, ("seq", "grp")),
        P(None, ("seq", "grp")),
        P(),
        P(),
        P(),
    )
    fast = dict(mesh.shape) == {"rep": 4, "seq": 4, "grp": 2}
    body = on_device_fast if fast else on_device
    return jax.shard_map(
        body, mesh=mesh, in_specs=in_specs, out_specs=out_specs, check_vma=False
    )
```

```python
import jax
import jax.numpy as jnp
from jax import lax
from jax.experimental import pallas as pl
from jax.experimental.pallas import tpu as pltpu
from jax.sharding import PartitionSpec as P

D = 768
FF = 3072
HEADS = 12
HEAD = 64
LAND = 64
KERNEL = 33
HALO = 16
NS_STEPS = 6
ITEMS = 4
STEP = 10
TOK_DEV = 256
GRP_DEV = 8
HIGHEST_PREC = lax.Precision.HIGHEST
EPS_NORM = 1e-05
BETA_ONE = 0.9
BETA_TWO = 0.999
ADAM_EPS = 1e-08
RATE_MATRIX = 0.02
RATE_NORM = 0.3
RATE_CONV = 0.1
DECAY_RATE = 0.01
MAX_NORM = 1.0


def extended(cells, sides, width):
    for axis, dim in sides:
        count = lax.axis_size(axis)
        ends = count - 1
        head = lax.slice_in_dim(cells, 0, width, axis=dim)
        tail = lax.slice_in_dim(cells, cells.shape[dim] - width, cells.shape[dim], axis=dim)
        cells = jnp.concatenate(
            [
                lax.ppermute(tail, axis, [(i, (i + 1) % count) for i in range(ends)]),
                cells,
                lax.ppermute(head, axis, [((i + 1) % count, i) for i in range(ends)]),
            ],
            axis=dim,
        )
    return cells


def locate(positions, lengths):
    ends = jnp.cumsum(lengths)
    starts = ends - lengths
    inside = (positions[:, None] >= starts[None, :]) & (positions[:, None] < ends[None, :])
    item_ids = jnp.sum((positions[:, None] >= ends[None, :]).astype(jnp.int32), axis=1)
    valid = (positions >= 0) & (positions < ends[-1])
    item_ids = jnp.where(valid, item_ids, -1)
    own_len = jnp.sum(jnp.where(inside, lengths[None, :], 0), axis=1)
    own_start = jnp.sum(jnp.where(inside, starts[None, :], 0), axis=1)
    segment = (positions - own_start) * LAND // jnp.maximum(own_len, 1)
    columns = jnp.where(valid, item_ids * LAND + segment, -1)
    return (item_ids, columns)


def landmark_counts(lengths):
    marks = jnp.arange(LAND + 1, dtype=jnp.int32)
    edges = (marks[None, :] * lengths[:, None] + LAND - 1) // LAND
    return (edges[:, 1:] - edges[:, :-1]).reshape(-1)


def layer_norm(hidden, gain_row, shift_row):
    row_mean = jnp.mean(hidden, axis=-1, keepdims=True)
    centred = hidden - row_mean
    variance = jnp.mean(centred * centred, axis=-1, keepdims=True)
    return centred * lax.rsqrt(variance + EPS_NORM) * gain_row + shift_row


def gelu_exact(values):
    return jax.nn.gelu(values, approximate=False)


def mixing_rest(mark_scores, num_all, den_all):
    key_values = (
        num_all.reshape(ITEMS, LAND, HEADS, HEAD) / den_all.reshape(ITEMS, LAND, HEADS)[..., None]
    )
    kernel_two = jax.nn.softmax(mark_scores, axis=-1)
    frobenius = jnp.sum(kernel_two * kernel_two, axis=(2, 3), keepdims=True)
    inverse = jnp.swapaxes(kernel_two, 2, 3) / frobenius
    identity = jnp.eye(LAND, dtype=kernel_two.dtype)
    for iteration in range(NS_STEPS):
        product = jnp.einsum("ahjk,ahkl->ahjl", kernel_two, inverse, precision=HIGHEST_PREC)
        inner = 7.0 * identity - product
        inner = 15.0 * identity - jnp.einsum(
            "ahjk,ahkl->ahjl", product, inner, precision=HIGHEST_PREC
        )
        inner = 13.0 * identity - jnp.einsum(
            "ahjk,ahkl->ahjl", product, inner, precision=HIGHEST_PREC
        )
        inverse = 0.25 * jnp.einsum("ahjk,ahkl->ahjl", inverse, inner, precision=HIGHEST_PREC)
    mixed_rows = jnp.einsum("ahjk,akhd->ajhd", inverse, key_values, precision=HIGHEST_PREC)
    return mixed_rows.reshape(ITEMS * LAND, HEADS * HEAD)


def adamw(weight, moment_one, moment_two, gradient, clip_factor, rate_value, decay_value):
    clipped = gradient * clip_factor
    moment_one = BETA_ONE * moment_one + (1.0 - BETA_ONE) * clipped
    moment_two = BETA_TWO * moment_two + (1.0 - BETA_TWO) * clipped * clipped
    first_hat = moment_one / (1.0 - BETA_ONE**STEP)
    second_hat = moment_two / (1.0 - BETA_TWO**STEP)
    weight = weight - rate_value * (
        first_hat / (jnp.sqrt(second_hat) + ADAM_EPS) + decay_value * weight
    )
    return (weight, moment_one, moment_two)


def contract_rows(left, right):
    return lax.dot_general(
        left, right, (((0,), (0,)), ((), ())), preferred_element_type=jnp.float32
    )


def contract_cols(left, right):
    return lax.dot_general(
        left, right, (((1,), (1,)), ((), ())), preferred_element_type=jnp.float32
    )


def on_device(
    tokens,
    cotangent,
    item_lengths,
    qkv_weight,
    qkv_first,
    qkv_second,
    out_weight,
    out_first,
    out_second,
    up_weight,
    up_first,
    up_second,
    down_weight,
    down_first,
    down_second,
    norm_params,
    norm_first,
    norm_second,
    conv_kernel,
    conv_first,
    conv_second,
):
    temper = HEAD ** (-0.5)
    col_total = ITEMS * LAND
    w_qkv, w_out, w_up, w_down, gains_low = (
        lax.all_gather(qkv_weight.astype(jnp.bfloat16), ("seq", "grp"), axis=0, tiled=True),
        lax.all_gather(out_weight.astype(jnp.bfloat16), ("seq", "grp"), axis=0, tiled=True),
        lax.all_gather(up_weight.astype(jnp.bfloat16), ("seq", "grp"), axis=0, tiled=True),
        lax.all_gather(down_weight.astype(jnp.bfloat16), ("seq", "grp"), axis=0, tiled=True),
        lax.all_gather(norm_params.astype(jnp.bfloat16), ("seq", "grp"), axis=1, tiled=True),
    )
    gains_all = gains_low.astype(jnp.float32)
    lengths = item_lengths[0]
    first_row = lax.axis_index(("seq", "grp")) * TOK_DEV
    positions = first_row - HALO + jnp.arange(TOK_DEV + 2 * HALO, dtype=jnp.int32)
    item_ext, column_ext = locate(positions, lengths)
    item_mid = item_ext[HALO : HALO + TOK_DEV]
    column_mid = column_ext[HALO : HALO + TOK_DEV]
    col_ids = jnp.arange(col_total, dtype=jnp.int32)
    col_hot = (column_mid[:, None] == col_ids[None, :]).astype(jnp.bfloat16)
    member = (item_mid[:, None] == (col_ids // LAND)[None, :]).astype(jnp.float32)
    counts_f = landmark_counts(lengths).astype(jnp.float32)
    projected = jnp.dot(tokens, w_qkv, preferred_element_type=jnp.float32)
    proj_low = projected.astype(jnp.bfloat16)
    queries = proj_low[:, :D]
    key_rows = proj_low[:, D : 2 * D]
    value_rows = proj_low[:, 2 * D :]
    land_sums = lax.psum(contract_rows(col_hot, proj_low[:, : 2 * D]), ("seq", "grp"))
    mean_q = (land_sums[:, :D] / counts_f[:, None]).astype(jnp.bfloat16)
    mean_k = (land_sums[:, D:] / counts_f[:, None]).astype(jnp.bfloat16)
    query_heads = queries.reshape(TOK_DEV, HEADS, HEAD)
    key_heads = key_rows.reshape(TOK_DEV, HEADS, HEAD)
    value_heads = value_rows.reshape(TOK_DEV, HEADS, HEAD)
    mean_q3 = mean_q.reshape(col_total, HEADS, HEAD)
    mean_k3 = mean_k.reshape(col_total, HEADS, HEAD)
    scores_key = (
        jnp.einsum("chd,phd->chp", mean_q3, key_heads, preferred_element_type=jnp.float32) * temper
    )
    expo_key = jnp.exp(scores_key) * jnp.transpose(member)[:, None, :]
    expo_low = expo_key.astype(jnp.bfloat16)
    num_part = jnp.einsum(
        "chp,phd->chd", expo_low, value_heads, preferred_element_type=jnp.float32
    ).reshape(col_total, D)
    num_all, den_all = lax.psum((num_part, jnp.sum(expo_key, axis=2)), ("seq", "grp"))
    query_marks4 = mean_q.reshape(ITEMS, LAND, HEADS, HEAD)
    key_marks4 = mean_k.reshape(ITEMS, LAND, HEADS, HEAD)
    mark_scores = (
        jnp.einsum("ajhd,akhd->ahjk", query_marks4, key_marks4, preferred_element_type=jnp.float32)
        * temper
    )
    mixed_rows, mix_pull = jax.vjp(mixing_rest, mark_scores, num_all, den_all)
    mixed3 = mixed_rows.astype(jnp.bfloat16).reshape(col_total, HEADS, HEAD)
    scores_tok = (
        jnp.einsum("phd,chd->phc", query_heads, mean_k3, preferred_element_type=jnp.float32)
        * temper
    )
    expo_tok = jnp.exp(scores_tok) * member[:, None, :]
    attn_probs = expo_tok / jnp.sum(expo_tok, axis=2, keepdims=True)
    probs_low = attn_probs.astype(jnp.bfloat16)
    attended = jnp.einsum(
        "phc,chd->phd", probs_low, mixed3, preferred_element_type=jnp.float32
    ).reshape(TOK_DEV, D)
    value_ext = extended(value_rows, ((("seq", "grp"), 0),), HALO)
    channel_taps = jnp.repeat(conv_kernel, HEAD, axis=0)
    same_masks = [
        (item_ext[offset : offset + TOK_DEV] == item_mid).astype(jnp.float32)
        for offset in range(KERNEL)
    ]
    conv_out = jnp.zeros((TOK_DEV, D), jnp.float32)
    for offset in range(KERNEL):
        conv_out = conv_out + value_ext[offset : offset + TOK_DEV] * (
            channel_taps[:, offset][None, :] * same_masks[offset][:, None]
        )
    branch = (attended + conv_out).astype(jnp.bfloat16)
    attn_out = jnp.dot(branch, w_out, preferred_element_type=jnp.float32)
    normed_one, norm_one_pull = jax.vjp(
        layer_norm, tokens.astype(jnp.float32) + attn_out, gains_all[0], gains_all[1]
    )
    normed_low = normed_one.astype(jnp.bfloat16)
    up_out = jnp.dot(normed_low, w_up, preferred_element_type=jnp.float32)
    activated, gelu_pull = jax.vjp(gelu_exact, up_out)
    act_low = activated.astype(jnp.bfloat16)
    down_out = jnp.dot(act_low, w_down, preferred_element_type=jnp.float32)
    result, norm_two_pull = jax.vjp(layer_norm, normed_one + down_out, gains_all[2], gains_all[3])
    d_hidden_two, d_gain_two, d_shift_two = norm_two_pull(cotangent.astype(jnp.float32))
    d_down_low = d_hidden_two.astype(jnp.bfloat16)
    grad_down = contract_rows(act_low, d_down_low)
    (d_up,) = gelu_pull(contract_cols(d_down_low, w_down))
    d_up_low = d_up.astype(jnp.bfloat16)
    grad_up = contract_rows(normed_low, d_up_low)
    d_normed = d_hidden_two + contract_cols(d_up_low, w_up)
    d_hidden_one, d_gain_one, d_shift_one = norm_one_pull(d_normed)
    d_attn_low = d_hidden_one.astype(jnp.bfloat16)
    grad_out = contract_rows(branch, d_attn_low)
    d_branch_low = contract_cols(d_attn_low, w_out).astype(jnp.bfloat16)
    d_branch_f = d_branch_low.astype(jnp.float32)
    d_branch_ext = extended(d_branch_low, ((("seq", "grp"), 0),), HALO)
    d_values_conv = jnp.zeros((TOK_DEV, D), jnp.float32)
    tap_grads = []
    for offset in range(KERNEL):
        d_values_conv = d_values_conv + d_branch_ext[offset : offset + TOK_DEV] * (
            channel_taps[:, KERNEL - 1 - offset][None, :] * same_masks[offset][:, None]
        )
        tap_grads.append(
            jnp.sum(
                d_branch_f * value_ext[offset : offset + TOK_DEV] * same_masks[offset][:, None],
                axis=0,
            )
        )
    grad_conv = jnp.sum(jnp.stack(tap_grads, axis=1).reshape(HEADS, HEAD, KERNEL), axis=1)
    d_attended = d_branch_low.reshape(TOK_DEV, HEADS, HEAD)
    d_mixed_part = jnp.einsum(
        "phc,phd->chd", probs_low, d_attended, preferred_element_type=jnp.float32
    ).reshape(col_total, D)
    d_probs = jnp.einsum("phd,chd->phc", d_attended, mixed3, preferred_element_type=jnp.float32)
    d_scores_tok = (
        attn_probs * (d_probs - jnp.sum(attn_probs * d_probs, axis=2, keepdims=True))
    ).astype(jnp.bfloat16)
    d_query_tok = (
        jnp.einsum("phc,chd->phd", d_scores_tok, mean_k3, preferred_element_type=jnp.float32)
        * temper
    )
    d_meank_part = (
        jnp.einsum(
            "phc,phd->chd", d_scores_tok, query_heads, preferred_element_type=jnp.float32
        ).reshape(col_total, D)
        * temper
    )
    d_mixed, d_meank_tok = lax.psum((d_mixed_part, d_meank_part), ("seq", "grp"))
    d_mark_scores, d_num, d_den = mix_pull(d_mixed)
    d_mark_scaled = d_mark_scores * temper
    d_mean_q_mix = jnp.einsum(
        "ahjk,akhd->ajhd", d_mark_scaled, key_marks4.astype(jnp.float32), precision=HIGHEST_PREC
    ).reshape(col_total, D)
    d_mean_k_mix = jnp.einsum(
        "ahjk,ajhd->akhd", d_mark_scaled, query_marks4.astype(jnp.float32), precision=HIGHEST_PREC
    ).reshape(col_total, D)
    d_num3 = d_num.reshape(col_total, HEADS, HEAD)
    d_expo = d_den[:, :, None] + jnp.einsum(
        "chd,phd->chp", d_num3, value_heads.astype(jnp.float32), precision=HIGHEST_PREC
    )
    d_scores_key = (expo_key * d_expo).astype(jnp.bfloat16)
    d_key_mix = (
        jnp.einsum("chp,chd->phd", d_scores_key, mean_q3, preferred_element_type=jnp.float32)
        * temper
    )
    d_meanq_part = (
        jnp.einsum(
            "chp,phd->chd", d_scores_key, key_heads, preferred_element_type=jnp.float32
        ).reshape(col_total, D)
        * temper
    )
    d_value_mix = jnp.einsum(
        "chp,chd->phd", expo_low.astype(jnp.float32), d_num3, precision=HIGHEST_PREC
    )
    d_meanq_tok = lax.psum(d_meanq_part, ("seq", "grp"))
    d_sums = (
        jnp.concatenate([d_mean_q_mix + d_meanq_tok, d_mean_k_mix + d_meank_tok], axis=1)
        / counts_f[:, None]
    )
    d_land_rows = jnp.dot(col_hot.astype(jnp.float32), d_sums, precision=HIGHEST_PREC)
    d_queries = d_query_tok.reshape(TOK_DEV, D) + d_land_rows[:, :D]
    d_keys = d_key_mix.reshape(TOK_DEV, D) + d_land_rows[:, D:]
    d_values = d_value_mix.reshape(TOK_DEV, D) + d_values_conv
    d_proj_low = jnp.concatenate([d_queries, d_keys, d_values], axis=1).astype(jnp.bfloat16)
    grad_qkv = contract_rows(tokens, d_proj_low)
    input_grad = (d_hidden_one + contract_cols(d_proj_low, w_qkv)).astype(jnp.bfloat16)
    grad_norms = jnp.stack([d_gain_one, d_shift_one, d_gain_two, d_shift_two])
    group_qkv, group_out, group_up, group_down, group_norm = (
        lax.psum_scatter(grad_qkv, ("seq", "grp"), scatter_dimension=0, tiled=True),
        lax.psum_scatter(grad_out, ("seq", "grp"), scatter_dimension=0, tiled=True),
        lax.psum_scatter(grad_up, ("seq", "grp"), scatter_dimension=0, tiled=True),
        lax.psum_scatter(grad_down, ("seq", "grp"), scatter_dimension=0, tiled=True),
        lax.psum_scatter(grad_norms, ("seq", "grp"), scatter_dimension=1, tiled=True),
    )
    shard_qkv, shard_out, shard_up, shard_down, shard_norm, conv_rep = (
        lax.psum(group_qkv.astype(jnp.bfloat16), "rep").astype(jnp.float32),
        lax.psum(group_out.astype(jnp.bfloat16), "rep").astype(jnp.float32),
        lax.psum(group_up.astype(jnp.bfloat16), "rep").astype(jnp.float32),
        lax.psum(group_down.astype(jnp.bfloat16), "rep").astype(jnp.float32),
        lax.psum(group_norm.astype(jnp.bfloat16), "rep").astype(jnp.float32),
        lax.psum(grad_conv.astype(jnp.bfloat16), "rep").astype(jnp.float32),
    )
    local_sq = (
        jnp.sum(shard_qkv * shard_qkv)
        + jnp.sum(shard_out * shard_out)
        + jnp.sum(shard_up * shard_up)
        + jnp.sum(shard_down * shard_down)
        + jnp.sum(shard_norm * shard_norm)
    )
    total_sq, conv_total = lax.psum((local_sq, conv_rep), ("seq", "grp"))
    grad_total = jnp.sqrt(total_sq + jnp.sum(conv_total * conv_total))
    clip_factor = MAX_NORM / jnp.maximum(grad_total, MAX_NORM)
    qkv_new = adamw(
        qkv_weight, qkv_first, qkv_second, shard_qkv, clip_factor, RATE_MATRIX, DECAY_RATE
    )
    out_new = adamw(
        out_weight, out_first, out_second, shard_out, clip_factor, RATE_MATRIX, DECAY_RATE
    )
    up_new = adamw(up_weight, up_first, up_second, shard_up, clip_factor, RATE_MATRIX, DECAY_RATE)
    down_new = adamw(
        down_weight, down_first, down_second, shard_down, clip_factor, RATE_MATRIX, DECAY_RATE
    )
    norm_new = adamw(norm_params, norm_first, norm_second, shard_norm, clip_factor, RATE_NORM, 0.0)
    conv_new = adamw(conv_kernel, conv_first, conv_second, conv_total, clip_factor, RATE_CONV, 0.0)
    return (
        result.astype(jnp.bfloat16),
        input_grad,
        grad_total,
        qkv_new[0],
        qkv_new[1],
        qkv_new[2],
        out_new[0],
        out_new[1],
        out_new[2],
        up_new[0],
        up_new[1],
        up_new[2],
        down_new[0],
        down_new[1],
        down_new[2],
        norm_new[0],
        norm_new[1],
        norm_new[2],
        conv_new[0],
        conv_new[1],
        conv_new[2],
    )


SHARD = D // GRP_DEV
BLK = (SHARD, D)


class Spot:
    def __init__(self):
        self.rep, self.seq, self.grp = lax.axis_index("rep"), lax.axis_index("seq"), lax.axis_index("grp")
        self.me = self.seq * 2 + self.grp
        self.xn = self.rep + 1 - 2 * lax.rem(self.rep, 2)
        self.yn = lax.rem(self.rep + 2, 4)
        self.dn = 3 - self.rep
        self.to_x = (self.xn, self.seq, self.grp)
        self.to_y = (self.yn, self.seq, self.grp)
        self.to_d = (self.dn, self.seq, self.grp)
        self.to_core = (self.rep, self.seq, 1 - self.grp)

    def z(self, step):
        return lax.rem(self.seq + step, 4)

    def to_z(self, step):
        return (self.rep, self.z(step), self.grp)

    def greet_all(self):
        self.signal_all()
        self.wait_all()

    def wait_all(self):
        pl.semaphore_wait(pltpu.get_barrier_semaphore(), GRP_DEV + 2)

    def signal_all(self):
        barrier = pltpu.get_barrier_semaphore()
        for device in (self.to_x, self.to_y, self.to_d):
            pl.semaphore_signal(barrier, inc=1, device_id=device, device_id_type=MESH_ID)
        for _, other in group_peers(self.me):
            pl.semaphore_signal(barrier, inc=1, device_id=place(self.rep, other), device_id_type=MESH_ID)


CHUNKS = 1
CHUNK = SHARD // CHUNKS
EARLY = tuple(range(CHUNKS))
UP, DOWN = CHUNKS, CHUNKS + 1


def unit_of(refs, part, shard, quarter):
    if part < UP:
        row = pl.multiple_of(shard * SHARD + part * CHUNK, CHUNK)
        return refs[0].at[pl.ds(row, CHUNK), pl.ds(pl.multiple_of(quarter * D, D), D)]
    if part == UP:
        row = pl.multiple_of(shard * SHARD, SHARD)
        return refs[1].at[pl.ds(row, SHARD), pl.ds(pl.multiple_of(quarter * D, D), D)]
    row = pl.multiple_of(shard * 4 * SHARD + quarter * SHARD, SHARD)
    return refs[2].at[pl.ds(row, SHARD), :]


def shard_of(refs, part, shard):
    if part < UP:
        row = pl.multiple_of(shard * SHARD + part * CHUNK, CHUNK)
        return refs[0].at[pl.ds(row, CHUNK), :]
    rows = SHARD if part == UP else 4 * SHARD
    return refs[part - UP + 1].at[pl.ds(pl.multiple_of(shard * rows, SHARD), rows), :]


class Gather:
    def __init__(self, spot, refs, sems):
        self.spot, self.refs = spot, refs
        (self.zs, self.zr, self.xs, self.xr, self.ys, self.yr, self.fs, self.fr, self.cs, self.cr) = sems

    def unit(self, part, seq, quarter):
        return unit_of(self.refs, part, seq * 2 + self.spot.grp, quarter)

    def start(self, part):
        spot = self.spot
        mine = self.unit(part, spot.seq, spot.rep)
        for sign in (1, -1):
            @pl.when((spot.seq + sign >= 0) & (spot.seq + sign <= 3))
            def _():
                push(mine, mine, self.zs.at[part, (sign + 1) // 2, spot.seq], self.zr.at[part, spot.seq],
                     (spot.rep, spot.seq + sign, spot.grp))
        own = shard_of(self.refs, part, spot.me)
        push(own, own, self.cs.at[part, 12], self.cr.at[part, 12], spot.to_core)

    def hop(self, part, far, spread=True):
        spot = self.spot
        for sign in (1, -1):
            src = lax.rem(spot.seq - sign * far + 4, 4)

            @pl.when((spot.seq - sign * far >= 0) & (spot.seq - sign * far <= 3))
            def _():
                unit = self.unit(part, src, spot.rep)
                arrive(unit, self.zr.at[part, src])

                @pl.when((spot.seq + sign >= 0) & (spot.seq + sign <= 3))
                def _():
                    push(unit, unit, self.zs.at[part, (sign + 1) // 2, src], self.zr.at[part, src],
                         (spot.rep, spot.seq + sign, spot.grp))

                if spread:
                    self.give(part, src)

    def give(self, part, src):
        spot = self.spot
        unit = self.unit(part, src, spot.rep)

        push(unit, unit, self.xs.at[part, src], self.xr.at[part, src], spot.to_x)
        push(unit, unit, self.ys.at[part, src], self.yr.at[part, src], spot.to_y)
        push(unit, unit, self.cs.at[part, src], self.cr.at[part, src], spot.to_core)

    def spread(self, part):
        for src in self.others():
            self.give(part, src)

    def others(self):
        return [self.spot.z(step) for step in range(1, 4)]

    def relay(self, part):
        spot = self.spot
        for src in self.others():
            unit = self.unit(part, src, spot.xn)
            arrive(unit, self.xr.at[part, src])

            @pl.when(lax.rem(src + part, 2) == 0)
            def _():
                push(unit, unit, self.fs.at[part, src], self.fr.at[part, src], spot.to_y)

            push(unit, unit, self.cs.at[part, 4 + src], self.cr.at[part, 4 + src], spot.to_core)

            unit = self.unit(part, src, spot.yn)
            arrive(unit, self.yr.at[part, src])

            @pl.when(lax.rem(src + part, 2) == 1)
            def _():
                push(unit, unit, self.fs.at[part, src], self.fr.at[part, src], spot.to_x)

            push(unit, unit, self.cs.at[part, 8 + src], self.cr.at[part, 8 + src], spot.to_core)

    def last(self, part):
        spot = self.spot
        for src in self.others():
            unit = self.unit(part, src, spot.dn)
            arrive(unit, self.fr.at[part, src])
            push(unit, unit, self.cs.at[part, 13 + src], self.cr.at[part, 13 + src], spot.to_core)

    def finish(self, part):
        spot = self.spot
        other = 1 - spot.grp
        arrive(shard_of(self.refs, part, spot.seq * 2 + other), self.cr.at[part, 12])
        for base, quarter in ((0, spot.rep), (4, spot.xn), (8, spot.yn), (13, spot.dn)):
            for src in self.others():
                arrive(unit_of(self.refs, part, src * 2 + other, quarter), self.cr.at[part, base + src])

    def sent(self, part):
        spot = self.spot
        unit = self.unit(part, spot.seq, spot.rep)
        for src in self.others():
            for sem in (self.xs, self.ys, self.fs):
                arrive(unit, sem.at[part, src])
            for base in (0, 4, 8, 13):
                arrive(unit, self.cs.at[part, base + src])
        arrive(shard_of(self.refs, part, spot.me), self.cs.at[part, 12])
        for sign in (1, -1):
            @pl.when((spot.seq + sign >= 0) & (spot.seq + sign <= 3))
            def _():
                arrive(unit, self.zs.at[part, (sign + 1) // 2, spot.seq])

                for far in range(1, 4):
                    src = spot.seq - sign * far

                    @pl.when((src >= 0) & (src <= 3))
                    def _():
                        arrive(unit, self.zs.at[part, (sign + 1) // 2, lax.rem(src + 4, 4)])


def gather_sems():
    dma = pltpu.SemaphoreType.DMA
    return [dma((CHUNKS + 2, 2, 4))] + [dma((CHUNKS + 2, n)) for n in (4, 4, 4, 4, 4, 4, 4, 17, 17)]


class Reduce:
    def __init__(self, spot, own, bufs, sems):
        self.spot, self.own = spot, own
        self.rc, self.first, self.rx, self.ry, self.r2x, self.r2y, self.rz, self.fin = bufs
        (self.cs, self.cr, self.xs, self.xr, self.ys, self.yr, self.x2s, self.x2r, self.y2s, self.y2r,
         self.zs, self.zr, self.fs, self.fr) = sems

    def cell(self, m, seq, quarter):
        if m == 0:
            return self.first.at[pl.ds(pl.multiple_of((quarter * 4 + seq) * SHARD, SHARD), SHARD), :]
        return self.rc.at[m - 1, seq, quarter]

    def bump(self, m, seq, quarter, *others):
        cell = self.cell(m, seq, quarter)
        total = cell[...].astype(F32)
        for other in others:
            total = total + other.astype(F32)
        cell[...] = total.astype(BF)

    def chip_sent(self, m):
        arrive(self.rc.at[0], self.cs.at[m])

    def chip(self, m, quarters=(0, 1, 2, 3)):
        spot = self.spot
        for quarter in quarters:
            for seq in range(4):
                push(self.own(m, seq * 2 + 1 - spot.grp, quarter), self.cell(m, seq, quarter),
                     self.cs.at[m], self.cr.at[m, quarter], spot.to_core)

    def plane(self, m, quarters=(0, 1, 2, 3)):
        spot = self.spot
        for quarter in quarters:
            arrive(self.rc.at[0, :, quarter], self.cr.at[m, quarter])

            @pl.loop(0, 4)
            def _(seq):
                self.bump(m, seq, quarter, self.own(m, seq * 2 + spot.grp, quarter)[...])

            @pl.when(spot.xn == quarter)
            def _():
                self.to_plane(m, quarter, 0, True, False)

            @pl.when(spot.yn == quarter)
            def _():
                self.to_plane(m, quarter, 0, False, True)

            @pl.when(spot.dn == quarter)
            def _():
                self.to_plane(m, quarter, 1, True, True)

    def to_plane(self, m, quarter, slot, along_x, along_y):
        spot = self.spot
        for j in range(2):
            if along_x:
                push(self.cell(m, j, quarter), self.rx.at[m, j, slot], self.xs.at[m], self.xr.at[m], spot.to_x)
            if along_y:
                push(self.cell(m, 2 + j, quarter), self.ry.at[m, j, slot], self.ys.at[m], self.yr.at[m], spot.to_y)

    def plane_two(self, m):
        spot = self.spot
        arrive(self.rx.at[m], self.xr.at[m])

        @pl.loop(0, 2)
        def _(j):
            self.bump(m, j, spot.yn, self.rx[m, j, 1])

        for j in range(2):
            push(self.cell(m, j, spot.yn), self.r2y.at[m, j], self.y2s.at[m], self.y2r.at[m], spot.to_y)
        arrive(self.ry.at[m], self.yr.at[m])

        @pl.loop(0, 2)
        def _(j):
            self.bump(m, 2 + j, spot.xn, self.ry[m, j, 1])

        for j in range(2):
            push(self.cell(m, 2 + j, spot.xn), self.r2x.at[m, j], self.x2s.at[m], self.x2r.at[m], spot.to_x)

    def line(self, m):
        spot = self.spot
        arrive(self.r2y.at[m], self.y2r.at[m])
        arrive(self.r2x.at[m], self.x2r.at[m])

        @pl.loop(0, 2)
        def _(j):
            self.bump(m, j, spot.rep, self.rx[m, j, 0], self.r2y[m, j])
            self.bump(m, 2 + j, spot.rep, self.ry[m, j, 0], self.r2x[m, j])

        near = spot.seq + 1 - 2 * lax.rem(spot.seq, 2)
        for slot, dest in enumerate((near, lax.rem(near + 2, 4))):
            push(self.cell(m, dest, spot.rep), self.rz.at[m, slot], self.zs.at[m, 0], self.zr.at[m, 0],
                 (spot.rep, near, spot.grp))

    def line_two(self, m):
        spot = self.spot
        far = spot.z(2)
        pair = self.rz.at[m, pl.ds(0, 2)]
        arrive(pair, self.zr.at[m, 0])
        self.bump(m, far, spot.rep, self.rz[m, 1])
        push(self.cell(m, far, spot.rep), self.rz.at[m, 2], self.zs.at[m, 1], self.zr.at[m, 1], spot.to_z(2))

    def total(self, m):
        spot = self.spot
        arrive(self.rz.at[m, 2], self.zr.at[m, 1])
        total = (
            self.cell(m, spot.seq, spot.rep)[...].astype(F32) + self.rz[m, 0].astype(F32) + self.rz[m, 2].astype(F32)
        ).astype(BF)
        self.fin[m, spot.rep] = total
        value = total.astype(F32)
        value = value * value
        rows = value[0:8]
        for k in range(1, SHARD // 8):
            rows = rows + value[8 * k : 8 * k + 8]
        square = rows[:, 0:128]
        for k in range(1, D // 128):
            square = square + rows[:, 128 * k : 128 * k + 128]
        return square

    def share(self, m):
        spot = self.spot
        mine = self.fin.at[m, spot.rep]
        devices = (spot.to_x, spot.to_y, spot.to_d) if m == 0 else (spot.to_x, spot.to_y)
        for step, device in enumerate(devices):
            push(mine, mine, self.fs.at[m, step], self.fr.at[m, spot.rep], device)

    def share_on(self, m):
        spot = self.spot
        source, device = (spot.yn, spot.to_x) if m == 2 else (spot.xn, spot.to_y)
        block = self.fin.at[m, source]
        arrive(block, self.fr.at[m, source])
        push(block, block, self.fs.at[m, 2], self.fr.at[m, source], device)

    def done(self, m):
        spot = self.spot
        rest = ((spot.xn, spot.yn, spot.dn), (spot.yn, spot.dn), (spot.xn, spot.dn))[m]
        for other in rest:
            arrive(self.fin.at[m, other], self.fr.at[m, other])

    def sent(self, m):
        arrive(self.rx.at[m], self.xs.at[m])
        arrive(self.ry.at[m], self.ys.at[m])
        arrive(self.r2x.at[m], self.x2s.at[m])
        arrive(self.r2y.at[m], self.y2s.at[m])
        arrive(self.rz.at[m, pl.ds(0, 2)], self.zs.at[m, 0])
        arrive(self.rz.at[m, 2], self.zs.at[m, 1])
        for step in range(3):
            arrive(self.fin.at[m, 0], self.fs.at[m, step])


def reduce_bufs():
    vm = pltpu.VMEM
    return [vm((2, 4, 4, *BLK), BF), vm((3, 2, 2, *BLK), BF), vm((3, 2, 2, *BLK), BF),
            vm((3, 2, *BLK), BF), vm((3, 2, *BLK), BF), vm((3, 3, *BLK), BF)]


def reduce_sems():
    dma = pltpu.SemaphoreType.DMA
    return [dma((3,)), dma((3, 4))] + [dma((3,)) for _ in range(8)] + [dma((3, 2)), dma((3, 2)), dma((3, 3)), dma((3, 4))]


class Small:
    def __init__(self, spot, src, one, two, pair, sems):
        self.spot, self.src, self.one, self.two, self.pair = spot, src, one, two, pair
        self.s1, self.r1, self.sp, self.rp, self.s2, self.r2 = sems

    def start(self):
        spot = self.spot
        for step, device in enumerate((spot.to_x, spot.to_y, spot.to_d)):
            push(self.src, self.one.at[spot.rep], self.s1.at[step], self.r1.at[spot.rep], device)

    def middle(self):
        spot = self.spot
        total = self.src[...]
        for other in (spot.xn, spot.yn, spot.dn):
            arrive(self.one.at[other], self.r1.at[other])
            total = total + self.one[other]
        self.pair[0] = total
        push(self.pair.at[0], self.pair.at[1], self.sp.at[0], self.rp.at[0], spot.to_core)

    def across(self):
        spot = self.spot
        arrive(self.pair.at[1], self.rp.at[0])
        self.two[spot.seq] = self.pair[0] + self.pair[1]
        mine = self.two.at[spot.seq]
        for step in range(1, 4):
            push(mine, mine, self.s2.at[step - 1], self.r2.at[spot.seq], spot.to_z(step))

    def end(self):
        spot = self.spot
        for step in range(1, 4):
            arrive(self.two.at[spot.z(step)], self.r2.at[spot.z(step)])
        total = self.two[0] + self.two[1] + self.two[2] + self.two[3]
        arrive(self.pair.at[0], self.sp.at[0])
        for step in range(3):
            arrive(self.one.at[0], self.s1.at[step])
            arrive(self.two.at[0], self.s2.at[step])
        return total


TOK = 256

TEMPER = HEAD ** (-0.5)
MESH_ID = pl.DeviceIdType.MESH
BF = jnp.bfloat16
F32 = jnp.float32
EXT = 384


def nn(left, right):
    return jnp.dot(left, right, preferred_element_type=F32)


def nt(left, right):
    return lax.dot_general(left, right, (((1,), (1,)), ((), ())), preferred_element_type=F32)


def tn(left, right):
    return lax.dot_general(left, right, (((0,), (0,)), ((), ())), preferred_element_type=F32)


def iota(shape, dim):
    return lax.broadcasted_iota(jnp.int32, shape, dim)


def split(value):
    high = value.astype(BF)
    return high, (value - high.astype(F32)).astype(BF)


def lane_head(shape):
    return iota(shape, len(shape) - 1) // HEAD


def block_diag(value):
    width = value.shape[1]
    heads = width // HEAD
    tiled = jnp.concatenate([value] * heads, axis=0)
    keep = (iota((width, width), 0) // HEAD) == (iota((width, width), 1) // HEAD)
    return jnp.where(keep, tiled, jnp.zeros_like(tiled))


def left_of(value):
    high, low = split(value)
    return jnp.concatenate([high, low], axis=0)


def right_of(value):
    high, low = split(value)
    return block_diag(high), block_diag(low)


def mm_parts(left, right):
    rows = left.shape[0] // 2
    both = nn(left, right[0])
    return both[:rows] + both[rows:] + nn(left[:rows], right[1])


def mm(left, right):
    return mm_parts(left_of(left), right_of(right))


def packed_eye(width):
    return (iota((LAND, width), 0) == iota((LAND, width), 1) % HEAD).astype(F32)


def head_total(row):
    heads = lane_head(row.shape)
    out = jnp.zeros_like(row)
    for head in range(row.shape[1] // HEAD):
        mine = heads == head
        out = jnp.where(mine, jnp.sum(jnp.where(mine, row, 0.0), axis=1, keepdims=True), out)
    return out


def head_rows(value, reduce_fn, neutral):
    heads = lane_head(value.shape)
    out = jnp.zeros_like(value)
    for head in range(value.shape[1] // HEAD):
        mine = heads == head
        out = jnp.where(mine, reduce_fn(jnp.where(mine, value, neutral), axis=1, keepdims=True), out)
    return out


def kernel_two(query_marks, key_marks):
    scores = nt(query_marks, block_diag(key_marks)) * TEMPER
    scores_t = nt(key_marks, block_diag(query_marks)) * TEMPER
    expo = jnp.exp(scores - head_rows(scores, jnp.max, -jnp.inf))
    plain = expo / head_rows(expo, jnp.sum, 0.0)
    expo_t = jnp.exp(scores_t - jnp.max(scores_t, axis=0, keepdims=True))
    flipped = expo_t / jnp.sum(expo_t, axis=0, keepdims=True)
    return plain, flipped


def newton(plains, flippeds, save):
    lefts = [left_of(p) for p in plains]
    invs = [
        f / head_total(jnp.sum(f * f, axis=0, keepdims=True)) for f in flippeds
    ]
    for it in range(NS_STEPS):
        prods = [mm_parts(a, right_of(z)) for a, z in zip(lefts, invs)]
        prights = [right_of(p) for p in prods]
        squares = [mm_parts(left_of(p), r) for p, r in zip(prods, prights)]
        steps = [mm_parts(left_of(z), r) for z, r in zip(invs, prights)]
        for index in range(len(invs)):
            save(it, index, invs[index], prods[index], squares[index], steps[index])
        invs = [
            0.25 * (13.0 * z - 15.0 * s + mm(7.0 * z - s, q)) for z, s, q in zip(invs, steps, squares)
        ]
    return invs


def lens_of(len_ref):
    l0, l1, l2, l3 = len_ref[0, 0], len_ref[0, 1], len_ref[0, 2], len_ref[0, 3]
    return (l0, l1, l2, l3), (0, l0, l0 + l1, l0 + l1 + l2)


def choose(item, values):
    out = jnp.where(item == 0, values[0], values[1])
    out = jnp.where(item == 2, values[2], out)
    return jnp.where(item == 3, values[3], out)


def column_edges(col, lens, starts):
    item = col // LAND
    seg = col % LAND
    length = choose(item, lens)
    start = choose(item, starts)
    low_edge = start + ((seg * length + LAND - 1) >> 6)
    high_edge = start + (((seg + 1) * length + LAND - 1) >> 6)
    return low_edge, high_edge, start, start + length


def item_of(pos, starts):
    return (
        (pos >= starts[1]).astype(jnp.int32)
        + (pos >= starts[2]).astype(jnp.int32)
        + (pos >= starts[3]).astype(jnp.int32)
    )


def pair_lanes(hp):
    return slice(128 * hp, 128 * hp + 128)


def both_heads(value):
    first = iota(value.shape, 1) < HEAD
    zero = jnp.zeros_like(value)
    return jnp.concatenate([jnp.where(first, value, zero), jnp.where(first, zero, value)], axis=0)


def pick_heads(value):
    rows = value.shape[0] // 2
    first = iota((rows, 128), 1) < HEAD
    return jnp.where(first, value[:rows], value[rows:])


def toeplitz(tap_row, same):
    wide = jnp.broadcast_to(tap_row, (TOK, EXT))
    return split(pltpu.roll(wide, 0, 1, stride=1, stride_axis=0) * same)


def conv_pair(taps_ref, hp, same, ext_pair):
    outs = []
    for head in (2 * hp, 2 * hp + 1):
        high, low = toeplitz(taps_ref[head : head + 1, :], same)
        outs.append(nn(high, ext_pair) + nn(low, ext_pair))
    first = iota((TOK, 128), 1) < HEAD
    return jnp.where(first, outs[0], outs[1])


def same_item(first_row, lens, starts, reverse=False):
    shape = (TOK, EXT)
    row = iota(shape, 0)
    if reverse:
        row = TOK - 1 - row
    pos = first_row + row
    other = first_row + iota(shape, 1) - HALO
    total = starts[3] + lens[3]
    inside = (other >= 0) & (other < total) & (item_of(pos, starts) == item_of(other, starts))
    return inside.astype(F32)


def group_peers(me):
    for step in range(1, GRP_DEV):
        yield step, lax.rem(me + step, GRP_DEV)


def place(rep, index):
    return (rep, index // 2, lax.rem(index, 2))


def greet(rep, me):
    barrier = pltpu.get_barrier_semaphore()
    for _, other in group_peers(me):
        pl.semaphore_signal(barrier, inc=1, device_id=place(rep, other), device_id_type=MESH_ID)
    pl.semaphore_wait(barrier, GRP_DEV - 1)


def push(src, dst, send_sem, recv_sem, device):
    copy = pltpu.make_async_remote_copy(
        src_ref=src, dst_ref=dst, send_sem=send_sem, recv_sem=recv_sem,
        device_id=device, device_id_type=MESH_ID,
    )
    copy.start()
    return copy


def attend_kernel(
    len_ref, x_ref, qkv_hbm, out_hbm, up_hbm, down_hbm, norm_ref, taps_ref,
    w_ref, wu_ref, wd_ref, wn_ref, q_ref, k_ref, v_ref, qm_ref, km_ref, wm_ref, a_ref, ext_ref,
    res_ref, vloc_ref, dloc_ref, resl_ref, vl_ref, dl_ref,
    win, halo, nd_src, nd_buf, wml, bias_cp, bias_pc, num_s, den_s, probs,
    qkv_st, out_st, up_st, down_st, hot_s, same_s, cv_s, res_s, wu_st, wd_st, norm_st, taps_s,
    win_s, win_r, halo_s, halo_r, nd_s, nd_r, wml_s, wml_r, load_s, norm_s, norm_r, *gather_sem,
):
    loads = [
        pltpu.make_async_copy(src, dst, load_s.at[i])
        for i, (src, dst) in enumerate(
            ((qkv_hbm, qkv_st), (out_hbm, out_st), (up_hbm, up_st), (down_hbm, down_st))
        )
    ]
    for load in loads:
        load.start()
    spot = Spot()
    rep, me = spot.rep, spot.me
    first_row = me * TOK
    is_owner = (me >= 1) & (me <= 6)
    lens, starts = lens_of(len_ref)
    def masks_for_columns():
        shape = (COLS, TOK)
        pos = first_row + iota(shape, 1)
        lo, hi, begin, end = column_edges(iota(shape, 0), lens, starts)
        hot_s[...] = ((pos >= lo) & (pos < hi)).astype(BF)
        bias_cp[...] = jnp.where((pos >= begin) & (pos < end), 0.0, -1e30)
        pshape = (TOK, COLS)
        ppos = first_row + iota(pshape, 0)
        _, _, pbegin, pend = column_edges(iota(pshape, 1), lens, starts)
        bias_pc[...] = jnp.where((ppos >= pbegin) & (ppos < pend), 0.0, -1e30)
        same_s[...] = same_item(first_row, lens, starts)

    gather = Gather(spot, (w_ref, wu_ref, wd_ref), gather_sem)
    row = pl.multiple_of(me * SHARD, SHARD)
    spot.signal_all()
    masks_for_columns()
    loads[0].wait()
    loads[1].wait()
    w_ref[pl.ds(row, SHARD), : 3 * D] = qkv_st[...].astype(BF)
    w_ref[pl.ds(row, SHARD), 3 * D :] = out_st[...].astype(BF)
    spot.wait_all()
    gather.start(0)
    loads[2].wait()
    loads[3].wait()
    wu_st[...] = up_st[...].astype(BF)
    wd_st[...] = down_st[...].astype(BF)
    own_up = pltpu.make_async_copy(wu_st, shard_of(gather.refs, UP, me), load_s.at[5])
    own_down = pltpu.make_async_copy(wd_st, shard_of(gather.refs, DOWN, me), load_s.at[6])
    own_up.start()
    own_down.start()
    norm_st[...] = jnp.zeros_like(norm_st)
    norm_st[0:4, 0:SHARD] = norm_ref[...]
    wn_ref[me] = norm_st[...].astype(BF)
    taps_s[...] = jnp.zeros_like(taps_s)
    taps_s[0:HEADS, 0:KERNEL] = taps_ref[...]
    own_up.wait()
    own_down.wait()
    gather.hop(0, 1)
    gather.hop(0, 2)
    gather.start(UP)
    gather.hop(0, 3)
    gather.hop(UP, 1, False)
    gather.relay(0)
    gather.hop(UP, 2, False)
    gather.start(DOWN)
    gather.last(0)
    gather.hop(UP, 3, False)
    gather.spread(UP)
    gather.finish(0)

    for part, ref in enumerate((q_ref, k_ref, v_ref)):
        ref[...] = nn(x_ref[...], w_ref[:, D * part : D * part + D]).astype(BF)

    @pl.when(me < GRP_DEV - 1)
    def _():
        push(v_ref.at[pl.ds(TOK - HALO, HALO)], halo.at[0], halo_s.at[0], halo_r.at[0], place(rep, me + 1))

    @pl.when(me > 0)
    def _():
        push(v_ref.at[pl.ds(0, HALO)], halo.at[1], halo_s.at[1], halo_r.at[1], place(rep, me - 1))

    qk = jnp.concatenate([q_ref[...], k_ref[...]], axis=1)
    hot = hot_s[...]
    wshape = (16, TOK)
    seg_hi = lens_edge(iota((LAND, TOK), 0) + 1, lens[1], starts[1])
    base = jnp.sum((seg_hi <= first_row).astype(jnp.int32).astype(F32), axis=0, keepdims=True).astype(jnp.int32)
    seg_w = base + iota(wshape, 0)
    wpos = first_row + iota(wshape, 1)
    whot = (
        (wpos >= lens_edge(seg_w, lens[1], starts[1]))
        & (wpos < lens_edge(seg_w + 1, lens[1], starts[1]))
        & (seg_w < LAND)
    ).astype(BF)
    wsum = nn(whot, qk)
    seg_c = base[:, :128] + iota((16, 128), 0)
    wcount = (lens_edge(seg_c + 1, lens[1], starts[1]) - lens_edge(seg_c, lens[1], starts[1])).astype(F32)
    wcount = jnp.concatenate([wcount] * 12, axis=1)
    win[me] = (wsum / wcount).astype(BF)
    gather.hop(DOWN, 1, False)
    push(win.at[me], win.at[me], win_s.at[0], win_r.at[me], spot.to_core)
    for step in range(1, 4):
        push(win.at[me], win.at[me], win_s.at[step], win_r.at[me], spot.to_z(step))
    for step, other in group_peers(me):
        push(wn_ref.at[me], wn_ref.at[me], norm_s.at[step - 1], norm_r.at[me], place(rep, other))

    sums = nn(hot, qk)
    clo, chi, _, _ = column_edges(iota((COLS, 128), 0), lens, starts)
    counts = (chi - clo).astype(F32)
    counts6 = jnp.concatenate([counts] * 6, axis=1)
    qm_ref[...] = (sums[:, :D] / counts6).astype(BF)
    km_ref[...] = (sums[:, D:] / counts6).astype(BF)

    @pl.when(me > 0)
    def _():
        pltpu.make_async_copy(halo.at[0], halo.at[0], halo_r.at[0]).wait()
        ext_ref[0:HALO] = halo[0]

    @pl.when(me == 0)
    def _():
        ext_ref[0:HALO] = jnp.zeros((HALO, D), BF)

    @pl.when(me < GRP_DEV - 1)
    def _():
        pltpu.make_async_copy(halo.at[1], halo.at[1], halo_r.at[1]).wait()
        ext_ref[HALO + TOK : 2 * HALO + TOK] = halo[1]

    @pl.when(me == GRP_DEV - 1)
    def _():
        ext_ref[HALO + TOK : 2 * HALO + TOK] = jnp.zeros((HALO, D), BF)

    ext_ref[HALO : HALO + TOK] = v_ref[...]
    ext_ref[2 * HALO + TOK :] = jnp.zeros((EXT - TOK - 2 * HALO, D), BF)
    for hp in range(6):
        lanes = pair_lanes(hp)
        cv_s[:, lanes] = conv_pair(taps_s, hp, same_s[...], ext_ref[:, lanes])
    gather.hop(DOWN, 2, False)
    for step in range(1, 4):
        slot = spot.z(4 - step) * 2 + spot.grp
        arrive(win.at[slot], win_r.at[slot])
        push(win.at[slot], win.at[slot], win_s.at[3 + step], win_r.at[slot], spot.to_core)
    for step in range(4):
        slot = spot.z(step) * 2 + 1 - spot.grp
        arrive(win.at[slot], win_r.at[slot])
    sshape = (LAND, 128)
    lane_dev = iota((LAND, 128), 1) // 16
    lane_w = iota((LAND, 128), 1) % 16
    seg_end = lens_edge(iota((LAND, 128), 0) + 1, lens[1], starts[1])
    bases = jnp.sum((seg_end <= lane_dev * TOK).astype(jnp.int32).astype(F32), axis=0, keepdims=True).astype(jnp.int32)
    scatter = (iota(sshape, 0) == bases + lane_w).astype(BF)
    long_rows = nn(scatter, win[...].reshape(128, 2 * D))
    qm_ref[LAND : 2 * LAND, :] = long_rows[:, :D].astype(BF)
    km_ref[LAND : 2 * LAND, :] = long_rows[:, D:].astype(BF)

    ones_wide = jnp.ones((TOK, 128), BF)
    ones_row = jnp.ones((8, TOK), BF)
    for hp in range(6):
        lanes = pair_lanes(hp)
        marks = both_heads(qm_ref[:, lanes])
        scores = nt(marks, k_ref[:, lanes]) * TEMPER
        expo = jnp.exp(scores + jnp.concatenate([bias_cp[...]] * 2, axis=0)).astype(BF)
        nd = nn(expo, jnp.concatenate([v_ref[:, lanes], ones_wide], axis=1))
        num = pick_heads(nd[:, :128])
        nd_src[hp, 0:LAND, :] = num[LAND : 2 * LAND]
        nd_src[hp, LAND : LAND + 8, :] = nt(
            ones_row, jnp.concatenate([expo[LAND : 2 * LAND], expo[COLS + LAND : COLS + 2 * LAND]], axis=0)
        )
        num_s[:, lanes] = num
        den_s[:, lanes] = pick_heads(nd[:, 128:])
    for owner in range(1, 7):
        @pl.when(me == owner)
        def _():
            nd_buf[owner] = nd_src[owner - 1]

        @pl.when(me != owner)
        def _():
            push(nd_src.at[owner - 1], nd_buf.at[me], nd_s.at[owner - 1], nd_r.at[me], place(rep, owner))

    gather.hop(DOWN, 3, False)
    gather.relay(UP)
    gather.spread(DOWN)
    wm_ref[...] = jnp.zeros_like(wm_ref)
    has_local = (me == 0) | (me == GRP_DEV - 1)
    slot_rows = (pl.multiple_of(jnp.where(me == 0, 0, 2 * LAND), LAND), 3 * LAND)
    cuts = [(slot, slice(256 * part, 256 * part + 256)) for slot in range(2) for part in range(3)]

    @pl.when(has_local)
    def _():
        def at(ref, slot, lanes):
            return ref[pl.ds(slot_rows[slot], LAND), lanes]

        plains, flippeds = zip(*[kernel_two(at(qm_ref, *c), at(km_ref, *c)) for c in cuts])

        def save(it, index, *mats):
            for m, mat in enumerate(mats):
                res_s[it, index, m] = mat

        invs = newton(plains, flippeds, save)
        keep = pltpu.make_async_copy(res_s, res_ref, load_s.at[4])
        keep.start()
        for (slot, lanes), inv in zip(cuts, invs):
            den = at(den_s, slot, lanes)
            den = jnp.where(den == 0.0, 1.0, den)
            val = at(num_s, slot, lanes) / den
            vloc_ref[slot, :, lanes] = val
            dloc_ref[slot, :, lanes] = den
            wm_ref[pl.ds(slot_rows[slot], LAND), lanes] = mm(inv, val).astype(BF)

    @pl.when(is_owner)
    def _():
        lanes = pl.ds(pl.multiple_of((me - 1) * 128, 128), 128)
        plain, flipped = kernel_two(qm_ref[LAND : 2 * LAND, lanes], km_ref[LAND : 2 * LAND, lanes])

        def save(it, index, *mats):
            for m, mat in enumerate(mats):
                resl_ref[it, m] = mat

        (inv,) = newton([plain], [flipped], save)
        for step, other in group_peers(me):
            pltpu.make_async_copy(nd_buf.at[other], nd_buf.at[other], nd_r.at[other]).wait()
        total = nd_buf[0]
        for j in range(1, GRP_DEV):
            total = total + nd_buf[j]
        row = total[LAND : LAND + 1, :]
        other_row = pltpu.roll(row, HEAD, 1)
        spread = jnp.where(iota((128, 128), 0) < HEAD, row, other_row)
        den = jnp.transpose(spread)[:LAND]
        val = total[:LAND] / den
        vl_ref[...] = val
        dl_ref[...] = den
        wml[me - 1] = mm(inv, val).astype(BF)
        for step, other in group_peers(me):
            push(wml.at[me - 1], wml.at[me - 1], wml_s.at[step - 1], wml_r.at[me - 1], place(rep, other))

    for hp in range(6):
        lanes = pair_lanes(hp)
        scores = nt(q_ref[:, lanes], both_heads(km_ref[:, lanes])) * TEMPER
        for half in range(2):
            expo = jnp.exp(scores[:, COLS * half : COLS * half + COLS] + bias_pc[...])
            probs[hp, :, COLS * half : COLS * half + COLS] = (
                expo / jnp.sum(expo, axis=1, keepdims=True)
            ).astype(BF)

    gather.last(UP)
    gather.relay(DOWN)
    for owner in range(1, 7):
        @pl.when(me != owner)
        def _():
            pltpu.make_async_copy(wml.at[owner - 1], wml.at[owner - 1], wml_r.at[owner - 1]).wait()

        wm_ref[LAND : 2 * LAND, pair_lanes(owner - 1)] = wml[owner - 1]
    for hp in range(6):
        lanes = pair_lanes(hp)
        att = nn(probs[hp], both_heads(wm_ref[:, lanes]))
        a_ref[:, lanes] = (att + cv_s[:, lanes]).astype(BF)

    gather.last(DOWN)
    for step, other in group_peers(me):
        arrive(wn_ref.at[other], norm_r.at[other])
        arrive(wn_ref.at[other], norm_s.at[step - 1])
    for part in (UP, DOWN):
        gather.finish(part)
    for part in (*EARLY, UP, DOWN):
        gather.sent(part)
    @pl.when(has_local)
    def _():
        pltpu.make_async_copy(res_s, res_ref, load_s.at[4]).wait()

    for step, other in group_peers(me):
        pltpu.make_async_copy(win.at[me], win.at[me], win_s.at[step - 1]).wait()
    for owner in range(1, 7):
        @pl.when(me != owner)
        def _():
            pltpu.make_async_copy(nd_src.at[owner - 1], nd_src.at[owner - 1], nd_s.at[owner - 1]).wait()

    @pl.when(is_owner)
    def _():
        for step, other in group_peers(me):
            pltpu.make_async_copy(wml.at[0], wml.at[0], wml_s.at[step - 1]).wait()

    @pl.when(me < GRP_DEV - 1)
    def _():
        pltpu.make_async_copy(halo.at[0], halo.at[0], halo_s.at[0]).wait()

    @pl.when(me > 0)
    def _():
        pltpu.make_async_copy(halo.at[1], halo.at[1], halo_s.at[1]).wait()


def arrive(ref, sem):
    pltpu.make_async_copy(ref, ref, sem).wait()


def lens_edge(seg, length, start):
    return start + ((seg * length + LAND - 1) >> 6)


COLS = ITEMS * LAND
VM = pl.BlockSpec(memory_space=pltpu.VMEM)
SM = pl.BlockSpec(memory_space=pltpu.SMEM)


def attend(item_lengths, tokens, qkv_weight, out_weight, up_weight, down_weight, norm_params, taps):
    sds = jax.ShapeDtypeStruct
    row = sds((TOK, D), BF)
    outs = [sds((D, 4 * D), BF), sds((D, FF), BF), sds((FF, D), BF), sds((8, 16, 128), BF),
            row, row, row, row, row, row, row, sds((EXT, D), BF),
            sds((NS_STEPS, 6, 4, LAND, 256), F32), sds((2, LAND, D), F32), sds((2, LAND, D), F32),
            sds((NS_STEPS, 4, LAND, 128), F32), sds((LAND, 128), F32), sds((LAND, 128), F32)]
    dma = pltpu.SemaphoreType.DMA
    vm = pltpu.VMEM
    scratch = [
        vm((8, 16, 2 * D), BF), vm((2, HALO, D), BF), vm((6, LAND + 8, 128), F32),
        vm((8, LAND + 8, 128), F32), vm((6, LAND, 128), BF),
        vm((COLS, TOK), F32), vm((TOK, COLS), F32), vm((COLS, D), F32),
        vm((COLS, D), F32), vm((6, TOK, 2 * COLS), BF),
        vm((SHARD, 3 * D), F32), vm((SHARD, D), F32), vm((SHARD, FF), F32), vm((4 * SHARD, D), F32),
        vm((COLS, TOK), BF), vm((TOK, EXT), F32), vm((TOK, D), F32),
        vm((NS_STEPS, 6, 4, LAND, 256), F32), vm((SHARD, FF), BF), vm((4 * SHARD, D), BF),
        vm((16, 128), F32), vm((16, EXT), F32),
        dma((7,)), dma((8,)), dma((2,)), dma((2,)), dma((6,)), dma((8,)), dma((7,)), dma((6,)),
        dma((7,)), dma((7,)), dma((8,)), *gather_sems(),
    ]
    anyspace = pl.BlockSpec(memory_space=pl.ANY)
    w_all, w_up, w_down, norms, *rest = pl.pallas_call(
        attend_kernel, out_shape=outs, in_specs=[SM, VM, anyspace, anyspace, anyspace, anyspace, VM, VM],
        out_specs=[VM, anyspace, anyspace] + [VM] * 9 + [anyspace] + [VM] * 5, scratch_shapes=scratch, name="attend",
        compiler_params=pltpu.CompilerParams(collective_id=1, has_side_effects=True, vmem_limit_bytes=60 * 2**20),
    )(item_lengths, tokens, qkv_weight, out_weight, up_weight, down_weight, norm_params, taps)
    return w_all, w_up, w_down, norms, rest


def nt_parts(left, right):
    rows = left.shape[0] // 2
    both = nt(left, right[0])
    return both[:rows] + both[rows:] + nt(left[:rows], right[1])


def flip(value):
    high, low = split(value)
    eye = packed_eye(value.shape[1]).astype(BF)
    return nt(eye, block_diag(high)) + nt(eye, block_diag(low))


def half_sum(value):
    rows = value.shape[0] // 2
    return value[:rows] + value[rows:]


def newton_back(qms, kms, vals, dens, dwms, load, turn=lambda it: None):
    count = len(qms)
    plains = [kernel_two(q, k)[0] for q, k in zip(qms, kms)]
    krights = [right_of(p) for p in plains]
    ups = [nt_parts(left_of(v), right_of(d)) for v, d in zip(vals, dwms)]
    turn(NS_STEPS - 1)
    last = [load(NS_STEPS - 1, i) for i in range(count)]
    finals = [0.25 * (13.0 * m[0] - 15.0 * m[3] + mm(7.0 * m[0] - m[3], m[2])) for m in last]
    dvals = [mm(flip(z), d) for z, d in zip(finals, dwms)]
    dkts = [jnp.zeros_like(p) for p in plains]
    for it in reversed(range(NS_STEPS)):
        if it < NS_STEPS - 1:
            turn(it)
        mats = [load(it, i) for i in range(count)]
        plefts = [left_of(m[1]) for m in mats]
        dys = [0.25 * mm(m[2], u) for m, u in zip(mats, ups)]
        dqs = [0.25 * mm(u, 7.0 * m[0] - m[3]) for m, u in zip(mats, ups)]
        drs = [-3.75 * u - dy for u, dy in zip(ups, dys)]
        dqrs = [right_of(d) for d in dqs]
        dps = [
            mm(dr, m[0]) + mm_parts(pl_, dqr) + mm(dq, m[1])
            for dr, m, pl_, dqr, dq in zip(drs, mats, plefts, dqrs, dqs)
        ]
        nexts = [
            3.25 * u + 7.0 * dy + mm_parts(pl_, right_of(dr))
            for u, dy, pl_, dr in zip(ups, dys, plefts, drs)
        ]
        dkts = [a + mm(m[0], d) for a, m, d in zip(dkts, mats, dps)]
        ups = [n + mm_parts(left_of(d), kr) for n, d, kr in zip(nexts, dps, krights)]
    outs = []
    for i in range(count):
        plain = plains[i]
        fro = head_total(jnp.sum(plain * plain, axis=0, keepdims=True))
        cross = head_total(jnp.sum(ups[i] * plain, axis=0, keepdims=True))
        dk = flip(dkts[i]) + ups[i] / fro - 2.0 * plain * (cross / (fro * fro))
        dscore = plain * (dk - head_rows(plain * dk, jnp.sum, 0.0)) * TEMPER
        dqm = half_sum(nn(left_of(dscore), block_diag(kms[i])))
        dkm = half_sum(nn(left_of(flip(dscore)), block_diag(qms[i])))
        dnum = (dvals[i] / dens[i]).astype(BF)
        dden = -head_rows(dnum.astype(F32) * vals[i], jnp.sum, 0.0)
        outs.append((dnum, dden, dqm, dkm))
    return outs


def twice(value):
    return jnp.concatenate([value, value], axis=0)


ERF_NUM = (0.00022905065861350646, 0.0034082910107109506, 0.050955695062380861, 0.18520832239976145, 1.128379143519084)
ERF_DEN = (-1.1791602954361697e-7, 0.000023547966471313185, 0.0010179625278914885, 0.014070470171167667,
           0.11098505178285362, 0.49746925110067538, 1.0)


def horner(value, coefs):
    out = jnp.full_like(value, coefs[0])
    for coef in coefs[1:]:
        out = out * value + coef
    return out


def erf_of(value):
    value = jnp.clip(value, -3.832506856900711, 3.832506856900711)
    square = value * value
    return value * horner(square, ERF_NUM) / horner(square, ERF_DEN)


def norm_stats(hidden):
    centred = hidden - jnp.mean(hidden, axis=-1, keepdims=True)
    scale = lax.rsqrt(jnp.mean(centred * centred, axis=-1, keepdims=True) + EPS_NORM)
    return centred * scale, scale


def norm_back(unit, scale, gain, grad):
    inner = grad * gain
    mean_one = jnp.mean(inner, axis=-1, keepdims=True)
    mean_two = jnp.mean(inner * unit, axis=-1, keepdims=True)
    return scale * (inner - mean_one - unit * mean_two)


FPART = 512


def back_kernel(
    len_ref, wn_ref, taps_ref, vl_ref, dl_ref, wa_hbm, wu_hbm, wd_hbm, res_hbm,
    x_hbm, a_hbm, cot_hbm, q_hbm, k_hbm, v_hbm, qm_hbm, km_hbm, wm_hbm, ext_hbm, vloc_hbm, dloc_hbm, resl_hbm,
    y_ref, gx_ref, fin_ref, total_ref, norm_ref,
    x_ref, a_ref, cot_ref, q_ref, k_ref, v_ref, qm_ref, km_ref, wm_ref, ext_ref, vloc_ref, dloc_ref, resl_ref, in_s, da_ref, dh_ref,
    wo, wu, wd, act, gu, gd, gains_ref, w_s, ready,
    small_s, rc, rx, ry, r2x, r2y, rz, one, two, pair, sq, q_one, q_two, q_pair,
    halo, dext, dwm_src, dwm_buf, dk1_src, dk1_buf, dn_buf, dq3_src, dq3_buf, ds_buf,
    bias_cp, dwm_s, dkm_s, dqm_s, dnum_s, dden_s, dq_s, dk_s, dv_s, dsum_s, res_s, load_s, res_sem,
    halo_s, halo_r, dwm_ss, dwm_r, dk1_ss, dk1_r, dn_ss, dn_r, dq3_ss, dq3_r, ds_ss, ds_r,
    s1, r1, s2, r2, sp, rp, t1, u1, t2, u2, tp, up, *red_sems,
):
    spot = Spot()
    spot.signal_all()
    rep, me = spot.rep, spot.me
    first_row = me * TOK
    is_owner = (me >= 1) & (me <= 6)
    has_local = (me == 0) | (me == GRP_DEV - 1)
    lens, starts = lens_of(len_ref)
    parts = FF // FPART
    loads = [
        pltpu.make_async_copy(src, dst, in_s.at[i])
        for i, (src, dst) in enumerate((
            (x_hbm, x_ref),
            (a_hbm, a_ref),
            (cot_hbm, cot_ref),
            (q_hbm, q_ref),
            (k_hbm, k_ref),
            (v_hbm, v_ref),
            (qm_hbm, qm_ref),
            (km_hbm, km_ref),
            (wm_hbm, wm_ref),
            (ext_hbm, ext_ref),
            (vloc_hbm, vloc_ref),
            (dloc_hbm, dloc_ref),
            (resl_hbm, resl_ref),
        ))
    ]
    w_loads = [pltpu.make_async_copy(wa_hbm.at[:, pl.ds(3 * D, D)], wo, w_s.at[0])]
    for j in range(parts):
        cols = pl.ds(j * FPART, FPART)
        w_loads.append(pltpu.make_async_copy(wu_hbm.at[:, cols], wu.at[:, cols], w_s.at[1 + 2 * j]))
        w_loads.append(pltpu.make_async_copy(wd_hbm.at[cols], wd.at[cols], w_s.at[2 + 2 * j]))
    for load in (*loads[:3], *w_loads, *loads[3:]):
        load.start()
    load_w = pltpu.make_async_copy(wa_hbm.at[:, pl.ds(0, 3 * D)], wu.at[:, pl.ds(0, 3 * D)], load_s.at[1])

    def residual(it):
        return pltpu.make_async_copy(res_hbm.at[it], res_s.at[it % 2], res_sem.at[it % 2])


    def own(m, shard, quarter):
        row = pl.multiple_of(shard * SHARD, SHARD)
        if m == 0 and quarter == 3:
            return wo.at[pl.ds(row, SHARD), :]
        if m < 2:
            return gu.at[pl.ds(row, SHARD), D * quarter : D * quarter + D]
        return gd.at[pl.ds(pl.multiple_of(4 * row + SHARD * quarter, SHARD), SHARD), :]

    red = Reduce(spot, own, (rc, gd, rx, ry, r2x, r2y, rz, fin_ref), red_sems)
    small = Small(spot, small_s, one, two, pair, (s1, r1, sp, rp, s2, r2))
    squares = Small(spot, sq, q_one, q_two, q_pair, (t1, u1, tp, up, t2, u2))

    def put_slope(j, value):
        for part in range(FPART // 256):
            for row in range(TOK // LAND):
                index = (j * (FPART // 256) + part) * (TOK // LAND) + row
                res_s[index // 24, index // 4 % 6, index % 4] = value[
                    LAND * row : LAND * row + LAND, 256 * part : 256 * part + 256
                ]

    def get_slope(j):
        columns = []
        for part in range(FPART // 256):
            base = (j * (FPART // 256) + part) * (TOK // LAND)
            columns.append(jnp.concatenate(
                [res_s[n // 24, n // 4 % 6, n % 4] for n in range(base, base + TOK // LAND)], axis=0
            ))
        return jnp.concatenate(columns, axis=1)

    gains = jnp.zeros((16, D), F32)
    lane = iota((16, D), 1)
    for i in range(GRP_DEV):
        wide = jnp.concatenate([wn_ref[i].astype(F32), jnp.zeros((16, D - 128), F32)], axis=1)
        gains = jnp.where((lane >= SHARD * i) & (lane < SHARD * i + SHARD), pltpu.roll(wide, SHARD * i, 1), gains)
    gains_ref[...] = gains
    for load in loads[:3]:
        load.wait()
    w_loads[0].wait()
    hidden = x_ref[...].astype(F32) + nn(a_ref[...], wo[...])
    unit, scale = norm_stats(hidden)
    dk_s[...] = unit
    gain_one, shift_one = gains_ref[0:1, :], gains_ref[1:2, :]
    normed_low = (unit * gain_one + shift_one).astype(BF)
    dq_s[...] = jnp.zeros_like(dq_s)
    for j in range(parts):
        cols = slice(j * FPART, j * FPART + FPART)
        w_loads[1 + 2 * j].wait()
        w_loads[2 + 2 * j].wait()
        up = nn(normed_low, wu[:, cols])
        cdf = 0.5 + 0.5 * erf_of(up * (0.5**0.5))
        low = (up * cdf).astype(BF)
        act[:, cols] = low
        put_slope(j, cdf + up * jnp.exp(-0.5 * up * up) * ((2.0 * 3.141592653589793) ** -0.5))
        dq_s[...] += nn(low, wd[cols, :])
    h2 = dk_s[...] * gain_one + shift_one + dq_s[...]
    unit_two, scale_two = norm_stats(h2)
    gain_two, shift_two = gains_ref[2:3, :], gains_ref[3:4, :]
    y_ref[...] = (unit_two * gain_two + shift_two).astype(BF)
    cot = cot_ref[...].astype(F32)
    small_s[2:3, :] = jnp.sum(cot * unit_two, axis=0, keepdims=True)
    small_s[3:4, :] = jnp.sum(cot, axis=0, keepdims=True)
    dh2 = norm_back(unit_two, scale_two, gain_two, cot)
    dv_s[...] = dh2
    down_low = dh2.astype(BF)
    dq_s[...] = jnp.zeros_like(dq_s)
    for j in range(parts):
        cols = slice(j * FPART, j * FPART + FPART)
        gd[cols, :] = tn(act[:, cols], down_low).astype(BF)
    spot.wait_all()
    red.chip(2)
    for j in range(parts):
        cols = slice(j * FPART, j * FPART + FPART)
        act[:, cols] = (get_slope(j) * nt(down_low, wd[cols, :])).astype(BF)
    for j in range(parts):
        cols = slice(j * FPART, j * FPART + FPART)
        du = act[:, cols]
        dq_s[...] += nt(du, wu[:, cols])
        gu[:, cols] = tn(normed_low, du).astype(BF)
    red.chip(1)

    @pl.when(has_local)
    def _():
        residual(NS_STEPS - 1).start()

    load_w.start()
    red.plane(2)
    red.chip_sent(2)
    pl.semaphore_signal(ready, inc=1, device_id=spot.to_core, device_id_type=MESH_ID)
    dx = dv_s[...] + dq_s[...]
    unit = dk_s[...]
    small_s[0:1, :] = jnp.sum(dx * unit, axis=0, keepdims=True)
    small_s[1:2, :] = jnp.sum(dx, axis=0, keepdims=True)
    dh = norm_back(unit, scale, gain_one, dx)
    dh_ref[...] = dh
    low = dh.astype(BF)
    da_ref[...] = nt(low, wo[...]).astype(BF)

    @pl.when(me < GRP_DEV - 1)
    def _():
        push(da_ref.at[pl.ds(TOK - HALO, HALO)], halo.at[0], halo_s.at[0], halo_r.at[0], place(rep, me + 1))

    @pl.when(me > 0)
    def _():
        push(da_ref.at[pl.ds(0, HALO)], halo.at[1], halo_s.at[1], halo_r.at[1], place(rep, me - 1))

    wo[...] = tn(a_ref[...], low).astype(BF)
    pl.semaphore_wait(ready, 1)
    red.chip(0, (3,))
    shape = (COLS, TOK)
    pos = first_row + iota(shape, 1)
    _, _, begin, end = column_edges(iota(shape, 0), lens, starts)
    bias_cp[...] = jnp.where((pos >= begin) & (pos < end), 0.0, -1e30)

    def to_owner(src, buf, send, recv, hp):
        owner = hp + 1

        @pl.when(me == owner)
        def _():
            buf[owner] = src[hp]

        @pl.when(me != owner)
        def _():
            push(src.at[hp], buf.at[me], send.at[hp], recv.at[me], place(rep, owner))

    for load in loads[3:]:
        load.wait()
    for hp in range(6):
        lanes = pair_lanes(hp)
        marks = both_heads(km_ref[:, lanes])
        scores = nt(marks, q_ref[:, lanes]) * TEMPER + twice(bias_cp[...])
        expo = jnp.exp(scores)
        dprob = nt(both_heads(wm_ref[:, lanes]), da_ref[:, lanes])
        lows, dss = [], []
        for half in range(2):
            part = slice(COLS * half, COLS * half + COLS)
            prob = expo[part] / jnp.sum(expo[part], axis=0, keepdims=True)
            inner = jnp.sum(prob * dprob[part], axis=0, keepdims=True)
            lows.append(prob.astype(BF))
            dss.append((prob * (dprob[part] - inner)).astype(BF))
        dscore = jnp.concatenate(dss, axis=0)
        dwm = pick_heads(nn(jnp.concatenate(lows, axis=0), da_ref[:, lanes]))
        dkm = pick_heads(nn(dscore, q_ref[:, lanes])) * TEMPER
        dq_s[:, lanes] = tn(dscore, marks) * TEMPER
        dwm_s[:, lanes] = dwm
        dkm_s[:, lanes] = dkm
        dwm_src[hp] = dwm[LAND : 2 * LAND]
        dk1_src[hp] = dkm[LAND : 2 * LAND].astype(BF)
        to_owner(dwm_src, dwm_buf, dwm_ss, dwm_r, hp)
    for hp in range(6):
        to_owner(dk1_src, dk1_buf, dk1_ss, dk1_r, hp)

    red.plane(1)
    red.chip_sent(1)
    @pl.when(me > 0)
    def _():
        arrive(halo.at[0], halo_r.at[0])
        dext[0:HALO] = halo[0]

    @pl.when(me == 0)
    def _():
        dext[0:HALO] = jnp.zeros((HALO, D), BF)

    @pl.when(me < GRP_DEV - 1)
    def _():
        arrive(halo.at[1], halo_r.at[1])
        dext[HALO + TOK : 2 * HALO + TOK] = halo[1]

    @pl.when(me == GRP_DEV - 1)
    def _():
        dext[HALO + TOK : 2 * HALO + TOK] = jnp.zeros((HALO, D), BF)

    dext[HALO : HALO + TOK] = da_ref[...]
    dext[2 * HALO + TOK :] = jnp.zeros((EXT - TOK - 2 * HALO, D), BF)
    same = same_item(first_row, lens, starts)
    for hp in range(6):
        lanes = pair_lanes(hp)
        dv_s[:, lanes] = conv_pair(taps_ref, hp, same, dext[:, lanes])
    dnum_s[...] = jnp.zeros_like(dnum_s)
    dden_s[...] = jnp.zeros_like(dden_s)
    dqm_s[...] = jnp.zeros_like(dqm_s)
    slot_rows = (pl.multiple_of(jnp.where(me == 0, 0, 2 * LAND), LAND), 3 * LAND)
    cuts = [(slot, slice(256 * part, 256 * part + 256)) for slot in range(2) for part in range(3)]

    @pl.when(has_local)
    def _():
        def at(ref, slot, lanes):
            return ref[pl.ds(slot_rows[slot], LAND), lanes]

        def turn(it):
            residual(it).wait()
            if it > 0:
                residual(it - 1).start()

        outs = newton_back(
            [at(qm_ref, *c) for c in cuts], [at(km_ref, *c) for c in cuts],
            [vloc_ref[slot, :, c] for slot, c in cuts], [dloc_ref[slot, :, c] for slot, c in cuts],
            [at(dwm_s, *c) for c in cuts],
            lambda it, i: [res_s[it % 2, i, m] for m in range(4)],
            turn,
        )
        for (slot, c), (dnum, dden, dqm, dkm) in zip(cuts, outs):
            rows = pl.ds(slot_rows[slot], LAND)
            dnum_s[rows, c] = dnum
            dden_s[rows, c] = dden
            dqm_s[rows, c] = dqm
            dkm_s[rows, c] = dkm_s[rows, c] + dkm

    @pl.when(is_owner)
    def _():
        lanes = pl.ds(pl.multiple_of((me - 1) * 128, 128), 128)
        for step, other in group_peers(me):
            arrive(dwm_buf.at[other], dwm_r.at[other])
        total = dwm_buf[0]
        for j in range(1, GRP_DEV):
            total = total + dwm_buf[j]
        ((dnum, dden, dqm, dkm),) = newton_back(
            [qm_ref[LAND : 2 * LAND, lanes]], [km_ref[LAND : 2 * LAND, lanes]],
            [vl_ref[...]], [dl_ref[...]], [total],
            lambda it, i: [resl_ref[it, m] for m in range(4)],
        )
        high, low = split(dden)
        dn_buf[me - 1, 0:LAND] = dnum
        dn_buf[me - 1, LAND : 2 * LAND] = jnp.where(iota((LAND, 128), 1) % HEAD < 32, high, low)
        for step, other in group_peers(me):
            push(dn_buf.at[me - 1], dn_buf.at[me - 1], dn_ss.at[step - 1], dn_r.at[me - 1], place(rep, other))
        dqm_s[LAND : 2 * LAND, 0:128] = dqm
        dqm_s[LAND : 2 * LAND, 128:256] = dkm

    same_back = same_item(first_row, lens, starts, reverse=True)
    turn = (iota((TOK, TOK), 0) + iota((TOK, TOK), 1) == TOK - 1).astype(BF)
    turned = nn(turn, da_ref[...]).astype(BF)
    for hp in range(6):
        lanes = pair_lanes(hp)
        pairs = nt(both_heads(turned[:, lanes]), ext_ref[:, lanes])
        for half in range(2):
            band = pltpu.roll(pairs[TOK * half : TOK * half + TOK] * same_back, 0, 1, stride=1, stride_axis=0)
            small_s[4 + 2 * hp + half : 5 + 2 * hp + half, :EXT] = jnp.sum(band, axis=0, keepdims=True)
    small_s[4:, EXT:] = jnp.zeros((HEADS, D - EXT), F32)
    small.start()
    red.plane_two(2)

    for owner in range(1, 7):
        lanes = pair_lanes(owner - 1)

        @pl.when(me != owner)
        def _():
            arrive(dn_buf.at[owner - 1], dn_r.at[owner - 1])

        dnum_s[LAND : 2 * LAND, lanes] = dn_buf[owner - 1, 0:LAND]
        packed = dn_buf[owner - 1, LAND : 2 * LAND].astype(F32)
        one = packed[:, 0:1] + packed[:, 32:33]
        two = packed[:, 64:65] + packed[:, 96:97]
        dden_s[LAND : 2 * LAND, lanes] = jnp.where(iota((LAND, 128), 1) < HEAD, one, two)
    for hp in range(6):
        lanes = pair_lanes(hp)
        marks = both_heads(qm_ref[:, lanes])
        expo = jnp.exp(nt(marks, k_ref[:, lanes]) * TEMPER + twice(bias_cp[...]))
        dnum = both_heads(dnum_s[:, lanes])
        dden = jnp.concatenate([dden_s[:, 128 * hp : 128 * hp + 1], dden_s[:, 128 * hp + 64 : 128 * hp + 65]], axis=0)
        dscore = (expo * (nt(dnum, v_ref[:, lanes]) + dden)).astype(BF)
        dqm = pick_heads(nn(dscore, k_ref[:, lanes])) * TEMPER
        dk_s[:, lanes] = tn(dscore, marks) * TEMPER
        dv_s[:, lanes] += tn(expo.astype(BF), dnum)
        dq3_src[hp] = dqm[LAND : 2 * LAND].astype(BF)
        to_owner(dq3_src, dq3_buf, dq3_ss, dq3_r, hp)

        @pl.when(jnp.logical_not(is_owner))
        def _():
            dqm_s[:, lanes] += dqm

    value_cols = slice(2 * D, 3 * D)
    act[:, value_cols] = dv_s[...].astype(BF)
    gu[:, value_cols] = tn(x_ref[...], act[:, value_cols]).astype(BF)
    red.chip(0, (2,))
    red.plane_two(1)
    red.plane(0, (3,))
    clo, chi, _, _ = column_edges(iota((COLS, 128), 0), lens, starts)
    counts = (chi - clo).astype(F32)

    @pl.when(is_owner)
    def _():
        lanes = pl.ds(pl.multiple_of((me - 1) * 128, 128), 128)
        for step, other in group_peers(me):
            arrive(dk1_buf.at[other], dk1_r.at[other])
            arrive(dq3_buf.at[other], dq3_r.at[other])
        total_q = dqm_s[LAND : 2 * LAND, 0:128]
        total_k = dqm_s[LAND : 2 * LAND, 128:256]
        for j in range(GRP_DEV):
            total_q = total_q + dq3_buf[j].astype(F32)
            total_k = total_k + dk1_buf[j].astype(F32)
        ds_buf[me - 1, 0] = (total_q / counts[LAND : 2 * LAND]).astype(BF)
        ds_buf[me - 1, 1] = (total_k / counts[LAND : 2 * LAND]).astype(BF)
        for step, other in group_peers(me):
            push(ds_buf.at[me - 1], ds_buf.at[me - 1], ds_ss.at[step - 1], ds_r.at[me - 1], place(rep, other))

    red.plane(0, (2,))
    for hp in range(6):
        lanes = pair_lanes(hp)
        dsum_s[:, lanes] = (dqm_s[:, lanes] / counts).astype(BF)
        dsum_s[:, D + 128 * hp : D + 128 * hp + 128] = (dkm_s[:, lanes] / counts).astype(BF)
    for owner in range(1, 7):
        @pl.when(me != owner)
        def _():
            arrive(ds_buf.at[owner - 1], ds_r.at[owner - 1])

        hp = owner - 1
        dsum_s[LAND : 2 * LAND, pair_lanes(hp)] = ds_buf[owner - 1, 0]
        dsum_s[LAND : 2 * LAND, D + 128 * hp : D + 128 * hp + 128] = ds_buf[owner - 1, 1]
    pshape = (TOK, COLS)
    ppos = first_row + iota(pshape, 0)
    plo, phi, _, _ = column_edges(iota(pshape, 1), lens, starts)
    hot = ((ppos >= plo) & (ppos < phi)).astype(BF)
    act[:, :D] = (dq_s[...] + nn(hot, dsum_s[:, :D])).astype(BF)
    act[:, D : 2 * D] = (dk_s[...] + nn(hot, dsum_s[:, D:])).astype(BF)
    for part in range(2):
        cols = slice(D * part, D * part + D)
        gu[:, cols] = tn(x_ref[...], act[:, cols]).astype(BF)
        red.chip(0, (part,))
    red.line(2)
    red.line(1)
    red.plane(0, (0, 1))
    load_w.wait()
    gx_ref[...] = (dh_ref[...] + nt(act[:, : 3 * D], wu[:, : 3 * D])).astype(BF)
    red.line_two(2)
    small.middle()
    red.line_two(1)
    red.plane_two(0)
    square = red.total(2)
    red.share(2)
    red.line(0)
    square = square + red.total(1)
    red.share(1)
    small.across()
    red.share_on(2)
    red.line_two(0)
    red.share_on(1)
    total = small.end()
    mine = pltpu.roll(total, lax.rem(D - me * SHARD, D), 1)
    taps_sum = pltpu.roll(total, D - (TOK - 1), 1)
    total_ref[:, :128] = mine[:, :128]
    total_ref[:, 128:] = taps_sum[:, :128]
    lane = iota((16, D), 1)
    real = (iota((16, D), 0) < 4) | ((lane >= TOK - 1) & (lane < TOK - 1 + KERNEL))
    extra = jnp.sum(jnp.where(real, total * total, 0.0), keepdims=True)
    sq[...] = square + red.total(0)
    squares.start()
    red.share(0)
    squares.middle()
    squares.across()
    all_squares = jnp.sum(squares.end(), keepdims=True) + extra
    norm_ref[...] = jnp.broadcast_to(jnp.sqrt(all_squares), (8, 128))
    for m in (2, 1, 0):
        red.done(m)
    red.chip_sent(0)
    for m in range(3):
        red.sent(m)
    for hp in range(6):
        @pl.when(me != hp + 1)
        def _():
            arrive(dwm_src.at[hp], dwm_ss.at[hp])
            arrive(dk1_src.at[hp], dk1_ss.at[hp])
            arrive(dq3_src.at[hp], dq3_ss.at[hp])

    @pl.when(is_owner)
    def _():
        for step, other in group_peers(me):
            arrive(dn_buf.at[0], dn_ss.at[step - 1])
            arrive(ds_buf.at[0], ds_ss.at[step - 1])

    @pl.when(me < GRP_DEV - 1)
    def _():
        arrive(halo.at[0], halo_s.at[0])

    @pl.when(me > 0)
    def _():
        arrive(halo.at[1], halo_s.at[1])


def backward(item_lengths, tokens, cotangent, norms, w_all, w_up, w_down, taps_back, branch, kept):
    sds = jax.ShapeDtypeStruct
    queries, key_rows, value_rows, mean_q, mean_k, mixed, ext, res, vloc, dloc, resl, vl, dl = kept
    outs = [sds((TOK, D), BF), sds((TOK, D), BF), sds((3, 4, *BLK), BF), sds((16, 256), F32), sds((8, 128), F32)]
    dma = pltpu.SemaphoreType.DMA
    vm = pltpu.VMEM
    moved = (tokens, branch, cotangent, queries, key_rows, value_rows, mean_q, mean_k, mixed, ext, vloc, dloc, resl)
    parts = FF // FPART
    scratch = [
        *[vm(a.shape, a.dtype) for a in moved], dma((len(moved),)), vm((TOK, D), BF), vm((TOK, D), F32),
        vm((D, D), BF), vm((D, FF), BF), vm((FF, D), BF), vm((TOK, FF), BF), vm((D, FF), BF), vm((FF, D), BF),
        vm((16, D), F32), dma((1 + 2 * parts,)), pltpu.SemaphoreType.REGULAR,
        vm((16, D), F32), *reduce_bufs(),
        vm((4, 16, D), F32), vm((4, 16, D), F32), vm((2, 16, D), F32), vm((8, 128), F32),
        vm((4, 8, 128), F32), vm((4, 8, 128), F32), vm((2, 8, 128), F32),
        vm((2, HALO, D), BF), vm((EXT, D), BF), vm((6, LAND, 128), F32), vm((8, LAND, 128), F32),
        vm((6, LAND, 128), BF), vm((8, LAND, 128), BF), vm((6, 2 * LAND, 128), BF),
        vm((6, LAND, 128), BF), vm((8, LAND, 128), BF), vm((6, 2, LAND, 128), BF),
        vm((COLS, TOK), F32), vm((COLS, D), F32), vm((COLS, D), F32), vm((COLS, D), F32),
        vm((COLS, D), BF), vm((COLS, D), F32), vm((TOK, D), F32), vm((TOK, D), F32), vm((TOK, D), F32),
        vm((COLS, 2 * D), BF), vm((2, 6, 4, LAND, 256), F32), dma((2,)), dma((2,)),
        dma((2,)), dma((2,)), dma((6,)), dma((8,)), dma((6,)), dma((8,)), dma((7,)), dma((6,)),
        dma((6,)), dma((8,)), dma((7,)), dma((6,)),
        *[dma((n,)) for n in (3, 4, 3, 4, 1, 1, 3, 4, 3, 4, 1, 1)],
        *reduce_sems(),
    ]
    anyspace = pl.BlockSpec(memory_space=pl.ANY)
    return pl.pallas_call(
        back_kernel, out_shape=outs, in_specs=[SM] + [VM] * 4 + [anyspace] * (4 + len(moved)),
        out_specs=[VM] * len(outs), scratch_shapes=scratch, name="backward",
        compiler_params=pltpu.CompilerParams(collective_id=2, has_side_effects=True, vmem_limit_bytes=VMEM_MOST),
    )(item_lengths, norms, taps_back, vl, dl, w_all, w_up, w_down, res, *moved)


VMEM_MOST = 63 * 2**20


ASTEPS = 6
AROWS = SHARD // ASTEPS


def adam_math(weight, one, two, grad, clip, rate, decay):
    grad = grad * clip
    one = BETA_ONE * one + (1.0 - BETA_ONE) * grad
    two = BETA_TWO * two + (1.0 - BETA_TWO) * grad * grad
    first_hat = one * (1.0 / (1.0 - BETA_ONE**STEP))
    second_hat = two * (1.0 / (1.0 - BETA_TWO**STEP))
    return weight - rate * (first_hat / (jnp.sqrt(second_hat) + ADAM_EPS) + decay * weight), one, two


def adam_kernel(norm_ref, total_ref, fin_ref, down_g_ref, *refs):
    ins, outs = refs[:18], refs[18:]
    clip = MAX_NORM / jnp.maximum(norm_ref[0, 0], MAX_NORM)

    def update(group, rows_cols, grad, rate, decay):
        got = [ref[rows_cols] for ref in ins[3 * group : 3 * group + 3]]
        for ref, value in zip(outs[3 * group : 3 * group + 3], adam_math(*got, grad, clip, rate, decay)):
            ref[rows_cols] = value

    for quarter in range(3):
        at = (slice(None), slice(D * quarter, D * quarter + D))
        update(0, at, fin_ref[0, quarter].astype(F32), RATE_MATRIX, DECAY_RATE)
    update(1, (slice(None), slice(None)), fin_ref[0, 3].astype(F32), RATE_MATRIX, DECAY_RATE)
    for quarter in range(4):
        at = (slice(None), slice(D * quarter, D * quarter + D))
        update(2, at, fin_ref[1, quarter].astype(F32), RATE_MATRIX, DECAY_RATE)
    update(3, (slice(None), slice(None)), down_g_ref[...].astype(F32), RATE_MATRIX, DECAY_RATE)
    whole = (slice(None), slice(None))
    update(4, whole, total_ref[0:4, 0:SHARD], RATE_NORM, 0.0)
    update(5, whole, total_ref[4:16, 128 : 128 + KERNEL], RATE_CONV, 0.0)


def adam(norm, total, fin, triples):
    sds = jax.ShapeDtypeStruct
    flat = [a for triple in triples for a in triple]
    row = lambda cols, rows=AROWS: pl.BlockSpec((rows, cols), lambda i: (i, 0))
    keep = lambda shape: pl.BlockSpec(shape, lambda i: (0, 0))
    specs = [row(3 * D)] * 3 + [row(D)] * 3 + [row(FF)] * 3 + [row(D, 4 * AROWS)] * 3
    specs += [keep((4, SHARD))] * 3 + [keep((HEADS, KERNEL))] * 3
    return pl.pallas_call(
        adam_kernel, name="adam", grid=(ASTEPS,),
        out_shape=[sds(a.shape, F32) for a in flat],
        in_specs=[pl.BlockSpec(memory_space=pltpu.SMEM), keep((16, 2 * 128)),
                  pl.BlockSpec((2, 4, AROWS, D), lambda i: (0, 0, i, 0)),
                  pl.BlockSpec((4 * AROWS, D), lambda i: (i + 2 * ASTEPS, 0)), *specs],
        out_specs=specs,
        compiler_params=pltpu.CompilerParams(vmem_limit_bytes=62 * 2**20),
    )(norm, total, fin, fin.reshape(12 * SHARD, D), *flat)


def on_device_fast(
    tokens, cotangent, item_lengths,
    qkv_weight, qkv_first, qkv_second, out_weight, out_first, out_second,
    up_weight, up_first, up_second, down_weight, down_first, down_second,
    norm_params, norm_first, norm_second, conv_kernel, conv_first, conv_second,
):
    taps_back = jnp.pad(conv_kernel[:, ::-1], ((0, 4), (0, EXT - KERNEL)))
    w_all, w_up, w_down, norms, rest = attend(
        item_lengths, tokens, qkv_weight, out_weight, up_weight, down_weight, norm_params, conv_kernel
    )
    queries, key_rows, value_rows, mean_q, mean_k, mixed, branch, value_ext, *resid = rest
    result, input_grad, fin, total, norm = backward(
        item_lengths, tokens, cotangent, norms, w_all, w_up, w_down, taps_back, branch,
        (queries, key_rows, value_rows, mean_q, mean_k, mixed, value_ext, *resid),
    )
    news = adam(
        norm, total, fin,
        (
            (qkv_weight, qkv_first, qkv_second), (out_weight, out_first, out_second),
            (up_weight, up_first, up_second), (down_weight, down_first, down_second),
            (norm_params, norm_first, norm_second), (conv_kernel, conv_first, conv_second),
        ),
    )
    return (result, input_grad, norm[0, 0], *news)


def solution(mesh):
    in_specs = (
        P(("rep", "seq", "grp"), None),
        P(("rep", "seq", "grp"), None),
        P("rep", None),
        P(("seq", "grp"), None),
        P(("seq", "grp"), None),
        P(("seq", "grp"), None),
        P(("seq", "grp"), None),
        P(("seq", "grp"), None),
        P(("seq", "grp"), None),
        P(("seq", "grp"), None),
        P(("seq", "grp"), None),
        P(("seq", "grp"), None),
        P(("seq", "grp"), None),
        P(("seq", "grp"), None),
        P(("seq", "grp"), None),
        P(None, ("seq", "grp")),
        P(None, ("seq", "grp")),
        P(None, ("seq", "grp")),
        P(),
        P(),
        P(),
    )
    out_specs = (
        P(("rep", "seq", "grp"), None),
        P(("rep", "seq", "grp"), None),
        P(),
        P(("seq", "grp"), None),
        P(("seq", "grp"), None),
        P(("seq", "grp"), None),
        P(("seq", "grp"), None),
        P(("seq", "grp"), None),
        P(("seq", "grp"), None),
        P(("seq", "grp"), None),
        P(("seq", "grp"), None),
        P(("seq", "grp"), None),
        P(("seq", "grp"), None),
        P(("seq", "grp"), None),
        P(("seq", "grp"), None),
        P(None, ("seq", "grp")),
        P(None, ("seq", "grp")),
        P(None, ("seq", "grp")),
        P(),
        P(),
        P(),
    )
    fast = dict(mesh.shape) == {"rep": 4, "seq": 4, "grp": 2}
    body = on_device_fast if fast else on_device
    return jax.shard_map(
        body, mesh=mesh, in_specs=in_specs, out_specs=out_specs, check_vma=False
    )
```

```python
import jax
import jax.numpy as jnp
from jax import lax
from jax.experimental import pallas as pl
from jax.experimental.pallas import tpu as pltpu
from jax.sharding import PartitionSpec as P

D = 768
FF = 3072
HEADS = 12
HEAD = 64
LAND = 64
KERNEL = 33
HALO = 16
NS_STEPS = 6
ITEMS = 4
STEP = 10
TOK_DEV = 256
GRP_DEV = 8
HIGHEST_PREC = lax.Precision.HIGHEST
EPS_NORM = 1e-05
BETA_ONE = 0.9
BETA_TWO = 0.999
ADAM_EPS = 1e-08
RATE_MATRIX = 0.02
RATE_NORM = 0.3
RATE_CONV = 0.1
DECAY_RATE = 0.01
MAX_NORM = 1.0


def extended(cells, sides, width):
    for axis, dim in sides:
        count = lax.axis_size(axis)
        ends = count - 1
        head = lax.slice_in_dim(cells, 0, width, axis=dim)
        tail = lax.slice_in_dim(cells, cells.shape[dim] - width, cells.shape[dim], axis=dim)
        cells = jnp.concatenate(
            [
                lax.ppermute(tail, axis, [(i, (i + 1) % count) for i in range(ends)]),
                cells,
                lax.ppermute(head, axis, [((i + 1) % count, i) for i in range(ends)]),
            ],
            axis=dim,
        )
    return cells


def locate(positions, lengths):
    ends = jnp.cumsum(lengths)
    starts = ends - lengths
    inside = (positions[:, None] >= starts[None, :]) & (positions[:, None] < ends[None, :])
    item_ids = jnp.sum((positions[:, None] >= ends[None, :]).astype(jnp.int32), axis=1)
    valid = (positions >= 0) & (positions < ends[-1])
    item_ids = jnp.where(valid, item_ids, -1)
    own_len = jnp.sum(jnp.where(inside, lengths[None, :], 0), axis=1)
    own_start = jnp.sum(jnp.where(inside, starts[None, :], 0), axis=1)
    segment = (positions - own_start) * LAND // jnp.maximum(own_len, 1)
    columns = jnp.where(valid, item_ids * LAND + segment, -1)
    return (item_ids, columns)


def landmark_counts(lengths):
    marks = jnp.arange(LAND + 1, dtype=jnp.int32)
    edges = (marks[None, :] * lengths[:, None] + LAND - 1) // LAND
    return (edges[:, 1:] - edges[:, :-1]).reshape(-1)


def layer_norm(hidden, gain_row, shift_row):
    row_mean = jnp.mean(hidden, axis=-1, keepdims=True)
    centred = hidden - row_mean
    variance = jnp.mean(centred * centred, axis=-1, keepdims=True)
    return centred * lax.rsqrt(variance + EPS_NORM) * gain_row + shift_row


def gelu_exact(values):
    return jax.nn.gelu(values, approximate=False)


def mixing_rest(mark_scores, num_all, den_all):
    key_values = (
        num_all.reshape(ITEMS, LAND, HEADS, HEAD) / den_all.reshape(ITEMS, LAND, HEADS)[..., None]
    )
    kernel_two = jax.nn.softmax(mark_scores, axis=-1)
    frobenius = jnp.sum(kernel_two * kernel_two, axis=(2, 3), keepdims=True)
    inverse = jnp.swapaxes(kernel_two, 2, 3) / frobenius
    identity = jnp.eye(LAND, dtype=kernel_two.dtype)
    for iteration in range(NS_STEPS):
        product = jnp.einsum("ahjk,ahkl->ahjl", kernel_two, inverse, precision=HIGHEST_PREC)
        inner = 7.0 * identity - product
        inner = 15.0 * identity - jnp.einsum(
            "ahjk,ahkl->ahjl", product, inner, precision=HIGHEST_PREC
        )
        inner = 13.0 * identity - jnp.einsum(
            "ahjk,ahkl->ahjl", product, inner, precision=HIGHEST_PREC
        )
        inverse = 0.25 * jnp.einsum("ahjk,ahkl->ahjl", inverse, inner, precision=HIGHEST_PREC)
    mixed_rows = jnp.einsum("ahjk,akhd->ajhd", inverse, key_values, precision=HIGHEST_PREC)
    return mixed_rows.reshape(ITEMS * LAND, HEADS * HEAD)


def adamw(weight, moment_one, moment_two, gradient, clip_factor, rate_value, decay_value):
    clipped = gradient * clip_factor
    moment_one = BETA_ONE * moment_one + (1.0 - BETA_ONE) * clipped
    moment_two = BETA_TWO * moment_two + (1.0 - BETA_TWO) * clipped * clipped
    first_hat = moment_one / (1.0 - BETA_ONE**STEP)
    second_hat = moment_two / (1.0 - BETA_TWO**STEP)
    weight = weight - rate_value * (
        first_hat / (jnp.sqrt(second_hat) + ADAM_EPS) + decay_value * weight
    )
    return (weight, moment_one, moment_two)


def contract_rows(left, right):
    return lax.dot_general(
        left, right, (((0,), (0,)), ((), ())), preferred_element_type=jnp.float32
    )


def contract_cols(left, right):
    return lax.dot_general(
        left, right, (((1,), (1,)), ((), ())), preferred_element_type=jnp.float32
    )


def on_device(
    tokens,
    cotangent,
    item_lengths,
    qkv_weight,
    qkv_first,
    qkv_second,
    out_weight,
    out_first,
    out_second,
    up_weight,
    up_first,
    up_second,
    down_weight,
    down_first,
    down_second,
    norm_params,
    norm_first,
    norm_second,
    conv_kernel,
    conv_first,
    conv_second,
):
    temper = HEAD ** (-0.5)
    col_total = ITEMS * LAND
    w_qkv, w_out, w_up, w_down, gains_low = (
        lax.all_gather(qkv_weight.astype(jnp.bfloat16), ("seq", "grp"), axis=0, tiled=True),
        lax.all_gather(out_weight.astype(jnp.bfloat16), ("seq", "grp"), axis=0, tiled=True),
        lax.all_gather(up_weight.astype(jnp.bfloat16), ("seq", "grp"), axis=0, tiled=True),
        lax.all_gather(down_weight.astype(jnp.bfloat16), ("seq", "grp"), axis=0, tiled=True),
        lax.all_gather(norm_params.astype(jnp.bfloat16), ("seq", "grp"), axis=1, tiled=True),
    )
    gains_all = gains_low.astype(jnp.float32)
    lengths = item_lengths[0]
    first_row = lax.axis_index(("seq", "grp")) * TOK_DEV
    positions = first_row - HALO + jnp.arange(TOK_DEV + 2 * HALO, dtype=jnp.int32)
    item_ext, column_ext = locate(positions, lengths)
    item_mid = item_ext[HALO : HALO + TOK_DEV]
    column_mid = column_ext[HALO : HALO + TOK_DEV]
    col_ids = jnp.arange(col_total, dtype=jnp.int32)
    col_hot = (column_mid[:, None] == col_ids[None, :]).astype(jnp.bfloat16)
    member = (item_mid[:, None] == (col_ids // LAND)[None, :]).astype(jnp.float32)
    counts_f = landmark_counts(lengths).astype(jnp.float32)
    projected = jnp.dot(tokens, w_qkv, preferred_element_type=jnp.float32)
    proj_low = projected.astype(jnp.bfloat16)
    queries = proj_low[:, :D]
    key_rows = proj_low[:, D : 2 * D]
    value_rows = proj_low[:, 2 * D :]
    land_sums = lax.psum(contract_rows(col_hot, proj_low[:, : 2 * D]), ("seq", "grp"))
    mean_q = (land_sums[:, :D] / counts_f[:, None]).astype(jnp.bfloat16)
    mean_k = (land_sums[:, D:] / counts_f[:, None]).astype(jnp.bfloat16)
    query_heads = queries.reshape(TOK_DEV, HEADS, HEAD)
    key_heads = key_rows.reshape(TOK_DEV, HEADS, HEAD)
    value_heads = value_rows.reshape(TOK_DEV, HEADS, HEAD)
    mean_q3 = mean_q.reshape(col_total, HEADS, HEAD)
    mean_k3 = mean_k.reshape(col_total, HEADS, HEAD)
    scores_key = (
        jnp.einsum("chd,phd->chp", mean_q3, key_heads, preferred_element_type=jnp.float32) * temper
    )
    expo_key = jnp.exp(scores_key) * jnp.transpose(member)[:, None, :]
    expo_low = expo_key.astype(jnp.bfloat16)
    num_part = jnp.einsum(
        "chp,phd->chd", expo_low, value_heads, preferred_element_type=jnp.float32
    ).reshape(col_total, D)
    num_all, den_all = lax.psum((num_part, jnp.sum(expo_key, axis=2)), ("seq", "grp"))
    query_marks4 = mean_q.reshape(ITEMS, LAND, HEADS, HEAD)
    key_marks4 = mean_k.reshape(ITEMS, LAND, HEADS, HEAD)
    mark_scores = (
        jnp.einsum("ajhd,akhd->ahjk", query_marks4, key_marks4, preferred_element_type=jnp.float32)
        * temper
    )
    mixed_rows, mix_pull = jax.vjp(mixing_rest, mark_scores, num_all, den_all)
    mixed3 = mixed_rows.astype(jnp.bfloat16).reshape(col_total, HEADS, HEAD)
    scores_tok = (
        jnp.einsum("phd,chd->phc", query_heads, mean_k3, preferred_element_type=jnp.float32)
        * temper
    )
    expo_tok = jnp.exp(scores_tok) * member[:, None, :]
    attn_probs = expo_tok / jnp.sum(expo_tok, axis=2, keepdims=True)
    probs_low = attn_probs.astype(jnp.bfloat16)
    attended = jnp.einsum(
        "phc,chd->phd", probs_low, mixed3, preferred_element_type=jnp.float32
    ).reshape(TOK_DEV, D)
    value_ext = extended(value_rows, ((("seq", "grp"), 0),), HALO)
    channel_taps = jnp.repeat(conv_kernel, HEAD, axis=0)
    same_masks = [
        (item_ext[offset : offset + TOK_DEV] == item_mid).astype(jnp.float32)
        for offset in range(KERNEL)
    ]
    conv_out = jnp.zeros((TOK_DEV, D), jnp.float32)
    for offset in range(KERNEL):
        conv_out = conv_out + value_ext[offset : offset + TOK_DEV] * (
            channel_taps[:, offset][None, :] * same_masks[offset][:, None]
        )
    branch = (attended + conv_out).astype(jnp.bfloat16)
    attn_out = jnp.dot(branch, w_out, preferred_element_type=jnp.float32)
    normed_one, norm_one_pull = jax.vjp(
        layer_norm, tokens.astype(jnp.float32) + attn_out, gains_all[0], gains_all[1]
    )
    normed_low = normed_one.astype(jnp.bfloat16)
    up_out = jnp.dot(normed_low, w_up, preferred_element_type=jnp.float32)
    activated, gelu_pull = jax.vjp(gelu_exact, up_out)
    act_low = activated.astype(jnp.bfloat16)
    down_out = jnp.dot(act_low, w_down, preferred_element_type=jnp.float32)
    result, norm_two_pull = jax.vjp(layer_norm, normed_one + down_out, gains_all[2], gains_all[3])
    d_hidden_two, d_gain_two, d_shift_two = norm_two_pull(cotangent.astype(jnp.float32))
    d_down_low = d_hidden_two.astype(jnp.bfloat16)
    grad_down = contract_rows(act_low, d_down_low)
    (d_up,) = gelu_pull(contract_cols(d_down_low, w_down))
    d_up_low = d_up.astype(jnp.bfloat16)
    grad_up = contract_rows(normed_low, d_up_low)
    d_normed = d_hidden_two + contract_cols(d_up_low, w_up)
    d_hidden_one, d_gain_one, d_shift_one = norm_one_pull(d_normed)
    d_attn_low = d_hidden_one.astype(jnp.bfloat16)
    grad_out = contract_rows(branch, d_attn_low)
    d_branch_low = contract_cols(d_attn_low, w_out).astype(jnp.bfloat16)
    d_branch_f = d_branch_low.astype(jnp.float32)
    d_branch_ext = extended(d_branch_low, ((("seq", "grp"), 0),), HALO)
    d_values_conv = jnp.zeros((TOK_DEV, D), jnp.float32)
    tap_grads = []
    for offset in range(KERNEL):
        d_values_conv = d_values_conv + d_branch_ext[offset : offset + TOK_DEV] * (
            channel_taps[:, KERNEL - 1 - offset][None, :] * same_masks[offset][:, None]
        )
        tap_grads.append(
            jnp.sum(
                d_branch_f * value_ext[offset : offset + TOK_DEV] * same_masks[offset][:, None],
                axis=0,
            )
        )
    grad_conv = jnp.sum(jnp.stack(tap_grads, axis=1).reshape(HEADS, HEAD, KERNEL), axis=1)
    d_attended = d_branch_low.reshape(TOK_DEV, HEADS, HEAD)
    d_mixed_part = jnp.einsum(
        "phc,phd->chd", probs_low, d_attended, preferred_element_type=jnp.float32
    ).reshape(col_total, D)
    d_probs = jnp.einsum("phd,chd->phc", d_attended, mixed3, preferred_element_type=jnp.float32)
    d_scores_tok = (
        attn_probs * (d_probs - jnp.sum(attn_probs * d_probs, axis=2, keepdims=True))
    ).astype(jnp.bfloat16)
    d_query_tok = (
        jnp.einsum("phc,chd->phd", d_scores_tok, mean_k3, preferred_element_type=jnp.float32)
        * temper
    )
    d_meank_part = (
        jnp.einsum(
            "phc,phd->chd", d_scores_tok, query_heads, preferred_element_type=jnp.float32
        ).reshape(col_total, D)
        * temper
    )
    d_mixed, d_meank_tok = lax.psum((d_mixed_part, d_meank_part), ("seq", "grp"))
    d_mark_scores, d_num, d_den = mix_pull(d_mixed)
    d_mark_scaled = d_mark_scores * temper
    d_mean_q_mix = jnp.einsum(
        "ahjk,akhd->ajhd", d_mark_scaled, key_marks4.astype(jnp.float32), precision=HIGHEST_PREC
    ).reshape(col_total, D)
    d_mean_k_mix = jnp.einsum(
        "ahjk,ajhd->akhd", d_mark_scaled, query_marks4.astype(jnp.float32), precision=HIGHEST_PREC
    ).reshape(col_total, D)
    d_num3 = d_num.reshape(col_total, HEADS, HEAD)
    d_expo = d_den[:, :, None] + jnp.einsum(
        "chd,phd->chp", d_num3, value_heads.astype(jnp.float32), precision=HIGHEST_PREC
    )
    d_scores_key = (expo_key * d_expo).astype(jnp.bfloat16)
    d_key_mix = (
        jnp.einsum("chp,chd->phd", d_scores_key, mean_q3, preferred_element_type=jnp.float32)
        * temper
    )
    d_meanq_part = (
        jnp.einsum(
            "chp,phd->chd", d_scores_key, key_heads, preferred_element_type=jnp.float32
        ).reshape(col_total, D)
        * temper
    )
    d_value_mix = jnp.einsum(
        "chp,chd->phd", expo_low.astype(jnp.float32), d_num3, precision=HIGHEST_PREC
    )
    d_meanq_tok = lax.psum(d_meanq_part, ("seq", "grp"))
    d_sums = (
        jnp.concatenate([d_mean_q_mix + d_meanq_tok, d_mean_k_mix + d_meank_tok], axis=1)
        / counts_f[:, None]
    )
    d_land_rows = jnp.dot(col_hot.astype(jnp.float32), d_sums, precision=HIGHEST_PREC)
    d_queries = d_query_tok.reshape(TOK_DEV, D) + d_land_rows[:, :D]
    d_keys = d_key_mix.reshape(TOK_DEV, D) + d_land_rows[:, D:]
    d_values = d_value_mix.reshape(TOK_DEV, D) + d_values_conv
    d_proj_low = jnp.concatenate([d_queries, d_keys, d_values], axis=1).astype(jnp.bfloat16)
    grad_qkv = contract_rows(tokens, d_proj_low)
    input_grad = (d_hidden_one + contract_cols(d_proj_low, w_qkv)).astype(jnp.bfloat16)
    grad_norms = jnp.stack([d_gain_one, d_shift_one, d_gain_two, d_shift_two])
    group_qkv, group_out, group_up, group_down, group_norm = (
        lax.psum_scatter(grad_qkv, ("seq", "grp"), scatter_dimension=0, tiled=True),
        lax.psum_scatter(grad_out, ("seq", "grp"), scatter_dimension=0, tiled=True),
        lax.psum_scatter(grad_up, ("seq", "grp"), scatter_dimension=0, tiled=True),
        lax.psum_scatter(grad_down, ("seq", "grp"), scatter_dimension=0, tiled=True),
        lax.psum_scatter(grad_norms, ("seq", "grp"), scatter_dimension=1, tiled=True),
    )
    shard_qkv, shard_out, shard_up, shard_down, shard_norm, conv_rep = (
        lax.psum(group_qkv.astype(jnp.bfloat16), "rep").astype(jnp.float32),
        lax.psum(group_out.astype(jnp.bfloat16), "rep").astype(jnp.float32),
        lax.psum(group_up.astype(jnp.bfloat16), "rep").astype(jnp.float32),
        lax.psum(group_down.astype(jnp.bfloat16), "rep").astype(jnp.float32),
        lax.psum(group_norm.astype(jnp.bfloat16), "rep").astype(jnp.float32),
        lax.psum(grad_conv.astype(jnp.bfloat16), "rep").astype(jnp.float32),
    )
    local_sq = (
        jnp.sum(shard_qkv * shard_qkv)
        + jnp.sum(shard_out * shard_out)
        + jnp.sum(shard_up * shard_up)
        + jnp.sum(shard_down * shard_down)
        + jnp.sum(shard_norm * shard_norm)
    )
    total_sq, conv_total = lax.psum((local_sq, conv_rep), ("seq", "grp"))
    grad_total = jnp.sqrt(total_sq + jnp.sum(conv_total * conv_total))
    clip_factor = MAX_NORM / jnp.maximum(grad_total, MAX_NORM)
    qkv_new = adamw(
        qkv_weight, qkv_first, qkv_second, shard_qkv, clip_factor, RATE_MATRIX, DECAY_RATE
    )
    out_new = adamw(
        out_weight, out_first, out_second, shard_out, clip_factor, RATE_MATRIX, DECAY_RATE
    )
    up_new = adamw(up_weight, up_first, up_second, shard_up, clip_factor, RATE_MATRIX, DECAY_RATE)
    down_new = adamw(
        down_weight, down_first, down_second, shard_down, clip_factor, RATE_MATRIX, DECAY_RATE
    )
    norm_new = adamw(norm_params, norm_first, norm_second, shard_norm, clip_factor, RATE_NORM, 0.0)
    conv_new = adamw(conv_kernel, conv_first, conv_second, conv_total, clip_factor, RATE_CONV, 0.0)
    return (
        result.astype(jnp.bfloat16),
        input_grad,
        grad_total,
        qkv_new[0],
        qkv_new[1],
        qkv_new[2],
        out_new[0],
        out_new[1],
        out_new[2],
        up_new[0],
        up_new[1],
        up_new[2],
        down_new[0],
        down_new[1],
        down_new[2],
        norm_new[0],
        norm_new[1],
        norm_new[2],
        conv_new[0],
        conv_new[1],
        conv_new[2],
    )


SHARD = D // GRP_DEV
BLK = (SHARD, D)


class Spot:
    def __init__(self):
        self.rep, self.seq, self.grp = lax.axis_index("rep"), lax.axis_index("seq"), lax.axis_index("grp")
        self.me = self.seq * 2 + self.grp
        self.xn = self.rep + 1 - 2 * lax.rem(self.rep, 2)
        self.yn = lax.rem(self.rep + 2, 4)
        self.dn = 3 - self.rep
        self.to_x = (self.xn, self.seq, self.grp)
        self.to_y = (self.yn, self.seq, self.grp)
        self.to_d = (self.dn, self.seq, self.grp)
        self.to_core = (self.rep, self.seq, 1 - self.grp)

    def z(self, step):
        return lax.rem(self.seq + step, 4)

    def to_z(self, step):
        return (self.rep, self.z(step), self.grp)

    def greet_all(self):
        self.signal_all()
        self.wait_all()

    def wait_all(self):
        pl.semaphore_wait(pltpu.get_barrier_semaphore(), GRP_DEV + 2)

    def signal_all(self):
        barrier = pltpu.get_barrier_semaphore()
        for device in (self.to_x, self.to_y, self.to_d):
            pl.semaphore_signal(barrier, inc=1, device_id=device, device_id_type=MESH_ID)
        for _, other in group_peers(self.me):
            pl.semaphore_signal(barrier, inc=1, device_id=place(self.rep, other), device_id_type=MESH_ID)


CHUNKS = 1
CHUNK = SHARD // CHUNKS
EARLY = tuple(range(CHUNKS))
UP, DOWN = CHUNKS, CHUNKS + 1


def unit_of(refs, part, shard, quarter):
    if part < UP:
        row = pl.multiple_of(shard * SHARD + part * CHUNK, CHUNK)
        return refs[0].at[pl.ds(row, CHUNK), pl.ds(pl.multiple_of(quarter * D, D), D)]
    if part == UP:
        row = pl.multiple_of(shard * SHARD, SHARD)
        return refs[1].at[pl.ds(row, SHARD), pl.ds(pl.multiple_of(quarter * D, D), D)]
    row = pl.multiple_of(shard * 4 * SHARD + quarter * SHARD, SHARD)
    return refs[2].at[pl.ds(row, SHARD), :]


def shard_of(refs, part, shard):
    if part < UP:
        row = pl.multiple_of(shard * SHARD + part * CHUNK, CHUNK)
        return refs[0].at[pl.ds(row, CHUNK), :]
    rows = SHARD if part == UP else 4 * SHARD
    return refs[part - UP + 1].at[pl.ds(pl.multiple_of(shard * rows, SHARD), rows), :]


class Gather:
    def __init__(self, spot, refs, sems):
        self.spot, self.refs = spot, refs
        (self.zs, self.zr, self.xs, self.xr, self.ys, self.yr, self.fs, self.fr, self.cs, self.cr) = sems

    def unit(self, part, seq, quarter):
        return unit_of(self.refs, part, seq * 2 + self.spot.grp, quarter)

    def start(self, part):
        spot = self.spot
        mine = self.unit(part, spot.seq, spot.rep)
        for sign in (1, -1):
            @pl.when((spot.seq + sign >= 0) & (spot.seq + sign <= 3))
            def _():
                push(mine, mine, self.zs.at[part, (sign + 1) // 2, spot.seq], self.zr.at[part, spot.seq],
                     (spot.rep, spot.seq + sign, spot.grp))
        own = shard_of(self.refs, part, spot.me)
        push(own, own, self.cs.at[part, 12], self.cr.at[part, 12], spot.to_core)

    def hop(self, part, far, spread=True):
        spot = self.spot
        for sign in (1, -1):
            src = lax.rem(spot.seq - sign * far + 4, 4)

            @pl.when((spot.seq - sign * far >= 0) & (spot.seq - sign * far <= 3))
            def _():
                unit = self.unit(part, src, spot.rep)
                arrive(unit, self.zr.at[part, src])

                @pl.when((spot.seq + sign >= 0) & (spot.seq + sign <= 3))
                def _():
                    push(unit, unit, self.zs.at[part, (sign + 1) // 2, src], self.zr.at[part, src],
                         (spot.rep, spot.seq + sign, spot.grp))

                if spread:
                    self.give(part, src)

    def give(self, part, src):
        spot = self.spot
        unit = self.unit(part, src, spot.rep)

        push(unit, unit, self.xs.at[part, src], self.xr.at[part, src], spot.to_x)
        push(unit, unit, self.ys.at[part, src], self.yr.at[part, src], spot.to_y)
        push(unit, unit, self.cs.at[part, src], self.cr.at[part, src], spot.to_core)

    def spread(self, part):
        for src in self.others():
            self.give(part, src)

    def others(self):
        return [self.spot.z(step) for step in range(1, 4)]

    def relay(self, part):
        spot = self.spot
        for src in self.others():
            unit = self.unit(part, src, spot.xn)
            arrive(unit, self.xr.at[part, src])

            @pl.when(lax.rem(src + part, 2) == 0)
            def _():
                push(unit, unit, self.fs.at[part, src], self.fr.at[part, src], spot.to_y)

            push(unit, unit, self.cs.at[part, 4 + src], self.cr.at[part, 4 + src], spot.to_core)

            unit = self.unit(part, src, spot.yn)
            arrive(unit, self.yr.at[part, src])

            @pl.when(lax.rem(src + part, 2) == 1)
            def _():
                push(unit, unit, self.fs.at[part, src], self.fr.at[part, src], spot.to_x)

            push(unit, unit, self.cs.at[part, 8 + src], self.cr.at[part, 8 + src], spot.to_core)

    def last(self, part):
        spot = self.spot
        for src in self.others():
            unit = self.unit(part, src, spot.dn)
            arrive(unit, self.fr.at[part, src])
            push(unit, unit, self.cs.at[part, 13 + src], self.cr.at[part, 13 + src], spot.to_core)

    def finish(self, part):
        spot = self.spot
        other = 1 - spot.grp
        arrive(shard_of(self.refs, part, spot.seq * 2 + other), self.cr.at[part, 12])
        for base, quarter in ((0, spot.rep), (4, spot.xn), (8, spot.yn), (13, spot.dn)):
            for src in self.others():
                arrive(unit_of(self.refs, part, src * 2 + other, quarter), self.cr.at[part, base + src])

    def sent(self, part):
        spot = self.spot
        unit = self.unit(part, spot.seq, spot.rep)
        for src in self.others():
            for sem in (self.xs, self.ys, self.fs):
                arrive(unit, sem.at[part, src])
            for base in (0, 4, 8, 13):
                arrive(unit, self.cs.at[part, base + src])
        arrive(shard_of(self.refs, part, spot.me), self.cs.at[part, 12])
        for sign in (1, -1):
            @pl.when((spot.seq + sign >= 0) & (spot.seq + sign <= 3))
            def _():
                arrive(unit, self.zs.at[part, (sign + 1) // 2, spot.seq])

                for far in range(1, 4):
                    src = spot.seq - sign * far

                    @pl.when((src >= 0) & (src <= 3))
                    def _():
                        arrive(unit, self.zs.at[part, (sign + 1) // 2, lax.rem(src + 4, 4)])


def gather_sems():
    dma = pltpu.SemaphoreType.DMA
    return [dma((CHUNKS + 2, 2, 4))] + [dma((CHUNKS + 2, n)) for n in (4, 4, 4, 4, 4, 4, 4, 17, 17)]


class Reduce:
    def __init__(self, spot, own, bufs, sems):
        self.spot, self.own = spot, own
        self.rc, self.first, self.rx, self.ry, self.r2x, self.r2y, self.rz, self.fin = bufs
        (self.cs, self.cr, self.xs, self.xr, self.ys, self.yr, self.x2s, self.x2r, self.y2s, self.y2r,
         self.zs, self.zr, self.fs, self.fr) = sems

    def cell(self, m, seq, quarter):
        if m == 0:
            return self.first.at[pl.ds(pl.multiple_of((quarter * 4 + seq) * SHARD, SHARD), SHARD), :]
        return self.rc.at[m - 1, seq, quarter]

    def bump(self, m, seq, quarter, *others):
        cell = self.cell(m, seq, quarter)
        total = cell[...].astype(F32)
        for other in others:
            total = total + other.astype(F32)
        cell[...] = total.astype(BF)

    def chip_sent(self, m):
        arrive(self.rc.at[0], self.cs.at[m])

    def chip(self, m, quarters=(0, 1, 2, 3)):
        spot = self.spot
        for quarter in quarters:
            for seq in range(4):
                push(self.own(m, seq * 2 + 1 - spot.grp, quarter), self.cell(m, seq, quarter),
                     self.cs.at[m], self.cr.at[m, quarter], spot.to_core)

    def plane(self, m, quarters=(0, 1, 2, 3)):
        spot = self.spot
        for quarter in quarters:
            arrive(self.rc.at[0, :, quarter], self.cr.at[m, quarter])

            @pl.loop(0, 4)
            def _(seq):
                self.bump(m, seq, quarter, self.own(m, seq * 2 + spot.grp, quarter)[...])

            @pl.when(spot.xn == quarter)
            def _():
                self.to_plane(m, quarter, 0, True, False)

            @pl.when(spot.yn == quarter)
            def _():
                self.to_plane(m, quarter, 0, False, True)

            @pl.when(spot.dn == quarter)
            def _():
                self.to_plane(m, quarter, 1, True, True)

    def to_plane(self, m, quarter, slot, along_x, along_y):
        spot = self.spot
        for j in range(2):
            if along_x:
                push(self.cell(m, j, quarter), self.rx.at[m, j, slot], self.xs.at[m], self.xr.at[m], spot.to_x)
            if along_y:
                push(self.cell(m, 2 + j, quarter), self.ry.at[m, j, slot], self.ys.at[m], self.yr.at[m], spot.to_y)

    def plane_two(self, m):
        spot = self.spot
        arrive(self.rx.at[m], self.xr.at[m])

        @pl.loop(0, 2)
        def _(j):
            self.bump(m, j, spot.yn, self.rx[m, j, 1])

        for j in range(2):
            push(self.cell(m, j, spot.yn), self.r2y.at[m, j], self.y2s.at[m], self.y2r.at[m], spot.to_y)
        arrive(self.ry.at[m], self.yr.at[m])

        @pl.loop(0, 2)
        def _(j):
            self.bump(m, 2 + j, spot.xn, self.ry[m, j, 1])

        for j in range(2):
            push(self.cell(m, 2 + j, spot.xn), self.r2x.at[m, j], self.x2s.at[m], self.x2r.at[m], spot.to_x)

    def line(self, m):
        spot = self.spot
        arrive(self.r2y.at[m], self.y2r.at[m])
        arrive(self.r2x.at[m], self.x2r.at[m])

        @pl.loop(0, 2)
        def _(j):
            self.bump(m, j, spot.rep, self.rx[m, j, 0], self.r2y[m, j])
            self.bump(m, 2 + j, spot.rep, self.ry[m, j, 0], self.r2x[m, j])

        near = spot.seq + 1 - 2 * lax.rem(spot.seq, 2)
        for slot, dest in enumerate((near, lax.rem(near + 2, 4))):
            push(self.cell(m, dest, spot.rep), self.rz.at[m, slot], self.zs.at[m, 0], self.zr.at[m, 0],
                 (spot.rep, near, spot.grp))

    def line_two(self, m):
        spot = self.spot
        far = spot.z(2)
        pair = self.rz.at[m, pl.ds(0, 2)]
        arrive(pair, self.zr.at[m, 0])
        self.bump(m, far, spot.rep, self.rz[m, 1])
        push(self.cell(m, far, spot.rep), self.rz.at[m, 2], self.zs.at[m, 1], self.zr.at[m, 1], spot.to_z(2))

    def total(self, m):
        spot = self.spot
        arrive(self.rz.at[m, 2], self.zr.at[m, 1])
        total = (
            self.cell(m, spot.seq, spot.rep)[...].astype(F32) + self.rz[m, 0].astype(F32) + self.rz[m, 2].astype(F32)
        ).astype(BF)
        self.fin[m, spot.rep] = total
        value = total.astype(F32)
        value = value * value
        rows = value[0:8]
        for k in range(1, SHARD // 8):
            rows = rows + value[8 * k : 8 * k + 8]
        square = rows[:, 0:128]
        for k in range(1, D // 128):
            square = square + rows[:, 128 * k : 128 * k + 128]
        return square

    def share(self, m):
        spot = self.spot
        mine = self.fin.at[m, spot.rep]
        devices = (spot.to_x, spot.to_y, spot.to_d) if m == 0 else (spot.to_x, spot.to_y)
        for step, device in enumerate(devices):
            push(mine, mine, self.fs.at[m, step], self.fr.at[m, spot.rep], device)

    def share_on(self, m):
        spot = self.spot
        source, device = (spot.yn, spot.to_x) if m == 2 else (spot.xn, spot.to_y)
        block = self.fin.at[m, source]
        arrive(block, self.fr.at[m, source])
        push(block, block, self.fs.at[m, 2], self.fr.at[m, source], device)

    def done(self, m):
        spot = self.spot
        rest = ((spot.xn, spot.yn, spot.dn), (spot.yn, spot.dn), (spot.xn, spot.dn))[m]
        for other in rest:
            arrive(self.fin.at[m, other], self.fr.at[m, other])

    def sent(self, m):
        arrive(self.rx.at[m], self.xs.at[m])
        arrive(self.ry.at[m], self.ys.at[m])
        arrive(self.r2x.at[m], self.x2s.at[m])
        arrive(self.r2y.at[m], self.y2s.at[m])
        arrive(self.rz.at[m, pl.ds(0, 2)], self.zs.at[m, 0])
        arrive(self.rz.at[m, 2], self.zs.at[m, 1])
        for step in range(3):
            arrive(self.fin.at[m, 0], self.fs.at[m, step])


def reduce_bufs():
    vm = pltpu.VMEM
    return [vm((2, 4, 4, *BLK), BF), vm((3, 2, 2, *BLK), BF), vm((3, 2, 2, *BLK), BF),
            vm((3, 2, *BLK), BF), vm((3, 2, *BLK), BF), vm((3, 3, *BLK), BF)]


def reduce_sems():
    dma = pltpu.SemaphoreType.DMA
    return [dma((3,)), dma((3, 4))] + [dma((3,)) for _ in range(8)] + [dma((3, 2)), dma((3, 2)), dma((3, 3)), dma((3, 4))]


class Small:
    def __init__(self, spot, src, one, two, pair, sems):
        self.spot, self.src, self.one, self.two, self.pair = spot, src, one, two, pair
        self.s1, self.r1, self.sp, self.rp, self.s2, self.r2 = sems

    def start(self):
        spot = self.spot
        for step, device in enumerate((spot.to_x, spot.to_y, spot.to_d)):
            push(self.src, self.one.at[spot.rep], self.s1.at[step], self.r1.at[spot.rep], device)

    def middle(self):
        spot = self.spot
        total = self.src[...]
        for other in (spot.xn, spot.yn, spot.dn):
            arrive(self.one.at[other], self.r1.at[other])
            total = total + self.one[other]
        self.pair[0] = total
        push(self.pair.at[0], self.pair.at[1], self.sp.at[0], self.rp.at[0], spot.to_core)

    def across(self):
        spot = self.spot
        arrive(self.pair.at[1], self.rp.at[0])
        self.two[spot.seq] = self.pair[0] + self.pair[1]
        mine = self.two.at[spot.seq]
        for step in range(1, 4):
            push(mine, mine, self.s2.at[step - 1], self.r2.at[spot.seq], spot.to_z(step))

    def end(self):
        spot = self.spot
        for step in range(1, 4):
            arrive(self.two.at[spot.z(step)], self.r2.at[spot.z(step)])
        total = self.two[0] + self.two[1] + self.two[2] + self.two[3]
        arrive(self.pair.at[0], self.sp.at[0])
        for step in range(3):
            arrive(self.one.at[0], self.s1.at[step])
            arrive(self.two.at[0], self.s2.at[step])
        return total


TOK = 256

TEMPER = HEAD ** (-0.5)
MESH_ID = pl.DeviceIdType.MESH
BF = jnp.bfloat16
F32 = jnp.float32
EXT = 384


def nn(left, right):
    return jnp.dot(left, right, preferred_element_type=F32)


def nt(left, right):
    return lax.dot_general(left, right, (((1,), (1,)), ((), ())), preferred_element_type=F32)


def tn(left, right):
    return lax.dot_general(left, right, (((0,), (0,)), ((), ())), preferred_element_type=F32)


def iota(shape, dim):
    return lax.broadcasted_iota(jnp.int32, shape, dim)


def split(value):
    high = value.astype(BF)
    return high, (value - high.astype(F32)).astype(BF)


def lane_head(shape):
    return iota(shape, len(shape) - 1) // HEAD


def block_diag(value):
    width = value.shape[1]
    heads = width // HEAD
    tiled = jnp.concatenate([value] * heads, axis=0)
    keep = (iota((width, width), 0) // HEAD) == (iota((width, width), 1) // HEAD)
    return jnp.where(keep, tiled, jnp.zeros_like(tiled))


def left_of(value):
    high, low = split(value)
    return jnp.concatenate([high, low], axis=0)


def right_of(value):
    high, low = split(value)
    return block_diag(high), block_diag(low)


def mm_parts(left, right):
    rows = left.shape[0] // 2
    both = nn(left, right[0])
    return both[:rows] + both[rows:] + nn(left[:rows], right[1])


def mm(left, right):
    return mm_parts(left_of(left), right_of(right))


def packed_eye(width):
    return (iota((LAND, width), 0) == iota((LAND, width), 1) % HEAD).astype(F32)


def head_total(row):
    heads = lane_head(row.shape)
    out = jnp.zeros_like(row)
    for head in range(row.shape[1] // HEAD):
        mine = heads == head
        out = jnp.where(mine, jnp.sum(jnp.where(mine, row, 0.0), axis=1, keepdims=True), out)
    return out


def head_rows(value, reduce_fn, neutral):
    heads = lane_head(value.shape)
    out = jnp.zeros_like(value)
    for head in range(value.shape[1] // HEAD):
        mine = heads == head
        out = jnp.where(mine, reduce_fn(jnp.where(mine, value, neutral), axis=1, keepdims=True), out)
    return out


def kernel_two(query_marks, key_marks):
    scores = nt(query_marks, block_diag(key_marks)) * TEMPER
    scores_t = nt(key_marks, block_diag(query_marks)) * TEMPER
    expo = jnp.exp(scores - head_rows(scores, jnp.max, -jnp.inf))
    plain = expo / head_rows(expo, jnp.sum, 0.0)
    expo_t = jnp.exp(scores_t - jnp.max(scores_t, axis=0, keepdims=True))
    flipped = expo_t / jnp.sum(expo_t, axis=0, keepdims=True)
    return plain, flipped


def newton(plains, flippeds, save):
    lefts = [left_of(p) for p in plains]
    invs = [
        f / head_total(jnp.sum(f * f, axis=0, keepdims=True)) for f in flippeds
    ]
    for it in range(NS_STEPS):
        prods = [mm_parts(a, right_of(z)) for a, z in zip(lefts, invs)]
        prights = [right_of(p) for p in prods]
        squares = [mm_parts(left_of(p), r) for p, r in zip(prods, prights)]
        steps = [mm_parts(left_of(z), r) for z, r in zip(invs, prights)]
        for index in range(len(invs)):
            save(it, index, invs[index], prods[index], squares[index], steps[index])
        invs = [
            0.25 * (13.0 * z - 15.0 * s + mm(7.0 * z - s, q)) for z, s, q in zip(invs, steps, squares)
        ]
    return invs


def lens_of(len_ref):
    l0, l1, l2, l3 = len_ref[0, 0], len_ref[0, 1], len_ref[0, 2], len_ref[0, 3]
    return (l0, l1, l2, l3), (0, l0, l0 + l1, l0 + l1 + l2)


def choose(item, values):
    out = jnp.where(item == 0, values[0], values[1])
    out = jnp.where(item == 2, values[2], out)
    return jnp.where(item == 3, values[3], out)


def column_edges(col, lens, starts):
    item = col // LAND
    seg = col % LAND
    length = choose(item, lens)
    start = choose(item, starts)
    low_edge = start + ((seg * length + LAND - 1) >> 6)
    high_edge = start + (((seg + 1) * length + LAND - 1) >> 6)
    return low_edge, high_edge, start, start + length


def item_of(pos, starts):
    return (
        (pos >= starts[1]).astype(jnp.int32)
        + (pos >= starts[2]).astype(jnp.int32)
        + (pos >= starts[3]).astype(jnp.int32)
    )


def pair_lanes(hp):
    return slice(128 * hp, 128 * hp + 128)


def both_heads(value):
    first = iota(value.shape, 1) < HEAD
    zero = jnp.zeros_like(value)
    return jnp.concatenate([jnp.where(first, value, zero), jnp.where(first, zero, value)], axis=0)


def pick_heads(value):
    rows = value.shape[0] // 2
    first = iota((rows, 128), 1) < HEAD
    return jnp.where(first, value[:rows], value[rows:])


def toeplitz(tap_row, same):
    wide = jnp.broadcast_to(tap_row, (TOK, EXT))
    return split(pltpu.roll(wide, 0, 1, stride=1, stride_axis=0) * same)


def conv_pair(taps_ref, hp, same, ext_pair):
    outs = []
    for head in (2 * hp, 2 * hp + 1):
        high, low = toeplitz(taps_ref[head : head + 1, :], same)
        outs.append(nn(high, ext_pair) + nn(low, ext_pair))
    first = iota((TOK, 128), 1) < HEAD
    return jnp.where(first, outs[0], outs[1])


def same_item(first_row, lens, starts, reverse=False):
    shape = (TOK, EXT)
    row = iota(shape, 0)
    if reverse:
        row = TOK - 1 - row
    pos = first_row + row
    other = first_row + iota(shape, 1) - HALO
    total = starts[3] + lens[3]
    inside = (other >= 0) & (other < total) & (item_of(pos, starts) == item_of(other, starts))
    return inside.astype(F32)


def group_peers(me):
    for step in range(1, GRP_DEV):
        yield step, lax.rem(me + step, GRP_DEV)


def place(rep, index):
    return (rep, index // 2, lax.rem(index, 2))


def greet(rep, me):
    barrier = pltpu.get_barrier_semaphore()
    for _, other in group_peers(me):
        pl.semaphore_signal(barrier, inc=1, device_id=place(rep, other), device_id_type=MESH_ID)
    pl.semaphore_wait(barrier, GRP_DEV - 1)


def push(src, dst, send_sem, recv_sem, device):
    copy = pltpu.make_async_remote_copy(
        src_ref=src, dst_ref=dst, send_sem=send_sem, recv_sem=recv_sem,
        device_id=device, device_id_type=MESH_ID,
    )
    copy.start()
    return copy


def attend_kernel(
    len_ref, x_ref, qkv_hbm, out_hbm, up_hbm, down_hbm, norm_ref, taps_ref,
    w_ref, wu_ref, wd_ref, wn_ref, q_ref, k_ref, v_ref, qm_ref, km_ref, wm_ref, a_ref, ext_ref,
    res_ref, vloc_ref, dloc_ref, resl_ref, vl_ref, dl_ref,
    win, halo, nd_src, nd_buf, wml, bias_cp, bias_pc, num_s, den_s, probs,
    qkv_st, out_st, up_st, down_st, hot_s, same_s, cv_s, res_s, wu_st, wd_st, norm_st, taps_s,
    win_s, win_r, halo_s, halo_r, nd_s, nd_r, wml_s, wml_r, load_s, norm_s, norm_r, *gather_sem,
):
    loads = [
        pltpu.make_async_copy(src, dst, load_s.at[i])
        for i, (src, dst) in enumerate(
            ((qkv_hbm, qkv_st), (out_hbm, out_st), (up_hbm, up_st), (down_hbm, down_st))
        )
    ]
    for load in loads:
        load.start()
    spot = Spot()
    rep, me = spot.rep, spot.me
    first_row = me * TOK
    is_owner = (me >= 1) & (me <= 6)
    lens, starts = lens_of(len_ref)
    def masks_for_columns():
        shape = (COLS, TOK)
        pos = first_row + iota(shape, 1)
        lo, hi, begin, end = column_edges(iota(shape, 0), lens, starts)
        hot_s[...] = ((pos >= lo) & (pos < hi)).astype(BF)
        bias_cp[...] = jnp.where((pos >= begin) & (pos < end), 0.0, -1e30)
        pshape = (TOK, COLS)
        ppos = first_row + iota(pshape, 0)
        _, _, pbegin, pend = column_edges(iota(pshape, 1), lens, starts)
        bias_pc[...] = jnp.where((ppos >= pbegin) & (ppos < pend), 0.0, -1e30)
        same_s[...] = same_item(first_row, lens, starts)

    gather = Gather(spot, (w_ref, wu_ref, wd_ref), gather_sem)
    row = pl.multiple_of(me * SHARD, SHARD)
    spot.signal_all()
    masks_for_columns()
    loads[0].wait()
    loads[1].wait()
    w_ref[pl.ds(row, SHARD), : 3 * D] = qkv_st[...].astype(BF)
    w_ref[pl.ds(row, SHARD), 3 * D :] = out_st[...].astype(BF)
    spot.wait_all()
    gather.start(0)
    loads[2].wait()
    loads[3].wait()
    wu_st[...] = up_st[...].astype(BF)
    wd_st[...] = down_st[...].astype(BF)
    own_up = pltpu.make_async_copy(wu_st, shard_of(gather.refs, UP, me), load_s.at[5])
    own_down = pltpu.make_async_copy(wd_st, shard_of(gather.refs, DOWN, me), load_s.at[6])
    own_up.start()
    own_down.start()
    norm_st[...] = jnp.zeros_like(norm_st)
    norm_st[0:4, 0:SHARD] = norm_ref[...]
    wn_ref[me] = norm_st[...].astype(BF)
    taps_s[...] = jnp.zeros_like(taps_s)
    taps_s[0:HEADS, 0:KERNEL] = taps_ref[...]
    own_up.wait()
    own_down.wait()
    gather.hop(0, 1)
    gather.hop(0, 2)
    gather.start(UP)
    gather.hop(0, 3)
    gather.hop(UP, 1, False)
    gather.relay(0)
    gather.hop(UP, 2, False)
    gather.start(DOWN)
    gather.last(0)
    gather.hop(UP, 3, False)
    gather.spread(UP)
    gather.finish(0)

    for part, ref in enumerate((q_ref, k_ref, v_ref)):
        ref[...] = nn(x_ref[...], w_ref[:, D * part : D * part + D]).astype(BF)

    @pl.when(me < GRP_DEV - 1)
    def _():
        push(v_ref.at[pl.ds(TOK - HALO, HALO)], halo.at[0], halo_s.at[0], halo_r.at[0], place(rep, me + 1))

    @pl.when(me > 0)
    def _():
        push(v_ref.at[pl.ds(0, HALO)], halo.at[1], halo_s.at[1], halo_r.at[1], place(rep, me - 1))

    qk = jnp.concatenate([q_ref[...], k_ref[...]], axis=1)
    hot = hot_s[...]
    wshape = (16, TOK)
    seg_hi = lens_edge(iota((LAND, TOK), 0) + 1, lens[1], starts[1])
    base = jnp.sum((seg_hi <= first_row).astype(jnp.int32).astype(F32), axis=0, keepdims=True).astype(jnp.int32)
    seg_w = base + iota(wshape, 0)
    wpos = first_row + iota(wshape, 1)
    whot = (
        (wpos >= lens_edge(seg_w, lens[1], starts[1]))
        & (wpos < lens_edge(seg_w + 1, lens[1], starts[1]))
        & (seg_w < LAND)
    ).astype(BF)
    wsum = nn(whot, qk)
    seg_c = base[:, :128] + iota((16, 128), 0)
    wcount = (lens_edge(seg_c + 1, lens[1], starts[1]) - lens_edge(seg_c, lens[1], starts[1])).astype(F32)
    wcount = jnp.concatenate([wcount] * 12, axis=1)
    win[me] = (wsum / wcount).astype(BF)
    gather.hop(DOWN, 1)
    push(win.at[me], win.at[me], win_s.at[0], win_r.at[me], spot.to_core)
    for step in range(1, 4):
        push(win.at[me], win.at[me], win_s.at[step], win_r.at[me], spot.to_z(step))
    for step, other in group_peers(me):
        push(wn_ref.at[me], wn_ref.at[me], norm_s.at[step - 1], norm_r.at[me], place(rep, other))

    sums = nn(hot, qk)
    clo, chi, _, _ = column_edges(iota((COLS, 128), 0), lens, starts)
    counts = (chi - clo).astype(F32)
    counts6 = jnp.concatenate([counts] * 6, axis=1)
    qm_ref[...] = (sums[:, :D] / counts6).astype(BF)
    km_ref[...] = (sums[:, D:] / counts6).astype(BF)

    @pl.when(me > 0)
    def _():
        pltpu.make_async_copy(halo.at[0], halo.at[0], halo_r.at[0]).wait()
        ext_ref[0:HALO] = halo[0]

    @pl.when(me == 0)
    def _():
        ext_ref[0:HALO] = jnp.zeros((HALO, D), BF)

    @pl.when(me < GRP_DEV - 1)
    def _():
        pltpu.make_async_copy(halo.at[1], halo.at[1], halo_r.at[1]).wait()
        ext_ref[HALO + TOK : 2 * HALO + TOK] = halo[1]

    @pl.when(me == GRP_DEV - 1)
    def _():
        ext_ref[HALO + TOK : 2 * HALO + TOK] = jnp.zeros((HALO, D), BF)

    ext_ref[HALO : HALO + TOK] = v_ref[...]
    ext_ref[2 * HALO + TOK :] = jnp.zeros((EXT - TOK - 2 * HALO, D), BF)
    for hp in range(6):
        lanes = pair_lanes(hp)
        cv_s[:, lanes] = conv_pair(taps_s, hp, same_s[...], ext_ref[:, lanes])
    gather.hop(DOWN, 2)
    for step in range(1, 4):
        slot = spot.z(4 - step) * 2 + spot.grp
        arrive(win.at[slot], win_r.at[slot])
        push(win.at[slot], win.at[slot], win_s.at[3 + step], win_r.at[slot], spot.to_core)
    for step in range(4):
        slot = spot.z(step) * 2 + 1 - spot.grp
        arrive(win.at[slot], win_r.at[slot])
    sshape = (LAND, 128)
    lane_dev = iota((LAND, 128), 1) // 16
    lane_w = iota((LAND, 128), 1) % 16
    seg_end = lens_edge(iota((LAND, 128), 0) + 1, lens[1], starts[1])
    bases = jnp.sum((seg_end <= lane_dev * TOK).astype(jnp.int32).astype(F32), axis=0, keepdims=True).astype(jnp.int32)
    scatter = (iota(sshape, 0) == bases + lane_w).astype(BF)
    long_rows = nn(scatter, win[...].reshape(128, 2 * D))
    qm_ref[LAND : 2 * LAND, :] = long_rows[:, :D].astype(BF)
    km_ref[LAND : 2 * LAND, :] = long_rows[:, D:].astype(BF)

    ones_wide = jnp.ones((TOK, 128), BF)
    ones_row = jnp.ones((8, TOK), BF)
    for hp in range(6):
        lanes = pair_lanes(hp)
        marks = both_heads(qm_ref[:, lanes])
        scores = nt(marks, k_ref[:, lanes]) * TEMPER
        expo = jnp.exp(scores + jnp.concatenate([bias_cp[...]] * 2, axis=0)).astype(BF)
        nd = nn(expo, jnp.concatenate([v_ref[:, lanes], ones_wide], axis=1))
        num = pick_heads(nd[:, :128])
        nd_src[hp, 0:LAND, :] = num[LAND : 2 * LAND]
        nd_src[hp, LAND : LAND + 8, :] = nt(
            ones_row, jnp.concatenate([expo[LAND : 2 * LAND], expo[COLS + LAND : COLS + 2 * LAND]], axis=0)
        )
        num_s[:, lanes] = num
        den_s[:, lanes] = pick_heads(nd[:, 128:])
    for owner in range(1, 7):
        @pl.when(me == owner)
        def _():
            nd_buf[owner] = nd_src[owner - 1]

        @pl.when(me != owner)
        def _():
            push(nd_src.at[owner - 1], nd_buf.at[me], nd_s.at[owner - 1], nd_r.at[me], place(rep, owner))

    gather.hop(DOWN, 3)
    gather.relay(UP)
    wm_ref[...] = jnp.zeros_like(wm_ref)
    has_local = (me == 0) | (me == GRP_DEV - 1)
    slot_rows = (pl.multiple_of(jnp.where(me == 0, 0, 2 * LAND), LAND), 3 * LAND)
    cuts = [(slot, slice(256 * part, 256 * part + 256)) for slot in range(2) for part in range(3)]

    @pl.when(has_local)
    def _():
        def at(ref, slot, lanes):
            return ref[pl.ds(slot_rows[slot], LAND), lanes]

        plains, flippeds = zip(*[kernel_two(at(qm_ref, *c), at(km_ref, *c)) for c in cuts])

        def save(it, index, *mats):
            for m, mat in enumerate(mats):
                res_s[it, index, m] = mat

        invs = newton(plains, flippeds, save)
        keep = pltpu.make_async_copy(res_s, res_ref, load_s.at[4])
        keep.start()
        for (slot, lanes), inv in zip(cuts, invs):
            den = at(den_s, slot, lanes)
            den = jnp.where(den == 0.0, 1.0, den)
            val = at(num_s, slot, lanes) / den
            vloc_ref[slot, :, lanes] = val
            dloc_ref[slot, :, lanes] = den
            wm_ref[pl.ds(slot_rows[slot], LAND), lanes] = mm(inv, val).astype(BF)

    @pl.when(is_owner)
    def _():
        lanes = pl.ds(pl.multiple_of((me - 1) * 128, 128), 128)
        plain, flipped = kernel_two(qm_ref[LAND : 2 * LAND, lanes], km_ref[LAND : 2 * LAND, lanes])

        def save(it, index, *mats):
            for m, mat in enumerate(mats):
                resl_ref[it, m] = mat

        (inv,) = newton([plain], [flipped], save)
        for step, other in group_peers(me):
            pltpu.make_async_copy(nd_buf.at[other], nd_buf.at[other], nd_r.at[other]).wait()
        total = nd_buf[0]
        for j in range(1, GRP_DEV):
            total = total + nd_buf[j]
        row = total[LAND : LAND + 1, :]
        other_row = pltpu.roll(row, HEAD, 1)
        spread = jnp.where(iota((128, 128), 0) < HEAD, row, other_row)
        den = jnp.transpose(spread)[:LAND]
        val = total[:LAND] / den
        vl_ref[...] = val
        dl_ref[...] = den
        wml[me - 1] = mm(inv, val).astype(BF)
        for step, other in group_peers(me):
            push(wml.at[me - 1], wml.at[me - 1], wml_s.at[step - 1], wml_r.at[me - 1], place(rep, other))

    for hp in range(6):
        lanes = pair_lanes(hp)
        scores = nt(q_ref[:, lanes], both_heads(km_ref[:, lanes])) * TEMPER
        for half in range(2):
            expo = jnp.exp(scores[:, COLS * half : COLS * half + COLS] + bias_pc[...])
            probs[hp, :, COLS * half : COLS * half + COLS] = (
                expo / jnp.sum(expo, axis=1, keepdims=True)
            ).astype(BF)

    gather.last(UP)
    gather.relay(DOWN)
    for owner in range(1, 7):
        @pl.when(me != owner)
        def _():
            pltpu.make_async_copy(wml.at[owner - 1], wml.at[owner - 1], wml_r.at[owner - 1]).wait()

        wm_ref[LAND : 2 * LAND, pair_lanes(owner - 1)] = wml[owner - 1]
    for hp in range(6):
        lanes = pair_lanes(hp)
        att = nn(probs[hp], both_heads(wm_ref[:, lanes]))
        a_ref[:, lanes] = (att + cv_s[:, lanes]).astype(BF)

    gather.last(DOWN)
    for step, other in group_peers(me):
        arrive(wn_ref.at[other], norm_r.at[other])
        arrive(wn_ref.at[other], norm_s.at[step - 1])
    for part in (UP, DOWN):
        gather.finish(part)
    for part in (*EARLY, UP, DOWN):
        gather.sent(part)
    @pl.when(has_local)
    def _():
        pltpu.make_async_copy(res_s, res_ref, load_s.at[4]).wait()

    for step, other in group_peers(me):
        pltpu.make_async_copy(win.at[me], win.at[me], win_s.at[step - 1]).wait()
    for owner in range(1, 7):
        @pl.when(me != owner)
        def _():
            pltpu.make_async_copy(nd_src.at[owner - 1], nd_src.at[owner - 1], nd_s.at[owner - 1]).wait()

    @pl.when(is_owner)
    def _():
        for step, other in group_peers(me):
            pltpu.make_async_copy(wml.at[0], wml.at[0], wml_s.at[step - 1]).wait()

    @pl.when(me < GRP_DEV - 1)
    def _():
        pltpu.make_async_copy(halo.at[0], halo.at[0], halo_s.at[0]).wait()

    @pl.when(me > 0)
    def _():
        pltpu.make_async_copy(halo.at[1], halo.at[1], halo_s.at[1]).wait()


def arrive(ref, sem):
    pltpu.make_async_copy(ref, ref, sem).wait()


def lens_edge(seg, length, start):
    return start + ((seg * length + LAND - 1) >> 6)


COLS = ITEMS * LAND
VM = pl.BlockSpec(memory_space=pltpu.VMEM)
SM = pl.BlockSpec(memory_space=pltpu.SMEM)


def attend(item_lengths, tokens, qkv_weight, out_weight, up_weight, down_weight, norm_params, taps):
    sds = jax.ShapeDtypeStruct
    row = sds((TOK, D), BF)
    outs = [sds((D, 4 * D), BF), sds((D, FF), BF), sds((FF, D), BF), sds((8, 16, 128), BF),
            row, row, row, row, row, row, row, sds((EXT, D), BF),
            sds((NS_STEPS, 6, 4, LAND, 256), F32), sds((2, LAND, D), F32), sds((2, LAND, D), F32),
            sds((NS_STEPS, 4, LAND, 128), F32), sds((LAND, 128), F32), sds((LAND, 128), F32)]
    dma = pltpu.SemaphoreType.DMA
    vm = pltpu.VMEM
    scratch = [
        vm((8, 16, 2 * D), BF), vm((2, HALO, D), BF), vm((6, LAND + 8, 128), F32),
        vm((8, LAND + 8, 128), F32), vm((6, LAND, 128), BF),
        vm((COLS, TOK), F32), vm((TOK, COLS), F32), vm((COLS, D), F32),
        vm((COLS, D), F32), vm((6, TOK, 2 * COLS), BF),
        vm((SHARD, 3 * D), F32), vm((SHARD, D), F32), vm((SHARD, FF), F32), vm((4 * SHARD, D), F32),
        vm((COLS, TOK), BF), vm((TOK, EXT), F32), vm((TOK, D), F32),
        vm((NS_STEPS, 6, 4, LAND, 256), F32), vm((SHARD, FF), BF), vm((4 * SHARD, D), BF),
        vm((16, 128), F32), vm((16, EXT), F32),
        dma((7,)), dma((8,)), dma((2,)), dma((2,)), dma((6,)), dma((8,)), dma((7,)), dma((6,)),
        dma((7,)), dma((7,)), dma((8,)), *gather_sems(),
    ]
    anyspace = pl.BlockSpec(memory_space=pl.ANY)
    w_all, w_up, w_down, norms, *rest = pl.pallas_call(
        attend_kernel, out_shape=outs, in_specs=[SM, VM, anyspace, anyspace, anyspace, anyspace, VM, VM],
        out_specs=[VM, anyspace, anyspace] + [VM] * 9 + [anyspace] + [VM] * 5, scratch_shapes=scratch, name="attend",
        compiler_params=pltpu.CompilerParams(collective_id=1, has_side_effects=True, vmem_limit_bytes=60 * 2**20),
    )(item_lengths, tokens, qkv_weight, out_weight, up_weight, down_weight, norm_params, taps)
    return w_all, w_up, w_down, norms, rest


def nt_parts(left, right):
    rows = left.shape[0] // 2
    both = nt(left, right[0])
    return both[:rows] + both[rows:] + nt(left[:rows], right[1])


def flip(value):
    high, low = split(value)
    eye = packed_eye(value.shape[1]).astype(BF)
    return nt(eye, block_diag(high)) + nt(eye, block_diag(low))


def half_sum(value):
    rows = value.shape[0] // 2
    return value[:rows] + value[rows:]


def newton_back(qms, kms, vals, dens, dwms, load, turn=lambda it: None):
    count = len(qms)
    plains = [kernel_two(q, k)[0] for q, k in zip(qms, kms)]
    krights = [right_of(p) for p in plains]
    ups = [nt_parts(left_of(v), right_of(d)) for v, d in zip(vals, dwms)]
    turn(NS_STEPS - 1)
    last = [load(NS_STEPS - 1, i) for i in range(count)]
    finals = [0.25 * (13.0 * m[0] - 15.0 * m[3] + mm(7.0 * m[0] - m[3], m[2])) for m in last]
    dvals = [mm(flip(z), d) for z, d in zip(finals, dwms)]
    dkts = [jnp.zeros_like(p) for p in plains]
    for it in reversed(range(NS_STEPS)):
        if it < NS_STEPS - 1:
            turn(it)
        mats = [load(it, i) for i in range(count)]
        plefts = [left_of(m[1]) for m in mats]
        dys = [0.25 * mm(m[2], u) for m, u in zip(mats, ups)]
        dqs = [0.25 * mm(u, 7.0 * m[0] - m[3]) for m, u in zip(mats, ups)]
        drs = [-3.75 * u - dy for u, dy in zip(ups, dys)]
        dqrs = [right_of(d) for d in dqs]
        dps = [
            mm(dr, m[0]) + mm_parts(pl_, dqr) + mm(dq, m[1])
            for dr, m, pl_, dqr, dq in zip(drs, mats, plefts, dqrs, dqs)
        ]
        nexts = [
            3.25 * u + 7.0 * dy + mm_parts(pl_, right_of(dr))
            for u, dy, pl_, dr in zip(ups, dys, plefts, drs)
        ]
        dkts = [a + mm(m[0], d) for a, m, d in zip(dkts, mats, dps)]
        ups = [n + mm_parts(left_of(d), kr) for n, d, kr in zip(nexts, dps, krights)]
    outs = []
    for i in range(count):
        plain = plains[i]
        fro = head_total(jnp.sum(plain * plain, axis=0, keepdims=True))
        cross = head_total(jnp.sum(ups[i] * plain, axis=0, keepdims=True))
        dk = flip(dkts[i]) + ups[i] / fro - 2.0 * plain * (cross / (fro * fro))
        dscore = plain * (dk - head_rows(plain * dk, jnp.sum, 0.0)) * TEMPER
        dqm = half_sum(nn(left_of(dscore), block_diag(kms[i])))
        dkm = half_sum(nn(left_of(flip(dscore)), block_diag(qms[i])))
        dnum = (dvals[i] / dens[i]).astype(BF)
        dden = -head_rows(dnum.astype(F32) * vals[i], jnp.sum, 0.0)
        outs.append((dnum, dden, dqm, dkm))
    return outs


def twice(value):
    return jnp.concatenate([value, value], axis=0)


ERF_NUM = (0.00022905065861350646, 0.0034082910107109506, 0.050955695062380861, 0.18520832239976145, 1.128379143519084)
ERF_DEN = (-1.1791602954361697e-7, 0.000023547966471313185, 0.0010179625278914885, 0.014070470171167667,
           0.11098505178285362, 0.49746925110067538, 1.0)


def horner(value, coefs):
    out = jnp.full_like(value, coefs[0])
    for coef in coefs[1:]:
        out = out * value + coef
    return out


def erf_of(value):
    value = jnp.clip(value, -3.832506856900711, 3.832506856900711)
    square = value * value
    return value * horner(square, ERF_NUM) / horner(square, ERF_DEN)


def norm_stats(hidden):
    centred = hidden - jnp.mean(hidden, axis=-1, keepdims=True)
    scale = lax.rsqrt(jnp.mean(centred * centred, axis=-1, keepdims=True) + EPS_NORM)
    return centred * scale, scale


def norm_back(unit, scale, gain, grad):
    inner = grad * gain
    mean_one = jnp.mean(inner, axis=-1, keepdims=True)
    mean_two = jnp.mean(inner * unit, axis=-1, keepdims=True)
    return scale * (inner - mean_one - unit * mean_two)


FPART = 512


def back_kernel(
    len_ref, wn_ref, taps_ref, vl_ref, dl_ref, wa_hbm, wu_hbm, wd_hbm, res_hbm,
    x_hbm, a_hbm, cot_hbm, q_hbm, k_hbm, v_hbm, qm_hbm, km_hbm, wm_hbm, ext_hbm, vloc_hbm, dloc_hbm, resl_hbm,
    y_ref, gx_ref, fin_ref, total_ref, norm_ref,
    x_ref, a_ref, cot_ref, q_ref, k_ref, v_ref, qm_ref, km_ref, wm_ref, ext_ref, vloc_ref, dloc_ref, resl_ref, in_s, da_ref, dh_ref,
    wo, wu, wd, act, gu, gd, gains_ref, w_s, ready,
    small_s, rc, rx, ry, r2x, r2y, rz, one, two, pair, sq, q_one, q_two, q_pair,
    halo, dext, dwm_src, dwm_buf, dk1_src, dk1_buf, dn_buf, dq3_src, dq3_buf, ds_buf,
    bias_cp, dwm_s, dkm_s, dqm_s, dnum_s, dden_s, dq_s, dk_s, dv_s, dsum_s, res_s, load_s, res_sem,
    halo_s, halo_r, dwm_ss, dwm_r, dk1_ss, dk1_r, dn_ss, dn_r, dq3_ss, dq3_r, ds_ss, ds_r,
    s1, r1, s2, r2, sp, rp, t1, u1, t2, u2, tp, up, *red_sems,
):
    spot = Spot()
    spot.signal_all()
    rep, me = spot.rep, spot.me
    first_row = me * TOK
    is_owner = (me >= 1) & (me <= 6)
    has_local = (me == 0) | (me == GRP_DEV - 1)
    lens, starts = lens_of(len_ref)
    parts = FF // FPART
    loads = [
        pltpu.make_async_copy(src, dst, in_s.at[i])
        for i, (src, dst) in enumerate((
            (x_hbm, x_ref),
            (a_hbm, a_ref),
            (cot_hbm, cot_ref),
            (q_hbm, q_ref),
            (k_hbm, k_ref),
            (v_hbm, v_ref),
            (qm_hbm, qm_ref),
            (km_hbm, km_ref),
            (wm_hbm, wm_ref),
            (ext_hbm, ext_ref),
            (vloc_hbm, vloc_ref),
            (dloc_hbm, dloc_ref),
            (resl_hbm, resl_ref),
        ))
    ]
    w_loads = [pltpu.make_async_copy(wa_hbm.at[:, pl.ds(3 * D, D)], wo, w_s.at[0])]
    for j in range(parts):
        cols = pl.ds(j * FPART, FPART)
        w_loads.append(pltpu.make_async_copy(wu_hbm.at[:, cols], wu.at[:, cols], w_s.at[1 + 2 * j]))
        w_loads.append(pltpu.make_async_copy(wd_hbm.at[cols], wd.at[cols], w_s.at[2 + 2 * j]))
    for load in (*loads[:3], *w_loads, *loads[3:]):
        load.start()
    load_w = pltpu.make_async_copy(wa_hbm.at[:, pl.ds(0, 3 * D)], wu.at[:, pl.ds(0, 3 * D)], load_s.at[1])

    def residual(it):
        return pltpu.make_async_copy(res_hbm.at[it], res_s.at[it % 2], res_sem.at[it % 2])


    def own(m, shard, quarter):
        row = pl.multiple_of(shard * SHARD, SHARD)
        if m == 0 and quarter == 3:
            return wo.at[pl.ds(row, SHARD), :]
        if m < 2:
            return gu.at[pl.ds(row, SHARD), D * quarter : D * quarter + D]
        return gd.at[pl.ds(pl.multiple_of(4 * row + SHARD * quarter, SHARD), SHARD), :]

    red = Reduce(spot, own, (rc, gd, rx, ry, r2x, r2y, rz, fin_ref), red_sems)
    small = Small(spot, small_s, one, two, pair, (s1, r1, sp, rp, s2, r2))
    squares = Small(spot, sq, q_one, q_two, q_pair, (t1, u1, tp, up, t2, u2))

    def put_slope(j, value):
        for part in range(FPART // 256):
            for row in range(TOK // LAND):
                index = (j * (FPART // 256) + part) * (TOK // LAND) + row
                res_s[index // 24, index // 4 % 6, index % 4] = value[
                    LAND * row : LAND * row + LAND, 256 * part : 256 * part + 256
                ]

    def get_slope(j):
        columns = []
        for part in range(FPART // 256):
            base = (j * (FPART // 256) + part) * (TOK // LAND)
            columns.append(jnp.concatenate(
                [res_s[n // 24, n // 4 % 6, n % 4] for n in range(base, base + TOK // LAND)], axis=0
            ))
        return jnp.concatenate(columns, axis=1)

    gains = jnp.zeros((16, D), F32)
    lane = iota((16, D), 1)
    for i in range(GRP_DEV):
        wide = jnp.concatenate([wn_ref[i].astype(F32), jnp.zeros((16, D - 128), F32)], axis=1)
        gains = jnp.where((lane >= SHARD * i) & (lane < SHARD * i + SHARD), pltpu.roll(wide, SHARD * i, 1), gains)
    gains_ref[...] = gains
    for load in loads[:3]:
        load.wait()
    w_loads[0].wait()
    hidden = x_ref[...].astype(F32) + nn(a_ref[...], wo[...])
    unit, scale = norm_stats(hidden)
    dk_s[...] = unit
    gain_one, shift_one = gains_ref[0:1, :], gains_ref[1:2, :]
    normed_low = (unit * gain_one + shift_one).astype(BF)
    dq_s[...] = jnp.zeros_like(dq_s)
    for j in range(parts):
        cols = slice(j * FPART, j * FPART + FPART)
        w_loads[1 + 2 * j].wait()
        w_loads[2 + 2 * j].wait()
        up = nn(normed_low, wu[:, cols])
        cdf = 0.5 + 0.5 * erf_of(up * (0.5**0.5))
        low = (up * cdf).astype(BF)
        act[:, cols] = low
        put_slope(j, cdf + up * jnp.exp(-0.5 * up * up) * ((2.0 * 3.141592653589793) ** -0.5))
        dq_s[...] += nn(low, wd[cols, :])
    h2 = dk_s[...] * gain_one + shift_one + dq_s[...]
    unit_two, scale_two = norm_stats(h2)
    gain_two, shift_two = gains_ref[2:3, :], gains_ref[3:4, :]
    y_ref[...] = (unit_two * gain_two + shift_two).astype(BF)
    cot = cot_ref[...].astype(F32)
    small_s[2:3, :] = jnp.sum(cot * unit_two, axis=0, keepdims=True)
    small_s[3:4, :] = jnp.sum(cot, axis=0, keepdims=True)
    dh2 = norm_back(unit_two, scale_two, gain_two, cot)
    dv_s[...] = dh2
    down_low = dh2.astype(BF)
    dq_s[...] = jnp.zeros_like(dq_s)
    for j in range(parts):
        cols = slice(j * FPART, j * FPART + FPART)
        gd[cols, :] = tn(act[:, cols], down_low).astype(BF)
    spot.wait_all()
    red.chip(2)
    for j in range(parts):
        cols = slice(j * FPART, j * FPART + FPART)
        act[:, cols] = (get_slope(j) * nt(down_low, wd[cols, :])).astype(BF)
    for j in range(parts):
        cols = slice(j * FPART, j * FPART + FPART)
        du = act[:, cols]
        dq_s[...] += nt(du, wu[:, cols])
        gu[:, cols] = tn(normed_low, du).astype(BF)
    red.chip(1)

    @pl.when(has_local)
    def _():
        residual(NS_STEPS - 1).start()

    load_w.start()
    red.plane(2)
    red.chip_sent(2)
    pl.semaphore_signal(ready, inc=1, device_id=spot.to_core, device_id_type=MESH_ID)
    dx = dv_s[...] + dq_s[...]
    unit = dk_s[...]
    small_s[0:1, :] = jnp.sum(dx * unit, axis=0, keepdims=True)
    small_s[1:2, :] = jnp.sum(dx, axis=0, keepdims=True)
    dh = norm_back(unit, scale, gain_one, dx)
    dh_ref[...] = dh
    low = dh.astype(BF)
    da_ref[...] = nt(low, wo[...]).astype(BF)

    @pl.when(me < GRP_DEV - 1)
    def _():
        push(da_ref.at[pl.ds(TOK - HALO, HALO)], halo.at[0], halo_s.at[0], halo_r.at[0], place(rep, me + 1))

    @pl.when(me > 0)
    def _():
        push(da_ref.at[pl.ds(0, HALO)], halo.at[1], halo_s.at[1], halo_r.at[1], place(rep, me - 1))

    wo[...] = tn(a_ref[...], low).astype(BF)
    pl.semaphore_wait(ready, 1)
    red.chip(0, (3,))
    shape = (COLS, TOK)
    pos = first_row + iota(shape, 1)
    _, _, begin, end = column_edges(iota(shape, 0), lens, starts)
    bias_cp[...] = jnp.where((pos >= begin) & (pos < end), 0.0, -1e30)

    def to_owner(src, buf, send, recv, hp):
        owner = hp + 1

        @pl.when(me == owner)
        def _():
            buf[owner] = src[hp]

        @pl.when(me != owner)
        def _():
            push(src.at[hp], buf.at[me], send.at[hp], recv.at[me], place(rep, owner))

    for load in loads[3:]:
        load.wait()
    for hp in range(6):
        lanes = pair_lanes(hp)
        marks = both_heads(km_ref[:, lanes])
        scores = nt(marks, q_ref[:, lanes]) * TEMPER + twice(bias_cp[...])
        expo = jnp.exp(scores)
        dprob = nt(both_heads(wm_ref[:, lanes]), da_ref[:, lanes])
        lows, dss = [], []
        for half in range(2):
            part = slice(COLS * half, COLS * half + COLS)
            prob = expo[part] / jnp.sum(expo[part], axis=0, keepdims=True)
            inner = jnp.sum(prob * dprob[part], axis=0, keepdims=True)
            lows.append(prob.astype(BF))
            dss.append((prob * (dprob[part] - inner)).astype(BF))
        dscore = jnp.concatenate(dss, axis=0)
        dwm = pick_heads(nn(jnp.concatenate(lows, axis=0), da_ref[:, lanes]))
        dkm = pick_heads(nn(dscore, q_ref[:, lanes])) * TEMPER
        dq_s[:, lanes] = tn(dscore, marks) * TEMPER
        dwm_s[:, lanes] = dwm
        dkm_s[:, lanes] = dkm
        dwm_src[hp] = dwm[LAND : 2 * LAND]
        dk1_src[hp] = dkm[LAND : 2 * LAND].astype(BF)
        to_owner(dwm_src, dwm_buf, dwm_ss, dwm_r, hp)
    for hp in range(6):
        to_owner(dk1_src, dk1_buf, dk1_ss, dk1_r, hp)

    red.plane(1)
    red.chip_sent(1)
    @pl.when(me > 0)
    def _():
        arrive(halo.at[0], halo_r.at[0])
        dext[0:HALO] = halo[0]

    @pl.when(me == 0)
    def _():
        dext[0:HALO] = jnp.zeros((HALO, D), BF)

    @pl.when(me < GRP_DEV - 1)
    def _():
        arrive(halo.at[1], halo_r.at[1])
        dext[HALO + TOK : 2 * HALO + TOK] = halo[1]

    @pl.when(me == GRP_DEV - 1)
    def _():
        dext[HALO + TOK : 2 * HALO + TOK] = jnp.zeros((HALO, D), BF)

    dext[HALO : HALO + TOK] = da_ref[...]
    dext[2 * HALO + TOK :] = jnp.zeros((EXT - TOK - 2 * HALO, D), BF)
    same = same_item(first_row, lens, starts)
    for hp in range(6):
        lanes = pair_lanes(hp)
        dv_s[:, lanes] = conv_pair(taps_ref, hp, same, dext[:, lanes])
    dnum_s[...] = jnp.zeros_like(dnum_s)
    dden_s[...] = jnp.zeros_like(dden_s)
    dqm_s[...] = jnp.zeros_like(dqm_s)
    slot_rows = (pl.multiple_of(jnp.where(me == 0, 0, 2 * LAND), LAND), 3 * LAND)
    cuts = [(slot, slice(256 * part, 256 * part + 256)) for slot in range(2) for part in range(3)]

    @pl.when(has_local)
    def _():
        def at(ref, slot, lanes):
            return ref[pl.ds(slot_rows[slot], LAND), lanes]

        def turn(it):
            residual(it).wait()
            if it > 0:
                residual(it - 1).start()

        outs = newton_back(
            [at(qm_ref, *c) for c in cuts], [at(km_ref, *c) for c in cuts],
            [vloc_ref[slot, :, c] for slot, c in cuts], [dloc_ref[slot, :, c] for slot, c in cuts],
            [at(dwm_s, *c) for c in cuts],
            lambda it, i: [res_s[it % 2, i, m] for m in range(4)],
            turn,
        )
        for (slot, c), (dnum, dden, dqm, dkm) in zip(cuts, outs):
            rows = pl.ds(slot_rows[slot], LAND)
            dnum_s[rows, c] = dnum
            dden_s[rows, c] = dden
            dqm_s[rows, c] = dqm
            dkm_s[rows, c] = dkm_s[rows, c] + dkm

    @pl.when(is_owner)
    def _():
        lanes = pl.ds(pl.multiple_of((me - 1) * 128, 128), 128)
        for step, other in group_peers(me):
            arrive(dwm_buf.at[other], dwm_r.at[other])
        total = dwm_buf[0]
        for j in range(1, GRP_DEV):
            total = total + dwm_buf[j]
        ((dnum, dden, dqm, dkm),) = newton_back(
            [qm_ref[LAND : 2 * LAND, lanes]], [km_ref[LAND : 2 * LAND, lanes]],
            [vl_ref[...]], [dl_ref[...]], [total],
            lambda it, i: [resl_ref[it, m] for m in range(4)],
        )
        high, low = split(dden)
        dn_buf[me - 1, 0:LAND] = dnum
        dn_buf[me - 1, LAND : 2 * LAND] = jnp.where(iota((LAND, 128), 1) % HEAD < 32, high, low)
        for step, other in group_peers(me):
            push(dn_buf.at[me - 1], dn_buf.at[me - 1], dn_ss.at[step - 1], dn_r.at[me - 1], place(rep, other))
        dqm_s[LAND : 2 * LAND, 0:128] = dqm
        dqm_s[LAND : 2 * LAND, 128:256] = dkm

    same_back = same_item(first_row, lens, starts, reverse=True)
    turn = (iota((TOK, TOK), 0) + iota((TOK, TOK), 1) == TOK - 1).astype(BF)
    turned = nn(turn, da_ref[...]).astype(BF)
    for hp in range(6):
        lanes = pair_lanes(hp)
        pairs = nt(both_heads(turned[:, lanes]), ext_ref[:, lanes])
        for half in range(2):
            band = pltpu.roll(pairs[TOK * half : TOK * half + TOK] * same_back, 0, 1, stride=1, stride_axis=0)
            small_s[4 + 2 * hp + half : 5 + 2 * hp + half, :EXT] = jnp.sum(band, axis=0, keepdims=True)
    small_s[4:, EXT:] = jnp.zeros((HEADS, D - EXT), F32)
    small.start()
    red.plane_two(2)

    for owner in range(1, 7):
        lanes = pair_lanes(owner - 1)

        @pl.when(me != owner)
        def _():
            arrive(dn_buf.at[owner - 1], dn_r.at[owner - 1])

        dnum_s[LAND : 2 * LAND, lanes] = dn_buf[owner - 1, 0:LAND]
        packed = dn_buf[owner - 1, LAND : 2 * LAND].astype(F32)
        one = packed[:, 0:1] + packed[:, 32:33]
        two = packed[:, 64:65] + packed[:, 96:97]
        dden_s[LAND : 2 * LAND, lanes] = jnp.where(iota((LAND, 128), 1) < HEAD, one, two)
    for hp in range(6):
        lanes = pair_lanes(hp)
        marks = both_heads(qm_ref[:, lanes])
        expo = jnp.exp(nt(marks, k_ref[:, lanes]) * TEMPER + twice(bias_cp[...]))
        dnum = both_heads(dnum_s[:, lanes])
        dden = jnp.concatenate([dden_s[:, 128 * hp : 128 * hp + 1], dden_s[:, 128 * hp + 64 : 128 * hp + 65]], axis=0)
        dscore = (expo * (nt(dnum, v_ref[:, lanes]) + dden)).astype(BF)
        dqm = pick_heads(nn(dscore, k_ref[:, lanes])) * TEMPER
        dk_s[:, lanes] = tn(dscore, marks) * TEMPER
        dv_s[:, lanes] += tn(expo.astype(BF), dnum)
        dq3_src[hp] = dqm[LAND : 2 * LAND].astype(BF)
        to_owner(dq3_src, dq3_buf, dq3_ss, dq3_r, hp)

        @pl.when(jnp.logical_not(is_owner))
        def _():
            dqm_s[:, lanes] += dqm

    value_cols = slice(2 * D, 3 * D)
    act[:, value_cols] = dv_s[...].astype(BF)
    gu[:, value_cols] = tn(x_ref[...], act[:, value_cols]).astype(BF)
    red.chip(0, (2,))
    red.plane_two(1)
    red.plane(0, (3,))
    clo, chi, _, _ = column_edges(iota((COLS, 128), 0), lens, starts)
    counts = (chi - clo).astype(F32)

    @pl.when(is_owner)
    def _():
        lanes = pl.ds(pl.multiple_of((me - 1) * 128, 128), 128)
        for step, other in group_peers(me):
            arrive(dk1_buf.at[other], dk1_r.at[other])
            arrive(dq3_buf.at[other], dq3_r.at[other])
        total_q = dqm_s[LAND : 2 * LAND, 0:128]
        total_k = dqm_s[LAND : 2 * LAND, 128:256]
        for j in range(GRP_DEV):
            total_q = total_q + dq3_buf[j].astype(F32)
            total_k = total_k + dk1_buf[j].astype(F32)
        ds_buf[me - 1, 0] = (total_q / counts[LAND : 2 * LAND]).astype(BF)
        ds_buf[me - 1, 1] = (total_k / counts[LAND : 2 * LAND]).astype(BF)
        for step, other in group_peers(me):
            push(ds_buf.at[me - 1], ds_buf.at[me - 1], ds_ss.at[step - 1], ds_r.at[me - 1], place(rep, other))

    red.plane(0, (2,))
    for hp in range(6):
        lanes = pair_lanes(hp)
        dsum_s[:, lanes] = (dqm_s[:, lanes] / counts).astype(BF)
        dsum_s[:, D + 128 * hp : D + 128 * hp + 128] = (dkm_s[:, lanes] / counts).astype(BF)
    for owner in range(1, 7):
        @pl.when(me != owner)
        def _():
            arrive(ds_buf.at[owner - 1], ds_r.at[owner - 1])

        hp = owner - 1
        dsum_s[LAND : 2 * LAND, pair_lanes(hp)] = ds_buf[owner - 1, 0]
        dsum_s[LAND : 2 * LAND, D + 128 * hp : D + 128 * hp + 128] = ds_buf[owner - 1, 1]
    pshape = (TOK, COLS)
    ppos = first_row + iota(pshape, 0)
    plo, phi, _, _ = column_edges(iota(pshape, 1), lens, starts)
    hot = ((ppos >= plo) & (ppos < phi)).astype(BF)
    act[:, :D] = (dq_s[...] + nn(hot, dsum_s[:, :D])).astype(BF)
    act[:, D : 2 * D] = (dk_s[...] + nn(hot, dsum_s[:, D:])).astype(BF)
    for part in range(2):
        cols = slice(D * part, D * part + D)
        gu[:, cols] = tn(x_ref[...], act[:, cols]).astype(BF)
        red.chip(0, (part,))
    red.line(2)
    red.line(1)
    red.plane(0, (0, 1))
    load_w.wait()
    gx_ref[...] = (dh_ref[...] + nt(act[:, : 3 * D], wu[:, : 3 * D])).astype(BF)
    red.line_two(2)
    small.middle()
    red.line_two(1)
    red.plane_two(0)
    square = red.total(2)
    red.share(2)
    red.line(0)
    square = square + red.total(1)
    red.share(1)
    small.across()
    red.share_on(2)
    red.line_two(0)
    red.share_on(1)
    total = small.end()
    mine = pltpu.roll(total, lax.rem(D - me * SHARD, D), 1)
    taps_sum = pltpu.roll(total, D - (TOK - 1), 1)
    total_ref[:, :128] = mine[:, :128]
    total_ref[:, 128:] = taps_sum[:, :128]
    lane = iota((16, D), 1)
    real = (iota((16, D), 0) < 4) | ((lane >= TOK - 1) & (lane < TOK - 1 + KERNEL))
    extra = jnp.sum(jnp.where(real, total * total, 0.0), keepdims=True)
    sq[...] = square + red.total(0)
    squares.start()
    red.share(0)
    squares.middle()
    squares.across()
    all_squares = jnp.sum(squares.end(), keepdims=True) + extra
    norm_ref[...] = jnp.broadcast_to(jnp.sqrt(all_squares), (8, 128))
    for m in (2, 1, 0):
        red.done(m)
    red.chip_sent(0)
    for m in range(3):
        red.sent(m)
    for hp in range(6):
        @pl.when(me != hp + 1)
        def _():
            arrive(dwm_src.at[hp], dwm_ss.at[hp])
            arrive(dk1_src.at[hp], dk1_ss.at[hp])
            arrive(dq3_src.at[hp], dq3_ss.at[hp])

    @pl.when(is_owner)
    def _():
        for step, other in group_peers(me):
            arrive(dn_buf.at[0], dn_ss.at[step - 1])
            arrive(ds_buf.at[0], ds_ss.at[step - 1])

    @pl.when(me < GRP_DEV - 1)
    def _():
        arrive(halo.at[0], halo_s.at[0])

    @pl.when(me > 0)
    def _():
        arrive(halo.at[1], halo_s.at[1])


def backward(item_lengths, tokens, cotangent, norms, w_all, w_up, w_down, taps_back, branch, kept):
    sds = jax.ShapeDtypeStruct
    queries, key_rows, value_rows, mean_q, mean_k, mixed, ext, res, vloc, dloc, resl, vl, dl = kept
    outs = [sds((TOK, D), BF), sds((TOK, D), BF), sds((3, 4, *BLK), BF), sds((16, 256), F32), sds((8, 128), F32)]
    dma = pltpu.SemaphoreType.DMA
    vm = pltpu.VMEM
    moved = (tokens, branch, cotangent, queries, key_rows, value_rows, mean_q, mean_k, mixed, ext, vloc, dloc, resl)
    parts = FF // FPART
    scratch = [
        *[vm(a.shape, a.dtype) for a in moved], dma((len(moved),)), vm((TOK, D), BF), vm((TOK, D), F32),
        vm((D, D), BF), vm((D, FF), BF), vm((FF, D), BF), vm((TOK, FF), BF), vm((D, FF), BF), vm((FF, D), BF),
        vm((16, D), F32), dma((1 + 2 * parts,)), pltpu.SemaphoreType.REGULAR,
        vm((16, D), F32), *reduce_bufs(),
        vm((4, 16, D), F32), vm((4, 16, D), F32), vm((2, 16, D), F32), vm((8, 128), F32),
        vm((4, 8, 128), F32), vm((4, 8, 128), F32), vm((2, 8, 128), F32),
        vm((2, HALO, D), BF), vm((EXT, D), BF), vm((6, LAND, 128), F32), vm((8, LAND, 128), F32),
        vm((6, LAND, 128), BF), vm((8, LAND, 128), BF), vm((6, 2 * LAND, 128), BF),
        vm((6, LAND, 128), BF), vm((8, LAND, 128), BF), vm((6, 2, LAND, 128), BF),
        vm((COLS, TOK), F32), vm((COLS, D), F32), vm((COLS, D), F32), vm((COLS, D), F32),
        vm((COLS, D), BF), vm((COLS, D), F32), vm((TOK, D), F32), vm((TOK, D), F32), vm((TOK, D), F32),
        vm((COLS, 2 * D), BF), vm((2, 6, 4, LAND, 256), F32), dma((2,)), dma((2,)),
        dma((2,)), dma((2,)), dma((6,)), dma((8,)), dma((6,)), dma((8,)), dma((7,)), dma((6,)),
        dma((6,)), dma((8,)), dma((7,)), dma((6,)),
        *[dma((n,)) for n in (3, 4, 3, 4, 1, 1, 3, 4, 3, 4, 1, 1)],
        *reduce_sems(),
    ]
    anyspace = pl.BlockSpec(memory_space=pl.ANY)
    return pl.pallas_call(
        back_kernel, out_shape=outs, in_specs=[SM] + [VM] * 4 + [anyspace] * (4 + len(moved)),
        out_specs=[VM] * len(outs), scratch_shapes=scratch, name="backward",
        compiler_params=pltpu.CompilerParams(collective_id=2, has_side_effects=True, vmem_limit_bytes=VMEM_MOST),
    )(item_lengths, norms, taps_back, vl, dl, w_all, w_up, w_down, res, *moved)


VMEM_MOST = 63 * 2**20


ASTEPS = 3
AROWS = SHARD // ASTEPS


def adam_math(weight, one, two, grad, clip, rate, decay):
    grad = grad * clip
    one = BETA_ONE * one + (1.0 - BETA_ONE) * grad
    two = BETA_TWO * two + (1.0 - BETA_TWO) * grad * grad
    first_hat = one * (1.0 / (1.0 - BETA_ONE**STEP))
    second_hat = two * (1.0 / (1.0 - BETA_TWO**STEP))
    return weight - rate * (first_hat / (jnp.sqrt(second_hat) + ADAM_EPS) + decay * weight), one, two


def adam_kernel(norm_ref, total_ref, fin_ref, down_g_ref, *refs):
    ins, outs = refs[:18], refs[18:]
    clip = MAX_NORM / jnp.maximum(norm_ref[0, 0], MAX_NORM)

    def update(group, rows_cols, grad, rate, decay):
        got = [ref[rows_cols] for ref in ins[3 * group : 3 * group + 3]]
        for ref, value in zip(outs[3 * group : 3 * group + 3], adam_math(*got, grad, clip, rate, decay)):
            ref[rows_cols] = value

    for quarter in range(3):
        at = (slice(None), slice(D * quarter, D * quarter + D))
        update(0, at, fin_ref[0, quarter].astype(F32), RATE_MATRIX, DECAY_RATE)
    update(1, (slice(None), slice(None)), fin_ref[0, 3].astype(F32), RATE_MATRIX, DECAY_RATE)
    for quarter in range(4):
        at = (slice(None), slice(D * quarter, D * quarter + D))
        update(2, at, fin_ref[1, quarter].astype(F32), RATE_MATRIX, DECAY_RATE)
    update(3, (slice(None), slice(None)), down_g_ref[...].astype(F32), RATE_MATRIX, DECAY_RATE)
    whole = (slice(None), slice(None))
    update(4, whole, total_ref[0:4, 0:SHARD], RATE_NORM, 0.0)
    update(5, whole, total_ref[4:16, 128 : 128 + KERNEL], RATE_CONV, 0.0)


def adam(norm, total, fin, triples):
    sds = jax.ShapeDtypeStruct
    flat = [a for triple in triples for a in triple]
    row = lambda cols, rows=AROWS: pl.BlockSpec((rows, cols), lambda i: (i, 0))
    keep = lambda shape: pl.BlockSpec(shape, lambda i: (0, 0))
    specs = [row(3 * D)] * 3 + [row(D)] * 3 + [row(FF)] * 3 + [row(D, 4 * AROWS)] * 3
    specs += [keep((4, SHARD))] * 3 + [keep((HEADS, KERNEL))] * 3
    return pl.pallas_call(
        adam_kernel, name="adam", grid=(ASTEPS,),
        out_shape=[sds(a.shape, F32) for a in flat],
        in_specs=[pl.BlockSpec(memory_space=pltpu.SMEM), keep((16, 2 * 128)),
                  pl.BlockSpec((2, 4, AROWS, D), lambda i: (0, 0, i, 0)),
                  pl.BlockSpec((4 * AROWS, D), lambda i: (i + 2 * ASTEPS, 0)), *specs],
        out_specs=specs,
        compiler_params=pltpu.CompilerParams(vmem_limit_bytes=62 * 2**20),
    )(norm, total, fin, fin.reshape(12 * SHARD, D), *flat)


def on_device_fast(
    tokens, cotangent, item_lengths,
    qkv_weight, qkv_first, qkv_second, out_weight, out_first, out_second,
    up_weight, up_first, up_second, down_weight, down_first, down_second,
    norm_params, norm_first, norm_second, conv_kernel, conv_first, conv_second,
):
    taps_back = jnp.pad(conv_kernel[:, ::-1], ((0, 4), (0, EXT - KERNEL)))
    w_all, w_up, w_down, norms, rest = attend(
        item_lengths, tokens, qkv_weight, out_weight, up_weight, down_weight, norm_params, conv_kernel
    )
    queries, key_rows, value_rows, mean_q, mean_k, mixed, branch, value_ext, *resid = rest
    result, input_grad, fin, total, norm = backward(
        item_lengths, tokens, cotangent, norms, w_all, w_up, w_down, taps_back, branch,
        (queries, key_rows, value_rows, mean_q, mean_k, mixed, value_ext, *resid),
    )
    news = adam(
        norm, total, fin,
        (
            (qkv_weight, qkv_first, qkv_second), (out_weight, out_first, out_second),
            (up_weight, up_first, up_second), (down_weight, down_first, down_second),
            (norm_params, norm_first, norm_second), (conv_kernel, conv_first, conv_second),
        ),
    )
    return (result, input_grad, norm[0, 0], *news)


def solution(mesh):
    in_specs = (
        P(("rep", "seq", "grp"), None),
        P(("rep", "seq", "grp"), None),
        P("rep", None),
        P(("seq", "grp"), None),
        P(("seq", "grp"), None),
        P(("seq", "grp"), None),
        P(("seq", "grp"), None),
        P(("seq", "grp"), None),
        P(("seq", "grp"), None),
        P(("seq", "grp"), None),
        P(("seq", "grp"), None),
        P(("seq", "grp"), None),
        P(("seq", "grp"), None),
        P(("seq", "grp"), None),
        P(("seq", "grp"), None),
        P(None, ("seq", "grp")),
        P(None, ("seq", "grp")),
        P(None, ("seq", "grp")),
        P(),
        P(),
        P(),
    )
    out_specs = (
        P(("rep", "seq", "grp"), None),
        P(("rep", "seq", "grp"), None),
        P(),
        P(("seq", "grp"), None),
        P(("seq", "grp"), None),
        P(("seq", "grp"), None),
        P(("seq", "grp"), None),
        P(("seq", "grp"), None),
        P(("seq", "grp"), None),
        P(("seq", "grp"), None),
        P(("seq", "grp"), None),
        P(("seq", "grp"), None),
        P(("seq", "grp"), None),
        P(("seq", "grp"), None),
        P(("seq", "grp"), None),
        P(None, ("seq", "grp")),
        P(None, ("seq", "grp")),
        P(None, ("seq", "grp")),
        P(),
        P(),
        P(),
    )
    fast = dict(mesh.shape) == {"rep": 4, "seq": 4, "grp": 2}
    body = on_device_fast if fast else on_device
    return jax.shard_map(
        body, mesh=mesh, in_specs=in_specs, out_specs=out_specs, check_vma=False
    )
```
